128 devices in a mesh: ctx: 32 (over x, y, core), section: 4 (over z).
Axes of the slice: x: 4, y: 4, z: 4, core: 2. Of those that a mesh axis runs over, the one named last changes fastest.
Arguments:
- query_rows: bfloat16 [65536, 1024], P(('ctx', 'section')), may hold values from -5 to 5
- key_rows: bfloat16 [65536, 128], P(('ctx', 'section')), may hold values from -5 to 5
- value_rows: bfloat16 [65536, 128], P(('ctx', 'section')), may hold values from -5 to 5
- attn_out: bfloat16 [65536, 1024], P(('ctx', 'section')), may hold values from -2 to 2
- out_grad: bfloat16 [65536, 1024], P(('ctx', 'section')), may hold values from -5 to 5
- log_total: float32 [8, 65536], P(None, ('ctx', 'section')), may hold values from -300 to 300, as said below
- doc_lengths: int32 [128], replicated, may hold values from 1 to 4096, as said below
Outputs:
- query_grad: bfloat16 [65536, 1024], P(('ctx', 'section'))
- key_grad: bfloat16 [65536, 128], P(('ctx', 'section'))
- value_grad: bfloat16 [65536, 128], P(('ctx', 'section'))
The draws below stay inside these ranges and needn't reach their ends.
Inputs may be any that keep to these rules, and one draw needn't show every extreme that they name: `log_total`: for every head h and row i, the log of the sum over visible j of exp(score[h, i, j]), with score and visibility from query_rows, key_rows and doc_lengths as in the reference program. `doc_lengths`: the documents fill all 65536 positions; the longest has exactly 4096 tokens.
All inputs are finite; a program needn't handle non-finite values.
Results may differ from the reference program's by a relative error of at most 0.005.
Values may be sent and summed in bfloat16 or wider, within the bound.
A program may use at most 64 MiB of HBM per device.

```python
import math
import jax
import jax.numpy as jnp
from jax import lax

H = 8
HD = 128
TILE = 512
TOKENS = 65536
MAXDOC = 4096
DOCS = 128


very_negative = -1e+30


def draw_key_rows(key, part):
    key = jax.random.fold_in(key, 7)
    drawn = jnp.clip(jax.random.normal(key, (TOKENS, HD), jnp.float32), -5.0, 5.0)
    return drawn.astype(jnp.bfloat16)


def draw_query_rows(key, part):
    key = jax.random.fold_in(key, 13)
    drawn = jnp.clip(jax.random.normal(key, (TOKENS, H * HD), jnp.float32), -5.0, 5.0)
    return drawn.astype(jnp.bfloat16)


def draw_doc_lengths(key, part):
    key = jax.random.fold_in(key, 21)
    weight_key, place_key = jax.random.split(key)
    others = DOCS - 1
    powers = jax.random.randint(weight_key, (others,), 0, 4).astype(jnp.int32)
    weights = jnp.left_shift(jnp.ones((others,), jnp.int32), powers)
    running = jnp.cumsum(weights).astype(jnp.int32)
    whole_weight = running[others - 1]
    spare = TOKENS - MAXDOC - others
    alloc = spare // whole_weight * running + spare % whole_weight * running // whole_weight
    earlier = jnp.concatenate([jnp.zeros((1,), jnp.int32), alloc[:-1]])
    rest = (1 + alloc - earlier).astype(jnp.int32)
    longest_at = jax.random.randint(place_key, (), 0, DOCS).astype(jnp.int32)
    index = jnp.arange(DOCS, dtype=jnp.int32)
    source = jnp.clip(jnp.where(index < longest_at, index, index - 1), 0, others - 1)
    return jnp.where(index == longest_at, MAXDOC, rest[source]).astype(jnp.int32)


def stat_starts(doc_lengths, positions):
    ends = jnp.cumsum(doc_lengths).astype(jnp.int32)
    before = jnp.where(ends[None, :] <= positions[:, None], ends[None, :], 0)
    return jnp.max(before, axis=1).astype(jnp.int32)


def draw_log_total(key, part):
    query_rows = draw_query_rows(key, part)
    key_rows = draw_key_rows(key, part)
    doc_lengths = draw_doc_lengths(key, part)
    width = HD
    heads = H
    scale = 1.0 / math.sqrt(width)
    positions = jnp.arange(TOKENS, dtype=jnp.int32)
    starts = stat_starts(doc_lengths, positions)
    key_pad = jnp.concatenate([jnp.zeros((MAXDOC, width), jnp.bfloat16), key_rows], axis=0)
    block_count = TOKENS // TILE
    tile_count = MAXDOC // TILE + 1
    tile_offsets = jnp.arange(TILE, dtype=jnp.int32)

    def block_stats(block):
        row_first = (block * TILE).astype(jnp.int32)
        queries = lax.dynamic_slice_in_dim(query_rows, row_first, TILE, 0).astype(jnp.float32).reshape(TILE, heads, width)
        row_start = lax.dynamic_slice_in_dim(starts, row_first, TILE, 0)

        def statistics_update(step, carry):
            col_first = (row_first - MAXDOC + step * TILE).astype(jnp.int32)
            key_block_slice = lax.dynamic_slice_in_dim(key_pad, (col_first + MAXDOC).astype(jnp.int32), TILE, 0).astype(jnp.float32)
            key_pos = col_first + tile_offsets
            row_pos = row_first + tile_offsets
            mask = (key_pos[None, :] >= row_start[:, None]) & (key_pos[None, :] <= row_pos[:, None])
            top, total = carry
            score = jnp.einsum('rhd,kd->hrk', queries, key_block_slice, precision=lax.Precision.HIGHEST) * scale
            masked = jnp.where(mask[None], score, very_negative)
            new_top = jnp.maximum(top, jnp.max(masked, axis=2))
            terms = jnp.where(mask[None], jnp.exp(score - new_top[:, :, None]), 0.0)
            return (new_top, total * jnp.exp(top - new_top) + jnp.sum(terms, axis=2))
        start_top = jnp.full((heads, TILE), very_negative, jnp.float32)
        start_total = jnp.zeros((heads, TILE), jnp.float32)
        top, total = lax.fori_loop(0, tile_count, statistics_update, (start_top, start_total))
        return top + jnp.log(total)
    stats = lax.map(block_stats, jnp.arange(block_count, dtype=jnp.int32))
    return stats.transpose(1, 0, 2).reshape(heads, TOKENS).astype(jnp.float32)


def block_scale(stream_key, extent, pieces, least, top_value):
    level = 1.0
    for position, shards_of in pieces:
        steps = jax.random.uniform(jax.random.fold_in(jax.random.fold_in(stream_key, 6), position), (shards_of,), jnp.float32, least / len(pieces), top_value / len(pieces))
        level = level * jnp.repeat(jnp.exp(steps), extent[position] // shards_of).reshape((-1,) + (1,) * (len(extent) - 1 - position))
    return level


def gaussian(rng, dims, scale, limit, pieces=(), held_as=jnp.bfloat16):
    result = jax.random.normal(rng, dims, jnp.float32) * scale
    if len(pieces) > 0:
        result = block_scale(rng, dims, pieces, -0.22, 0.18) * result
    return jnp.clip(result, min=-limit, max=limit).astype(held_as)


def setup_inputs(seed: int = 0) -> dict:
    key_list = jax.random.split(jax.random.key(seed), 8)
    query_rows = draw_query_rows(jax.random.fold_in(key_list[7], 71), 0)
    key_rows = draw_key_rows(jax.random.fold_in(key_list[7], 71), 0)
    value_rows = gaussian(key_list[2], (TOKENS, HD), 1.0, 5.0, ((0, 128),))
    attn_out = gaussian(key_list[3], (TOKENS, H * HD), 0.3, 2.0, ((0, 128),))
    out_grad = gaussian(key_list[4], (TOKENS, H * HD), 1.0, 5.0, ((0, 128),))
    log_total = draw_log_total(jax.random.fold_in(key_list[7], 71), 0)
    doc_lengths = draw_doc_lengths(jax.random.fold_in(key_list[7], 71), 0)
    return dict(query_rows=query_rows, key_rows=key_rows, value_rows=value_rows, attn_out=attn_out, out_grad=out_grad, log_total=log_total, doc_lengths=doc_lengths)


def doc_starts(doc_lengths, positions):
    ends = jnp.cumsum(doc_lengths).astype(jnp.int32)
    before = jnp.where(ends[None, :] <= positions[:, None], ends[None, :], 0)
    return lax.optimization_barrier(jnp.max(before, axis=1)).astype(jnp.int32)

def reference(query_rows, key_rows, value_rows, attn_out, out_grad, log_total, doc_lengths):
    seq_rows = query_rows.shape[0]
    width = key_rows.shape[1]
    heads = query_rows.shape[1] // width
    scale = 1.0 / math.sqrt(width)
    positions = jnp.arange(seq_rows, dtype=jnp.int32)
    starts = doc_starts(doc_lengths, positions)
    pad_rows = jnp.zeros((MAXDOC, width), key_rows.dtype)
    key_pad = jnp.concatenate([pad_rows, key_rows], axis=0)
    value_pad = jnp.concatenate([pad_rows, value_rows], axis=0)
    block_count = seq_rows // TILE
    tile_count = MAXDOC // TILE + 1
    tile_offsets = jnp.arange(TILE, dtype=jnp.int32)

    def block_rows(block):
        row_first = (block * TILE).astype(jnp.int32)
        queries = lax.dynamic_slice_in_dim(query_rows, row_first, TILE, 0).astype(jnp.float32).reshape(TILE, heads, width)
        row_start = lax.dynamic_slice_in_dim(starts, row_first, TILE, 0)
        return (row_first, queries, row_start)

    def tile_keys(row_first, step, row_start):
        col_first = (row_first - MAXDOC + step * TILE).astype(jnp.int32)
        at_pad = (col_first + MAXDOC).astype(jnp.int32)
        key_block_slice = lax.dynamic_slice_in_dim(key_pad, at_pad, TILE, 0).astype(jnp.float32)
        value_block_slice = lax.dynamic_slice_in_dim(value_pad, at_pad, TILE, 0).astype(jnp.float32)
        key_pos = col_first + tile_offsets
        row_pos = row_first + tile_offsets
        mask = (key_pos[None, :] >= row_start[:, None]) & (key_pos[None, :] <= row_pos[:, None])
        needed = col_first + TILE - 1 >= row_start[0]
        return (at_pad, key_block_slice, value_block_slice, mask, needed)
    block_ids = jnp.arange(block_count, dtype=jnp.int32)
    log_totals = log_total.reshape(heads, block_count, TILE).transpose(1, 0, 2)

    def block_grads(carry, inputs):
        block, block_log = inputs
        row_first, queries, row_start = block_rows(block)
        grads = lax.dynamic_slice_in_dim(out_grad, row_first, TILE, 0).astype(jnp.float32).reshape(TILE, heads, width)
        outs = lax.dynamic_slice_in_dim(attn_out, row_first, TILE, 0).astype(jnp.float32).reshape(TILE, heads, width)
        delta = jnp.einsum('rhd,rhd->hr', grads, outs)

        def grad_step(step, inner):
            at_pad, key_block_slice, value_block_slice, mask, needed = tile_keys(row_first, step.astype(jnp.int32), row_start)

            def update(state):
                query_acc, key_acc, value_acc = state
                score = jnp.einsum('rhd,kd->hrk', queries, key_block_slice) * scale
                prob = jnp.where(mask[None], jnp.exp(score - block_log[:, :, None]), 0.0)
                prob_grad = jnp.einsum('rhd,kd->hrk', grads, value_block_slice)
                score_grad = prob * (prob_grad - delta[:, :, None])
                probability_half = lax.optimization_barrier(prob.astype(jnp.bfloat16)).astype(jnp.float32)
                halved_scores = lax.optimization_barrier(score_grad.astype(jnp.bfloat16)).astype(jnp.float32)
                query_acc = query_acc + jnp.einsum('hrk,kd->rhd', halved_scores, key_block_slice)
                key_terms = jnp.einsum('hrk,rhd->kd', halved_scores, queries)
                value_terms = jnp.einsum('hrk,rhd->kd', probability_half, grads)
                key_acc = lax.dynamic_update_slice_in_dim(key_acc, lax.dynamic_slice_in_dim(key_acc, at_pad, TILE, 0) + key_terms, at_pad, 0)
                value_acc = lax.dynamic_update_slice_in_dim(value_acc, lax.dynamic_slice_in_dim(value_acc, at_pad, TILE, 0) + value_terms, at_pad, 0)
                return (query_acc, key_acc, value_acc)
            return lax.cond(needed, update, lambda state: state, inner)
        start_query = jnp.zeros((TILE, heads, width), jnp.float32)
        query_acc, key_acc, value_acc = lax.fori_loop(0, tile_count, grad_step, (start_query, carry[0], carry[1]))
        query_block = (query_acc * scale).astype(jnp.bfloat16).reshape(TILE, heads * width)
        return ((key_acc, value_acc), query_block)
    start_keys = jnp.zeros((seq_rows + MAXDOC, width), jnp.float32)
    start_values = jnp.zeros((seq_rows + MAXDOC, width), jnp.float32)
    sums, query_blocks = lax.scan(block_grads, (start_keys, start_values), (block_ids, log_totals))
    query_grad = query_blocks.reshape(seq_rows, heads * width)
    key_grad = (sums[0][MAXDOC:] * scale).astype(jnp.bfloat16)
    value_grad = sums[1][MAXDOC:].astype(jnp.bfloat16)
    return (query_grad, key_grad, value_grad)
```

```python
import functools
import math

import jax
import jax.numpy as jnp
from jax import lax
from jax.experimental import pallas as pl
from jax.experimental.pallas import tpu as pltpu
from jax.sharding import PartitionSpec as P

W = 128
B = 256
LOG2E = math.log2(math.e)


def nn(a, b):
    return jnp.dot(a, b, preferred_element_type=jnp.float32)


def nt(a, b):
    return lax.dot_general(a, b, (((1,), (1,)), ((), ())), preferred_element_type=jnp.float32)


def place():
    ctx = lax.axis_index("ctx")
    return ctx // 2, lax.axis_index("section"), ctx % 2


def attend_kernel(
    heads, docs_ref, q_ref, g_ref, l2_ref, delta_ref, k_ref, v_ref, dq_ref, dk_ref, dv_ref,
    dqt, dka, dva, bias
):
    column, z, core = place()
    scale = 1.0 / math.sqrt(W)
    lengths = docs_ref[...].astype(jnp.float32)
    docs = lengths.shape[1]
    upto = lax.broadcasted_iota(jnp.int32, (docs, docs), 1) <= lax.broadcasted_iota(
        jnp.int32, (docs, docs), 0
    )
    ends = jnp.sum(jnp.where(upto, lengths, 0.0), axis=1, keepdims=True)
    dka[...] = jnp.zeros_like(dka)
    dva[...] = jnp.zeros_like(dva)
    dqt[...] = jnp.zeros_like(dqt)
    window = (column - 1) * 8 * 2 * B

    def half_of(b):
        return jnp.where(b % 8 >= 4, 1 - core, core)

    def query_block(qb, carry):
        first = column * 16 * B + (z + 4 * (qb // 2)) * 2 * B + (qb % 2) * B
        pos = first.astype(jnp.float32) + lax.broadcasted_iota(jnp.int32, (1, B), 1).astype(
            jnp.float32
        )
        start = jnp.max(jnp.where(ends <= pos, ends, 0.0), axis=0, keepdims=True)
        start_lo = jnp.min(start).astype(jnp.int32)
        start_hi = jnp.max(start).astype(jnp.int32)
        rel = start_lo - window
        lo = rel // (2 * B)
        lo = jnp.where(rel % (2 * B) >= half_of(lo) * B + B, lo + 1, lo)
        diag = 8 + z + 4 * (qb // 2)
        hi = jnp.where(half_of(diag) <= qb % 2, diag + 1, diag)

        def work(b, masked):
            k = k_ref[b]
            v = v_ref[b]
            kt = k.T
            dk = jnp.zeros((B, W), jnp.float32)
            dv = jnp.zeros((B, W), jnp.float32)
            for h in range(heads):
                rows = slice(h * B, (h + 1) * B)
                q = q_ref[qb, rows, :]
                g = g_ref[qb, rows, :]
                x = nt(k, q) * (scale * LOG2E) - l2_ref[qb, :, rows]
                if masked:
                    x = x + bias[...]
                p = jnp.exp2(x)
                ds = p * (nt(v, g) - delta_ref[qb, :, rows])
                ph = p.astype(jnp.bfloat16)
                dh = ds.astype(jnp.bfloat16)
                dv = dv + nn(ph, g)
                dk = dk + nn(dh, q)
                dqt[qb, :, rows] += nn(kt, dh)
            dka[b] += dk
            dva[b] += dv

        def step(b, inner):
            key = window + b * 2 * B + half_of(b) * B
            full = (key >= start_hi) & (key + B - 1 <= first)

            @pl.when(full)
            def _():
                work(b, False)

            @pl.when(jnp.logical_not(full))
            def _():
                kpos = (
                    key + lax.broadcasted_iota(jnp.int32, (B, B), 0)
                ).astype(jnp.float32)
                bias[...] = jnp.where((kpos >= start) & (kpos <= pos), 0.0, -jnp.inf)
                work(b, True)

            return inner

        lax.fori_loop(lo, hi, step, 0)
        for h in range(heads):
            dq_ref[qb, :, h * W : (h + 1) * W] = (
                (dqt[qb, :, h * B : (h + 1) * B] * scale).T.astype(jnp.bfloat16)
            )
        return carry

    lax.fori_loop(0, 4, query_block, 0)
    dk_ref[...] = (dka[...] * scale).astype(jnp.bfloat16)
    dv_ref[...] = dva[...].astype(jnp.bfloat16)


def attend(docs, q, g, l2, delta, k, v, heads):
    vmem = pl.BlockSpec(memory_space=pltpu.VMEM)
    return pl.pallas_call(
        functools.partial(attend_kernel, heads),
        out_shape=(
            jax.ShapeDtypeStruct((4, B, heads * W), jnp.bfloat16),
            jax.ShapeDtypeStruct((16, B, W), jnp.bfloat16),
            jax.ShapeDtypeStruct((16, B, W), jnp.bfloat16),
        ),
        in_specs=[vmem] * 7,
        out_specs=(vmem, vmem, vmem),
        scratch_shapes=[
            pltpu.VMEM((4, W, heads * B), jnp.float32),
            pltpu.VMEM((16, B, W), jnp.float32),
            pltpu.VMEM((16, B, W), jnp.float32),
            pltpu.VMEM((B, B), jnp.float32),
        ],
        compiler_params=pltpu.CompilerParams(vmem_limit_bytes=48 * 1024 * 1024),
        cost_estimate=pl.CostEstimate(
            flops=20 * 10 * heads * B * B * W, bytes_accessed=16 << 20, transcendentals=0
        ),
    )(docs, q, g, l2, delta, k, v)


def on_device(query_rows, key_rows, value_rows, attn_out, out_grad, log_total, doc_lengths):
    column, z, core = place()
    rows, features = query_rows.shape
    heads = features // W
    devices = lax.axis_size("ctx")
    swap = [(i, i ^ 1) for i in range(devices)]
    ahead = [(i, i + 2) for i in range(devices - 2)]
    back = [(i + 2, i) for i in range(devices - 2)]

    def stacked(x):
        return x.reshape(rows // B, B, heads, W).transpose(0, 2, 1, 3).reshape(-1, heads * B, W)

    def lanes(x):
        return x.reshape(heads, rows // B, B).transpose(1, 0, 2).reshape(-1, 1, heads * B)

    delta = jnp.einsum(
        "rhd,rhd->hr",
        out_grad.reshape(rows, heads, W),
        attn_out.reshape(rows, heads, W),
        preferred_element_type=jnp.float32,
    )
    mine = (stacked(query_rows), stacked(out_grad), lanes(log_total * LOG2E), lanes(delta))
    theirs = lax.ppermute(mine, "ctx", swap)

    def pair(a, b):
        return jnp.where(core == 0, jnp.concatenate([a, b]), jnp.concatenate([b, a]))

    q, g, l2, dl = (pair(a, b) for a, b in zip(mine, theirs))

    kv = jnp.stack([key_rows, value_rows]).reshape(2, 2, B, W)
    own_half = kv[:, 0]
    sent_half = kv[:, 1]
    got = lax.ppermute(sent_half, "ctx", swap)
    chunk = jnp.where(core == 0, jnp.stack([own_half, got]), jnp.stack([got, own_half]))
    column_kv = lax.all_gather(chunk, "section", axis=1)
    column_kv = column_kv.reshape(8, 2, B, W)
    before_kv = lax.ppermute(column_kv, "ctx", ahead)
    k = jnp.concatenate([before_kv[:, 0], column_kv[:, 0]])
    v = jnp.concatenate([before_kv[:, 1], column_kv[:, 1]])
    dq, dk, dv = attend(doc_lengths[None, :], q, g, l2, dl, k, v, heads)

    dq = dq.reshape(2, rows, features)
    dq_mine = jnp.where(core == 0, dq[0], dq[1])
    dq_theirs = lax.ppermute(jnp.where(core == 0, dq[1], dq[0]), "ctx", swap)
    query_grad = (dq_mine.astype(jnp.float32) + dq_theirs.astype(jnp.float32)).astype(jnp.bfloat16)

    part = jnp.stack([dk, dv], axis=1)
    returned = lax.ppermute(part[:8], "ctx", back)
    total = part[8:].astype(jnp.float32) + returned.astype(jnp.float32)
    total = total.reshape(2, 4, 2, B, W).transpose(1, 0, 2, 3, 4)
    total = lax.psum_scatter(total, "section", scatter_dimension=0, tiled=True)[0]
    keep = jnp.where(core == 0, total[0], total[1])
    give = jnp.where(core == 0, total[1], total[0])
    other = lax.ppermute(give.astype(jnp.bfloat16), "ctx", swap)
    whole = jnp.concatenate([keep.astype(jnp.bfloat16), other], axis=1)
    return query_grad, whole[0], whole[1]


def solution(mesh):
    rows = P(("ctx", "section"), None)
    return jax.shard_map(
        on_device,
        mesh=mesh,
        in_specs=(rows, rows, rows, rows, rows, P(None, ("ctx", "section")), P()),
        out_specs=(rows, rows, rows),
        check_vma=False,
    )
```

```python
import functools
import math

import jax
import jax.numpy as jnp
from jax import lax
from jax.experimental import pallas as pl
from jax.experimental.pallas import tpu as pltpu
from jax.sharding import PartitionSpec as P

MESH = pl.DeviceIdType.MESH
W = 128
B = 256
LOG2E = math.log2(math.e)
OWN, BEFORE = 1, 0


def nn(a, b):
    return jnp.dot(a, b, preferred_element_type=jnp.float32)


def nt(a, b):
    return lax.dot_general(a, b, (((1,), (1,)), ((), ())), preferred_element_type=jnp.float32)


def place():
    ctx = lax.axis_index("ctx")
    return ctx // 2, lax.axis_index("section"), ctx % 2


def slot(side, z, j):
    return side * 8 + z * 2 + j


class Links:
    def __init__(self, columns):
        self.column, self.z, self.core = place()
        ctx = lax.axis_index("ctx")
        self.up = lax.rem(self.z + 1, 4)
        self.down = lax.rem(self.z + 3, 4)
        self.across = lax.rem(self.z + 2, 4)
        self.sibling = (ctx + 1 - 2 * self.core, self.z)
        self.above = (ctx, self.up)
        self.below = (ctx, self.down)
        self.has_next = self.column < columns - 1
        self.has_last = self.column > 0
        self.next = (jnp.where(self.has_next, ctx + 2, ctx), self.z)
        self.last = (jnp.where(self.has_last, ctx - 2, ctx), self.z)

    def barrier(self):
        barrier = pltpu.get_barrier_semaphore()

        def greet(device):
            pl.semaphore_signal(barrier, inc=1, device_id=device, device_id_type=MESH)

        greet(self.sibling)
        greet(self.above)
        greet(self.below)
        pl.when(self.has_next)(lambda: greet(self.next))
        pl.when(self.has_last)(lambda: greet(self.last))
        peers = 3 + self.has_next.astype(jnp.int32) + self.has_last.astype(jnp.int32)
        pl.semaphore_wait(barrier, peers)


class Route:
    def __init__(self, sems, index, device, source, target, sends=True, gets=True, arrival=None):
        self.sends, self.gets = sends, gets
        landed = target if arrival is None else arrival
        send, recv = sems[0].at[index], sems[1].at[index]
        self.make = lambda end: pltpu.make_async_remote_copy(
            source, end, send, recv, device_id=device, device_id_type=MESH
        )
        self.target, self.landed = target, landed

    @staticmethod
    def only(condition, act):
        if condition is True:
            act()
        else:
            pl.when(condition)(act)

    def start(self):
        self.only(self.sends, lambda: self.make(self.target).start())

    def arrived(self):
        self.only(self.gets, lambda: self.make(self.landed).wait_recv())

    def sent(self):
        self.only(self.sends, lambda: self.make(self.target).wait_send())


def gather_kernel(
    columns, heads, q_ref, g_ref, o_ref, k_ref, v_ref, log_ref,
    q_other, g_other, stat_own, stat_other, window,
    g_vmem, o_vmem, stat, local, send, recv,
):
    at = Links(columns)
    z, core, up, down, across = at.z, at.core, at.up, at.down, at.across
    sems = (send, recv)
    load_g = pltpu.make_async_copy(g_ref, g_vmem, local.at[0])
    load_o = pltpu.make_async_copy(o_ref, o_vmem, local.at[1])
    load_g.start()
    load_o.start()
    mine = window.at[slot(OWN, z, core)]
    keep_k = pltpu.make_async_copy(k_ref.at[:B], mine.at[0], local.at[2])
    keep_v = pltpu.make_async_copy(v_ref.at[:B], mine.at[1], local.at[3])
    keep_k.start()
    keep_v.start()
    at.barrier()

    theirs = window.at[slot(OWN, z, 1 - core)]
    swap_k = Route(sems, 0, at.sibling, k_ref.at[B:], mine.at[0], arrival=theirs.at[0])
    swap_v = Route(sems, 1, at.sibling, v_ref.at[B:], mine.at[1], arrival=theirs.at[1])
    swap_k.start()
    swap_v.start()
    rows = q_ref.shape[0]
    bulk = []
    for part in range(2):
        some = slice(part * rows // 2, (part + 1) * rows // 2)
        bulk.append(Route(sems, 2 + part, at.sibling, q_ref.at[some], q_other.at[some]))
        bulk.append(Route(sems, 4 + part, at.sibling, g_ref.at[some], g_other.at[some]))
    for copy in bulk:
        copy.start()

    def passed(index, device, side, sent, j, got, sends=True, gets=True):
        there = window.at[slot(side, sent, j)]
        return Route(sems, index, device, there, there, sends, gets, window.at[slot(side, got, j)])

    up_0 = passed(6, at.above, OWN, z, 0, down)
    up_1 = passed(7, at.above, OWN, z, 1, down)
    down_0 = passed(8, at.below, OWN, z, 0, up)
    down_1 = passed(9, at.below, OWN, z, 1, up, z == 0, z == 3)
    far_0 = passed(10, at.below, OWN, up, 0, across)
    far_1 = passed(11, at.above, OWN, down, 1, across)

    def later(index, zc, j, when=True):
        here = window.at[slot(OWN, zc, j)]
        there = window.at[slot(BEFORE, zc, j)]
        sends = at.has_next if when is True else at.has_next & when
        gets = at.has_last if when is True else at.has_last & when
        return Route(sems, index, at.next, here, there, sends, gets)

    next_0 = later(12, z, 0)
    next_1 = later(13, z, 1)
    next_far_0 = later(14, across, 0, z < 2)
    next_far_1 = later(15, across, 1)
    last = at.has_last
    before_up_0 = passed(16, at.above, BEFORE, z, 0, down, last & (z == 3), last & (z == 0))
    before_up_1 = passed(17, at.above, BEFORE, z, 1, down, last, last)
    before_down_0 = passed(18, at.below, BEFORE, z, 0, up, last & (z != 0), last & (z != 3))
    before_down_1 = passed(19, at.below, BEFORE, z, 1, up, last, last)

    keep_k.wait()
    keep_v.wait()
    swap_k.arrived()
    swap_v.arrived()
    for copy in (down_0, up_1, next_1, next_0, up_0, down_1):
        copy.start()

    load_g.wait()
    load_o.wait()
    ones = jnp.ones((8, W), jnp.bfloat16)
    for h in range(heads):
        cols = slice(h * W, (h + 1) * W)
        product = g_vmem[:, cols].astype(jnp.float32) * o_vmem[:, cols].astype(jnp.float32)
        high = product.astype(jnp.bfloat16)
        low = (product - high.astype(jnp.float32)).astype(jnp.bfloat16)
        total = nt(ones, high) + nt(ones, low)
        stat[1, h : h + 1, :] = total[0:1]
    stat[0] = log_ref[...] * LOG2E
    stats = Route(sems, 20, at.sibling, stat, stat_other)
    stats.start()
    keep_stat = pltpu.make_async_copy(stat, stat_own, local.at[4])
    keep_stat.start()

    down_0.arrived()
    far_0.start()
    up_1.arrived()
    far_1.start()
    next_0.arrived()
    next_1.arrived()
    for copy in (before_down_1, before_up_1, before_down_0, before_up_0):
        copy.start()
    far_0.arrived()
    far_1.arrived()
    next_far_1.start()
    next_far_0.start()
    for copy in (up_0, down_1, before_up_0, before_up_1, before_down_0, before_down_1):
        copy.arrived()
    next_far_0.arrived()
    next_far_1.arrived()
    for copy in bulk:
        copy.arrived()
    stats.arrived()
    keep_stat.wait()
    for copy in (
        [swap_k, swap_v, up_0, up_1, down_0, down_1, far_0, far_1, next_0, next_1, next_far_0]
        + [next_far_1, before_up_0, before_up_1, before_down_0, before_down_1, stats]
        + bulk
    ):
        copy.sent()


def gather(columns, q, g, o, k, v, log_total):
    rows, features = q.shape
    heads = features // W
    some = pl.BlockSpec(memory_space=pl.ANY)
    vmem = pl.BlockSpec(memory_space=pltpu.VMEM)
    return pl.pallas_call(
        functools.partial(gather_kernel, columns, heads),
        out_shape=(
            jax.ShapeDtypeStruct((rows, features), q.dtype),
            jax.ShapeDtypeStruct((rows, features), q.dtype),
            jax.ShapeDtypeStruct((2, heads, rows), jnp.float32),
            jax.ShapeDtypeStruct((2, heads, rows), jnp.float32),
            jax.ShapeDtypeStruct((16, 2, B, W), k.dtype),
        ),
        in_specs=[some] * 5 + [vmem],
        out_specs=(some,) * 5,
        scratch_shapes=[
            pltpu.VMEM((rows, features), g.dtype),
            pltpu.VMEM((rows, features), g.dtype),
            pltpu.VMEM((2, heads, rows), jnp.float32),
            pltpu.SemaphoreType.DMA((5,)),
            pltpu.SemaphoreType.DMA((21,)),
            pltpu.SemaphoreType.DMA((21,)),
        ],
        compiler_params=pltpu.CompilerParams(
            collective_id=0, has_side_effects=True, vmem_limit_bytes=32 << 20
        ),
    )(q, g, o, k, v, log_total)


def attend_kernel(
    heads, docs_ref, qa_hbm, qb_hbm, ga_hbm, gb_hbm, stat_a, stat_b, window_ref,
    dq_own, dq_other, part_ref,
    q_ref, g_ref, dqt, dka, dva, bias, sem,
):
    column, z, core = place()
    scale = 1.0 / math.sqrt(W)
    loads = []
    for n, (source, target) in enumerate(
        ((qa_hbm, q_ref.at[0]), (ga_hbm, g_ref.at[0]), (qb_hbm, q_ref.at[1]), (gb_hbm, g_ref.at[1]))
    ):
        loads.append(pltpu.make_async_copy(source, target, sem.at[n]))
        loads[-1].start()
    lengths = docs_ref[...].astype(jnp.float32)
    docs = lengths.shape[1]
    upto = lax.broadcasted_iota(jnp.int32, (docs, docs), 1) <= lax.broadcasted_iota(
        jnp.int32, (docs, docs), 0
    )
    ends = jnp.sum(jnp.where(upto, lengths, 0.0), axis=1, keepdims=True)
    dka[...] = jnp.zeros_like(dka)
    dva[...] = jnp.zeros_like(dva)
    eye = (
        lax.broadcasted_iota(jnp.int32, (B, B), 0) == lax.broadcasted_iota(jnp.int32, (B, B), 1)
    ).astype(jnp.bfloat16)
    window = (column - 1) * 16 * B

    def half_of(b):
        return jnp.where(b % 8 >= 4, 1 - core, core)

    def query_block(side, stat_ref, dq_ref, part):
        here = pl.ds(part * B, B)
        tile = z + 4 * (core if side == 0 else 1 - core)
        first = column * 16 * B + tile * 2 * B + part * B
        pos = first.astype(jnp.float32) + lax.broadcasted_iota(jnp.int32, (1, B), 1).astype(
            jnp.float32
        )
        start = jnp.max(jnp.where(ends <= pos, ends, 0.0), axis=0, keepdims=True)
        start_lo = jnp.min(start).astype(jnp.int32)
        start_hi = jnp.max(start).astype(jnp.int32)
        rel = start_lo - window
        lo = rel // (2 * B)
        lo = jnp.where(rel % (2 * B) >= half_of(lo) * B + B, lo + 1, lo)
        hi = jnp.where(half_of(8 + tile) <= part, 9 + tile, 8 + tile)
        dqt[...] = jnp.zeros_like(dqt)

        def work(b, masked):
            at = slot(b // 8, b % 4, b % 8 // 4)
            k = window_ref[at, 0]
            v = window_ref[at, 1]
            kt = k.T
            dk = jnp.zeros((B, W), jnp.float32)
            dv = jnp.zeros((B, W), jnp.float32)
            for h in range(heads):
                cols = slice(h * W, (h + 1) * W)
                rows = slice(h * B, (h + 1) * B)
                q = q_ref[side, here, cols]
                g = g_ref[side, here, cols]
                x = nt(k, q) * (scale * LOG2E) - stat_ref[0, h : h + 1, here]
                if masked:
                    x = x + bias[...]
                p = jnp.exp2(x)
                ds = p * (nt(v, g) - stat_ref[1, h : h + 1, here])
                ph = p.astype(jnp.bfloat16)
                dh = ds.astype(jnp.bfloat16)
                dv = dv + nn(ph, g)
                dk = dk + nn(dh, q)
                dqt[:, rows] += nn(kt, dh)
            dka[at] += dk
            dva[at] += dv

        def step(b, inner):
            key = window + b * 2 * B + half_of(b) * B
            full = (key >= start_hi) & (key + B - 1 <= first)

            @pl.when(full)
            def _():
                work(b, False)

            @pl.when(jnp.logical_not(full))
            def _():
                kpos = (key + lax.broadcasted_iota(jnp.int32, (B, B), 0)).astype(jnp.float32)
                bias[...] = jnp.where((kpos >= start) & (kpos <= pos), 0.0, -jnp.inf)
                work(b, True)

            return inner

        lax.fori_loop(lo, hi, step, 0)
        for h in range(heads):
            held = (dqt[:, h * B : (h + 1) * B] * scale).astype(jnp.bfloat16)
            dq_ref[here, h * W : (h + 1) * W] = nt(eye, held).astype(jnp.bfloat16)

    for side, stat_ref, dq_ref in ((0, stat_a, dq_own), (1, stat_b, dq_other)):
        loads[2 * side].wait()
        loads[2 * side + 1].wait()

        @pl.loop(0, 2)
        def _(part):
            query_block(side, stat_ref, dq_ref, part)

    for s in range(16):
        part_ref[s, 0] = (dka[s] * scale).astype(jnp.bfloat16)
        part_ref[s, 1] = dva[s].astype(jnp.bfloat16)


def attend(docs, q_own, q_other, g_own, g_other, stat_own, stat_other, window):
    rows, features = q_own.shape
    heads = features // W
    vmem = pl.BlockSpec(memory_space=pltpu.VMEM)
    some = pl.BlockSpec(memory_space=pl.ANY)
    return pl.pallas_call(
        functools.partial(attend_kernel, heads),
        out_shape=(
            jax.ShapeDtypeStruct((rows, features), jnp.bfloat16),
            jax.ShapeDtypeStruct((rows, features), jnp.bfloat16),
            jax.ShapeDtypeStruct((16, 2, B, W), jnp.bfloat16),
        ),
        in_specs=[vmem] + [some] * 4 + [vmem] * 3,
        out_specs=(vmem, vmem, vmem),
        scratch_shapes=[
            pltpu.VMEM((2, rows, features), jnp.bfloat16),
            pltpu.VMEM((2, rows, features), jnp.bfloat16),
            pltpu.VMEM((W, heads * B), jnp.float32),
            pltpu.VMEM((16, B, W), jnp.float32),
            pltpu.VMEM((16, B, W), jnp.float32),
            pltpu.VMEM((B, B), jnp.float32),
            pltpu.SemaphoreType.DMA((4,)),
        ],
        compiler_params=pltpu.CompilerParams(vmem_limit_bytes=48 << 20),
        cost_estimate=pl.CostEstimate(
            flops=20 * 10 * heads * B * B * W, bytes_accessed=16 << 20, transcendentals=0
        ),
    )(docs, q_own, q_other, g_own, g_other, stat_own, stat_other, window)


def return_kernel(
    columns, dq_ref, part_ref, dq_got, dk_ref, dv_ref,
    part, across_got, beside_got, beside_sum, later_got, far_got, far_sum, near_sum, near_got,
    final, local, send, recv,
):
    at = Links(columns)
    z, core, up, down, across = at.z, at.core, at.up, at.down, at.across
    sems = (send, recv)
    load = pltpu.make_async_copy(part_ref, part, local.at[0])
    load.start()
    at.barrier()
    has_next, has_last = at.has_next, at.has_last

    def given(side, zc, j):
        return part_ref.at[slot(side, zc, j)]

    def held(side, zc, j):
        return part[slot(side, zc, j)].astype(jnp.float32)

    far_back = [
        Route(
            sems, j, at.last, given(BEFORE, across, j), across_got.at[j],
            has_last & (z < 2) if j == 0 else has_last,
            has_next & (z < 2) if j == 0 else has_next,
        )
        for j in range(2)
    ]
    side_up = [
        Route(
            sems, 2 + j, at.above, given(BEFORE, up, j), beside_got.at[0, j],
            has_last & (z != 3) if j == 0 else has_last,
            has_last & (z != 0) if j == 0 else has_last,
        )
        for j in range(2)
    ]
    side_down = [
        Route(
            sems, 4 + j, at.below, given(BEFORE, down, j), beside_got.at[1, j],
            has_last & (z == 0) if j == 0 else has_last,
            has_last & (z == 3) if j == 0 else has_last,
        )
        for j in range(2)
    ]
    dq_half = dq_ref.shape[0] // 2
    bulk = [
        Route(
            sems, 6 + n, at.sibling,
            dq_ref.at[n * dq_half : (n + 1) * dq_half],
            dq_got.at[n * dq_half : (n + 1) * dq_half],
        )
        for n in range(2)
    ]
    back = [
        Route(sems, 8 + j, at.last, beside_sum.at[j], later_got.at[j], has_last, has_next)
        for j in range(2)
    ]
    far_up = Route(sems, 10, at.above, far_sum.at[0], far_got.at[0])
    far_down = Route(sems, 11, at.below, far_sum.at[1], far_got.at[1])
    near_up_0 = Route(sems, 12, at.above, near_sum.at[0], near_got.at[0])
    near_up_1 = Route(sems, 13, at.above, given(OWN, up, 1), near_got.at[1], z == 3, z == 0)
    near_down_0 = Route(sems, 14, at.below, given(OWN, down, 0), near_got.at[2])
    near_down_1 = Route(sems, 15, at.below, near_sum.at[1], near_got.at[3])

    for copy in (far_back[1], far_back[0], side_up[1], side_down[1], side_up[0], side_down[0]):
        copy.start()
    near_down_0.start()
    near_up_1.start()
    for copy in bulk:
        copy.start()
    load.wait()

    @pl.when(has_last)
    def _():
        for copy in side_up + side_down:
            copy.arrived()
        for j in range(2):
            final[j] = held(BEFORE, z, j)
        final[1] += beside_got[0, 1].astype(jnp.float32) + beside_got[1, 1].astype(jnp.float32)

        @pl.when(z != 0)
        def _():
            final[0] += beside_got[0, 0].astype(jnp.float32)

        @pl.when(z == 3)
        def _():
            final[0] += beside_got[1, 0].astype(jnp.float32)

        beside_sum[...] = final[...].astype(jnp.bfloat16)
        for copy in back:
            copy.start()

    def add_across(j):
        far_back[j].make(across_got.at[j]).wait_recv()
        final[j] += across_got[j].astype(jnp.float32)

    for j in range(2):
        final[j] = held(OWN, across, j)
        pl.when(far_back[j].gets)(functools.partial(add_across, j))
        far_sum[j] = final[j].astype(jnp.bfloat16)
    far_up.start()
    far_down.start()
    far_up.arrived()
    near_sum[0] = (held(OWN, up, 0) + far_got[0].astype(jnp.float32)).astype(jnp.bfloat16)
    near_up_0.start()
    far_down.arrived()
    near_sum[1] = (held(OWN, down, 1) + far_got[1].astype(jnp.float32)).astype(jnp.bfloat16)
    near_down_1.start()
    near_down_0.arrived()
    near_up_0.arrived()
    final[0] = (
        held(OWN, z, 0) + near_got[0].astype(jnp.float32) + near_got[2].astype(jnp.float32)
    )
    near_up_1.arrived()
    near_down_1.arrived()
    final[1] = held(OWN, z, 1) + near_got[3].astype(jnp.float32)

    @pl.when(z == 0)
    def _():
        final[1] += near_got[1].astype(jnp.float32)

    @pl.when(has_next)
    def _():
        for j in range(2):
            back[j].arrived()
            final[j] += later_got[j].astype(jnp.float32)

    far_up.sent()
    far_down.sent()
    far_sum[0] = final[1 - core].astype(jnp.bfloat16)
    give_k = Route(sems, 16, at.sibling, far_sum.at[0, 0], dk_ref.at[B:])
    give_v = Route(sems, 17, at.sibling, far_sum.at[0, 1], dv_ref.at[B:])
    give_k.start()
    give_v.start()
    dk_ref[:B] = final[core, 0].astype(jnp.bfloat16)
    dv_ref[:B] = final[core, 1].astype(jnp.bfloat16)
    give_k.arrived()
    give_v.arrived()
    for copy in bulk:
        copy.arrived()
    for copy in (
        far_back + side_up + side_down + bulk + back
        + [near_up_0, near_up_1, near_down_0, near_down_1, give_k, give_v]
    ):
        copy.sent()


def give_back(columns, dq_other, part):
    rows, features = dq_other.shape
    some = pl.BlockSpec(memory_space=pl.ANY)
    vmem = pl.BlockSpec(memory_space=pltpu.VMEM)
    block = (2, B, W)
    return pl.pallas_call(
        functools.partial(return_kernel, columns),
        out_shape=(
            jax.ShapeDtypeStruct((rows, features), jnp.bfloat16),
            jax.ShapeDtypeStruct((rows, W), jnp.bfloat16),
            jax.ShapeDtypeStruct((rows, W), jnp.bfloat16),
        ),
        in_specs=[some] * 2,
        out_specs=(some, vmem, vmem),
        scratch_shapes=[
            pltpu.VMEM((16, *block), jnp.bfloat16),
            pltpu.VMEM((2, *block), jnp.bfloat16),
            pltpu.VMEM((2, 2, *block), jnp.bfloat16),
            pltpu.VMEM((2, *block), jnp.bfloat16),
            pltpu.VMEM((2, *block), jnp.bfloat16),
            pltpu.VMEM((2, *block), jnp.bfloat16),
            pltpu.VMEM((2, *block), jnp.bfloat16),
            pltpu.VMEM((2, *block), jnp.bfloat16),
            pltpu.VMEM((4, *block), jnp.bfloat16),
            pltpu.VMEM((2, *block), jnp.float32),
            pltpu.SemaphoreType.DMA((1,)),
            pltpu.SemaphoreType.DMA((18,)),
            pltpu.SemaphoreType.DMA((18,)),
        ],
        compiler_params=pltpu.CompilerParams(
            collective_id=1, has_side_effects=True, vmem_limit_bytes=32 << 20
        ),
    )(dq_other, part)


def solution(mesh):
    columns = mesh.shape["ctx"] // 2

    def on_device(q, k, v, o, g, log_total, doc_lengths):
        q_other, g_other, stat_own, stat_other, window = gather(columns, q, g, o, k, v, log_total)
        dq_own, dq_other, part = attend(
            doc_lengths[None, :], q, q_other, g, g_other, stat_own, stat_other, window
        )
        dq_got, dk, dv = give_back(columns, dq_other, part)
        dq = (dq_own.astype(jnp.float32) + dq_got.astype(jnp.float32)).astype(jnp.bfloat16)
        return dq, dk, dv

    rows = P(("ctx", "section"), None)
    return jax.shard_map(
        on_device,
        mesh=mesh,
        in_specs=(rows, rows, rows, rows, rows, P(None, ("ctx", "section")), P()),
        out_specs=(rows, rows, rows),
        check_vma=False,
    )
```

```python
import functools
import math

import jax
import jax.numpy as jnp
from jax import lax
from jax.experimental import pallas as pl
from jax.experimental.pallas import tpu as pltpu
from jax.sharding import PartitionSpec as P

MESH = pl.DeviceIdType.MESH
W = 128
B = 256
VMEM = 58 << 20
LOG2E = math.log2(math.e)
OWN, BEFORE = 1, 0


def nn(a, b):
    return jnp.dot(a, b, preferred_element_type=jnp.float32)


def nt(a, b):
    return lax.dot_general(a, b, (((1,), (1,)), ((), ())), preferred_element_type=jnp.float32)


def place():
    ctx = lax.axis_index("ctx")
    return ctx // 2, lax.axis_index("section"), ctx % 2


def slot(side, z, j):
    return side * 8 + z * 2 + j


class Links:
    def __init__(self, columns):
        self.column, self.z, self.core = place()
        ctx = lax.axis_index("ctx")
        self.up = lax.rem(self.z + 1, 4)
        self.down = lax.rem(self.z + 3, 4)
        self.across = lax.rem(self.z + 2, 4)
        self.sibling = (ctx + 1 - 2 * self.core, self.z)
        self.above = (ctx, self.up)
        self.below = (ctx, self.down)
        self.has_next = self.column < columns - 1
        self.has_last = self.column > 0
        self.next = (jnp.where(self.has_next, ctx + 2, ctx), self.z)
        self.last = (jnp.where(self.has_last, ctx - 2, ctx), self.z)

    def barrier(self):
        barrier = pltpu.get_barrier_semaphore()

        def greet(device):
            pl.semaphore_signal(barrier, inc=1, device_id=device, device_id_type=MESH)

        greet(self.sibling)
        greet(self.above)
        greet(self.below)
        pl.when(self.has_next)(lambda: greet(self.next))
        pl.when(self.has_last)(lambda: greet(self.last))
        peers = 3 + self.has_next.astype(jnp.int32) + self.has_last.astype(jnp.int32)
        pl.semaphore_wait(barrier, peers)


class Route:
    def __init__(self, sems, index, device, source, target, sends=True, gets=True, arrival=None):
        self.sends, self.gets = sends, gets
        landed = target if arrival is None else arrival
        send, recv = sems[0].at[index], sems[1].at[index]
        self.make = lambda end: pltpu.make_async_remote_copy(
            source, end, send, recv, device_id=device, device_id_type=MESH
        )
        self.target, self.landed = target, landed

    @staticmethod
    def only(condition, act):
        if condition is True:
            act()
        else:
            pl.when(condition)(act)

    def start(self):
        self.only(self.sends, lambda: self.make(self.target).start())

    def arrived(self):
        self.only(self.gets, lambda: self.make(self.landed).wait_recv())

    def sent(self):
        self.only(self.sends, lambda: self.make(self.target).wait_send())


def gather_kernel(
    columns, heads, q_ref, g_ref, o_ref, k_ref, v_ref, log_ref,
    q_other, g_other, stat_both, window,
    g_vmem, o_vmem, stat, local, send, recv,
):
    at = Links(columns)
    z, core, up, down, across = at.z, at.core, at.up, at.down, at.across
    sems = (send, recv)
    load_g = pltpu.make_async_copy(g_ref, g_vmem, local.at[0])
    load_o = pltpu.make_async_copy(o_ref, o_vmem, local.at[1])
    load_g.start()
    load_o.start()
    load_log = pltpu.make_async_copy(log_ref, stat.at[0], local.at[5])
    load_log.start()
    mine = window.at[slot(OWN, z, core)]
    keep_k = pltpu.make_async_copy(k_ref.at[:B], mine.at[0], local.at[2])
    keep_v = pltpu.make_async_copy(v_ref.at[:B], mine.at[1], local.at[3])
    keep_k.start()
    keep_v.start()
    at.barrier()

    theirs = window.at[slot(OWN, z, 1 - core)]
    swap_k = Route(sems, 0, at.sibling, k_ref.at[B:], mine.at[0], arrival=theirs.at[0])
    swap_v = Route(sems, 1, at.sibling, v_ref.at[B:], mine.at[1], arrival=theirs.at[1])
    swap_k.start()
    swap_v.start()
    rows = q_ref.shape[0]
    bulk = []
    for part in range(2):
        some = slice(part * rows // 2, (part + 1) * rows // 2)
        bulk.append(Route(sems, 2 + part, at.sibling, q_ref.at[some], q_other.at[some]))
        bulk.append(Route(sems, 4 + part, at.sibling, g_ref.at[some], g_other.at[some]))
    for copy in bulk:
        copy.start()

    def passed(index, device, side, sent, j, got, sends=True, gets=True):
        there = window.at[slot(side, sent, j)]
        return Route(sems, index, device, there, there, sends, gets, window.at[slot(side, got, j)])

    up_0 = passed(6, at.above, OWN, z, 0, down)
    up_1 = passed(7, at.above, OWN, z, 1, down)
    down_0 = passed(8, at.below, OWN, z, 0, up)
    down_1 = passed(9, at.below, OWN, z, 1, up, z == 0, z == 3)
    far_0 = passed(10, at.below, OWN, up, 0, across)
    far_1 = passed(11, at.above, OWN, down, 1, across)

    def later(index, zc, j, when=True):
        here = window.at[slot(OWN, zc, j)]
        there = window.at[slot(BEFORE, zc, j)]
        sends = at.has_next if when is True else at.has_next & when
        gets = at.has_last if when is True else at.has_last & when
        return Route(sems, index, at.next, here, there, sends, gets)

    next_0 = later(12, z, 0)
    next_1 = later(13, z, 1)
    next_far_0 = later(14, across, 0, z < 2)
    next_far_1 = later(15, across, 1)
    last = at.has_last
    before_up_0 = passed(16, at.above, BEFORE, z, 0, down, last & (z == 3), last & (z == 0))
    before_up_1 = passed(17, at.above, BEFORE, z, 1, down, last, last)
    before_down_0 = passed(18, at.below, BEFORE, z, 0, up, last & (z != 0), last & (z != 3))
    before_down_1 = passed(19, at.below, BEFORE, z, 1, up, last, last)

    keep_k.wait()
    keep_v.wait()
    swap_k.arrived()
    swap_v.arrived()
    for copy in (down_0, up_1, next_1, next_0, up_0, down_1):
        copy.start()

    load_g.wait()
    load_o.wait()
    ones = jnp.ones((8, W), jnp.bfloat16)
    for h in range(heads):
        cols = slice(h * W, (h + 1) * W)
        product = g_vmem[:, cols].astype(jnp.float32) * o_vmem[:, cols].astype(jnp.float32)
        high = product.astype(jnp.bfloat16)
        low = (product - high.astype(jnp.float32)).astype(jnp.bfloat16)
        total = nt(ones, high) + nt(ones, low)
        stat[1, h : h + 1, :] = total[0:1]
    load_log.wait()
    stat[0] = stat[0] * LOG2E
    stats = Route(sems, 20, at.sibling, stat, stat_both.at[1])
    stats.start()
    keep_stat = pltpu.make_async_copy(stat, stat_both.at[0], local.at[4])
    keep_stat.start()

    down_0.arrived()
    far_0.start()
    up_1.arrived()
    far_1.start()
    next_0.arrived()
    next_1.arrived()
    for copy in (before_down_1, before_up_1, before_down_0, before_up_0):
        copy.start()
    far_0.arrived()
    far_1.arrived()
    next_far_1.start()
    next_far_0.start()
    for copy in (up_0, down_1, before_up_0, before_up_1, before_down_0, before_down_1):
        copy.arrived()
    next_far_0.arrived()
    next_far_1.arrived()
    for copy in bulk:
        copy.arrived()
    stats.arrived()
    keep_stat.wait()
    for copy in (
        [swap_k, swap_v, up_0, up_1, down_0, down_1, far_0, far_1, next_0, next_1, next_far_0]
        + [next_far_1, before_up_0, before_up_1, before_down_0, before_down_1, stats]
        + bulk
    ):
        copy.sent()


def gather(columns, q, g, o, k, v, log_total):
    rows, features = q.shape
    heads = features // W
    some = pl.BlockSpec(memory_space=pl.ANY)
    return pl.pallas_call(
        functools.partial(gather_kernel, columns, heads),
        out_shape=(
            jax.ShapeDtypeStruct((rows, features), q.dtype),
            jax.ShapeDtypeStruct((rows, features), q.dtype),
            jax.ShapeDtypeStruct((2, 2, heads, rows), jnp.float32),
            jax.ShapeDtypeStruct((16, 2, B, W), k.dtype),
        ),
        in_specs=[some] * 6,
        out_specs=(some,) * 4,
        scratch_shapes=[
            pltpu.VMEM((rows, features), g.dtype),
            pltpu.VMEM((rows, features), g.dtype),
            pltpu.VMEM((2, heads, rows), jnp.float32),
            pltpu.SemaphoreType.DMA((6,)),
            pltpu.SemaphoreType.DMA((21,)),
            pltpu.SemaphoreType.DMA((21,)),
        ],
        compiler_params=pltpu.CompilerParams(
            collective_id=0, has_side_effects=True, vmem_limit_bytes=VMEM
        ),
    )(q, g, o, k, v, log_total)


def attend_kernel(
    heads, docs_ref, qa_hbm, qb_hbm, ga_hbm, gb_hbm, stat_hbm, window_hbm, dq_hbm, part_hbm,
    q_ref, g_ref, stat_ref, window_ref, dq_ref, part_ref, dqt, dka, dva, bias, get, put
):
    column, z, core = place()
    loads = [
        pltpu.make_async_copy(source, target, get.at[n])
        for n, (source, target) in enumerate(
            (
                (stat_hbm, stat_ref), (window_hbm, window_ref),
                (qa_hbm, q_ref.at[0]), (ga_hbm, g_ref.at[0]),
                (qb_hbm, q_ref.at[1]), (gb_hbm, g_ref.at[1]),
            )
        )
    ]
    for load in loads:
        load.start()
    scale = 1.0 / math.sqrt(W)
    lengths = docs_ref[...].astype(jnp.float32)
    docs = lengths.shape[1]
    upto = lax.broadcasted_iota(jnp.int32, (docs, docs), 1) <= lax.broadcasted_iota(
        jnp.int32, (docs, docs), 0
    )
    ends = jnp.sum(jnp.where(upto, lengths, 0.0), axis=1, keepdims=True)
    dka[...] = jnp.zeros_like(dka)
    dva[...] = jnp.zeros_like(dva)
    eye = (
        lax.broadcasted_iota(jnp.int32, (B, B), 0) == lax.broadcasted_iota(jnp.int32, (B, B), 1)
    ).astype(jnp.bfloat16)
    window = (column - 1) * 16 * B

    def half_of(b):
        return jnp.where(b % 8 >= 4, 1 - core, core)

    for load in loads:
        load.wait()

    @pl.loop(0, 4)
    def _(block):
        side, part = block // 2, block % 2
        here = pl.ds(pl.multiple_of(part * B, B), B)
        tile = z + 4 * jnp.where(side == 0, core, 1 - core)
        first = column * 16 * B + tile * 2 * B + part * B
        pos = first.astype(jnp.float32) + lax.broadcasted_iota(jnp.int32, (1, B), 1).astype(
            jnp.float32
        )
        start = jnp.max(jnp.where(ends <= pos, ends, 0.0), axis=0, keepdims=True)
        start_lo = jnp.min(start).astype(jnp.int32)
        start_hi = jnp.max(start).astype(jnp.int32)
        rel = start_lo - window
        lo = rel // (2 * B)
        lo = jnp.where(rel % (2 * B) >= half_of(lo) * B + B, lo + 1, lo)
        hi = jnp.where(half_of(8 + tile) <= part, 9 + tile, 8 + tile)
        dqt[...] = jnp.zeros_like(dqt)

        def work(b, masked):
            at = slot(b // 8, b % 4, b % 8 // 4)
            k = window_ref[at, 0]
            v = window_ref[at, 1]
            ps, ds, qs, gs = [], [], [], []
            for h in range(heads):
                cols = slice(h * W, (h + 1) * W)
                q = q_ref[side, here, cols]
                g = g_ref[side, here, cols]
                x = nt(k, q) * (scale * LOG2E) - stat_ref[side, 0, h : h + 1, here]
                if masked:
                    x = x + bias[...]
                p = jnp.exp2(x)
                d = p * (nt(v, g) - stat_ref[side, 1, h : h + 1, here])
                ps.append(p.astype(jnp.bfloat16))
                ds.append(d.astype(jnp.bfloat16))
                qs.append(q)
                gs.append(g)
            dh = jnp.concatenate(ds, axis=1)
            dva[at] += nn(jnp.concatenate(ps, axis=1), jnp.concatenate(gs, axis=0))
            dka[at] += nn(dh, jnp.concatenate(qs, axis=0))
            dqt[...] += nn(k.T, dh)

        def step(b, inner):
            key = window + b * 2 * B + half_of(b) * B
            full = (key >= start_hi) & (key + B - 1 <= first)

            @pl.when(full)
            def _():
                work(b, False)

            @pl.when(jnp.logical_not(full))
            def _():
                kpos = (key + lax.broadcasted_iota(jnp.int32, (B, B), 0)).astype(jnp.float32)
                bias[...] = jnp.where((kpos >= start) & (kpos <= pos), 0.0, -jnp.inf)
                work(b, True)

            return inner

        lax.fori_loop(lo, hi, step, 0)
        for h in range(heads):
            held = (dqt[:, h * B : (h + 1) * B] * scale).astype(jnp.bfloat16)
            dq_ref[block, :, h * W : (h + 1) * W] = nt(eye, held).astype(jnp.bfloat16)
        pltpu.make_async_copy(dq_ref.at[block], dq_hbm.at[side, here], put.at[block]).start()

    @pl.loop(0, 16)
    def _(s):
        part_ref[s, 0] = (dka[s] * scale).astype(jnp.bfloat16)
        part_ref[s, 1] = dva[s].astype(jnp.bfloat16)
        pltpu.make_async_copy(part_ref.at[s], part_hbm.at[s], put.at[4 + s]).start()

    for block in range(4):
        here = slice(block % 2 * B, (block % 2 + 1) * B)
        pltpu.make_async_copy(dq_ref.at[block], dq_hbm.at[block // 2, here], put.at[block]).wait()
    for s in range(16):
        pltpu.make_async_copy(part_ref.at[s], part_hbm.at[s], put.at[4 + s]).wait()


def attend(docs, q, q_other, g, g_other, stat, window):
    rows, features = q.shape
    heads = features // W
    some = pl.BlockSpec(memory_space=pl.ANY)
    both = (2, rows, features)
    return pl.pallas_call(
        functools.partial(attend_kernel, heads),
        out_shape=(
            jax.ShapeDtypeStruct(both, jnp.bfloat16),
            jax.ShapeDtypeStruct(window.shape, jnp.bfloat16),
        ),
        in_specs=[pl.BlockSpec(memory_space=pltpu.VMEM)] + [some] * 6,
        out_specs=(some, some),
        scratch_shapes=[
            pltpu.VMEM(both, q.dtype),
            pltpu.VMEM(both, q.dtype),
            pltpu.VMEM(stat.shape, stat.dtype),
            pltpu.VMEM(window.shape, window.dtype),
            pltpu.VMEM((4, B, features), jnp.bfloat16),
            pltpu.VMEM(window.shape, jnp.bfloat16),
            pltpu.VMEM((W, heads * B), jnp.float32),
            pltpu.VMEM((16, B, W), jnp.float32),
            pltpu.VMEM((16, B, W), jnp.float32),
            pltpu.VMEM((B, B), jnp.float32),
            pltpu.SemaphoreType.DMA((6,)),
            pltpu.SemaphoreType.DMA((20,)),
        ],
        compiler_params=pltpu.CompilerParams(vmem_limit_bytes=VMEM),
        cost_estimate=pl.CostEstimate(
            flops=20 * 10 * heads * B * B * W, bytes_accessed=16 << 20, transcendentals=0
        ),
    )(docs, q, q_other, g, g_other, stat, window)


def return_kernel(
    columns, dq_ref, part_ref, dq_got, dk_ref, dv_ref,
    part, across_got, beside_got, beside_sum, later_got, far_got, far_sum, near_sum, near_got,
    final, local, send, recv,
):
    at = Links(columns)
    z, core, up, down, across = at.z, at.core, at.up, at.down, at.across
    sems = (send, recv)
    load = pltpu.make_async_copy(part_ref, part, local.at[0])
    load.start()
    at.barrier()
    has_next, has_last = at.has_next, at.has_last

    def given(side, zc, j):
        return part_ref.at[slot(side, zc, j)]

    def held(side, zc, j):
        return part[slot(side, zc, j)].astype(jnp.float32)

    far_back = [
        Route(
            sems, j, at.last, given(BEFORE, across, j), across_got.at[j],
            has_last & (z < 2) if j == 0 else has_last,
            has_next & (z < 2) if j == 0 else has_next,
        )
        for j in range(2)
    ]
    side_up = [
        Route(
            sems, 2 + j, at.above, given(BEFORE, up, j), beside_got.at[0, j],
            has_last & (z != 3) if j == 0 else has_last,
            has_last & (z != 0) if j == 0 else has_last,
        )
        for j in range(2)
    ]
    side_down = [
        Route(
            sems, 4 + j, at.below, given(BEFORE, down, j), beside_got.at[1, j],
            has_last & (z == 0) if j == 0 else has_last,
            has_last & (z == 3) if j == 0 else has_last,
        )
        for j in range(2)
    ]
    dq_half = dq_ref.shape[1] // 2
    bulk = [
        Route(
            sems, 6 + n, at.sibling,
            dq_ref.at[1, n * dq_half : (n + 1) * dq_half],
            dq_got.at[n * dq_half : (n + 1) * dq_half],
        )
        for n in range(2)
    ]
    back = [
        Route(sems, 8 + j, at.last, beside_sum.at[j], later_got.at[j], has_last, has_next)
        for j in range(2)
    ]
    far_up = Route(sems, 10, at.above, far_sum.at[0], far_got.at[0])
    far_down = Route(sems, 11, at.below, far_sum.at[1], far_got.at[1])
    near_up_0 = Route(sems, 12, at.above, near_sum.at[0], near_got.at[0])
    near_up_1 = Route(sems, 13, at.above, given(OWN, up, 1), near_got.at[1], z == 3, z == 0)
    near_down_0 = Route(sems, 14, at.below, given(OWN, down, 0), near_got.at[2])
    near_down_1 = Route(sems, 15, at.below, near_sum.at[1], near_got.at[3])

    for copy in (far_back[1], far_back[0], side_up[1], side_down[1], side_up[0], side_down[0]):
        copy.start()
    near_down_0.start()
    near_up_1.start()
    for copy in bulk:
        copy.start()
    load.wait()

    @pl.when(has_last)
    def _():
        for copy in side_up + side_down:
            copy.arrived()
        for j in range(2):
            final[j] = held(BEFORE, z, j)
        final[1] += beside_got[0, 1].astype(jnp.float32) + beside_got[1, 1].astype(jnp.float32)

        @pl.when(z != 0)
        def _():
            final[0] += beside_got[0, 0].astype(jnp.float32)

        @pl.when(z == 3)
        def _():
            final[0] += beside_got[1, 0].astype(jnp.float32)

        beside_sum[...] = final[...].astype(jnp.bfloat16)
        for copy in back:
            copy.start()

    def add_across(j):
        far_back[j].make(across_got.at[j]).wait_recv()
        final[j] += across_got[j].astype(jnp.float32)

    for j in range(2):
        final[j] = held(OWN, across, j)
        pl.when(far_back[j].gets)(functools.partial(add_across, j))
        far_sum[j] = final[j].astype(jnp.bfloat16)
    far_up.start()
    far_down.start()
    far_up.arrived()
    near_sum[0] = (held(OWN, up, 0) + far_got[0].astype(jnp.float32)).astype(jnp.bfloat16)
    near_up_0.start()
    far_down.arrived()
    near_sum[1] = (held(OWN, down, 1) + far_got[1].astype(jnp.float32)).astype(jnp.bfloat16)
    near_down_1.start()
    near_down_0.arrived()
    near_up_0.arrived()
    final[0] = (
        held(OWN, z, 0) + near_got[0].astype(jnp.float32) + near_got[2].astype(jnp.float32)
    )
    near_up_1.arrived()
    near_down_1.arrived()
    final[1] = held(OWN, z, 1) + near_got[3].astype(jnp.float32)

    @pl.when(z == 0)
    def _():
        final[1] += near_got[1].astype(jnp.float32)

    @pl.when(has_next)
    def _():
        for j in range(2):
            back[j].arrived()
            final[j] += later_got[j].astype(jnp.float32)

    far_up.sent()
    far_down.sent()
    far_sum[0] = final[1 - core].astype(jnp.bfloat16)
    give_k = Route(sems, 16, at.sibling, far_sum.at[0, 0], dk_ref.at[B:])
    give_v = Route(sems, 17, at.sibling, far_sum.at[0, 1], dv_ref.at[B:])
    give_k.start()
    give_v.start()
    dk_ref[:B] = final[core, 0].astype(jnp.bfloat16)
    dv_ref[:B] = final[core, 1].astype(jnp.bfloat16)
    give_k.arrived()
    give_v.arrived()
    for copy in bulk:
        copy.arrived()
    for copy in (
        far_back + side_up + side_down + bulk + back
        + [near_up_0, near_up_1, near_down_0, near_down_1, give_k, give_v]
    ):
        copy.sent()


def give_back(columns, dq, part):
    rows, features = dq.shape[1:]
    some = pl.BlockSpec(memory_space=pl.ANY)
    vmem = pl.BlockSpec(memory_space=pltpu.VMEM)
    block = (2, B, W)
    return pl.pallas_call(
        functools.partial(return_kernel, columns),
        out_shape=(
            jax.ShapeDtypeStruct((rows, features), jnp.bfloat16),
            jax.ShapeDtypeStruct((rows, W), jnp.bfloat16),
            jax.ShapeDtypeStruct((rows, W), jnp.bfloat16),
        ),
        in_specs=[some] * 2,
        out_specs=(some, vmem, vmem),
        scratch_shapes=[
            pltpu.VMEM((16, *block), jnp.bfloat16),
            pltpu.VMEM((2, *block), jnp.bfloat16),
            pltpu.VMEM((2, 2, *block), jnp.bfloat16),
            pltpu.VMEM((2, *block), jnp.bfloat16),
            pltpu.VMEM((2, *block), jnp.bfloat16),
            pltpu.VMEM((2, *block), jnp.bfloat16),
            pltpu.VMEM((2, *block), jnp.bfloat16),
            pltpu.VMEM((2, *block), jnp.bfloat16),
            pltpu.VMEM((4, *block), jnp.bfloat16),
            pltpu.VMEM((2, *block), jnp.float32),
            pltpu.SemaphoreType.DMA((1,)),
            pltpu.SemaphoreType.DMA((18,)),
            pltpu.SemaphoreType.DMA((18,)),
        ],
        compiler_params=pltpu.CompilerParams(
            collective_id=1, has_side_effects=True, vmem_limit_bytes=VMEM
        ),
    )(dq, part)


def solution(mesh):
    columns = mesh.shape["ctx"] // 2

    def on_device(q, k, v, o, g, log_total, doc_lengths):
        q_other, g_other, stat, window = gather(columns, q, g, o, k, v, log_total)
        dq, part = attend(doc_lengths[None, :], q, q_other, g, g_other, stat, window)
        dq_got, dk, dv = give_back(columns, dq, part)
        dq = (dq[0].astype(jnp.float32) + dq_got.astype(jnp.float32)).astype(jnp.bfloat16)
        return dq, dk, dv

    rows = P(("ctx", "section"), None)
    return jax.shard_map(
        on_device,
        mesh=mesh,
        in_specs=(rows, rows, rows, rows, rows, P(None, ("ctx", "section")), P()),
        out_specs=(rows, rows, rows),
        check_vma=False,
    )
```

```python
import functools
import math

import jax
import jax.numpy as jnp
from jax import lax
from jax.experimental import pallas as pl
from jax.experimental.pallas import tpu as pltpu
from jax.sharding import PartitionSpec as P

MESH = pl.DeviceIdType.MESH
W = 128
B = 256
VMEM = 58 << 20
LOG2E = math.log2(math.e)
OWN, BEFORE = 1, 0


def nn(a, b):
    return jnp.dot(a, b, preferred_element_type=jnp.float32)


def nt(a, b):
    return lax.dot_general(a, b, (((1,), (1,)), ((), ())), preferred_element_type=jnp.float32)


def place():
    ctx = lax.axis_index("ctx")
    return ctx // 2, lax.axis_index("section"), ctx % 2


def slot(side, z, j):
    return side * 8 + z * 2 + j


def doc_ends(docs_ref):
    lengths = docs_ref[...].astype(jnp.float32)
    docs = lengths.shape[1]
    upto = lax.broadcasted_iota(jnp.int32, (docs, docs), 1) <= lax.broadcasted_iota(
        jnp.int32, (docs, docs), 0
    )
    return jnp.sum(jnp.where(upto, lengths, 0.0), axis=1, keepdims=True)


def positions(first):
    return first.astype(jnp.float32) + lax.broadcasted_iota(jnp.int32, (1, B), 1).astype(
        jnp.float32
    )


def doc_start(ends, pos):
    return jnp.max(jnp.where(ends <= pos, ends, 0.0), axis=0, keepdims=True)


def hidden(key, start, pos):
    kpos = (key + lax.broadcasted_iota(jnp.int32, (B, B), 0)).astype(jnp.float32)
    return jnp.where((kpos >= start) & (kpos <= pos), 0.0, -jnp.inf)


def identity(n):
    at = [lax.broadcasted_iota(jnp.int32, (n, n), d) for d in range(2)]
    return (at[0] == at[1]).astype(jnp.bfloat16)


def gradients(k, v, qs, gs, logs, deltas, bias=None):
    ps, ds = [], []
    for q, g, log, delta in zip(qs, gs, logs, deltas):
        x = nt(k, q) * (LOG2E / math.sqrt(W)) - log
        if bias is not None:
            x = x + bias[...]
        p = jnp.exp2(x)
        d = p * (nt(v, g) - delta)
        ps.append(p.astype(jnp.bfloat16))
        ds.append(d.astype(jnp.bfloat16))
    dh = jnp.concatenate(ds, axis=1)
    dv = nn(jnp.concatenate(ps, axis=1), jnp.concatenate(gs, axis=0))
    dk = nn(dh, jnp.concatenate(qs, axis=0))
    return dk, dv, nn(k.T, dh)


class Links:
    def __init__(self, columns):
        self.column, self.z, self.core = place()
        ctx = lax.axis_index("ctx")
        self.up = lax.rem(self.z + 1, 4)
        self.down = lax.rem(self.z + 3, 4)
        self.across = lax.rem(self.z + 2, 4)
        self.sibling = (ctx + 1 - 2 * self.core, self.z)
        self.above = (ctx, self.up)
        self.below = (ctx, self.down)
        self.has_next = self.column < columns - 1
        self.has_last = self.column > 0
        self.next = (jnp.where(self.has_next, ctx + 2, ctx), self.z)
        self.last = (jnp.where(self.has_last, ctx - 2, ctx), self.z)

    def barrier(self):
        barrier = pltpu.get_barrier_semaphore()

        def greet(device):
            pl.semaphore_signal(barrier, inc=1, device_id=device, device_id_type=MESH)

        greet(self.sibling)
        greet(self.above)
        greet(self.below)
        pl.when(self.has_next)(lambda: greet(self.next))
        pl.when(self.has_last)(lambda: greet(self.last))
        peers = 3 + self.has_next.astype(jnp.int32) + self.has_last.astype(jnp.int32)
        pl.semaphore_wait(barrier, peers)


class Route:
    def __init__(self, sems, index, device, source, target, sends=True, gets=True, arrival=None):
        self.sends, self.gets = sends, gets
        landed = target if arrival is None else arrival
        send, recv = sems[0].at[index], sems[1].at[index]
        self.make = lambda end: pltpu.make_async_remote_copy(
            source, end, send, recv, device_id=device, device_id_type=MESH
        )
        self.target, self.landed = target, landed

    @staticmethod
    def only(condition, act):
        if condition is True:
            act()
        else:
            pl.when(condition)(act)

    def start(self):
        self.only(self.sends, lambda: self.make(self.target).start())

    def arrived(self):
        self.only(self.gets, lambda: self.make(self.landed).wait_recv())

    def sent(self):
        self.only(self.sends, lambda: self.make(self.target).wait_send())


def gather_kernel(
    columns, heads, q_ref, g_ref, o_ref, k_ref, v_ref, log_ref,
    q_other, g_other, stat_both, window,
    g_vmem, o_vmem, stat, local, send, recv,
):
    at = Links(columns)
    z, core, up, down, across = at.z, at.core, at.up, at.down, at.across
    sems = (send, recv)
    load_g = pltpu.make_async_copy(g_ref, g_vmem, local.at[0])
    load_o = pltpu.make_async_copy(o_ref, o_vmem, local.at[1])
    load_g.start()
    load_o.start()
    load_log = pltpu.make_async_copy(log_ref, stat.at[0], local.at[5])
    load_log.start()
    mine = window.at[slot(OWN, z, core)]
    keep_k = pltpu.make_async_copy(k_ref.at[:B], mine.at[0], local.at[2])
    keep_v = pltpu.make_async_copy(v_ref.at[:B], mine.at[1], local.at[3])
    keep_k.start()
    keep_v.start()
    at.barrier()

    theirs = window.at[slot(OWN, z, 1 - core)]
    swap_k = Route(sems, 0, at.sibling, k_ref.at[B:], mine.at[0], arrival=theirs.at[0])
    swap_v = Route(sems, 1, at.sibling, v_ref.at[B:], mine.at[1], arrival=theirs.at[1])
    swap_k.start()
    swap_v.start()
    rows = q_ref.shape[0]
    bulk = []
    for part in range(2):
        some = slice(part * rows // 2, (part + 1) * rows // 2)
        bulk.append(Route(sems, 2 + part, at.sibling, q_ref.at[some], q_other.at[some]))
        bulk.append(Route(sems, 4 + part, at.sibling, g_ref.at[some], g_other.at[some]))
    for copy in bulk:
        copy.start()

    def passed(index, device, side, sent, j, got, sends=True, gets=True):
        there = window.at[slot(side, sent, j)]
        return Route(sems, index, device, there, there, sends, gets, window.at[slot(side, got, j)])

    up_0 = passed(6, at.above, OWN, z, 0, down)
    up_1 = passed(7, at.above, OWN, z, 1, down)
    down_0 = passed(8, at.below, OWN, z, 0, up)
    down_1 = passed(9, at.below, OWN, z, 1, up, z == 0, z == 3)
    far_0 = passed(10, at.below, OWN, up, 0, across)
    far_1 = passed(11, at.above, OWN, down, 1, across)

    def later(index, zc, j, when=True):
        here = window.at[slot(OWN, zc, j)]
        there = window.at[slot(BEFORE, zc, j)]
        sends = at.has_next if when is True else at.has_next & when
        gets = at.has_last if when is True else at.has_last & when
        return Route(sems, index, at.next, here, there, sends, gets)

    next_0 = later(12, z, 0)
    next_1 = later(13, z, 1)
    next_far_0 = later(14, across, 0, z < 2)
    next_far_1 = later(15, across, 1)
    last = at.has_last
    before_up_0 = passed(16, at.above, BEFORE, z, 0, down, last & (z == 3), last & (z == 0))
    before_up_1 = passed(17, at.above, BEFORE, z, 1, down, last, last)
    before_down_0 = passed(18, at.below, BEFORE, z, 0, up, last & (z != 0), last & (z != 3))
    before_down_1 = passed(19, at.below, BEFORE, z, 1, up, last, last)

    keep_k.wait()
    keep_v.wait()
    swap_k.arrived()
    swap_v.arrived()
    for copy in (down_0, up_1, next_1, next_0, up_0, down_1):
        copy.start()

    load_g.wait()
    load_o.wait()
    ones = jnp.ones((8, W), jnp.bfloat16)
    for h in range(heads):
        cols = slice(h * W, (h + 1) * W)
        product = g_vmem[:, cols].astype(jnp.float32) * o_vmem[:, cols].astype(jnp.float32)
        high = product.astype(jnp.bfloat16)
        low = (product - high.astype(jnp.float32)).astype(jnp.bfloat16)
        total = nt(ones, high) + nt(ones, low)
        stat[1, h : h + 1, :] = total[0:1]
    load_log.wait()
    stat[0] = stat[0] * LOG2E
    stats = Route(sems, 20, at.sibling, stat, stat_both.at[1])
    stats.start()
    keep_stat = pltpu.make_async_copy(stat, stat_both.at[0], local.at[4])
    keep_stat.start()

    down_0.arrived()
    far_0.start()
    up_1.arrived()
    far_1.start()
    next_0.arrived()
    next_1.arrived()
    for copy in (before_down_1, before_up_1, before_down_0, before_up_0):
        copy.start()
    far_0.arrived()
    far_1.arrived()
    next_far_1.start()
    next_far_0.start()
    for copy in (up_0, down_1, before_up_0, before_up_1, before_down_0, before_down_1):
        copy.arrived()
    next_far_0.arrived()
    next_far_1.arrived()
    for copy in bulk:
        copy.arrived()
    stats.arrived()
    keep_stat.wait()
    for copy in (
        [swap_k, swap_v, up_0, up_1, down_0, down_1, far_0, far_1, next_0, next_1, next_far_0]
        + [next_far_1, before_up_0, before_up_1, before_down_0, before_down_1, stats]
        + bulk
    ):
        copy.sent()


def gather(columns, q, g, o, k, v, log_total):
    rows, features = q.shape
    heads = features // W
    some = pl.BlockSpec(memory_space=pl.ANY)
    return pl.pallas_call(
        functools.partial(gather_kernel, columns, heads),
        out_shape=(
            jax.ShapeDtypeStruct((rows, features), q.dtype),
            jax.ShapeDtypeStruct((rows, features), q.dtype),
            jax.ShapeDtypeStruct((2, 2, heads, rows), jnp.float32),
            jax.ShapeDtypeStruct((16, 2, B, W), k.dtype),
        ),
        in_specs=[some] * 6,
        out_specs=(some,) * 4,
        scratch_shapes=[
            pltpu.VMEM((rows, features), g.dtype),
            pltpu.VMEM((rows, features), g.dtype),
            pltpu.VMEM((2, heads, rows), jnp.float32),
            pltpu.SemaphoreType.DMA((6,)),
            pltpu.SemaphoreType.DMA((21,)),
            pltpu.SemaphoreType.DMA((21,)),
        ],
        compiler_params=pltpu.CompilerParams(
            collective_id=0, has_side_effects=True, vmem_limit_bytes=VMEM
        ),
    )(q, g, o, k, v, log_total)


def attend_kernel(
    heads, docs_ref, qa_hbm, qb_hbm, ga_hbm, gb_hbm, stat_hbm, window_hbm,
    dq_own, dq_other, part_hbm,
    q_ref, g_ref, stat_ref, window_ref, dqt, dqh, part_ref, dka, dva, bias, starts, bounds, get, put,
):
    column, z, core = place()
    loads = [
        pltpu.make_async_copy(source, target, get.at[n])
        for n, (source, target) in enumerate(
            (
                (stat_hbm, stat_ref),
                (window_hbm.at[:8], window_ref.at[:8]), (window_hbm.at[8:], window_ref.at[8:]),
                (qa_hbm, q_ref.at[0]), (ga_hbm, g_ref.at[0]),
                (qb_hbm, q_ref.at[1]), (gb_hbm, g_ref.at[1]),
            )
        )
    ]
    for load in loads:
        load.start()
    ends = doc_ends(docs_ref)
    window = (column - 1) * 16 * B

    def half_of(b):
        return jnp.where(b % 8 >= 4, 1 - core, core)

    def tile_of(side):
        return z + 4 * (core if side == 0 else 1 - core)

    for block in range(4):
        side, part = divmod(block, 2)
        first = column * 16 * B + tile_of(side) * 2 * B + part * B
        start = doc_start(ends, positions(first))
        starts[block] = start
        rel = jnp.min(start).astype(jnp.int32) - window
        lo = rel // (2 * B)
        lo = jnp.where(rel % (2 * B) >= half_of(lo) * B + B, lo + 1, lo)
        bounds[0, block] = lo
        bounds[1, block] = jnp.max(start).astype(jnp.int32)
    dka[...] = jnp.zeros_like(dka)
    dva[...] = jnp.zeros_like(dva)
    dqt[...] = jnp.zeros_like(dqt)
    for load in loads[:5]:
        load.wait()

    @pl.loop(0, 4)
    def _(block):
        side, part = block // 2, block % 2
        here = pl.ds(pl.multiple_of(part * B, B), B)

        @pl.when(block == 2)
        def _():
            for load in loads[5:]:
                load.wait()

        def work(b, masked):
            at = slot(b // 8, b % 4, b % 8 // 4)
            dk, dv, dq = gradients(
                window_ref[at, 0],
                window_ref[at, 1],
                [q_ref[side, here, h * W : (h + 1) * W] for h in range(heads)],
                [g_ref[side, here, h * W : (h + 1) * W] for h in range(heads)],
                [stat_ref[side, 0, h : h + 1, here] for h in range(heads)],
                [stat_ref[side, 1, h : h + 1, here] for h in range(heads)],
                bias if masked else None,
            )
            dva[at] += dv
            dka[at] += dk
            dqt[block] += dq

        def step(b, inner):
            key = window + b * 2 * B + half_of(b) * B
            full = key >= bounds[1, block]

            @pl.when(full)
            def _():
                work(b, False)

            @pl.when(jnp.logical_not(full))
            def _():
                kpos = (key + lax.broadcasted_iota(jnp.int32, (B, B), 0)).astype(jnp.float32)
                bias[...] = jnp.where(kpos >= starts[block], 0.0, -jnp.inf)
                work(b, True)

            return inner

        diagonal = 8 + z + 4 * jnp.where(side == 0, core, 1 - core)
        lax.fori_loop(bounds[0, block], diagonal, step, 0)

        @pl.when(side == 0)
        def _():
            pltpu.make_async_copy(dqt.at[block], dq_own.at[part], put.at[block]).start()

        @pl.when(side == 1)
        def _():
            dqh[part] = dqt[block].astype(jnp.bfloat16)
            pltpu.make_async_copy(dqh.at[part], dq_other.at[part], put.at[block]).start()

    @pl.loop(0, 16)
    def _(s):
        part_ref[s, 0] = (dka[s] * (1.0 / math.sqrt(W))).astype(jnp.bfloat16)
        part_ref[s, 1] = dva[s].astype(jnp.bfloat16)
        pltpu.make_async_copy(part_ref.at[s], part_hbm.at[s], put.at[4 + s]).start()

    for part in range(2):
        pltpu.make_async_copy(dqt.at[part], dq_own.at[part], put.at[part]).wait()
        pltpu.make_async_copy(dqh.at[part], dq_other.at[part], put.at[2 + part]).wait()
    for s in range(16):
        pltpu.make_async_copy(part_ref.at[s], part_hbm.at[s], put.at[4 + s]).wait()


def attend(docs, q, q_other, g, g_other, stat, window):
    rows, features = q.shape
    heads = features // W
    some = pl.BlockSpec(memory_space=pl.ANY)
    both = (2, rows, features)
    turned = (2, W, heads * B)
    return pl.pallas_call(
        functools.partial(attend_kernel, heads),
        out_shape=(
            jax.ShapeDtypeStruct(turned, jnp.float32),
            jax.ShapeDtypeStruct(turned, jnp.bfloat16),
            jax.ShapeDtypeStruct(window.shape, jnp.bfloat16),
        ),
        in_specs=[pl.BlockSpec(memory_space=pltpu.VMEM)] + [some] * 6,
        out_specs=(some,) * 3,
        scratch_shapes=[
            pltpu.VMEM(both, q.dtype),
            pltpu.VMEM(both, q.dtype),
            pltpu.VMEM(stat.shape, stat.dtype),
            pltpu.VMEM(window.shape, window.dtype),
            pltpu.VMEM((4, W, heads * B), jnp.float32),
            pltpu.VMEM(turned, jnp.bfloat16),
            pltpu.VMEM(window.shape, jnp.bfloat16),
            pltpu.VMEM((16, B, W), jnp.float32),
            pltpu.VMEM((16, B, W), jnp.float32),
            pltpu.VMEM((B, B), jnp.float32),
            pltpu.VMEM((4, 1, B), jnp.float32),
            pltpu.SMEM((2, 4), jnp.int32),
            pltpu.SemaphoreType.DMA((7,)),
            pltpu.SemaphoreType.DMA((20,)),
        ],
        compiler_params=pltpu.CompilerParams(vmem_limit_bytes=VMEM),
        cost_estimate=pl.CostEstimate(
            flops=20 * 10 * heads * B * B * W, bytes_accessed=16 << 20, transcendentals=0
        ),
    )(docs, q, q_other, g, g_other, stat, window)


def return_kernel(
    columns, heads, docs_ref, q_hbm, k_hbm, v_hbm, g_hbm, stat_hbm, dq_own, dq_other, part_ref,
    dq_hbm, dk_hbm, dv_hbm,
    q_ref, k_ref, v_ref, g_ref, stat, dqt, dq_got, dq_out, dk_ref, dv_ref, dka, dva, bias,
    part, across_got, beside_got, beside_sum, later_got, far_got, far_sum, near_sum, near_got,
    final, local, put, send, recv,
):
    at = Links(columns)
    z, core, up, down, across = at.z, at.core, at.up, at.down, at.across
    sems = (send, recv)
    load = pltpu.make_async_copy(part_ref, part, local.at[0])
    load.start()
    loads = [
        pltpu.make_async_copy(source, target, local.at[1 + n])
        for n, (source, target) in enumerate(
            (
                (q_hbm, q_ref), (g_hbm, g_ref), (k_hbm, k_ref), (v_hbm, v_ref),
                (stat_hbm.at[0], stat), (dq_own, dqt),
            )
        )
    ]
    for copy in loads:
        copy.start()
    at.barrier()
    has_next, has_last = at.has_next, at.has_last

    def given(side, zc, j):
        return part_ref.at[slot(side, zc, j)]

    def held(side, zc, j):
        return part[slot(side, zc, j)].astype(jnp.float32)

    far_back = [
        Route(
            sems, j, at.last, given(BEFORE, across, j), across_got.at[j],
            has_last & (z < 2) if j == 0 else has_last,
            has_next & (z < 2) if j == 0 else has_next,
        )
        for j in range(2)
    ]
    side_up = [
        Route(
            sems, 2 + j, at.above, given(BEFORE, up, j), beside_got.at[0, j],
            has_last & (z != 3) if j == 0 else has_last,
            has_last & (z != 0) if j == 0 else has_last,
        )
        for j in range(2)
    ]
    side_down = [
        Route(
            sems, 4 + j, at.below, given(BEFORE, down, j), beside_got.at[1, j],
            has_last & (z == 0) if j == 0 else has_last,
            has_last & (z == 3) if j == 0 else has_last,
        )
        for j in range(2)
    ]
    bulk = [
        Route(sems, 6 + n, at.sibling, dq_other.at[n], dq_got.at[n]) for n in range(2)
    ]
    back = [
        Route(sems, 8 + j, at.last, beside_sum.at[j], later_got.at[j], has_last, has_next)
        for j in range(2)
    ]
    far_up = Route(sems, 10, at.above, far_sum.at[0], far_got.at[0])
    far_down = Route(sems, 11, at.below, far_sum.at[1], far_got.at[1])
    near_up_0 = Route(sems, 12, at.above, near_sum.at[0], near_got.at[0])
    near_up_1 = Route(sems, 13, at.above, given(OWN, up, 1), near_got.at[1], z == 3, z == 0)
    near_down_0 = Route(sems, 14, at.below, given(OWN, down, 0), near_got.at[2])
    near_down_1 = Route(sems, 15, at.below, near_sum.at[1], near_got.at[3])

    for copy in (far_back[1], far_back[0], side_up[1], side_down[1], side_up[0], side_down[0]):
        copy.start()
    near_down_0.start()
    near_up_1.start()
    for copy in bulk:
        copy.start()
    load.wait()

    @pl.when(has_last)
    def _():
        for copy in side_up + side_down:
            copy.arrived()
        for j in range(2):
            final[j] = held(BEFORE, z, j)
        final[1] += beside_got[0, 1].astype(jnp.float32) + beside_got[1, 1].astype(jnp.float32)

        @pl.when(z != 0)
        def _():
            final[0] += beside_got[0, 0].astype(jnp.float32)

        @pl.when(z == 3)
        def _():
            final[0] += beside_got[1, 0].astype(jnp.float32)

        beside_sum[...] = final[...].astype(jnp.bfloat16)
        for copy in back:
            copy.start()

    def add_across(j):
        far_back[j].make(across_got.at[j]).wait_recv()
        final[j] += across_got[j].astype(jnp.float32)

    for j in range(2):
        final[j] = held(OWN, across, j)
        pl.when(far_back[j].gets)(functools.partial(add_across, j))
        far_sum[j] = final[j].astype(jnp.bfloat16)
    far_up.start()
    far_down.start()
    for copy in loads:
        copy.wait()
    ends = doc_ends(docs_ref)
    tile = at.column * 16 * B + (z + 4 * core) * 2 * B
    dka[...] = jnp.zeros_like(dka)
    dva[...] = jnp.zeros_like(dva)

    def diagonal(n):
        block, b = (n + 1) // 2, n // 2
        here = pl.ds(pl.multiple_of(block * B, B), B)
        there = pl.ds(pl.multiple_of(b * B, B), B)
        pos = positions(tile + block * B)
        bias[...] = hidden(tile + b * B, doc_start(ends, pos), pos)
        dk, dv, dq = gradients(
            k_ref[there],
            v_ref[there],
            [q_ref[here, h * W : (h + 1) * W] for h in range(heads)],
            [g_ref[here, h * W : (h + 1) * W] for h in range(heads)],
            [stat[0, h : h + 1, here] for h in range(heads)],
            [stat[1, h : h + 1, here] for h in range(heads)],
            bias,
        )
        dka[b] += dk
        dva[b] += dv
        dqt[block] += dq

    pl.loop(0, 1)(diagonal)
    far_up.arrived()
    near_sum[0] = (held(OWN, up, 0) + far_got[0].astype(jnp.float32)).astype(jnp.bfloat16)
    near_up_0.start()
    far_down.arrived()
    near_sum[1] = (held(OWN, down, 1) + far_got[1].astype(jnp.float32)).astype(jnp.bfloat16)
    near_down_1.start()
    pl.loop(1, 3)(diagonal)
    for copy in bulk:
        copy.arrived()
    eye = identity(B)
    for block in range(2):
        for h in range(heads):
            rows = slice(h * B, (h + 1) * B)
            total = dqt[block, :, rows] + dq_got[block, :, rows].astype(jnp.float32)
            rounded = (total * (1.0 / math.sqrt(W))).astype(jnp.bfloat16)
            turned = nt(eye, rounded).astype(jnp.bfloat16)
            dq_out[block * B : (block + 1) * B, h * W : (h + 1) * W] = turned
    out_q = pltpu.make_async_copy(dq_out, dq_hbm, put.at[0])
    out_q.start()
    near_down_0.arrived()
    near_up_0.arrived()
    final[0] = (
        held(OWN, z, 0) + near_got[0].astype(jnp.float32) + near_got[2].astype(jnp.float32)
    )
    near_up_1.arrived()
    near_down_1.arrived()
    final[1] = held(OWN, z, 1) + near_got[3].astype(jnp.float32)

    @pl.when(z == 0)
    def _():
        final[1] += near_got[1].astype(jnp.float32)

    @pl.when(has_next)
    def _():
        for j in range(2):
            back[j].arrived()
            final[j] += later_got[j].astype(jnp.float32)

    far_up.sent()
    far_down.sent()
    far_sum[0] = final[1 - core].astype(jnp.bfloat16)
    give_k = Route(sems, 16, at.sibling, far_sum.at[0, 0], dk_ref.at[B:])
    give_v = Route(sems, 17, at.sibling, far_sum.at[0, 1], dv_ref.at[B:])
    give_k.start()
    give_v.start()
    scale = 1.0 / math.sqrt(W)
    dk_ref[:B] = (final[core, 0] + dka[0] * scale).astype(jnp.bfloat16)
    dv_ref[:B] = (final[core, 1] + dva[0]).astype(jnp.bfloat16)
    give_k.arrived()
    give_v.arrived()
    dk_ref[B:] = (dk_ref[B:].astype(jnp.float32) + dka[1] * scale).astype(jnp.bfloat16)
    dv_ref[B:] = (dv_ref[B:].astype(jnp.float32) + dva[1]).astype(jnp.bfloat16)
    out_k = pltpu.make_async_copy(dk_ref, dk_hbm, put.at[1])
    out_v = pltpu.make_async_copy(dv_ref, dv_hbm, put.at[2])
    out_k.start()
    out_v.start()
    for copy in (out_q, out_k, out_v):
        copy.wait()
    for copy in (
        far_back + side_up + side_down + bulk + back
        + [near_up_0, near_up_1, near_down_0, near_down_1, give_k, give_v]
    ):
        copy.sent()


def give_back(columns, docs, q, k, v, g, stat, dq_own, dq_other, part):
    rows, features = q.shape
    heads = features // W
    some = pl.BlockSpec(memory_space=pl.ANY)
    vmem = pl.BlockSpec(memory_space=pltpu.VMEM)
    block = (2, B, W)
    return pl.pallas_call(
        functools.partial(return_kernel, columns, heads),
        out_shape=(
            jax.ShapeDtypeStruct((rows, features), jnp.bfloat16),
            jax.ShapeDtypeStruct((rows, W), jnp.bfloat16),
            jax.ShapeDtypeStruct((rows, W), jnp.bfloat16),
        ),
        in_specs=[vmem] + [some] * 8,
        out_specs=(some,) * 3,
        scratch_shapes=[
            pltpu.VMEM(q.shape, q.dtype),
            pltpu.VMEM(k.shape, k.dtype),
            pltpu.VMEM(v.shape, v.dtype),
            pltpu.VMEM(g.shape, g.dtype),
            pltpu.VMEM(stat.shape[1:], stat.dtype),
            pltpu.VMEM(dq_own.shape, dq_own.dtype),
            pltpu.VMEM(dq_other.shape, dq_other.dtype),
            pltpu.VMEM(q.shape, jnp.bfloat16),
            pltpu.VMEM((rows, W), jnp.bfloat16),
            pltpu.VMEM((rows, W), jnp.bfloat16),
            pltpu.VMEM((2, B, W), jnp.float32),
            pltpu.VMEM((2, B, W), jnp.float32),
            pltpu.VMEM((B, B), jnp.float32),
            pltpu.VMEM((16, *block), jnp.bfloat16),
            pltpu.VMEM((2, *block), jnp.bfloat16),
            pltpu.VMEM((2, 2, *block), jnp.bfloat16),
            pltpu.VMEM((2, *block), jnp.bfloat16),
            pltpu.VMEM((2, *block), jnp.bfloat16),
            pltpu.VMEM((2, *block), jnp.bfloat16),
            pltpu.VMEM((2, *block), jnp.bfloat16),
            pltpu.VMEM((2, *block), jnp.bfloat16),
            pltpu.VMEM((4, *block), jnp.bfloat16),
            pltpu.VMEM((2, *block), jnp.float32),
            pltpu.SemaphoreType.DMA((7,)),
            pltpu.SemaphoreType.DMA((3,)),
            pltpu.SemaphoreType.DMA((18,)),
            pltpu.SemaphoreType.DMA((18,)),
        ],
        compiler_params=pltpu.CompilerParams(
            collective_id=1, has_side_effects=True, vmem_limit_bytes=VMEM
        ),
    )(docs, q, k, v, g, stat, dq_own, dq_other, part)


def publish_kernel(*refs):
    sources, targets, sems = refs[:3], refs[3:6], refs[6]
    copies = [
        pltpu.make_async_copy(source, target, sems.at[n])
        for n, (source, target) in enumerate(zip(sources, targets))
    ]
    for copy in copies:
        copy.start()
    for copy in copies:
        copy.wait()


def publish(*results):
    some = pl.BlockSpec(memory_space=pl.ANY)
    return pl.pallas_call(
        publish_kernel,
        out_shape=tuple(jax.ShapeDtypeStruct(x.shape, x.dtype) for x in results),
        in_specs=[some] * 3,
        out_specs=(some,) * 3,
        scratch_shapes=[pltpu.SemaphoreType.DMA((3,))],
        compiler_params=pltpu.CompilerParams(vmem_limit_bytes=VMEM),
    )(*results)


def solution(mesh):
    columns = mesh.shape["ctx"] // 2

    def on_device(q, k, v, o, g, log_total, doc_lengths):
        q_other, g_other, stat, window = gather(columns, q, g, o, k, v, log_total)
        docs = doc_lengths[None, :]
        dq_own, dq_other, part = attend(docs, q, q_other, g, g_other, stat, window)
        dq, dk, dv = give_back(columns, docs, q, k, v, g, stat, dq_own, dq_other, part)
        return publish(dq, dk, dv)

    rows = P(("ctx", "section"), None)
    return jax.shard_map(
        on_device,
        mesh=mesh,
        in_specs=(rows, rows, rows, rows, rows, P(None, ("ctx", "section")), P()),
        out_specs=(rows, rows, rows),
        check_vma=False,
    )
```

```python
import functools
import math

import jax
import jax.numpy as jnp
from jax import lax
from jax.experimental import pallas as pl
from jax.experimental.pallas import tpu as pltpu
from jax.sharding import PartitionSpec as P

MESH = pl.DeviceIdType.MESH
W = 128
B = 256
VMEM = 58 << 20
LOG2E = math.log2(math.e)
OWN, BEFORE = 1, 0


def nn(a, b):
    return jnp.dot(a, b, preferred_element_type=jnp.float32)


def nt(a, b):
    return lax.dot_general(a, b, (((1,), (1,)), ((), ())), preferred_element_type=jnp.float32)


def place():
    ctx = lax.axis_index("ctx")
    return ctx // 2, lax.axis_index("section"), ctx % 2


def slot(side, z, j):
    return side * 8 + z * 2 + j


def doc_ends(docs_ref):
    lengths = docs_ref[...].astype(jnp.float32)
    docs = lengths.shape[1]
    upto = lax.broadcasted_iota(jnp.int32, (docs, docs), 1) <= lax.broadcasted_iota(
        jnp.int32, (docs, docs), 0
    )
    return jnp.sum(jnp.where(upto, lengths, 0.0), axis=1, keepdims=True)


def positions(first):
    return first.astype(jnp.float32) + lax.broadcasted_iota(jnp.int32, (1, B), 1).astype(
        jnp.float32
    )


def doc_start(ends, pos):
    return jnp.max(jnp.where(ends <= pos, ends, 0.0), axis=0, keepdims=True)


def hidden(key, start, pos):
    kpos = (key + lax.broadcasted_iota(jnp.int32, (B, B), 0)).astype(jnp.float32)
    return jnp.where((kpos >= start) & (kpos <= pos), 0.0, -jnp.inf)


def identity(n):
    at = [lax.broadcasted_iota(jnp.int32, (n, n), d) for d in range(2)]
    return (at[0] == at[1]).astype(jnp.bfloat16)


def gradients(k, v, qs, gs, logs, deltas, bias=None):
    ps, ds = [], []
    for q, g, log, delta in zip(qs, gs, logs, deltas):
        x = nt(k, q) * (LOG2E / math.sqrt(W)) - log
        if bias is not None:
            x = x + bias[...]
        p = jnp.exp2(x)
        d = p * (nt(v, g) - delta)
        ps.append(p.astype(jnp.bfloat16))
        ds.append(d.astype(jnp.bfloat16))
    dh = jnp.concatenate(ds, axis=1)
    dv = nn(jnp.concatenate(ps, axis=1), jnp.concatenate(gs, axis=0))
    dk = nn(dh, jnp.concatenate(qs, axis=0))
    return dk, dv, nn(k.T, dh)


class Links:
    def __init__(self, columns):
        self.column, self.z, self.core = place()
        ctx = lax.axis_index("ctx")
        self.up = lax.rem(self.z + 1, 4)
        self.down = lax.rem(self.z + 3, 4)
        self.across = lax.rem(self.z + 2, 4)
        self.sibling = (ctx + 1 - 2 * self.core, self.z)
        self.above = (ctx, self.up)
        self.below = (ctx, self.down)
        self.has_next = self.column < columns - 1
        self.has_last = self.column > 0
        self.next = (jnp.where(self.has_next, ctx + 2, ctx), self.z)
        self.last = (jnp.where(self.has_last, ctx - 2, ctx), self.z)

    def barrier(self):
        barrier = pltpu.get_barrier_semaphore()

        def greet(device):
            pl.semaphore_signal(barrier, inc=1, device_id=device, device_id_type=MESH)

        greet(self.sibling)
        greet(self.above)
        greet(self.below)
        pl.when(self.has_next)(lambda: greet(self.next))
        pl.when(self.has_last)(lambda: greet(self.last))
        peers = 3 + self.has_next.astype(jnp.int32) + self.has_last.astype(jnp.int32)
        pl.semaphore_wait(barrier, peers)


class Route:
    def __init__(self, sems, index, device, source, target, sends=True, gets=True, arrival=None):
        self.sends, self.gets = sends, gets
        landed = target if arrival is None else arrival
        send, recv = sems[0].at[index], sems[1].at[index]
        self.make = lambda end: pltpu.make_async_remote_copy(
            source, end, send, recv, device_id=device, device_id_type=MESH
        )
        self.target, self.landed = target, landed

    @staticmethod
    def only(condition, act):
        if condition is True:
            act()
        else:
            pl.when(condition)(act)

    def start(self):
        self.only(self.sends, lambda: self.make(self.target).start())

    def arrived(self):
        self.only(self.gets, lambda: self.make(self.landed).wait_recv())

    def sent(self):
        self.only(self.sends, lambda: self.make(self.target).wait_send())


def gather_kernel(
    columns, heads, q_ref, g_ref, o_ref, k_ref, v_ref, log_ref,
    q_other, g_other, stat_both, window_out,
    q_vmem, g_vmem, o_vmem, q_got, g_got, swap, stat, window, local, put, send, recv,
):
    at = Links(columns)
    z, core, up, down, across = at.z, at.core, at.up, at.down, at.across
    sems = (send, recv)
    mine = window.at[slot(OWN, z, core)]
    loads = [
        pltpu.make_async_copy(source, target, local.at[n])
        for n, (source, target) in enumerate(
            (
                (k_ref.at[B:], swap.at[0]), (v_ref.at[B:], swap.at[1]),
                (k_ref.at[:B], mine.at[0]), (v_ref.at[:B], mine.at[1]),
                (q_ref, q_vmem), (g_ref, g_vmem), (o_ref, o_vmem), (log_ref, stat.at[0, 0]),
            )
        )
    ]
    for copy in loads:
        copy.start()
    at.barrier()

    theirs = window.at[slot(OWN, z, 1 - core)]
    halves = Route(sems, 0, at.sibling, swap, mine, arrival=theirs)
    for copy in loads[:4]:
        copy.wait()
    halves.start()
    rows = q_ref.shape[0]
    bulk = []
    for part in range(2):
        some = slice(part * rows // 2, (part + 1) * rows // 2)
        bulk.append(Route(sems, 2 + part, at.sibling, q_vmem.at[some], q_got.at[some]))
        bulk.append(Route(sems, 4 + part, at.sibling, g_vmem.at[some], g_got.at[some]))

    def passed(index, device, side, sent, j, got, sends=True, gets=True):
        there = window.at[slot(side, sent, j)]
        return Route(sems, index, device, there, there, sends, gets, window.at[slot(side, got, j)])

    up_0 = passed(6, at.above, OWN, z, 0, down)
    up_1 = passed(7, at.above, OWN, z, 1, down)
    down_0 = passed(8, at.below, OWN, z, 0, up)
    down_1 = passed(9, at.below, OWN, z, 1, up, z == 0, z == 3)
    far_0 = passed(10, at.below, OWN, up, 0, across)
    far_1 = passed(11, at.above, OWN, down, 1, across)

    def later(index, zc, j, when=True):
        here = window.at[slot(OWN, zc, j)]
        there = window.at[slot(BEFORE, zc, j)]
        sends = at.has_next if when is True else at.has_next & when
        gets = at.has_last if when is True else at.has_last & when
        return Route(sems, index, at.next, here, there, sends, gets)

    next_0 = later(12, z, 0)
    next_1 = later(13, z, 1)
    next_far_0 = later(14, across, 0, z < 2)
    next_far_1 = later(15, across, 1)
    last = at.has_last
    before_up_0 = passed(16, at.above, BEFORE, z, 0, down, last & (z == 3), last & (z == 0))
    before_up_1 = passed(17, at.above, BEFORE, z, 1, down, last, last)
    before_down_0 = passed(18, at.below, BEFORE, z, 0, up, last & (z != 0), last & (z != 3))
    before_down_1 = passed(19, at.below, BEFORE, z, 1, up, last, last)

    halves.arrived()
    for copy in (up_1, down_0, next_1, up_0, down_1, next_0):
        copy.start()
    loads[4].wait()
    loads[5].wait()
    for copy in bulk:
        copy.start()

    loads[6].wait()
    loads[7].wait()
    ones = jnp.ones((8, W), jnp.bfloat16)
    for h in range(heads):
        cols = slice(h * W, (h + 1) * W)
        product = g_vmem[:, cols].astype(jnp.float32) * o_vmem[:, cols].astype(jnp.float32)
        high = product.astype(jnp.bfloat16)
        low = (product - high.astype(jnp.float32)).astype(jnp.bfloat16)
        total = nt(ones, high) + nt(ones, low)
        stat[0, 1, h : h + 1, :] = total[0:1]
    stat[0, 0] = stat[0, 0] * LOG2E
    stats = Route(sems, 20, at.sibling, stat.at[0], stat.at[1])
    stats.start()

    up_1.arrived()
    far_1.start()
    down_0.arrived()
    far_0.start()
    next_1.arrived()
    before_down_1.start()
    before_up_1.start()
    next_0.arrived()
    before_down_0.start()
    before_up_0.start()
    far_0.arrived()
    next_far_0.start()
    far_1.arrived()
    next_far_1.start()
    for copy in bulk:
        copy.arrived()
    stats.arrived()
    up_0.arrived()
    down_1.arrived()
    outs = [
        pltpu.make_async_copy(source, target, put.at[n])
        for n, (source, target) in enumerate(
            (
                (q_got, q_other), (g_got, g_other), (stat, stat_both),
                (window.at[8:], window_out.at[8:]), (window.at[:8], window_out.at[:8]),
            )
        )
    ]
    for copy in outs[:4]:
        copy.start()
    for copy in (before_up_0, before_up_1, before_down_0, before_down_1, next_far_0, next_far_1):
        copy.arrived()
    outs[4].start()
    for copy in (
        [halves, up_0, up_1, down_0, down_1, far_0, far_1, next_0, next_1, next_far_0]
        + [next_far_1, before_up_0, before_up_1, before_down_0, before_down_1, stats]
        + bulk
    ):
        copy.sent()
    for copy in outs:
        copy.wait()


def gather(columns, q, g, o, k, v, log_total):
    rows, features = q.shape
    heads = features // W
    some = pl.BlockSpec(memory_space=pl.ANY)
    window = (16, 2, B, W)
    stat = (2, 2, heads, rows)
    return pl.pallas_call(
        functools.partial(gather_kernel, columns, heads),
        out_shape=(
            jax.ShapeDtypeStruct(q.shape, q.dtype),
            jax.ShapeDtypeStruct(q.shape, q.dtype),
            jax.ShapeDtypeStruct(stat, jnp.float32),
            jax.ShapeDtypeStruct(window, k.dtype),
        ),
        in_specs=[some] * 6,
        out_specs=(some,) * 4,
        scratch_shapes=[
            pltpu.VMEM(q.shape, q.dtype),
            pltpu.VMEM(q.shape, q.dtype),
            pltpu.VMEM(q.shape, q.dtype),
            pltpu.VMEM(q.shape, q.dtype),
            pltpu.VMEM(q.shape, q.dtype),
            pltpu.VMEM((2, B, W), k.dtype),
            pltpu.VMEM(stat, jnp.float32),
            pltpu.VMEM(window, k.dtype),
            pltpu.SemaphoreType.DMA((8,)),
            pltpu.SemaphoreType.DMA((5,)),
            pltpu.SemaphoreType.DMA((21,)),
            pltpu.SemaphoreType.DMA((21,)),
        ],
        compiler_params=pltpu.CompilerParams(
            collective_id=0, has_side_effects=True, vmem_limit_bytes=VMEM
        ),
    )(q, g, o, k, v, log_total)


def attend_kernel(
    heads, docs_ref, qa_hbm, qb_hbm, ga_hbm, gb_hbm, stat_hbm, window_hbm,
    dq_own, dq_other, part_hbm,
    q_ref, g_ref, stat_ref, window_ref, dqt, dqh, part_ref, dka, dva, bias, starts, bounds, get, put,
):
    column, z, core = place()
    loads = [
        pltpu.make_async_copy(source, target, get.at[n])
        for n, (source, target) in enumerate(
            (
                (stat_hbm, stat_ref),
                (window_hbm.at[:8], window_ref.at[:8]), (window_hbm.at[8:], window_ref.at[8:]),
                (qa_hbm, q_ref.at[0]), (ga_hbm, g_ref.at[0]),
                (qb_hbm, q_ref.at[1]), (gb_hbm, g_ref.at[1]),
            )
        )
    ]
    for load in loads:
        load.start()
    ends = doc_ends(docs_ref)
    window = (column - 1) * 16 * B

    def half_of(b):
        return jnp.where(b % 8 >= 4, 1 - core, core)

    def tile_of(side):
        return z + 4 * (core if side == 0 else 1 - core)

    for block in range(4):
        side, part = divmod(block, 2)
        first = column * 16 * B + tile_of(side) * 2 * B + part * B
        start = doc_start(ends, positions(first))
        starts[block] = start
        rel = jnp.min(start).astype(jnp.int32) - window
        lo = rel // (2 * B)
        lo = jnp.where(rel % (2 * B) >= half_of(lo) * B + B, lo + 1, lo)
        bounds[0, block] = lo
        bounds[1, block] = jnp.max(start).astype(jnp.int32)
    dka[...] = jnp.zeros_like(dka)
    dva[...] = jnp.zeros_like(dva)
    dqt[...] = jnp.zeros_like(dqt)
    for load in loads[:5]:
        load.wait()

    @pl.loop(0, 4)
    def _(block):
        side, part = block // 2, block % 2
        here = pl.ds(pl.multiple_of(part * B, B), B)

        @pl.when(block == 2)
        def _():
            for load in loads[5:]:
                load.wait()

        def work(b, masked):
            at = slot(b // 8, b % 4, b % 8 // 4)
            dk, dv, dq = gradients(
                window_ref[at, 0],
                window_ref[at, 1],
                [q_ref[side, here, h * W : (h + 1) * W] for h in range(heads)],
                [g_ref[side, here, h * W : (h + 1) * W] for h in range(heads)],
                [stat_ref[side, 0, h : h + 1, here] for h in range(heads)],
                [stat_ref[side, 1, h : h + 1, here] for h in range(heads)],
                bias if masked else None,
            )
            dva[at] += dv
            dka[at] += dk
            dqt[block] += dq

        def step(b, inner):
            key = window + b * 2 * B + half_of(b) * B
            full = key >= bounds[1, block]

            @pl.when(full)
            def _():
                work(b, False)

            @pl.when(jnp.logical_not(full))
            def _():
                kpos = (key + lax.broadcasted_iota(jnp.int32, (B, B), 0)).astype(jnp.float32)
                bias[...] = jnp.where(kpos >= starts[block], 0.0, -jnp.inf)
                work(b, True)

            return inner

        diagonal = 8 + z + 4 * jnp.where(side == 0, core, 1 - core)
        lax.fori_loop(bounds[0, block], diagonal, step, 0)

        @pl.when(side == 0)
        def _():
            pltpu.make_async_copy(dqt.at[block], dq_own.at[part], put.at[block]).start()

        @pl.when(side == 1)
        def _():
            dqh[part] = dqt[block].astype(jnp.bfloat16)
            pltpu.make_async_copy(dqh.at[part], dq_other.at[part], put.at[block]).start()

    @pl.loop(0, 16)
    def _(s):
        part_ref[s, 0] = (dka[s] * (1.0 / math.sqrt(W))).astype(jnp.bfloat16)
        part_ref[s, 1] = dva[s].astype(jnp.bfloat16)
        pltpu.make_async_copy(part_ref.at[s], part_hbm.at[s], put.at[4 + s]).start()

    for part in range(2):
        pltpu.make_async_copy(dqt.at[part], dq_own.at[part], put.at[part]).wait()
        pltpu.make_async_copy(dqh.at[part], dq_other.at[part], put.at[2 + part]).wait()
    for s in range(16):
        pltpu.make_async_copy(part_ref.at[s], part_hbm.at[s], put.at[4 + s]).wait()


def attend(docs, q, q_other, g, g_other, stat, window):
    rows, features = q.shape
    heads = features // W
    some = pl.BlockSpec(memory_space=pl.ANY)
    both = (2, rows, features)
    turned = (2, W, heads * B)
    return pl.pallas_call(
        functools.partial(attend_kernel, heads),
        out_shape=(
            jax.ShapeDtypeStruct(turned, jnp.float32),
            jax.ShapeDtypeStruct(turned, jnp.bfloat16),
            jax.ShapeDtypeStruct(window.shape, jnp.bfloat16),
        ),
        in_specs=[pl.BlockSpec(memory_space=pltpu.VMEM)] + [some] * 6,
        out_specs=(some,) * 3,
        scratch_shapes=[
            pltpu.VMEM(both, q.dtype),
            pltpu.VMEM(both, q.dtype),
            pltpu.VMEM(stat.shape, stat.dtype),
            pltpu.VMEM(window.shape, window.dtype),
            pltpu.VMEM((4, W, heads * B), jnp.float32),
            pltpu.VMEM(turned, jnp.bfloat16),
            pltpu.VMEM(window.shape, jnp.bfloat16),
            pltpu.VMEM((16, B, W), jnp.float32),
            pltpu.VMEM((16, B, W), jnp.float32),
            pltpu.VMEM((B, B), jnp.float32),
            pltpu.VMEM((4, 1, B), jnp.float32),
            pltpu.SMEM((2, 4), jnp.int32),
            pltpu.SemaphoreType.DMA((7,)),
            pltpu.SemaphoreType.DMA((20,)),
        ],
        compiler_params=pltpu.CompilerParams(vmem_limit_bytes=VMEM),
        cost_estimate=pl.CostEstimate(
            flops=20 * 10 * heads * B * B * W, bytes_accessed=16 << 20, transcendentals=0
        ),
    )(docs, q, q_other, g, g_other, stat, window)


def return_kernel(
    columns, heads, docs_ref, q_hbm, k_hbm, v_hbm, g_hbm, stat_hbm, dq_own, dq_other, part_ref,
    dq_hbm, dk_hbm, dv_hbm,
    q_ref, k_ref, v_ref, g_ref, stat, dqt, dq_sent, dq_got, dq_out, dk_ref, dv_ref, dka, dva, bias,
    part, across_got, beside_got, beside_sum, later_got, far_got, far_sum, near_sum, near_got,
    final, local, put, send, recv,
):
    at = Links(columns)
    z, core, up, down, across = at.z, at.core, at.up, at.down, at.across
    sems = (send, recv)
    load = pltpu.make_async_copy(part_ref.at[:8], part.at[:8], local.at[0])
    load_own = pltpu.make_async_copy(part_ref.at[8:], part.at[8:], local.at[1])
    load_dq = pltpu.make_async_copy(dq_other, dq_sent, local.at[2])
    load.start()
    load_own.start()
    load_dq.start()
    loads = [
        pltpu.make_async_copy(source, target, local.at[3 + n])
        for n, (source, target) in enumerate(
            (
                (q_hbm, q_ref), (g_hbm, g_ref), (k_hbm, k_ref), (v_hbm, v_ref),
                (stat_hbm.at[0], stat), (dq_own, dqt),
            )
        )
    ]
    for copy in loads:
        copy.start()
    at.barrier()
    has_next, has_last = at.has_next, at.has_last

    def given(side, zc, j):
        return part.at[slot(side, zc, j)]

    def held(side, zc, j):
        return part[slot(side, zc, j)].astype(jnp.float32)

    far_back = [
        Route(
            sems, j, at.last, given(BEFORE, across, j), across_got.at[j],
            has_last & (z < 2) if j == 0 else has_last,
            has_next & (z < 2) if j == 0 else has_next,
        )
        for j in range(2)
    ]
    side_up = [
        Route(
            sems, 2 + j, at.above, given(BEFORE, up, j), beside_got.at[0, j],
            has_last & (z != 3) if j == 0 else has_last,
            has_last & (z != 0) if j == 0 else has_last,
        )
        for j in range(2)
    ]
    side_down = [
        Route(
            sems, 4 + j, at.below, given(BEFORE, down, j), beside_got.at[1, j],
            has_last & (z == 0) if j == 0 else has_last,
            has_last & (z == 3) if j == 0 else has_last,
        )
        for j in range(2)
    ]
    bulk = [
        Route(sems, 6 + n, at.sibling, dq_sent.at[n], dq_got.at[n]) for n in range(2)
    ]
    back = [
        Route(sems, 8 + j, at.last, beside_sum.at[j], later_got.at[j], has_last, has_next)
        for j in range(2)
    ]
    far_up = Route(sems, 10, at.above, far_sum.at[0], far_got.at[0])
    far_down = Route(sems, 11, at.below, far_sum.at[1], far_got.at[1])
    near_up_0 = Route(sems, 12, at.above, near_sum.at[0], near_got.at[0])
    near_up_1 = Route(sems, 13, at.above, given(OWN, up, 1), near_got.at[1], z == 3, z == 0)
    near_down_0 = Route(sems, 14, at.below, given(OWN, down, 0), near_got.at[2])
    near_down_1 = Route(sems, 15, at.below, near_sum.at[1], near_got.at[3])

    load.wait()
    for copy in (far_back[1], side_up[1], side_down[1], far_back[0], side_up[0], side_down[0]):
        copy.start()
    load_own.wait()
    near_down_0.start()
    near_up_1.start()
    load_dq.wait()
    for copy in bulk:
        copy.start()

    @pl.when(has_last)
    def _():
        for copy in side_up + side_down:
            copy.arrived()
        for j in range(2):
            final[j] = held(BEFORE, z, j)
        final[1] += beside_got[0, 1].astype(jnp.float32) + beside_got[1, 1].astype(jnp.float32)

        @pl.when(z != 0)
        def _():
            final[0] += beside_got[0, 0].astype(jnp.float32)

        @pl.when(z == 3)
        def _():
            final[0] += beside_got[1, 0].astype(jnp.float32)

        beside_sum[...] = final[...].astype(jnp.bfloat16)
        for copy in back:
            copy.start()

    def add_across(j):
        far_back[j].make(across_got.at[j]).wait_recv()
        final[j] += across_got[j].astype(jnp.float32)

    for j in range(2):
        final[j] = held(OWN, across, j)
        pl.when(far_back[j].gets)(functools.partial(add_across, j))
        far_sum[j] = final[j].astype(jnp.bfloat16)
    far_up.start()
    far_down.start()
    for copy in loads:
        copy.wait()
    ends = doc_ends(docs_ref)
    tile = at.column * 16 * B + (z + 4 * core) * 2 * B
    dka[...] = jnp.zeros_like(dka)
    dva[...] = jnp.zeros_like(dva)

    def diagonal(n):
        block, b = (n + 1) // 2, n // 2
        here = pl.ds(pl.multiple_of(block * B, B), B)
        there = pl.ds(pl.multiple_of(b * B, B), B)
        pos = positions(tile + block * B)
        bias[...] = hidden(tile + b * B, doc_start(ends, pos), pos)
        dk, dv, dq = gradients(
            k_ref[there],
            v_ref[there],
            [q_ref[here, h * W : (h + 1) * W] for h in range(heads)],
            [g_ref[here, h * W : (h + 1) * W] for h in range(heads)],
            [stat[0, h : h + 1, here] for h in range(heads)],
            [stat[1, h : h + 1, here] for h in range(heads)],
            bias,
        )
        dka[b] += dk
        dva[b] += dv
        dqt[block] += dq

    pl.loop(0, 1)(diagonal)
    far_up.arrived()
    near_sum[0] = (held(OWN, up, 0) + far_got[0].astype(jnp.float32)).astype(jnp.bfloat16)
    near_up_0.start()
    far_down.arrived()
    near_sum[1] = (held(OWN, down, 1) + far_got[1].astype(jnp.float32)).astype(jnp.bfloat16)
    near_down_1.start()
    pl.loop(1, 3)(diagonal)
    for copy in bulk:
        copy.arrived()
    eye = identity(B)
    for block in range(2):
        for h in range(heads):
            rows = slice(h * B, (h + 1) * B)
            total = dqt[block, :, rows] + dq_got[block, :, rows].astype(jnp.float32)
            rounded = (total * (1.0 / math.sqrt(W))).astype(jnp.bfloat16)
            turned = nt(eye, rounded).astype(jnp.bfloat16)
            dq_out[block * B : (block + 1) * B, h * W : (h + 1) * W] = turned
    out_q = pltpu.make_async_copy(dq_out, dq_hbm, put.at[0])
    out_q.start()
    near_down_0.arrived()
    near_up_0.arrived()
    final[0] = (
        held(OWN, z, 0) + near_got[0].astype(jnp.float32) + near_got[2].astype(jnp.float32)
    )
    near_up_1.arrived()
    near_down_1.arrived()
    final[1] = held(OWN, z, 1) + near_got[3].astype(jnp.float32)

    @pl.when(z == 0)
    def _():
        final[1] += near_got[1].astype(jnp.float32)

    @pl.when(has_next)
    def _():
        for j in range(2):
            back[j].arrived()
            final[j] += later_got[j].astype(jnp.float32)

    far_up.sent()
    far_down.sent()
    far_sum[0] = final[1 - core].astype(jnp.bfloat16)
    give_k = Route(sems, 16, at.sibling, far_sum.at[0, 0], dk_ref.at[B:])
    give_v = Route(sems, 17, at.sibling, far_sum.at[0, 1], dv_ref.at[B:])
    give_k.start()
    give_v.start()
    scale = 1.0 / math.sqrt(W)
    dk_ref[:B] = (final[core, 0] + dka[0] * scale).astype(jnp.bfloat16)
    dv_ref[:B] = (final[core, 1] + dva[0]).astype(jnp.bfloat16)
    give_k.arrived()
    give_v.arrived()
    dk_ref[B:] = (dk_ref[B:].astype(jnp.float32) + dka[1] * scale).astype(jnp.bfloat16)
    dv_ref[B:] = (dv_ref[B:].astype(jnp.float32) + dva[1]).astype(jnp.bfloat16)
    out_k = pltpu.make_async_copy(dk_ref, dk_hbm, put.at[1])
    out_v = pltpu.make_async_copy(dv_ref, dv_hbm, put.at[2])
    out_k.start()
    out_v.start()
    for copy in (out_q, out_k, out_v):
        copy.wait()
    for copy in (
        far_back + side_up + side_down + bulk + back
        + [near_up_0, near_up_1, near_down_0, near_down_1, give_k, give_v]
    ):
        copy.sent()


def give_back(columns, docs, q, k, v, g, stat, dq_own, dq_other, part):
    rows, features = q.shape
    heads = features // W
    some = pl.BlockSpec(memory_space=pl.ANY)
    vmem = pl.BlockSpec(memory_space=pltpu.VMEM)
    block = (2, B, W)
    return pl.pallas_call(
        functools.partial(return_kernel, columns, heads),
        out_shape=(
            jax.ShapeDtypeStruct((rows, features), jnp.bfloat16),
            jax.ShapeDtypeStruct((rows, W), jnp.bfloat16),
            jax.ShapeDtypeStruct((rows, W), jnp.bfloat16),
        ),
        in_specs=[vmem] + [some] * 8,
        out_specs=(some,) * 3,
        scratch_shapes=[
            pltpu.VMEM(q.shape, q.dtype),
            pltpu.VMEM(k.shape, k.dtype),
            pltpu.VMEM(v.shape, v.dtype),
            pltpu.VMEM(g.shape, g.dtype),
            pltpu.VMEM(stat.shape[1:], stat.dtype),
            pltpu.VMEM(dq_own.shape, dq_own.dtype),
            pltpu.VMEM(dq_other.shape, dq_other.dtype),
            pltpu.VMEM(dq_other.shape, dq_other.dtype),
            pltpu.VMEM(q.shape, jnp.bfloat16),
            pltpu.VMEM((rows, W), jnp.bfloat16),
            pltpu.VMEM((rows, W), jnp.bfloat16),
            pltpu.VMEM((2, B, W), jnp.float32),
            pltpu.VMEM((2, B, W), jnp.float32),
            pltpu.VMEM((B, B), jnp.float32),
            pltpu.VMEM((16, *block), jnp.bfloat16),
            pltpu.VMEM((2, *block), jnp.bfloat16),
            pltpu.VMEM((2, 2, *block), jnp.bfloat16),
            pltpu.VMEM((2, *block), jnp.bfloat16),
            pltpu.VMEM((2, *block), jnp.bfloat16),
            pltpu.VMEM((2, *block), jnp.bfloat16),
            pltpu.VMEM((2, *block), jnp.bfloat16),
            pltpu.VMEM((2, *block), jnp.bfloat16),
            pltpu.VMEM((4, *block), jnp.bfloat16),
            pltpu.VMEM((2, *block), jnp.float32),
            pltpu.SemaphoreType.DMA((9,)),
            pltpu.SemaphoreType.DMA((3,)),
            pltpu.SemaphoreType.DMA((18,)),
            pltpu.SemaphoreType.DMA((18,)),
        ],
        compiler_params=pltpu.CompilerParams(
            collective_id=1, has_side_effects=True, vmem_limit_bytes=VMEM
        ),
    )(docs, q, k, v, g, stat, dq_own, dq_other, part)


def publish_kernel(*refs):
    sources, targets, held, get, put = refs[:3], refs[3:6], refs[6:9], refs[9], refs[10]
    pieces = []
    for source, target, mid in zip(sources, targets, held):
        rows = min(source.shape[0], 128 * 1024 // source.shape[1])
        for at in range(0, source.shape[0], rows):
            here = slice(at, at + rows)
            n = len(pieces)
            pieces.append(
                (
                    pltpu.make_async_copy(source.at[here], mid.at[here], get.at[n]),
                    pltpu.make_async_copy(mid.at[here], target.at[here], put.at[n]),
                )
            )
    for into, _ in pieces:
        into.start()
    for into, out in pieces:
        into.wait()
        out.start()
    for _, out in pieces:
        out.wait()


def publish(*results):
    some = pl.BlockSpec(memory_space=pl.ANY)
    return pl.pallas_call(
        publish_kernel,
        out_shape=tuple(jax.ShapeDtypeStruct(x.shape, x.dtype) for x in results),
        in_specs=[some] * 3,
        out_specs=(some,) * 3,
        scratch_shapes=[pltpu.VMEM(x.shape, x.dtype) for x in results]
        + [pltpu.SemaphoreType.DMA((6,))] * 2,
        compiler_params=pltpu.CompilerParams(vmem_limit_bytes=VMEM),
    )(*results)


def solution(mesh):
    columns = mesh.shape["ctx"] // 2

    def on_device(q, k, v, o, g, log_total, doc_lengths):
        q_other, g_other, stat, window = gather(columns, q, g, o, k, v, log_total)
        docs = doc_lengths[None, :]
        dq_own, dq_other, part = attend(docs, q, q_other, g, g_other, stat, window)
        dq, dk, dv = give_back(columns, docs, q, k, v, g, stat, dq_own, dq_other, part)
        return publish(dq, dk, dv)

    rows = P(("ctx", "section"), None)
    return jax.shard_map(
        on_device,
        mesh=mesh,
        in_specs=(rows, rows, rows, rows, rows, P(None, ("ctx", "section")), P()),
        out_specs=(rows, rows, rows),
        check_vma=False,
    )
```

```python
import functools
import math

import jax
import jax.numpy as jnp
from jax import lax
from jax.experimental import pallas as pl
from jax.experimental.pallas import tpu as pltpu
from jax.sharding import PartitionSpec as P

MESH = pl.DeviceIdType.MESH
W = 128
B = 256
VMEM = 58 << 20
LOG2E = math.log2(math.e)
OWN, BEFORE = 1, 0


def nn(a, b):
    return jnp.dot(a, b, preferred_element_type=jnp.float32)


def nt(a, b):
    return lax.dot_general(a, b, (((1,), (1,)), ((), ())), preferred_element_type=jnp.float32)


def place():
    ctx = lax.axis_index("ctx")
    return ctx // 2, lax.axis_index("section"), ctx % 2


def slot(side, z, j):
    return side * 8 + z * 2 + j


def doc_ends(docs_ref):
    lengths = docs_ref[...].astype(jnp.float32)
    docs = lengths.shape[1]
    upto = lax.broadcasted_iota(jnp.int32, (docs, docs), 1) <= lax.broadcasted_iota(
        jnp.int32, (docs, docs), 0
    )
    return jnp.sum(jnp.where(upto, lengths, 0.0), axis=1, keepdims=True)


def positions(first):
    return first.astype(jnp.float32) + lax.broadcasted_iota(jnp.int32, (1, B), 1).astype(
        jnp.float32
    )


def doc_start(ends, pos):
    return jnp.max(jnp.where(ends <= pos, ends, 0.0), axis=0, keepdims=True)


def hidden(key, start, pos):
    kpos = (key + lax.broadcasted_iota(jnp.int32, (B, B), 0)).astype(jnp.float32)
    return jnp.where((kpos >= start) & (kpos <= pos), 0.0, -jnp.inf)


def identity(n):
    at = [lax.broadcasted_iota(jnp.int32, (n, n), d) for d in range(2)]
    return (at[0] == at[1]).astype(jnp.bfloat16)


def gradients(heads, k, v, qt, gt, log, delta, bias=None):
    ps, ds = [], []
    for h in range(heads):
        rows = slice(h * B, (h + 1) * B)
        x = nn(k, qt[:, rows]) * (LOG2E / math.sqrt(W)) - log(h)
        if bias is not None:
            x = x + bias[...]
        p = jnp.exp2(x)
        d = p * (nn(v, gt[:, rows]) - delta(h))
        ps.append(p.astype(jnp.bfloat16))
        ds.append(d.astype(jnp.bfloat16))
    dh = jnp.concatenate(ds, axis=1)
    dv = nt(gt[...], jnp.concatenate(ps, axis=1))
    dk = nt(qt[...], dh)
    return dk, dv, nn(k.T, dh)


class Links:
    def __init__(self, columns):
        self.column, self.z, self.core = place()
        ctx = lax.axis_index("ctx")
        self.up = lax.rem(self.z + 1, 4)
        self.down = lax.rem(self.z + 3, 4)
        self.across = lax.rem(self.z + 2, 4)
        self.sibling = (ctx + 1 - 2 * self.core, self.z)
        self.above = (ctx, self.up)
        self.below = (ctx, self.down)
        self.has_next = self.column < columns - 1
        self.has_last = self.column > 0
        self.next = (jnp.where(self.has_next, ctx + 2, ctx), self.z)
        self.last = (jnp.where(self.has_last, ctx - 2, ctx), self.z)

    def barrier(self):
        barrier = pltpu.get_barrier_semaphore()

        def greet(device):
            pl.semaphore_signal(barrier, inc=1, device_id=device, device_id_type=MESH)

        greet(self.sibling)
        greet(self.above)
        greet(self.below)
        pl.when(self.has_next)(lambda: greet(self.next))
        pl.when(self.has_last)(lambda: greet(self.last))
        peers = 3 + self.has_next.astype(jnp.int32) + self.has_last.astype(jnp.int32)
        pl.semaphore_wait(barrier, peers)


class Route:
    def __init__(self, sems, index, device, source, target, sends=True, gets=True, arrival=None):
        self.sends, self.gets = sends, gets
        landed = target if arrival is None else arrival
        send, recv = sems[0].at[index], sems[1].at[index]
        self.make = lambda end: pltpu.make_async_remote_copy(
            source, end, send, recv, device_id=device, device_id_type=MESH
        )
        self.target, self.landed = target, landed

    @staticmethod
    def only(condition, act):
        if condition is True:
            act()
        else:
            pl.when(condition)(act)

    def start(self):
        self.only(self.sends, lambda: self.make(self.target).start())

    def arrived(self):
        self.only(self.gets, lambda: self.make(self.landed).wait_recv())

    def sent(self):
        self.only(self.sends, lambda: self.make(self.target).wait_send())


def gather_kernel(
    columns, heads, q_ref, g_ref, o_ref, k_ref, v_ref, log_ref,
    q_out, g_out, stat_both, window_out,
    q_vmem, g_vmem, o_vmem, qt, gt, swap, stat, window, local, put, send, recv,
):
    at = Links(columns)
    z, core, up, down, across = at.z, at.core, at.up, at.down, at.across
    sems = (send, recv)
    mine = window.at[slot(OWN, z, core)]
    loads = [
        pltpu.make_async_copy(source, target, local.at[n])
        for n, (source, target) in enumerate(
            (
                (k_ref.at[B:], swap.at[0]), (v_ref.at[B:], swap.at[1]),
                (k_ref.at[:B], mine.at[0]), (v_ref.at[:B], mine.at[1]),
                (q_ref, q_vmem), (g_ref, g_vmem), (o_ref, o_vmem), (log_ref, stat.at[0, 0]),
            )
        )
    ]
    for copy in loads:
        copy.start()
    at.barrier()

    theirs = window.at[slot(OWN, z, 1 - core)]
    halves = Route(sems, 0, at.sibling, swap, mine, arrival=theirs)
    for copy in loads[:4]:
        copy.wait()
    halves.start()
    bulk = []
    for part in range(2):
        bulk.append(Route(sems, 2 + part, at.sibling, qt.at[0, part], qt.at[1, part]))
        bulk.append(Route(sems, 4 + part, at.sibling, gt.at[0, part], gt.at[1, part]))

    def passed(index, device, side, sent, j, got, sends=True, gets=True):
        there = window.at[slot(side, sent, j)]
        return Route(sems, index, device, there, there, sends, gets, window.at[slot(side, got, j)])

    up_0 = passed(6, at.above, OWN, z, 0, down)
    up_1 = passed(7, at.above, OWN, z, 1, down)
    down_0 = passed(8, at.below, OWN, z, 0, up)
    down_1 = passed(9, at.below, OWN, z, 1, up, z == 0, z == 3)
    far_0 = passed(10, at.below, OWN, up, 0, across)
    far_1 = passed(11, at.above, OWN, down, 1, across)

    def later(index, zc, j, when=True):
        here = window.at[slot(OWN, zc, j)]
        there = window.at[slot(BEFORE, zc, j)]
        sends = at.has_next if when is True else at.has_next & when
        gets = at.has_last if when is True else at.has_last & when
        return Route(sems, index, at.next, here, there, sends, gets)

    next_0 = later(12, z, 0)
    next_1 = later(13, z, 1)
    next_far_0 = later(14, across, 0, z < 2)
    next_far_1 = later(15, across, 1)
    last = at.has_last
    before_up_0 = passed(16, at.above, BEFORE, z, 0, down, last & (z == 3), last & (z == 0))
    before_up_1 = passed(17, at.above, BEFORE, z, 1, down, last, last)
    before_down_0 = passed(18, at.below, BEFORE, z, 0, up, last & (z != 0), last & (z != 3))
    before_down_1 = passed(19, at.below, BEFORE, z, 1, up, last, last)

    halves.arrived()
    for copy in (up_1, down_0, next_1, up_0, down_1, next_0):
        copy.start()
    loads[4].wait()
    loads[5].wait()
    eye = identity(W)
    for part in range(2):
        here = slice(part * B, (part + 1) * B)
        for h in range(heads):
            cols = slice(h * W, (h + 1) * W)
            across_heads = slice(h * B, (h + 1) * B)
            qt[0, part, :, across_heads] = nt(eye, q_vmem[here, cols]).astype(jnp.bfloat16)
            gt[0, part, :, across_heads] = nt(eye, g_vmem[here, cols]).astype(jnp.bfloat16)
        for copy in bulk[2 * part : 2 * part + 2]:
            copy.start()

    loads[6].wait()
    loads[7].wait()
    ones = jnp.ones((8, W), jnp.bfloat16)
    for h in range(heads):
        cols = slice(h * W, (h + 1) * W)
        product = g_vmem[:, cols].astype(jnp.float32) * o_vmem[:, cols].astype(jnp.float32)
        high = product.astype(jnp.bfloat16)
        low = (product - high.astype(jnp.float32)).astype(jnp.bfloat16)
        total = nt(ones, high) + nt(ones, low)
        stat[0, 1, h : h + 1, :] = total[0:1]
    stat[0, 0] = stat[0, 0] * LOG2E
    stats = Route(sems, 20, at.sibling, stat.at[0], stat.at[1])
    stats.start()

    up_1.arrived()
    far_1.start()
    down_0.arrived()
    far_0.start()
    next_1.arrived()
    before_down_1.start()
    before_up_1.start()
    next_0.arrived()
    before_down_0.start()
    before_up_0.start()
    far_0.arrived()
    next_far_0.start()
    far_1.arrived()
    next_far_1.start()
    for copy in bulk:
        copy.arrived()
    stats.arrived()
    up_0.arrived()
    down_1.arrived()
    outs = [
        pltpu.make_async_copy(source, target, put.at[n])
        for n, (source, target) in enumerate(
            (
                (qt, q_out), (gt, g_out), (stat, stat_both),
                (window.at[8:], window_out.at[8:]), (window.at[:8], window_out.at[:8]),
            )
        )
    ]
    for copy in outs[:4]:
        copy.start()
    for copy in (before_up_0, before_up_1, before_down_0, before_down_1, next_far_0, next_far_1):
        copy.arrived()
    outs[4].start()
    for copy in (
        [halves, up_0, up_1, down_0, down_1, far_0, far_1, next_0, next_1, next_far_0]
        + [next_far_1, before_up_0, before_up_1, before_down_0, before_down_1, stats]
        + bulk
    ):
        copy.sent()
    for copy in outs:
        copy.wait()


def gather(columns, q, g, o, k, v, log_total):
    rows, features = q.shape
    heads = features // W
    some = pl.BlockSpec(memory_space=pl.ANY)
    window = (16, 2, B, W)
    stat = (2, 2, heads, rows)
    turned = (2, rows // B, W, heads * B)
    return pl.pallas_call(
        functools.partial(gather_kernel, columns, heads),
        out_shape=(
            jax.ShapeDtypeStruct(turned, q.dtype),
            jax.ShapeDtypeStruct(turned, q.dtype),
            jax.ShapeDtypeStruct(stat, jnp.float32),
            jax.ShapeDtypeStruct(window, k.dtype),
        ),
        in_specs=[some] * 6,
        out_specs=(some,) * 4,
        scratch_shapes=[
            pltpu.VMEM(q.shape, q.dtype),
            pltpu.VMEM(q.shape, q.dtype),
            pltpu.VMEM(q.shape, q.dtype),
            pltpu.VMEM(turned, q.dtype),
            pltpu.VMEM(turned, q.dtype),
            pltpu.VMEM((2, B, W), k.dtype),
            pltpu.VMEM(stat, jnp.float32),
            pltpu.VMEM(window, k.dtype),
            pltpu.SemaphoreType.DMA((8,)),
            pltpu.SemaphoreType.DMA((5,)),
            pltpu.SemaphoreType.DMA((21,)),
            pltpu.SemaphoreType.DMA((21,)),
        ],
        compiler_params=pltpu.CompilerParams(
            collective_id=0, has_side_effects=True, vmem_limit_bytes=VMEM
        ),
    )(q, g, o, k, v, log_total)


def attend_kernel(
    heads, docs_ref, q_hbm, g_hbm, stat_hbm, window_hbm,
    dq_own, dq_other, part_hbm,
    q_ref, g_ref, stat_ref, window_ref, dqt, dqh, part_ref, dka, dva, bias, starts, bounds, get, put,
):
    column, z, core = place()
    loads = [
        pltpu.make_async_copy(source, target, get.at[n])
        for n, (source, target) in enumerate(
            (
                (stat_hbm, stat_ref),
                (window_hbm.at[:8], window_ref.at[:8]), (window_hbm.at[8:], window_ref.at[8:]),
                (q_hbm.at[0], q_ref.at[0]), (g_hbm.at[0], g_ref.at[0]),
                (q_hbm.at[1], q_ref.at[1]), (g_hbm.at[1], g_ref.at[1]),
            )
        )
    ]
    for load in loads:
        load.start()
    ends = doc_ends(docs_ref)
    window = (column - 1) * 16 * B

    def half_of(b):
        return jnp.where(b % 8 >= 4, 1 - core, core)

    def tile_of(side):
        return z + 4 * (core if side == 0 else 1 - core)

    for block in range(4):
        side, part = divmod(block, 2)
        first = column * 16 * B + tile_of(side) * 2 * B + part * B
        start = doc_start(ends, positions(first))
        starts[block] = start
        rel = jnp.min(start).astype(jnp.int32) - window
        lo = rel // (2 * B)
        lo = jnp.where(rel % (2 * B) >= half_of(lo) * B + B, lo + 1, lo)
        bounds[0, block] = lo
        bounds[1, block] = jnp.max(start).astype(jnp.int32)
    dka[...] = jnp.zeros_like(dka)
    dva[...] = jnp.zeros_like(dva)
    dqt[...] = jnp.zeros_like(dqt)
    for load in loads[:5]:
        load.wait()

    @pl.loop(0, 4)
    def _(block):
        side, part = block // 2, block % 2
        here = pl.ds(pl.multiple_of(part * B, B), B)

        @pl.when(block == 2)
        def _():
            for load in loads[5:]:
                load.wait()

        def work(b, masked):
            at = slot(b // 8, b % 4, b % 8 // 4)
            dk, dv, dq = gradients(
                heads,
                window_ref[at, 0],
                window_ref[at, 1],
                q_ref.at[side, part],
                g_ref.at[side, part],
                lambda h: stat_ref[side, 0, h : h + 1, here],
                lambda h: stat_ref[side, 1, h : h + 1, here],
                bias if masked else None,
            )
            dva[at] += dv
            dka[at] += dk
            dqt[block] += dq

        def step(b, inner):
            key = window + b * 2 * B + half_of(b) * B
            full = key >= bounds[1, block]

            @pl.when(full)
            def _():
                work(b, False)

            @pl.when(jnp.logical_not(full))
            def _():
                kpos = (key + lax.broadcasted_iota(jnp.int32, (B, B), 0)).astype(jnp.float32)
                bias[...] = jnp.where(kpos >= starts[block], 0.0, -jnp.inf)
                work(b, True)

            return inner

        diagonal = 8 + z + 4 * jnp.where(side == 0, core, 1 - core)
        lax.fori_loop(bounds[0, block], diagonal, step, 0)

        @pl.when(side == 0)
        def _():
            pltpu.make_async_copy(dqt.at[block], dq_own.at[part], put.at[block]).start()

        @pl.when(side == 1)
        def _():
            dqh[part] = dqt[block].astype(jnp.bfloat16)
            pltpu.make_async_copy(dqh.at[part], dq_other.at[part], put.at[block]).start()

    @pl.loop(0, 16)
    def _(s):
        part_ref[s, 0] = (dka[s] * (1.0 / math.sqrt(W))).astype(jnp.bfloat16)
        part_ref[s, 1] = dva[s].astype(jnp.bfloat16)
        pltpu.make_async_copy(part_ref.at[s], part_hbm.at[s], put.at[4 + s]).start()

    for part in range(2):
        pltpu.make_async_copy(dqt.at[part], dq_own.at[part], put.at[part]).wait()
        pltpu.make_async_copy(dqh.at[part], dq_other.at[part], put.at[2 + part]).wait()
    for s in range(16):
        pltpu.make_async_copy(part_ref.at[s], part_hbm.at[s], put.at[4 + s]).wait()


def attend(docs, q, g, stat, window):
    heads = stat.shape[2]
    turned = q.shape[1:]
    parts = (16, 2, W, B)
    some = pl.BlockSpec(memory_space=pl.ANY)
    return pl.pallas_call(
        functools.partial(attend_kernel, heads),
        out_shape=(
            jax.ShapeDtypeStruct(turned, jnp.float32),
            jax.ShapeDtypeStruct(turned, jnp.bfloat16),
            jax.ShapeDtypeStruct(parts, jnp.bfloat16),
        ),
        in_specs=[pl.BlockSpec(memory_space=pltpu.VMEM)] + [some] * 4,
        out_specs=(some,) * 3,
        scratch_shapes=[
            pltpu.VMEM(q.shape, q.dtype),
            pltpu.VMEM(g.shape, g.dtype),
            pltpu.VMEM(stat.shape, stat.dtype),
            pltpu.VMEM(window.shape, window.dtype),
            pltpu.VMEM((4, W, heads * B), jnp.float32),
            pltpu.VMEM(turned, jnp.bfloat16),
            pltpu.VMEM(parts, jnp.bfloat16),
            pltpu.VMEM((16, W, B), jnp.float32),
            pltpu.VMEM((16, W, B), jnp.float32),
            pltpu.VMEM((B, B), jnp.float32),
            pltpu.VMEM((4, 1, B), jnp.float32),
            pltpu.SMEM((2, 4), jnp.int32),
            pltpu.SemaphoreType.DMA((7,)),
            pltpu.SemaphoreType.DMA((20,)),
        ],
        compiler_params=pltpu.CompilerParams(vmem_limit_bytes=VMEM),
        cost_estimate=pl.CostEstimate(
            flops=20 * 10 * heads * B * B * W, bytes_accessed=16 << 20, transcendentals=0
        ),
    )(docs, q, g, stat, window)


def return_kernel(
    columns, heads, docs_ref, k_hbm, v_hbm, q_hbm, g_hbm, stat_hbm, dq_own, dq_other, part_ref,
    dq_hbm, dk_hbm, dv_hbm,
    q_ref, k_ref, v_ref, g_ref, stat, dqt, dq_sent, dq_got, dq_out, dk_ref, dv_ref, dka, dva, bias,
    part, across_got, beside_got, beside_sum, later_got, far_got, far_sum, near_sum, near_got,
    final, given_half, local, put, send, recv,
):
    at = Links(columns)
    z, core, up, down, across = at.z, at.core, at.up, at.down, at.across
    sems = (send, recv)
    load = pltpu.make_async_copy(part_ref.at[:8], part.at[:8], local.at[0])
    load_own = pltpu.make_async_copy(part_ref.at[8:], part.at[8:], local.at[1])
    load_dq = pltpu.make_async_copy(dq_other, dq_sent, local.at[2])
    load.start()
    load_own.start()
    load_dq.start()
    loads = [
        pltpu.make_async_copy(source, target, local.at[3 + n])
        for n, (source, target) in enumerate(
            (
                (q_hbm.at[0], q_ref), (g_hbm.at[0], g_ref), (k_hbm, k_ref), (v_hbm, v_ref),
                (stat_hbm.at[0], stat), (dq_own, dqt),
            )
        )
    ]
    for copy in loads:
        copy.start()
    at.barrier()
    has_next, has_last = at.has_next, at.has_last

    def given(side, zc, j):
        return part.at[slot(side, zc, j)]

    def held(side, zc, j):
        return part[slot(side, zc, j)].astype(jnp.float32)

    far_back = [
        Route(
            sems, j, at.last, given(BEFORE, across, j), across_got.at[j],
            has_last & (z < 2) if j == 0 else has_last,
            has_next & (z < 2) if j == 0 else has_next,
        )
        for j in range(2)
    ]
    side_up = [
        Route(
            sems, 2 + j, at.above, given(BEFORE, up, j), beside_got.at[0, j],
            has_last & (z != 3) if j == 0 else has_last,
            has_last & (z != 0) if j == 0 else has_last,
        )
        for j in range(2)
    ]
    side_down = [
        Route(
            sems, 4 + j, at.below, given(BEFORE, down, j), beside_got.at[1, j],
            has_last & (z == 0) if j == 0 else has_last,
            has_last & (z == 3) if j == 0 else has_last,
        )
        for j in range(2)
    ]
    bulk = [
        Route(sems, 6 + n, at.sibling, dq_sent.at[n], dq_got.at[n]) for n in range(2)
    ]
    back = [
        Route(sems, 8 + j, at.last, beside_sum.at[j], later_got.at[j], has_last, has_next)
        for j in range(2)
    ]
    far_up = Route(sems, 10, at.above, far_sum.at[0], far_got.at[0])
    far_down = Route(sems, 11, at.below, far_sum.at[1], far_got.at[1])
    near_up_0 = Route(sems, 12, at.above, near_sum.at[0], near_got.at[0])
    near_up_1 = Route(sems, 13, at.above, given(OWN, up, 1), near_got.at[1], z == 3, z == 0)
    near_down_0 = Route(sems, 14, at.below, given(OWN, down, 0), near_got.at[2])
    near_down_1 = Route(sems, 15, at.below, near_sum.at[1], near_got.at[3])

    load.wait()
    for copy in (far_back[1], side_up[1], side_down[1], far_back[0], side_up[0], side_down[0]):
        copy.start()
    load_own.wait()
    near_down_0.start()
    near_up_1.start()
    load_dq.wait()
    for copy in bulk:
        copy.start()

    @pl.when(has_last)
    def _():
        for copy in side_up + side_down:
            copy.arrived()
        for j in range(2):
            final[j] = held(BEFORE, z, j)
        final[1] += beside_got[0, 1].astype(jnp.float32) + beside_got[1, 1].astype(jnp.float32)

        @pl.when(z != 0)
        def _():
            final[0] += beside_got[0, 0].astype(jnp.float32)

        @pl.when(z == 3)
        def _():
            final[0] += beside_got[1, 0].astype(jnp.float32)

        beside_sum[...] = final[...].astype(jnp.bfloat16)
        for copy in back:
            copy.start()

    def add_across(j):
        far_back[j].make(across_got.at[j]).wait_recv()
        final[j] += across_got[j].astype(jnp.float32)

    for j in range(2):
        final[j] = held(OWN, across, j)
        pl.when(far_back[j].gets)(functools.partial(add_across, j))
        far_sum[j] = final[j].astype(jnp.bfloat16)
    far_up.start()
    far_down.start()
    for copy in loads:
        copy.wait()
    ends = doc_ends(docs_ref)
    tile = at.column * 16 * B + (z + 4 * core) * 2 * B
    dka[...] = jnp.zeros_like(dka)
    dva[...] = jnp.zeros_like(dva)

    def diagonal(n):
        block, b = (n + 1) // 2, n // 2
        here = pl.ds(pl.multiple_of(block * B, B), B)
        there = pl.ds(pl.multiple_of(b * B, B), B)
        pos = positions(tile + block * B)
        bias[...] = hidden(tile + b * B, doc_start(ends, pos), pos)
        dk, dv, dq = gradients(
            heads,
            k_ref[there],
            v_ref[there],
            q_ref.at[block],
            g_ref.at[block],
            lambda h: stat[0, h : h + 1, here],
            lambda h: stat[1, h : h + 1, here],
            bias,
        )
        dka[b] += dk
        dva[b] += dv
        dqt[block] += dq

    pl.loop(0, 1)(diagonal)
    far_up.arrived()
    near_sum[0] = (held(OWN, up, 0) + far_got[0].astype(jnp.float32)).astype(jnp.bfloat16)
    near_up_0.start()
    far_down.arrived()
    near_sum[1] = (held(OWN, down, 1) + far_got[1].astype(jnp.float32)).astype(jnp.bfloat16)
    near_down_1.start()
    pl.loop(1, 3)(diagonal)
    for copy in bulk:
        copy.arrived()
    eye = identity(B)
    for block in range(2):
        for h in range(heads):
            rows = slice(h * B, (h + 1) * B)
            total = dqt[block, :, rows] + dq_got[block, :, rows].astype(jnp.float32)
            rounded = (total * (1.0 / math.sqrt(W))).astype(jnp.bfloat16)
            turned = nt(eye, rounded).astype(jnp.bfloat16)
            dq_out[block * B : (block + 1) * B, h * W : (h + 1) * W] = turned
    out_q = pltpu.make_async_copy(dq_out, dq_hbm, put.at[0])
    out_q.start()
    near_down_0.arrived()
    near_up_0.arrived()
    final[0] = (
        held(OWN, z, 0) + near_got[0].astype(jnp.float32) + near_got[2].astype(jnp.float32)
    )
    near_up_1.arrived()
    near_down_1.arrived()
    final[1] = held(OWN, z, 1) + near_got[3].astype(jnp.float32)

    @pl.when(z == 0)
    def _():
        final[1] += near_got[1].astype(jnp.float32)

    @pl.when(has_next)
    def _():
        for j in range(2):
            back[j].arrived()
            final[j] += later_got[j].astype(jnp.float32)

    far_up.sent()
    far_down.sent()
    far_sum[0] = final[1 - core].astype(jnp.bfloat16)
    give = Route(sems, 16, at.sibling, far_sum.at[0], given_half)
    give.start()
    scale = 1.0 / math.sqrt(W)

    def turn(x):
        return nt(eye, x.astype(jnp.bfloat16)).astype(jnp.bfloat16)

    dk_ref[:B] = turn(final[core, 0] + dka[0] * scale)
    dv_ref[:B] = turn(final[core, 1] + dva[0])
    give.arrived()
    dk_ref[B:] = turn(given_half[0].astype(jnp.float32) + dka[1] * scale)
    dv_ref[B:] = turn(given_half[1].astype(jnp.float32) + dva[1])
    out_k = pltpu.make_async_copy(dk_ref, dk_hbm, put.at[1])
    out_v = pltpu.make_async_copy(dv_ref, dv_hbm, put.at[2])
    out_k.start()
    out_v.start()
    for copy in (out_q, out_k, out_v):
        copy.wait()
    for copy in (
        far_back + side_up + side_down + bulk + back
        + [near_up_0, near_up_1, near_down_0, near_down_1, give]
    ):
        copy.sent()


def give_back(columns, docs, k, v, q, g, stat, dq_own, dq_other, part):
    rows = k.shape[0]
    heads = stat.shape[2]
    features = heads * W
    some = pl.BlockSpec(memory_space=pl.ANY)
    vmem = pl.BlockSpec(memory_space=pltpu.VMEM)
    block = (2, W, B)
    return pl.pallas_call(
        functools.partial(return_kernel, columns, heads),
        out_shape=(
            jax.ShapeDtypeStruct((rows, features), jnp.bfloat16),
            jax.ShapeDtypeStruct((rows, W), jnp.bfloat16),
            jax.ShapeDtypeStruct((rows, W), jnp.bfloat16),
        ),
        in_specs=[vmem] + [some] * 8,
        out_specs=(some,) * 3,
        scratch_shapes=[
            pltpu.VMEM(q.shape[1:], q.dtype),
            pltpu.VMEM(k.shape, k.dtype),
            pltpu.VMEM(v.shape, v.dtype),
            pltpu.VMEM(g.shape[1:], g.dtype),
            pltpu.VMEM(stat.shape[1:], stat.dtype),
            pltpu.VMEM(dq_own.shape, dq_own.dtype),
            pltpu.VMEM(dq_other.shape, dq_other.dtype),
            pltpu.VMEM(dq_other.shape, dq_other.dtype),
            pltpu.VMEM((rows, features), jnp.bfloat16),
            pltpu.VMEM((rows, W), jnp.bfloat16),
            pltpu.VMEM((rows, W), jnp.bfloat16),
            pltpu.VMEM((2, W, B), jnp.float32),
            pltpu.VMEM((2, W, B), jnp.float32),
            pltpu.VMEM((B, B), jnp.float32),
            pltpu.VMEM((16, *block), jnp.bfloat16),
            pltpu.VMEM((2, *block), jnp.bfloat16),
            pltpu.VMEM((2, 2, *block), jnp.bfloat16),
            pltpu.VMEM((2, *block), jnp.bfloat16),
            pltpu.VMEM((2, *block), jnp.bfloat16),
            pltpu.VMEM((2, *block), jnp.bfloat16),
            pltpu.VMEM((2, *block), jnp.bfloat16),
            pltpu.VMEM((2, *block), jnp.bfloat16),
            pltpu.VMEM((4, *block), jnp.bfloat16),
            pltpu.VMEM((2, *block), jnp.float32),
            pltpu.VMEM(block, jnp.bfloat16),
            pltpu.SemaphoreType.DMA((9,)),
            pltpu.SemaphoreType.DMA((3,)),
            pltpu.SemaphoreType.DMA((18,)),
            pltpu.SemaphoreType.DMA((18,)),
        ],
        compiler_params=pltpu.CompilerParams(
            collective_id=1, has_side_effects=True, vmem_limit_bytes=VMEM
        ),
    )(docs, k, v, q, g, stat, dq_own, dq_other, part)


def publish_kernel(*refs):
    sources, targets, held, get, put = refs[:3], refs[3:6], refs[6:9], refs[9], refs[10]
    pieces = []
    for source, target, mid in zip(sources, targets, held):
        rows = min(source.shape[0], 128 * 1024 // source.shape[1])
        for at in range(0, source.shape[0], rows):
            here = slice(at, at + rows)
            n = len(pieces)
            pieces.append(
                (
                    pltpu.make_async_copy(source.at[here], mid.at[here], get.at[n]),
                    pltpu.make_async_copy(mid.at[here], target.at[here], put.at[n]),
                )
            )
    for into, _ in pieces:
        into.start()
    for into, out in pieces:
        into.wait()
        out.start()
    for _, out in pieces:
        out.wait()


def publish(*results):
    some = pl.BlockSpec(memory_space=pl.ANY)
    return pl.pallas_call(
        publish_kernel,
        out_shape=tuple(jax.ShapeDtypeStruct(x.shape, x.dtype) for x in results),
        in_specs=[some] * 3,
        out_specs=(some,) * 3,
        scratch_shapes=[pltpu.VMEM(x.shape, x.dtype) for x in results]
        + [pltpu.SemaphoreType.DMA((6,))] * 2,
        compiler_params=pltpu.CompilerParams(vmem_limit_bytes=VMEM),
    )(*results)


def solution(mesh):
    columns = mesh.shape["ctx"] // 2

    def on_device(q, k, v, o, g, log_total, doc_lengths):
        qt, gt, stat, window = gather(columns, q, g, o, k, v, log_total)
        docs = doc_lengths[None, :]
        dq_own, dq_other, part = attend(docs, qt, gt, stat, window)
        dq, dk, dv = give_back(columns, docs, k, v, qt, gt, stat, dq_own, dq_other, part)
        return publish(dq, dk, dv)

    rows = P(("ctx", "section"), None)
    return jax.shard_map(
        on_device,
        mesh=mesh,
        in_specs=(rows, rows, rows, rows, rows, P(None, ("ctx", "section")), P()),
        out_specs=(rows, rows, rows),
        check_vma=False,
    )
```

```python
import functools
import math

import jax
import jax.numpy as jnp
from jax import lax
from jax.experimental import pallas as pl
from jax.experimental.pallas import tpu as pltpu
from jax.sharding import PartitionSpec as P

MESH = pl.DeviceIdType.MESH
W = 128
B = 256
VMEM = 58 << 20
LOG2E = math.log2(math.e)
OWN, BEFORE = 1, 0


def nn(a, b):
    return jnp.dot(a, b, preferred_element_type=jnp.float32)


def nt(a, b):
    return lax.dot_general(a, b, (((1,), (1,)), ((), ())), preferred_element_type=jnp.float32)


def place():
    ctx = lax.axis_index("ctx")
    return ctx // 2, lax.axis_index("section"), ctx % 2


def slot(side, z, j):
    return side * 8 + z * 2 + j


def doc_ends(docs_ref):
    lengths = docs_ref[...].astype(jnp.float32)
    docs = lengths.shape[1]
    upto = lax.broadcasted_iota(jnp.int32, (docs, docs), 1) <= lax.broadcasted_iota(
        jnp.int32, (docs, docs), 0
    )
    return jnp.sum(jnp.where(upto, lengths, 0.0), axis=1, keepdims=True)


def positions(first):
    return first.astype(jnp.float32) + lax.broadcasted_iota(jnp.int32, (1, B), 1).astype(
        jnp.float32
    )


def doc_start(ends, pos):
    return jnp.max(jnp.where(ends <= pos, ends, 0.0), axis=0, keepdims=True)


def hidden(key, start, pos):
    kpos = (key + lax.broadcasted_iota(jnp.int32, (B, B), 0)).astype(jnp.float32)
    return jnp.where((kpos >= start) & (kpos <= pos), 0.0, -jnp.inf)


def identity(n):
    at = [lax.broadcasted_iota(jnp.int32, (n, n), d) for d in range(2)]
    return (at[0] == at[1]).astype(jnp.bfloat16)


def gradients(k, v, qs, gs, logs, deltas, bias=None):
    ps, ds = [], []
    for q, g, log, delta in zip(qs, gs, logs, deltas):
        x = nt(k, q) * (LOG2E / math.sqrt(W)) - log
        if bias is not None:
            x = x + bias[...]
        p = jnp.exp2(x)
        d = p * (nt(v, g) - delta)
        ps.append(p.astype(jnp.bfloat16))
        ds.append(d.astype(jnp.bfloat16))
    dh = jnp.concatenate(ds, axis=1)
    dv = nn(jnp.concatenate(ps, axis=1), jnp.concatenate(gs, axis=0))
    dk = nn(dh, jnp.concatenate(qs, axis=0))
    return dk, dv, nn(k.T, dh)


class Links:
    def __init__(self, columns):
        self.column, self.z, self.core = place()
        ctx = lax.axis_index("ctx")
        self.up = lax.rem(self.z + 1, 4)
        self.down = lax.rem(self.z + 3, 4)
        self.across = lax.rem(self.z + 2, 4)
        self.sibling = (ctx + 1 - 2 * self.core, self.z)
        self.above = (ctx, self.up)
        self.below = (ctx, self.down)
        self.has_next = self.column < columns - 1
        self.has_last = self.column > 0
        self.next = (jnp.where(self.has_next, ctx + 2, ctx), self.z)
        self.last = (jnp.where(self.has_last, ctx - 2, ctx), self.z)

    def barrier(self):
        barrier = pltpu.get_barrier_semaphore()

        def greet(device):
            pl.semaphore_signal(barrier, inc=1, device_id=device, device_id_type=MESH)

        greet(self.sibling)
        greet(self.above)
        greet(self.below)
        pl.when(self.has_next)(lambda: greet(self.next))
        pl.when(self.has_last)(lambda: greet(self.last))
        peers = 3 + self.has_next.astype(jnp.int32) + self.has_last.astype(jnp.int32)
        pl.semaphore_wait(barrier, peers)


class Route:
    def __init__(self, sems, index, device, source, target, sends=True, gets=True, arrival=None):
        self.sends, self.gets = sends, gets
        landed = target if arrival is None else arrival
        send, recv = sems[0].at[index], sems[1].at[index]
        self.make = lambda end: pltpu.make_async_remote_copy(
            source, end, send, recv, device_id=device, device_id_type=MESH
        )
        self.target, self.landed = target, landed

    @staticmethod
    def only(condition, act):
        if condition is True:
            act()
        else:
            pl.when(condition)(act)

    def start(self):
        self.only(self.sends, lambda: self.make(self.target).start())

    def arrived(self):
        self.only(self.gets, lambda: self.make(self.landed).wait_recv())

    def sent(self):
        self.only(self.sends, lambda: self.make(self.target).wait_send())


def gather_kernel(
    columns, heads, q_ref, g_ref, o_ref, k_ref, v_ref, log_ref,
    q_other, g_other, stat_both, window_out,
    q_vmem, g_vmem, o_vmem, q_got, g_got, swap, stat, window, local, put, send, recv,
):
    at = Links(columns)
    z, core, up, down, across = at.z, at.core, at.up, at.down, at.across
    sems = (send, recv)
    mine = window.at[slot(OWN, z, core)]
    loads = [
        pltpu.make_async_copy(source, target, local.at[n])
        for n, (source, target) in enumerate(
            (
                (k_ref.at[B:], swap.at[0]), (v_ref.at[B:], swap.at[1]),
                (k_ref.at[:B], mine.at[0]), (v_ref.at[:B], mine.at[1]),
                (q_ref, q_vmem), (g_ref, g_vmem), (o_ref, o_vmem), (log_ref, stat.at[0, 0]),
            )
        )
    ]
    for copy in loads:
        copy.start()
    at.barrier()

    theirs = window.at[slot(OWN, z, 1 - core)]
    halves = Route(sems, 0, at.sibling, swap, mine, arrival=theirs)
    for copy in loads[:4]:
        copy.wait()
    halves.start()
    rows = q_ref.shape[0]
    bulk = []
    for part in range(2):
        some = slice(part * rows // 2, (part + 1) * rows // 2)
        bulk.append(Route(sems, 2 + part, at.sibling, q_vmem.at[some], q_got.at[some]))
        bulk.append(Route(sems, 4 + part, at.sibling, g_vmem.at[some], g_got.at[some]))

    def passed(index, device, side, sent, j, got, sends=True, gets=True):
        there = window.at[slot(side, sent, j)]
        return Route(sems, index, device, there, there, sends, gets, window.at[slot(side, got, j)])

    up_0 = passed(6, at.above, OWN, z, 0, down)
    up_1 = passed(7, at.above, OWN, z, 1, down)
    down_0 = passed(8, at.below, OWN, z, 0, up)
    down_1 = passed(9, at.below, OWN, z, 1, up, z == 0, z == 3)
    far_0 = passed(10, at.below, OWN, up, 0, across)
    far_1 = passed(11, at.above, OWN, down, 1, across)

    def later(index, zc, j, when=True):
        here = window.at[slot(OWN, zc, j)]
        there = window.at[slot(BEFORE, zc, j)]
        sends = at.has_next if when is True else at.has_next & when
        gets = at.has_last if when is True else at.has_last & when
        return Route(sems, index, at.next, here, there, sends, gets)

    next_0 = later(12, z, 0)
    next_1 = later(13, z, 1)
    next_far_0 = later(14, across, 0, z < 2)
    next_far_1 = later(15, across, 1)
    last = at.has_last
    before_up_0 = passed(16, at.above, BEFORE, z, 0, down, last & (z == 3), last & (z == 0))
    before_up_1 = passed(17, at.above, BEFORE, z, 1, down, last, last)
    before_down_0 = passed(18, at.below, BEFORE, z, 0, up, last & (z != 0), last & (z != 3))
    before_down_1 = passed(19, at.below, BEFORE, z, 1, up, last, last)

    halves.arrived()
    for copy in (up_1, down_0, next_1, up_0, down_1, next_0):
        copy.start()
    loads[4].wait()
    loads[5].wait()
    for copy in bulk:
        copy.start()

    loads[6].wait()
    loads[7].wait()
    ones = jnp.ones((8, W), jnp.bfloat16)
    for h in range(heads):
        cols = slice(h * W, (h + 1) * W)
        product = g_vmem[:, cols].astype(jnp.float32) * o_vmem[:, cols].astype(jnp.float32)
        high = product.astype(jnp.bfloat16)
        low = (product - high.astype(jnp.float32)).astype(jnp.bfloat16)
        total = nt(ones, high) + nt(ones, low)
        stat[0, 1, h : h + 1, :] = total[0:1]
    stat[0, 0] = stat[0, 0] * LOG2E
    stats = Route(sems, 20, at.sibling, stat.at[0], stat.at[1])
    stats.start()

    up_1.arrived()
    far_1.start()
    down_0.arrived()
    far_0.start()
    next_1.arrived()
    before_down_1.start()
    before_up_1.start()
    next_0.arrived()
    before_down_0.start()
    before_up_0.start()
    far_0.arrived()
    next_far_0.start()
    far_1.arrived()
    next_far_1.start()
    for copy in bulk:
        copy.arrived()
    stats.arrived()
    up_0.arrived()
    down_1.arrived()
    outs = [
        pltpu.make_async_copy(source, target, put.at[n])
        for n, (source, target) in enumerate(
            (
                (q_got, q_other), (g_got, g_other), (stat, stat_both),
                (window.at[8:], window_out.at[8:]), (window.at[:8], window_out.at[:8]),
            )
        )
    ]
    for copy in outs[:4]:
        copy.start()
    for copy in (before_up_0, before_up_1, before_down_0, before_down_1, next_far_0, next_far_1):
        copy.arrived()
    outs[4].start()
    for copy in (
        [halves, up_0, up_1, down_0, down_1, far_0, far_1, next_0, next_1, next_far_0]
        + [next_far_1, before_up_0, before_up_1, before_down_0, before_down_1, stats]
        + bulk
    ):
        copy.sent()
    for copy in outs:
        copy.wait()


def gather(columns, q, g, o, k, v, log_total):
    rows, features = q.shape
    heads = features // W
    some = pl.BlockSpec(memory_space=pl.ANY)
    window = (16, 2, B, W)
    stat = (2, 2, heads, rows)
    return pl.pallas_call(
        functools.partial(gather_kernel, columns, heads),
        out_shape=(
            jax.ShapeDtypeStruct(q.shape, q.dtype),
            jax.ShapeDtypeStruct(q.shape, q.dtype),
            jax.ShapeDtypeStruct(stat, jnp.float32),
            jax.ShapeDtypeStruct(window, k.dtype),
        ),
        in_specs=[some] * 6,
        out_specs=(some,) * 4,
        scratch_shapes=[
            pltpu.VMEM(q.shape, q.dtype),
            pltpu.VMEM(q.shape, q.dtype),
            pltpu.VMEM(q.shape, q.dtype),
            pltpu.VMEM(q.shape, q.dtype),
            pltpu.VMEM(q.shape, q.dtype),
            pltpu.VMEM((2, B, W), k.dtype),
            pltpu.VMEM(stat, jnp.float32),
            pltpu.VMEM(window, k.dtype),
            pltpu.SemaphoreType.DMA((8,)),
            pltpu.SemaphoreType.DMA((5,)),
            pltpu.SemaphoreType.DMA((21,)),
            pltpu.SemaphoreType.DMA((21,)),
        ],
        compiler_params=pltpu.CompilerParams(
            collective_id=0, has_side_effects=True, vmem_limit_bytes=VMEM
        ),
    )(q, g, o, k, v, log_total)


def attend_kernel(
    heads, docs_ref, qa_hbm, qb_hbm, ga_hbm, gb_hbm, stat_hbm, window_hbm,
    dq_own, dq_other, part_hbm,
    q_ref, g_ref, stat_ref, window_ref, dqt, dqh, part_ref, dka, dva, bias, starts, bounds, get, put,
):
    column, z, core = place()
    loads = [
        pltpu.make_async_copy(source, target, get.at[n])
        for n, (source, target) in enumerate(
            (
                (stat_hbm, stat_ref),
                (window_hbm.at[:8], window_ref.at[:8]), (window_hbm.at[8:], window_ref.at[8:]),
                (qa_hbm, q_ref.at[0]), (ga_hbm, g_ref.at[0]),
                (qb_hbm, q_ref.at[1]), (gb_hbm, g_ref.at[1]),
            )
        )
    ]
    for load in loads:
        load.start()
    ends = doc_ends(docs_ref)
    window = (column - 1) * 16 * B

    def half_of(b):
        return jnp.where(b % 8 >= 4, 1 - core, core)

    def tile_of(side):
        return z + 4 * (core if side == 0 else 1 - core)

    for block in range(4):
        side, part = divmod(block, 2)
        first = column * 16 * B + tile_of(side) * 2 * B + part * B
        start = doc_start(ends, positions(first))
        starts[block] = start
        low = jnp.min(start).astype(jnp.int32) - window
        last = jnp.max(start).astype(jnp.int32) - window
        b = low // (2 * B)
        bounds[0, block] = jnp.where(low % (2 * B) >= half_of(b) * B + B, b + 1, b)
        b = last // (2 * B)
        bounds[1, block] = jnp.where(last % (2 * B) > half_of(b) * B, b + 1, b)
    dka[...] = jnp.zeros_like(dka)
    dva[...] = jnp.zeros_like(dva)
    dqt[...] = jnp.zeros_like(dqt)
    for load in loads[:5]:
        load.wait()

    @pl.loop(0, 4)
    def _(block):
        side, part = block // 2, block % 2
        here = pl.ds(pl.multiple_of(part * B, B), B)

        @pl.when(block == 2)
        def _():
            for load in loads[5:]:
                load.wait()

        def work(first, count, mask=None):
            at = [slot(b // 8, b % 4, b % 8 // 4) for b in (first + n for n in range(count))]
            dk, dv, dq = gradients(
                jnp.concatenate([window_ref[n, 0] for n in at], axis=0),
                jnp.concatenate([window_ref[n, 1] for n in at], axis=0),
                [q_ref[side, here, h * W : (h + 1) * W] for h in range(heads)],
                [g_ref[side, here, h * W : (h + 1) * W] for h in range(heads)],
                [stat_ref[side, 0, h : h + 1, here] for h in range(heads)],
                [stat_ref[side, 1, h : h + 1, here] for h in range(heads)],
                mask,
            )
            for n in range(count):
                dva[at[n]] += dv[n * B : (n + 1) * B]
                dka[at[n]] += dk[n * B : (n + 1) * B]
            dqt[block] += dq

        low, cut = bounds[0, block], bounds[1, block]
        diagonal = 8 + z + 4 * jnp.where(side == 0, core, 1 - core)
        cut = jnp.minimum(cut, diagonal)
        cut = cut + (diagonal - cut) % 2

        @pl.loop(low, cut)
        def _(b):
            key = window + b * 2 * B + half_of(b) * B
            kpos = (key + lax.broadcasted_iota(jnp.int32, (B, B), 0)).astype(jnp.float32)
            bias[...] = jnp.where(kpos >= starts[block], 0.0, -jnp.inf)
            work(b, 1, bias)

        @pl.loop(0, (diagonal - jnp.maximum(low, cut)) // 2)
        def _(n):
            work(cut + 2 * n, 2)

        @pl.when(side == 0)
        def _():
            pltpu.make_async_copy(dqt.at[block], dq_own.at[part], put.at[block]).start()

        @pl.when(side == 1)
        def _():
            dqh[part] = dqt[block].astype(jnp.bfloat16)
            pltpu.make_async_copy(dqh.at[part], dq_other.at[part], put.at[block]).start()

    @pl.loop(0, 16)
    def _(s):
        part_ref[s, 0] = (dka[s] * (1.0 / math.sqrt(W))).astype(jnp.bfloat16)
        part_ref[s, 1] = dva[s].astype(jnp.bfloat16)
        pltpu.make_async_copy(part_ref.at[s], part_hbm.at[s], put.at[4 + s]).start()

    for part in range(2):
        pltpu.make_async_copy(dqt.at[part], dq_own.at[part], put.at[part]).wait()
        pltpu.make_async_copy(dqh.at[part], dq_other.at[part], put.at[2 + part]).wait()
    for s in range(16):
        pltpu.make_async_copy(part_ref.at[s], part_hbm.at[s], put.at[4 + s]).wait()


def attend(docs, q, q_other, g, g_other, stat, window):
    rows, features = q.shape
    heads = features // W
    some = pl.BlockSpec(memory_space=pl.ANY)
    both = (2, rows, features)
    turned = (2, W, heads * B)
    return pl.pallas_call(
        functools.partial(attend_kernel, heads),
        out_shape=(
            jax.ShapeDtypeStruct(turned, jnp.float32),
            jax.ShapeDtypeStruct(turned, jnp.bfloat16),
            jax.ShapeDtypeStruct(window.shape, jnp.bfloat16),
        ),
        in_specs=[pl.BlockSpec(memory_space=pltpu.VMEM)] + [some] * 6,
        out_specs=(some,) * 3,
        scratch_shapes=[
            pltpu.VMEM(both, q.dtype),
            pltpu.VMEM(both, q.dtype),
            pltpu.VMEM(stat.shape, stat.dtype),
            pltpu.VMEM(window.shape, window.dtype),
            pltpu.VMEM((4, W, heads * B), jnp.float32),
            pltpu.VMEM(turned, jnp.bfloat16),
            pltpu.VMEM(window.shape, jnp.bfloat16),
            pltpu.VMEM((16, B, W), jnp.float32),
            pltpu.VMEM((16, B, W), jnp.float32),
            pltpu.VMEM((B, B), jnp.float32),
            pltpu.VMEM((4, 1, B), jnp.float32),
            pltpu.SMEM((2, 4), jnp.int32),
            pltpu.SemaphoreType.DMA((7,)),
            pltpu.SemaphoreType.DMA((20,)),
        ],
        compiler_params=pltpu.CompilerParams(vmem_limit_bytes=VMEM),
        cost_estimate=pl.CostEstimate(
            flops=20 * 10 * heads * B * B * W, bytes_accessed=16 << 20, transcendentals=0
        ),
    )(docs, q, q_other, g, g_other, stat, window)


def return_kernel(
    columns, heads, docs_ref, q_hbm, k_hbm, v_hbm, g_hbm, stat_hbm, dq_own, dq_other, part_ref,
    dq_hbm, dk_hbm, dv_hbm,
    q_ref, k_ref, v_ref, g_ref, stat, dqt, dq_sent, dq_got, dq_out, dk_ref, dv_ref, dka, dva, bias,
    part, across_got, beside_got, beside_sum, later_got, far_got, far_sum, near_sum, near_got,
    final, local, put, send, recv,
):
    at = Links(columns)
    z, core, up, down, across = at.z, at.core, at.up, at.down, at.across
    sems = (send, recv)
    load = pltpu.make_async_copy(part_ref.at[:8], part.at[:8], local.at[0])
    load_own = pltpu.make_async_copy(part_ref.at[8:], part.at[8:], local.at[1])
    load_dq = pltpu.make_async_copy(dq_other, dq_sent, local.at[2])
    load.start()
    load_own.start()
    load_dq.start()
    loads = [
        pltpu.make_async_copy(source, target, local.at[3 + n])
        for n, (source, target) in enumerate(
            (
                (q_hbm, q_ref), (g_hbm, g_ref), (k_hbm, k_ref), (v_hbm, v_ref),
                (stat_hbm.at[0], stat), (dq_own, dqt),
            )
        )
    ]
    for copy in loads:
        copy.start()
    at.barrier()
    has_next, has_last = at.has_next, at.has_last

    def given(side, zc, j):
        return part.at[slot(side, zc, j)]

    def held(side, zc, j):
        return part[slot(side, zc, j)].astype(jnp.float32)

    far_back = [
        Route(
            sems, j, at.last, given(BEFORE, across, j), across_got.at[j],
            has_last & (z < 2) if j == 0 else has_last,
            has_next & (z < 2) if j == 0 else has_next,
        )
        for j in range(2)
    ]
    side_up = [
        Route(
            sems, 2 + j, at.above, given(BEFORE, up, j), beside_got.at[0, j],
            has_last & (z != 3) if j == 0 else has_last,
            has_last & (z != 0) if j == 0 else has_last,
        )
        for j in range(2)
    ]
    side_down = [
        Route(
            sems, 4 + j, at.below, given(BEFORE, down, j), beside_got.at[1, j],
            has_last & (z == 0) if j == 0 else has_last,
            has_last & (z == 3) if j == 0 else has_last,
        )
        for j in range(2)
    ]
    bulk = [
        Route(sems, 6 + n, at.sibling, dq_sent.at[n], dq_got.at[n]) for n in range(2)
    ]
    back = [
        Route(sems, 8 + j, at.last, beside_sum.at[j], later_got.at[j], has_last, has_next)
        for j in range(2)
    ]
    far_up = Route(sems, 10, at.above, far_sum.at[0], far_got.at[0])
    far_down = Route(sems, 11, at.below, far_sum.at[1], far_got.at[1])
    near_up_0 = Route(sems, 12, at.above, near_sum.at[0], near_got.at[0])
    near_up_1 = Route(sems, 13, at.above, given(OWN, up, 1), near_got.at[1], z == 3, z == 0)
    near_down_0 = Route(sems, 14, at.below, given(OWN, down, 0), near_got.at[2])
    near_down_1 = Route(sems, 15, at.below, near_sum.at[1], near_got.at[3])

    load.wait()
    for copy in (far_back[1], side_up[1], side_down[1], far_back[0], side_up[0], side_down[0]):
        copy.start()
    load_own.wait()
    near_down_0.start()
    near_up_1.start()
    load_dq.wait()
    for copy in bulk:
        copy.start()

    @pl.when(has_last)
    def _():
        for copy in side_up + side_down:
            copy.arrived()
        for j in range(2):
            final[j] = held(BEFORE, z, j)
        final[1] += beside_got[0, 1].astype(jnp.float32) + beside_got[1, 1].astype(jnp.float32)

        @pl.when(z != 0)
        def _():
            final[0] += beside_got[0, 0].astype(jnp.float32)

        @pl.when(z == 3)
        def _():
            final[0] += beside_got[1, 0].astype(jnp.float32)

        beside_sum[...] = final[...].astype(jnp.bfloat16)
        for copy in back:
            copy.start()

    def add_across(j):
        far_back[j].make(across_got.at[j]).wait_recv()
        final[j] += across_got[j].astype(jnp.float32)

    for j in range(2):
        final[j] = held(OWN, across, j)
        pl.when(far_back[j].gets)(functools.partial(add_across, j))
        far_sum[j] = final[j].astype(jnp.bfloat16)
    far_up.start()
    far_down.start()
    for copy in loads:
        copy.wait()
    ends = doc_ends(docs_ref)
    tile = at.column * 16 * B + (z + 4 * core) * 2 * B
    dka[...] = jnp.zeros_like(dka)
    dva[...] = jnp.zeros_like(dva)

    def diagonal(n):
        block, b = (n + 1) // 2, n // 2
        here = pl.ds(pl.multiple_of(block * B, B), B)
        there = pl.ds(pl.multiple_of(b * B, B), B)
        pos = positions(tile + block * B)
        bias[...] = hidden(tile + b * B, doc_start(ends, pos), pos)
        dk, dv, dq = gradients(
            k_ref[there],
            v_ref[there],
            [q_ref[here, h * W : (h + 1) * W] for h in range(heads)],
            [g_ref[here, h * W : (h + 1) * W] for h in range(heads)],
            [stat[0, h : h + 1, here] for h in range(heads)],
            [stat[1, h : h + 1, here] for h in range(heads)],
            bias,
        )
        dka[b] += dk
        dva[b] += dv
        dqt[block] += dq

    pl.loop(0, 1)(diagonal)
    far_up.arrived()
    near_sum[0] = (held(OWN, up, 0) + far_got[0].astype(jnp.float32)).astype(jnp.bfloat16)
    near_up_0.start()
    far_down.arrived()
    near_sum[1] = (held(OWN, down, 1) + far_got[1].astype(jnp.float32)).astype(jnp.bfloat16)
    near_down_1.start()
    pl.loop(1, 3)(diagonal)
    for copy in bulk:
        copy.arrived()
    eye = identity(B)
    for block in range(2):
        for h in range(heads):
            rows = slice(h * B, (h + 1) * B)
            total = dqt[block, :, rows] + dq_got[block, :, rows].astype(jnp.float32)
            rounded = (total * (1.0 / math.sqrt(W))).astype(jnp.bfloat16)
            turned = nt(eye, rounded).astype(jnp.bfloat16)
            dq_out[block * B : (block + 1) * B, h * W : (h + 1) * W] = turned
    out_q = pltpu.make_async_copy(dq_out, dq_hbm, put.at[0])
    out_q.start()
    near_down_0.arrived()
    near_up_0.arrived()
    final[0] = (
        held(OWN, z, 0) + near_got[0].astype(jnp.float32) + near_got[2].astype(jnp.float32)
    )
    near_up_1.arrived()
    near_down_1.arrived()
    final[1] = held(OWN, z, 1) + near_got[3].astype(jnp.float32)

    @pl.when(z == 0)
    def _():
        final[1] += near_got[1].astype(jnp.float32)

    @pl.when(has_next)
    def _():
        for j in range(2):
            back[j].arrived()
            final[j] += later_got[j].astype(jnp.float32)

    far_up.sent()
    far_down.sent()
    far_sum[0] = final[1 - core].astype(jnp.bfloat16)
    give_k = Route(sems, 16, at.sibling, far_sum.at[0, 0], dk_ref.at[B:])
    give_v = Route(sems, 17, at.sibling, far_sum.at[0, 1], dv_ref.at[B:])
    give_k.start()
    give_v.start()
    scale = 1.0 / math.sqrt(W)
    dk_ref[:B] = (final[core, 0] + dka[0] * scale).astype(jnp.bfloat16)
    dv_ref[:B] = (final[core, 1] + dva[0]).astype(jnp.bfloat16)
    give_k.arrived()
    give_v.arrived()
    dk_ref[B:] = (dk_ref[B:].astype(jnp.float32) + dka[1] * scale).astype(jnp.bfloat16)
    dv_ref[B:] = (dv_ref[B:].astype(jnp.float32) + dva[1]).astype(jnp.bfloat16)
    out_k = pltpu.make_async_copy(dk_ref, dk_hbm, put.at[1])
    out_v = pltpu.make_async_copy(dv_ref, dv_hbm, put.at[2])
    out_k.start()
    out_v.start()
    for copy in (out_q, out_k, out_v):
        copy.wait()
    for copy in (
        far_back + side_up + side_down + bulk + back
        + [near_up_0, near_up_1, near_down_0, near_down_1, give_k, give_v]
    ):
        copy.sent()


def give_back(columns, docs, q, k, v, g, stat, dq_own, dq_other, part):
    rows, features = q.shape
    heads = features // W
    some = pl.BlockSpec(memory_space=pl.ANY)
    vmem = pl.BlockSpec(memory_space=pltpu.VMEM)
    block = (2, B, W)
    return pl.pallas_call(
        functools.partial(return_kernel, columns, heads),
        out_shape=(
            jax.ShapeDtypeStruct((rows, features), jnp.bfloat16),
            jax.ShapeDtypeStruct((rows, W), jnp.bfloat16),
            jax.ShapeDtypeStruct((rows, W), jnp.bfloat16),
        ),
        in_specs=[vmem] + [some] * 8,
        out_specs=(some,) * 3,
        scratch_shapes=[
            pltpu.VMEM(q.shape, q.dtype),
            pltpu.VMEM(k.shape, k.dtype),
            pltpu.VMEM(v.shape, v.dtype),
            pltpu.VMEM(g.shape, g.dtype),
            pltpu.VMEM(stat.shape[1:], stat.dtype),
            pltpu.VMEM(dq_own.shape, dq_own.dtype),
            pltpu.VMEM(dq_other.shape, dq_other.dtype),
            pltpu.VMEM(dq_other.shape, dq_other.dtype),
            pltpu.VMEM(q.shape, jnp.bfloat16),
            pltpu.VMEM((rows, W), jnp.bfloat16),
            pltpu.VMEM((rows, W), jnp.bfloat16),
            pltpu.VMEM((2, B, W), jnp.float32),
            pltpu.VMEM((2, B, W), jnp.float32),
            pltpu.VMEM((B, B), jnp.float32),
            pltpu.VMEM((16, *block), jnp.bfloat16),
            pltpu.VMEM((2, *block), jnp.bfloat16),
            pltpu.VMEM((2, 2, *block), jnp.bfloat16),
            pltpu.VMEM((2, *block), jnp.bfloat16),
            pltpu.VMEM((2, *block), jnp.bfloat16),
            pltpu.VMEM((2, *block), jnp.bfloat16),
            pltpu.VMEM((2, *block), jnp.bfloat16),
            pltpu.VMEM((2, *block), jnp.bfloat16),
            pltpu.VMEM((4, *block), jnp.bfloat16),
            pltpu.VMEM((2, *block), jnp.float32),
            pltpu.SemaphoreType.DMA((9,)),
            pltpu.SemaphoreType.DMA((3,)),
            pltpu.SemaphoreType.DMA((18,)),
            pltpu.SemaphoreType.DMA((18,)),
        ],
        compiler_params=pltpu.CompilerParams(
            collective_id=1, has_side_effects=True, vmem_limit_bytes=VMEM
        ),
    )(docs, q, k, v, g, stat, dq_own, dq_other, part)


def publish_kernel(*refs):
    sources, targets, held, get, put = refs[:3], refs[3:6], refs[6:9], refs[9], refs[10]
    pieces = []
    for source, target, mid in zip(sources, targets, held):
        rows = min(source.shape[0], 128 * 1024 // source.shape[1])
        for at in range(0, source.shape[0], rows):
            here = slice(at, at + rows)
            n = len(pieces)
            pieces.append(
                (
                    pltpu.make_async_copy(source.at[here], mid.at[here], get.at[n]),
                    pltpu.make_async_copy(mid.at[here], target.at[here], put.at[n]),
                )
            )
    for into, _ in pieces:
        into.start()
    for into, out in pieces:
        into.wait()
        out.start()
    for _, out in pieces:
        out.wait()


def publish(*results):
    some = pl.BlockSpec(memory_space=pl.ANY)
    return pl.pallas_call(
        publish_kernel,
        out_shape=tuple(jax.ShapeDtypeStruct(x.shape, x.dtype) for x in results),
        in_specs=[some] * 3,
        out_specs=(some,) * 3,
        scratch_shapes=[pltpu.VMEM(x.shape, x.dtype) for x in results]
        + [pltpu.SemaphoreType.DMA((6,))] * 2,
        compiler_params=pltpu.CompilerParams(vmem_limit_bytes=VMEM),
    )(*results)


def solution(mesh):
    columns = mesh.shape["ctx"] // 2

    def on_device(q, k, v, o, g, log_total, doc_lengths):
        q_other, g_other, stat, window = gather(columns, q, g, o, k, v, log_total)
        docs = doc_lengths[None, :]
        dq_own, dq_other, part = attend(docs, q, q_other, g, g_other, stat, window)
        dq, dk, dv = give_back(columns, docs, q, k, v, g, stat, dq_own, dq_other, part)
        return publish(dq, dk, dv)

    rows = P(("ctx", "section"), None)
    return jax.shard_map(
        on_device,
        mesh=mesh,
        in_specs=(rows, rows, rows, rows, rows, P(None, ("ctx", "section")), P()),
        out_specs=(rows, rows, rows),
        check_vma=False,
    )
```

```python
import functools
import math

import jax
import jax.numpy as jnp
from jax import lax
from jax.experimental import pallas as pl
from jax.experimental.pallas import tpu as pltpu
from jax.sharding import PartitionSpec as P

MESH = pl.DeviceIdType.MESH
W = 128
B = 256
VMEM = 58 << 20
LOG2E = math.log2(math.e)
OWN, BEFORE = 1, 0


def nn(a, b):
    return jnp.dot(a, b, preferred_element_type=jnp.float32)


def nt(a, b):
    return lax.dot_general(a, b, (((1,), (1,)), ((), ())), preferred_element_type=jnp.float32)


def place():
    ctx = lax.axis_index("ctx")
    return ctx // 2, lax.axis_index("section"), ctx % 2


def slot(side, z, j):
    return side * 8 + z * 2 + j


def doc_ends(docs_ref):
    lengths = docs_ref[...].astype(jnp.float32)
    docs = lengths.shape[1]
    upto = lax.broadcasted_iota(jnp.int32, (docs, docs), 1) <= lax.broadcasted_iota(
        jnp.int32, (docs, docs), 0
    )
    return jnp.sum(jnp.where(upto, lengths, 0.0), axis=1, keepdims=True)


def positions(first):
    return first.astype(jnp.float32) + lax.broadcasted_iota(jnp.int32, (1, B), 1).astype(
        jnp.float32
    )


def doc_start(ends, pos):
    return jnp.max(jnp.where(ends <= pos, ends, 0.0), axis=0, keepdims=True)


def hidden(key, start, pos):
    kpos = (key + lax.broadcasted_iota(jnp.int32, (B, B), 0)).astype(jnp.float32)
    return jnp.where((kpos >= start) & (kpos <= pos), 0.0, -jnp.inf)


def identity(n):
    at = [lax.broadcasted_iota(jnp.int32, (n, n), d) for d in range(2)]
    return (at[0] == at[1]).astype(jnp.bfloat16)


def gradients(k, v, qs, gs, logs, deltas, bias=None):
    ps, ds = [], []
    for q, g, log, delta in zip(qs, gs, logs, deltas):
        x = nt(k, q) * (LOG2E / math.sqrt(W)) - log
        if bias is not None:
            x = x + bias[...]
        p = jnp.exp2(x)
        d = p * (nt(v, g) - delta)
        ps.append(p.astype(jnp.bfloat16))
        ds.append(d.astype(jnp.bfloat16))
    dh = jnp.concatenate(ds, axis=1)
    dv = nn(jnp.concatenate(ps, axis=1), jnp.concatenate(gs, axis=0))
    dk = nn(dh, jnp.concatenate(qs, axis=0))
    return dk, dv, nn(k.T, dh)


class Links:
    def __init__(self, columns):
        self.column, self.z, self.core = place()
        ctx = lax.axis_index("ctx")
        self.up = lax.rem(self.z + 1, 4)
        self.down = lax.rem(self.z + 3, 4)
        self.across = lax.rem(self.z + 2, 4)
        self.sibling = (ctx + 1 - 2 * self.core, self.z)
        self.above = (ctx, self.up)
        self.below = (ctx, self.down)
        self.has_next = self.column < columns - 1
        self.has_last = self.column > 0
        self.next = (jnp.where(self.has_next, ctx + 2, ctx), self.z)
        self.last = (jnp.where(self.has_last, ctx - 2, ctx), self.z)
        self.next_across = (self.next[0], self.across)
        self.last_across = (self.last[0], self.across)

    def barrier(self, straight=False):
        barrier = pltpu.get_barrier_semaphore()

        def greet(*devices):
            for device in devices:
                pl.semaphore_signal(barrier, inc=1, device_id=device, device_id_type=MESH)

        greet(self.sibling, self.above, self.below)
        later = (self.next, self.next_across) if straight else (self.next,)
        earlier = (self.last, self.last_across) if straight else (self.last,)
        pl.when(self.has_next)(lambda: greet(*later))
        pl.when(self.has_last)(lambda: greet(*earlier))
        columns = self.has_next.astype(jnp.int32) + self.has_last.astype(jnp.int32)
        pl.semaphore_wait(barrier, 3 + len(later) * columns)


class Route:
    def __init__(self, sems, index, device, source, target, sends=True, gets=True, arrival=None):
        self.sends, self.gets = sends, gets
        landed = target if arrival is None else arrival
        send, recv = sems[0].at[index], sems[1].at[index]
        self.make = lambda end: pltpu.make_async_remote_copy(
            source, end, send, recv, device_id=device, device_id_type=MESH
        )
        self.target, self.landed = target, landed

    @staticmethod
    def only(condition, act):
        if condition is True:
            act()
        else:
            pl.when(condition)(act)

    def start(self):
        self.only(self.sends, lambda: self.make(self.target).start())

    def arrived(self):
        self.only(self.gets, lambda: self.make(self.landed).wait_recv())

    def sent(self):
        self.only(self.sends, lambda: self.make(self.target).wait_send())


def gather_kernel(
    columns, heads, docs_ref, q_ref, g_ref, o_ref, k_ref, v_ref, log_ref,
    q_other, g_other, stat_both, window_out, dq_out, kv_out,
    q_both, g_both, o_vmem, swap, stat, window, dqt, dkv, bias, local, put, send, recv,
):
    at = Links(columns)
    z, core, up, down, across = at.z, at.core, at.up, at.down, at.across
    sems = (send, recv)
    mine = window.at[slot(OWN, z, core)]
    loads = [
        pltpu.make_async_copy(source, target, local.at[n])
        for n, (source, target) in enumerate(
            (
                (k_ref.at[B:], swap.at[0]), (v_ref.at[B:], swap.at[1]),
                (k_ref.at[:B], mine.at[0]), (v_ref.at[:B], mine.at[1]),
                (q_ref, q_both.at[0]), (g_ref, g_both.at[0]), (o_ref, o_vmem), (log_ref, stat.at[0, 0]),
            )
        )
    ]
    for copy in loads:
        copy.start()
    at.barrier()

    theirs = window.at[slot(OWN, z, 1 - core)]
    halves = Route(sems, 0, at.sibling, swap, mine, arrival=theirs)
    for copy in loads[:4]:
        copy.wait()
    halves.start()
    rows = q_ref.shape[0]
    bulk = []
    for part in range(2):
        some = slice(part * rows // 2, (part + 1) * rows // 2)
        bulk.append(Route(sems, 2 + part, at.sibling, q_both.at[0, some], q_both.at[1, some]))
        bulk.append(Route(sems, 4 + part, at.sibling, g_both.at[0, some], g_both.at[1, some]))

    def passed(index, device, side, sent, j, got, sends=True, gets=True):
        there = window.at[slot(side, sent, j)]
        return Route(sems, index, device, there, there, sends, gets, window.at[slot(side, got, j)])

    up_0 = passed(6, at.above, OWN, z, 0, down)
    up_1 = passed(7, at.above, OWN, z, 1, down)
    down_0 = passed(8, at.below, OWN, z, 0, up)
    down_1 = passed(9, at.below, OWN, z, 1, up, z == 0, z == 3)
    far_0 = passed(10, at.below, OWN, up, 0, across)
    far_1 = passed(11, at.above, OWN, down, 1, across)

    def later(index, zc, j, when=True):
        here = window.at[slot(OWN, zc, j)]
        there = window.at[slot(BEFORE, zc, j)]
        sends = at.has_next if when is True else at.has_next & when
        gets = at.has_last if when is True else at.has_last & when
        return Route(sems, index, at.next, here, there, sends, gets)

    next_0 = later(12, z, 0)
    next_1 = later(13, z, 1)
    next_far_0 = later(14, across, 0, z < 2)
    next_far_1 = later(15, across, 1)
    last = at.has_last
    before_up_0 = passed(16, at.above, BEFORE, z, 0, down, last & (z == 3), last & (z == 0))
    before_up_1 = passed(17, at.above, BEFORE, z, 1, down, last, last)
    before_down_0 = passed(18, at.below, BEFORE, z, 0, up, last & (z != 0), last & (z != 3))
    before_down_1 = passed(19, at.below, BEFORE, z, 1, up, last, last)

    halves.arrived()
    for copy in (up_1, down_0, next_1, up_0, down_1, next_0):
        copy.start()
    loads[4].wait()
    loads[5].wait()
    for copy in bulk:
        copy.start()

    loads[6].wait()
    loads[7].wait()
    ones = jnp.ones((8, W), jnp.bfloat16)
    for h in range(heads):
        cols = slice(h * W, (h + 1) * W)
        product = g_both[0, :, cols].astype(jnp.float32) * o_vmem[:, cols].astype(jnp.float32)
        high = product.astype(jnp.bfloat16)
        low = (product - high.astype(jnp.float32)).astype(jnp.bfloat16)
        total = nt(ones, high) + nt(ones, low)
        stat[0, 1, h : h + 1, :] = total[0:1]
    stat[0, 0] = stat[0, 0] * LOG2E
    stats = Route(sems, 20, at.sibling, stat.at[0], stat.at[1])
    stats.start()

    up_1.arrived()
    far_1.start()
    down_0.arrived()
    far_0.start()

    ends = doc_ends(docs_ref)
    column = at.column * 16 * B
    near_4 = jnp.where(z > 0, slot(OWN, down, 1), slot(OWN, 3, 0))
    near_0 = jnp.where(z > 0, slot(OWN, down, 0), slot(BEFORE, 3, 1))

    def half_of(tile):
        return jnp.where((tile + 8) % 8 >= 4, 1 - core, core)

    def near(side, part, tile, keys, key_tiles, out):
        here = pl.ds(pl.multiple_of(part * B, B), B)
        start = doc_start(ends, positions(column + tile * 2 * B + part * B))
        for n, key_tile in enumerate(key_tiles):
            key = column + key_tile * 2 * B + half_of(key_tile) * B
            kpos = (key + lax.broadcasted_iota(jnp.int32, (B, B), 0)).astype(jnp.float32)
            bias[n * B : (n + 1) * B] = jnp.where(kpos >= start, 0.0, -jnp.inf)
        dk, dv, dq = gradients(
            jnp.concatenate([window[n, 0] for n in keys], axis=0),
            jnp.concatenate([window[n, 1] for n in keys], axis=0),
            [q_both[side, here, h * W : (h + 1) * W] for h in range(heads)],
            [g_both[side, here, h * W : (h + 1) * W] for h in range(heads)],
            [stat[side, 0, h : h + 1, here] for h in range(heads)],
            [stat[side, 1, h : h + 1, here] for h in range(heads)],
            bias.at[: len(keys) * B],
        )
        for n in range(len(keys)):
            dkv[out + n, 0] += dk[n * B : (n + 1) * B]
            dkv[out + n, 1] += dv[n * B : (n + 1) * B]
        dqt[side * 2 + part] = dq

    dkv[...] = jnp.zeros_like(dkv)

    @pl.when(at.column == 0)
    def _():
        window[slot(BEFORE, 3, 1)] = jnp.zeros((2, B, W), window.dtype)

    for copy in bulk:
        copy.arrived()
    stats.arrived()
    up_0.arrived()
    puts = [
        pltpu.make_async_copy(source, target, put.at[n])
        for n, (source, target) in enumerate(
            (
                (q_both.at[1], q_other), (g_both.at[1], g_other), (stat, stat_both),
                (window.at[8:], window_out.at[8:]), (window.at[:8], window_out.at[:8]),
                (dqt, dq_out), (dkv, kv_out),
            )
        )
    ]
    for copy in puts[:3]:
        copy.start()
    near(1 - core, 0, z + 4, [slot(OWN, z, 0), near_4], [z, z + 3], 0)
    next_1.arrived()
    before_down_1.start()
    before_up_1.start()
    far_0.arrived()
    next_far_0.start()
    far_1.arrived()
    next_far_1.start()
    next_0.arrived()
    before_down_0.start()
    before_up_0.start()
    down_1.arrived()
    puts[3].start()
    near(1 - core, 1, z + 4, [slot(OWN, z, 0), near_4], [z, z + 3], 0)
    before_up_1.arrived()
    pl.loop(0, 2)(lambda part: near(core, part, z, [near_0], [z - 1], 2))
    puts[5].start()
    puts[6].start()
    for copy in (before_up_0, before_down_0, before_down_1, next_far_0, next_far_1):
        copy.arrived()
    puts[4].start()
    for copy in (
        [halves, up_0, up_1, down_0, down_1, far_0, far_1, next_0, next_1, next_far_0]
        + [next_far_1, before_up_0, before_up_1, before_down_0, before_down_1, stats]
        + bulk
    ):
        copy.sent()
    for copy in puts:
        copy.wait()


def gather(columns, docs, q, g, o, k, v, log_total):
    rows, features = q.shape
    heads = features // W
    some = pl.BlockSpec(memory_space=pl.ANY)
    window = (16, 2, B, W)
    stat = (2, 2, heads, rows)
    turned = (4, W, heads * B)
    sums = (3, 2, B, W)
    return pl.pallas_call(
        functools.partial(gather_kernel, columns, heads),
        out_shape=(
            jax.ShapeDtypeStruct(q.shape, q.dtype),
            jax.ShapeDtypeStruct(q.shape, q.dtype),
            jax.ShapeDtypeStruct(stat, jnp.float32),
            jax.ShapeDtypeStruct(window, k.dtype),
            jax.ShapeDtypeStruct(turned, jnp.float32),
            jax.ShapeDtypeStruct(sums, jnp.float32),
        ),
        in_specs=[pl.BlockSpec(memory_space=pltpu.VMEM)] + [some] * 6,
        out_specs=(some,) * 6,
        scratch_shapes=[
            pltpu.VMEM((2, rows, features), q.dtype),
            pltpu.VMEM((2, rows, features), q.dtype),
            pltpu.VMEM(q.shape, q.dtype),
            pltpu.VMEM((2, B, W), k.dtype),
            pltpu.VMEM(stat, jnp.float32),
            pltpu.VMEM(window, k.dtype),
            pltpu.VMEM(turned, jnp.float32),
            pltpu.VMEM(sums, jnp.float32),
            pltpu.VMEM((2 * B, B), jnp.float32),
            pltpu.SemaphoreType.DMA((8,)),
            pltpu.SemaphoreType.DMA((7,)),
            pltpu.SemaphoreType.DMA((21,)),
            pltpu.SemaphoreType.DMA((21,)),
        ],
        compiler_params=pltpu.CompilerParams(
            collective_id=0, has_side_effects=True, vmem_limit_bytes=VMEM
        ),
    )(docs, q, g, o, k, v, log_total)


def attend_kernel(
    heads, docs_ref, qa_hbm, qb_hbm, ga_hbm, gb_hbm, stat_hbm, window_hbm, dq_hbm, kv_hbm,
    dq_own, dq_other, part_hbm,
    q_ref, g_ref, stat_ref, window_ref, dqt, dqh, part_ref, dka, dva, dkv, bias, starts, bounds, get, put,
):
    column, z, core = place()
    loads = [
        pltpu.make_async_copy(source, target, get.at[n])
        for n, (source, target) in enumerate(
            (
                (stat_hbm, stat_ref),
                (window_hbm.at[:8], window_ref.at[:8]), (window_hbm.at[8:], window_ref.at[8:]),
                (kv_hbm, dkv), (qa_hbm, q_ref.at[0]), (ga_hbm, g_ref.at[0]),
                (dq_hbm.at[:2], dqt.at[:2]),
                (qb_hbm, q_ref.at[1]), (gb_hbm, g_ref.at[1]), (dq_hbm.at[2:], dqt.at[2:]),
            )
        )
    ]
    for load in loads:
        load.start()
    ends = doc_ends(docs_ref)
    window = (column - 1) * 16 * B

    def half_of(b):
        return jnp.where(b % 8 >= 4, 1 - core, core)

    def tile_of(side):
        return z + 4 * (core if side == 0 else 1 - core)

    for block in range(4):
        side, part = divmod(block, 2)
        first = column * 16 * B + tile_of(side) * 2 * B + part * B
        start = doc_start(ends, positions(first))
        starts[block] = start
        low = jnp.min(start).astype(jnp.int32) - window
        last = jnp.max(start).astype(jnp.int32) - window
        b = low // (2 * B)
        bounds[0, block] = jnp.where(low % (2 * B) >= half_of(b) * B + B, b + 1, b)
        b = last // (2 * B)
        bounds[1, block] = jnp.where(last % (2 * B) > half_of(b) * B, b + 1, b)
    dka[...] = jnp.zeros_like(dka)
    dva[...] = jnp.zeros_like(dva)
    for load in loads[:7]:
        load.wait()
    down = lax.rem(z + 3, 4)
    nears = (
        slot(OWN, z, 0),
        jnp.where(z > 0, slot(OWN, down, 1), slot(OWN, 3, 0)),
        jnp.where(z > 0, slot(OWN, down, 0), slot(BEFORE, 3, 1)),
    )
    for n, at in enumerate(nears):
        dka[at] = dkv[n, 0]
        dva[at] = dkv[n, 1]

    @pl.loop(0, 4)
    def _(block):
        side, part = block // 2, block % 2
        here = pl.ds(pl.multiple_of(part * B, B), B)

        @pl.when(block == 2)
        def _():
            for load in loads[7:]:
                load.wait()

        def work(blocks, mask=None):
            at = [slot(b // 8, b % 4, b % 8 // 4) for b in blocks]
            dk, dv, dq = gradients(
                jnp.concatenate([window_ref[n, 0] for n in at], axis=0),
                jnp.concatenate([window_ref[n, 1] for n in at], axis=0),
                [q_ref[side, here, h * W : (h + 1) * W] for h in range(heads)],
                [g_ref[side, here, h * W : (h + 1) * W] for h in range(heads)],
                [stat_ref[side, 0, h : h + 1, here] for h in range(heads)],
                [stat_ref[side, 1, h : h + 1, here] for h in range(heads)],
                mask,
            )
            for n in range(len(at)):
                dva[at[n]] += dv[n * B : (n + 1) * B]
                dka[at[n]] += dk[n * B : (n + 1) * B]
            dqt[block] += dq

        second = jnp.where(side == 0, core, 1 - core)
        end = 7 + z + 4 * second
        skip = jnp.where(second == 1, 8 + z, 16)

        def counted(b):
            return jnp.where(b > skip, b - 1, b)

        def real(n):
            return jnp.where(n >= skip, n + 1, n)

        end = counted(end)
        low = counted(bounds[0, block])
        cut = jnp.minimum(counted(bounds[1, block]), end)
        cut = cut + (end - cut) % 2

        @pl.loop(low, cut)
        def _(n):
            b = real(n)
            key = window + b * 2 * B + half_of(b) * B
            kpos = (key + lax.broadcasted_iota(jnp.int32, (B, B), 0)).astype(jnp.float32)
            bias[...] = jnp.where(kpos >= starts[block], 0.0, -jnp.inf)
            work([b], bias)

        @pl.loop(0, (end - jnp.maximum(low, cut)) // 2)
        def _(n):
            work([real(cut + 2 * n), real(cut + 2 * n + 1)])

        @pl.when(side == 0)
        def _():
            pltpu.make_async_copy(dqt.at[block], dq_own.at[part], put.at[block]).start()

        @pl.when(side == 1)
        def _():
            dqh[part] = dqt[block].astype(jnp.bfloat16)
            pltpu.make_async_copy(dqh.at[part], dq_other.at[part], put.at[block]).start()

    @pl.loop(0, 16)
    def _(s):
        part_ref[s, 0] = (dka[s] * (1.0 / math.sqrt(W))).astype(jnp.bfloat16)
        part_ref[s, 1] = dva[s].astype(jnp.bfloat16)
        pltpu.make_async_copy(part_ref.at[s], part_hbm.at[s], put.at[4 + s]).start()

    for part in range(2):
        pltpu.make_async_copy(dqt.at[part], dq_own.at[part], put.at[part]).wait()
        pltpu.make_async_copy(dqh.at[part], dq_other.at[part], put.at[2 + part]).wait()
    for s in range(16):
        pltpu.make_async_copy(part_ref.at[s], part_hbm.at[s], put.at[4 + s]).wait()


def attend(docs, q, q_other, g, g_other, stat, window, dq, sums):
    rows, features = q.shape
    heads = features // W
    some = pl.BlockSpec(memory_space=pl.ANY)
    both = (2, rows, features)
    turned = (2, W, heads * B)
    return pl.pallas_call(
        functools.partial(attend_kernel, heads),
        out_shape=(
            jax.ShapeDtypeStruct(turned, jnp.float32),
            jax.ShapeDtypeStruct(turned, jnp.bfloat16),
            jax.ShapeDtypeStruct(window.shape, jnp.bfloat16),
        ),
        in_specs=[pl.BlockSpec(memory_space=pltpu.VMEM)] + [some] * 8,
        out_specs=(some,) * 3,
        scratch_shapes=[
            pltpu.VMEM(both, q.dtype),
            pltpu.VMEM(both, q.dtype),
            pltpu.VMEM(stat.shape, stat.dtype),
            pltpu.VMEM(window.shape, window.dtype),
            pltpu.VMEM((4, W, heads * B), jnp.float32),
            pltpu.VMEM(turned, jnp.bfloat16),
            pltpu.VMEM(window.shape, jnp.bfloat16),
            pltpu.VMEM((16, B, W), jnp.float32),
            pltpu.VMEM((16, B, W), jnp.float32),
            pltpu.VMEM(sums.shape, jnp.float32),
            pltpu.VMEM((B, B), jnp.float32),
            pltpu.VMEM((4, 1, B), jnp.float32),
            pltpu.SMEM((2, 4), jnp.int32),
            pltpu.SemaphoreType.DMA((10,)),
            pltpu.SemaphoreType.DMA((20,)),
        ],
        compiler_params=pltpu.CompilerParams(vmem_limit_bytes=VMEM),
        cost_estimate=pl.CostEstimate(
            flops=20 * 10 * heads * B * B * W, bytes_accessed=16 << 20, transcendentals=0
        ),
    )(docs, q, q_other, g, g_other, stat, window, dq, sums)


def return_kernel(
    columns, heads, docs_ref, q_hbm, k_hbm, v_hbm, g_hbm, stat_hbm, dq_own, dq_other, part_ref,
    dq_hbm, dk_hbm, dv_hbm,
    q_ref, k_ref, v_ref, g_ref, stat, dqt, dq_sent, dq_got, dq_out, dk_ref, dv_ref, dka, dva, bias,
    part, across_got, beside_got, beside_sum, later_got, far_got, near_sum, near_got,
    final, given_half, local, put, send, recv,
):
    at = Links(columns)
    z, core, up, down, across = at.z, at.core, at.up, at.down, at.across
    sems = (send, recv)
    load = pltpu.make_async_copy(part_ref.at[:8], part.at[:8], local.at[0])
    load_own = pltpu.make_async_copy(part_ref.at[8:], part.at[8:], local.at[1])
    load_dq = pltpu.make_async_copy(dq_other, dq_sent, local.at[2])
    load.start()
    load_own.start()
    load_dq.start()
    loads = [
        pltpu.make_async_copy(source, target, local.at[3 + n])
        for n, (source, target) in enumerate(
            (
                (q_hbm, q_ref), (g_hbm, g_ref), (k_hbm, k_ref), (v_hbm, v_ref),
                (stat_hbm.at[0], stat), (dq_own, dqt),
            )
        )
    ]
    for copy in loads:
        copy.start()
    at.barrier(straight=True)
    has_next, has_last = at.has_next, at.has_last

    def given(side, zc, j):
        return part.at[slot(side, zc, j)]

    def held(side, zc, j):
        return part[slot(side, zc, j)].astype(jnp.float32)

    far_back = [
        Route(
            sems, j, at.last_across, given(BEFORE, across, j), across_got.at[j],
            has_last & (z < 2) if j == 0 else has_last,
            has_next & (z >= 2) if j == 0 else has_next,
        )
        for j in range(2)
    ]
    side_up = [
        Route(
            sems, 2 + j, at.above, given(BEFORE, up, j), beside_got.at[0, j],
            has_last & (z != 3) if j == 0 else has_last,
            has_last & (z != 0) if j == 0 else has_last,
        )
        for j in range(2)
    ]
    side_down = [
        Route(
            sems, 4 + j, at.below, given(BEFORE, down, j), beside_got.at[1, j],
            has_last & (z == 0) if j == 0 else has_last,
            has_last & (z == 3) if j == 0 else has_last,
        )
        for j in range(2)
    ]
    bulk = [
        Route(sems, 6 + n, at.sibling, dq_sent.at[n], dq_got.at[n]) for n in range(2)
    ]
    back = [
        Route(sems, 8 + j, at.last, beside_sum.at[j], later_got.at[j], has_last, has_next)
        for j in range(2)
    ]
    far_up = Route(sems, 10, at.above, given(OWN, across, 0), far_got.at[0])
    far_down = Route(
        sems, 11, at.below, given(OWN, across, 1), far_got.at[1], z >= 2, (z == 1) | (z == 2)
    )
    near_up_0 = Route(sems, 12, at.above, near_sum.at[0], near_got.at[0])
    near_up_1 = Route(sems, 13, at.above, given(OWN, up, 1), near_got.at[1], z == 3, z == 0)
    near_down_0 = Route(sems, 14, at.below, given(OWN, down, 0), near_got.at[2])
    near_down_1 = Route(sems, 15, at.below, near_sum.at[1], near_got.at[3], z != 0, z != 3)

    load.wait()
    for copy in (far_back[1], side_up[1], side_down[1], far_back[0], side_up[0], side_down[0]):
        copy.start()
    load_own.wait()
    for copy in (far_up, far_down, near_down_0, near_up_1):
        copy.start()
    load_dq.wait()
    for copy in bulk:
        copy.start()
    for copy in loads:
        copy.wait()
    ends = doc_ends(docs_ref)
    tile = at.column * 16 * B + (z + 4 * core) * 2 * B
    dka[...] = jnp.zeros_like(dka)
    dva[...] = jnp.zeros_like(dva)

    def diagonal(n):
        block, b = (n + 1) // 2, n // 2
        here = pl.ds(pl.multiple_of(block * B, B), B)
        there = pl.ds(pl.multiple_of(b * B, B), B)
        pos = positions(tile + block * B)
        bias[...] = hidden(tile + b * B, doc_start(ends, pos), pos)
        dk, dv, dq = gradients(
            k_ref[there],
            v_ref[there],
            [q_ref[here, h * W : (h + 1) * W] for h in range(heads)],
            [g_ref[here, h * W : (h + 1) * W] for h in range(heads)],
            [stat[0, h : h + 1, here] for h in range(heads)],
            [stat[1, h : h + 1, here] for h in range(heads)],
            bias,
        )
        dka[b] += dk
        dva[b] += dv
        dqt[block] += dq

    pl.loop(0, 3)(diagonal)

    @pl.when(has_last)
    def _():
        for copy in side_up + side_down:
            copy.arrived()
        for j in range(2):
            final[j] = held(BEFORE, z, j)
        final[1] += beside_got[0, 1].astype(jnp.float32) + beside_got[1, 1].astype(jnp.float32)

        @pl.when(z != 0)
        def _():
            final[0] += beside_got[0, 0].astype(jnp.float32)

        @pl.when(z == 3)
        def _():
            final[0] += beside_got[1, 0].astype(jnp.float32)

        beside_sum[...] = final[...].astype(jnp.bfloat16)
        for copy in back:
            copy.start()

    far_up.arrived()
    near_sum[0] = (held(OWN, up, 0) + far_got[0].astype(jnp.float32)).astype(jnp.bfloat16)
    near_up_0.start()

    @pl.when((z == 1) | (z == 2))
    def _():
        far_down.make(far_got.at[1]).wait_recv()
        total = held(OWN, down, 1) + far_got[1].astype(jnp.float32)
        near_sum[1] = total.astype(jnp.bfloat16)

    @pl.when(z == 3)
    def _():
        near_sum[1] = given(OWN, down, 1)[...]

    near_down_1.start()
    for copy in bulk:
        copy.arrived()
    eye = identity(B)
    for block in range(2):
        for h in range(heads):
            rows = slice(h * B, (h + 1) * B)
            total = dqt[block, :, rows] + dq_got[block, :, rows].astype(jnp.float32)
            rounded = (total * (1.0 / math.sqrt(W))).astype(jnp.bfloat16)
            turned = nt(eye, rounded).astype(jnp.bfloat16)
            dq_out[block * B : (block + 1) * B, h * W : (h + 1) * W] = turned
    out_q = pltpu.make_async_copy(dq_out, dq_hbm, put.at[0])
    out_q.start()
    near_down_0.arrived()
    near_up_0.arrived()
    final[0] = (
        held(OWN, z, 0) + near_got[0].astype(jnp.float32) + near_got[2].astype(jnp.float32)
    )
    final[1] = held(OWN, z, 1)

    @pl.when(z == 0)
    def _():
        near_up_1.make(near_got.at[1]).wait_recv()
        final[1] += near_got[1].astype(jnp.float32)

    @pl.when(z != 3)
    def _():
        near_down_1.make(near_got.at[3]).wait_recv()
        final[1] += near_got[3].astype(jnp.float32)

    @pl.when(has_next)
    def _():
        far_back[1].make(across_got.at[1]).wait_recv()
        final[1] += across_got[1].astype(jnp.float32)
        for j in range(2):
            back[j].arrived()
            final[j] += later_got[j].astype(jnp.float32)

    @pl.when(has_next & (z >= 2))
    def _():
        far_back[0].make(across_got.at[0]).wait_recv()
        final[0] += across_got[0].astype(jnp.float32)

    given_half[...] = final[1 - core].astype(jnp.bfloat16)
    give_k = Route(sems, 16, at.sibling, given_half.at[0], dk_ref.at[B:])
    give_v = Route(sems, 17, at.sibling, given_half.at[1], dv_ref.at[B:])
    give_k.start()
    give_v.start()
    scale = 1.0 / math.sqrt(W)
    dk_ref[:B] = (final[core, 0] + dka[0] * scale).astype(jnp.bfloat16)
    dv_ref[:B] = (final[core, 1] + dva[0]).astype(jnp.bfloat16)
    give_k.arrived()
    give_v.arrived()
    dk_ref[B:] = (dk_ref[B:].astype(jnp.float32) + dka[1] * scale).astype(jnp.bfloat16)
    dv_ref[B:] = (dv_ref[B:].astype(jnp.float32) + dva[1]).astype(jnp.bfloat16)
    out_k = pltpu.make_async_copy(dk_ref, dk_hbm, put.at[1])
    out_v = pltpu.make_async_copy(dv_ref, dv_hbm, put.at[2])
    out_k.start()
    out_v.start()
    for copy in (out_q, out_k, out_v):
        copy.wait()
    for copy in (
        far_back + side_up + side_down + bulk + back
        + [far_up, far_down, near_up_0, near_up_1, near_down_0, near_down_1, give_k, give_v]
    ):
        copy.sent()


def give_back(columns, docs, q, k, v, g, stat, dq_own, dq_other, part):
    rows, features = q.shape
    heads = features // W
    some = pl.BlockSpec(memory_space=pl.ANY)
    vmem = pl.BlockSpec(memory_space=pltpu.VMEM)
    block = (2, B, W)
    return pl.pallas_call(
        functools.partial(return_kernel, columns, heads),
        out_shape=(
            jax.ShapeDtypeStruct((rows, features), jnp.bfloat16),
            jax.ShapeDtypeStruct((rows, W), jnp.bfloat16),
            jax.ShapeDtypeStruct((rows, W), jnp.bfloat16),
        ),
        in_specs=[vmem] + [some] * 8,
        out_specs=(some,) * 3,
        scratch_shapes=[
            pltpu.VMEM(q.shape, q.dtype),
            pltpu.VMEM(k.shape, k.dtype),
            pltpu.VMEM(v.shape, v.dtype),
            pltpu.VMEM(g.shape, g.dtype),
            pltpu.VMEM(stat.shape[1:], stat.dtype),
            pltpu.VMEM(dq_own.shape, dq_own.dtype),
            pltpu.VMEM(dq_other.shape, dq_other.dtype),
            pltpu.VMEM(dq_other.shape, dq_other.dtype),
            pltpu.VMEM(q.shape, jnp.bfloat16),
            pltpu.VMEM((rows, W), jnp.bfloat16),
            pltpu.VMEM((rows, W), jnp.bfloat16),
            pltpu.VMEM((2, B, W), jnp.float32),
            pltpu.VMEM((2, B, W), jnp.float32),
            pltpu.VMEM((B, B), jnp.float32),
            pltpu.VMEM((16, *block), jnp.bfloat16),
            pltpu.VMEM((2, *block), jnp.bfloat16),
            pltpu.VMEM((2, 2, *block), jnp.bfloat16),
            pltpu.VMEM((2, *block), jnp.bfloat16),
            pltpu.VMEM((2, *block), jnp.bfloat16),
            pltpu.VMEM((2, *block), jnp.bfloat16),
            pltpu.VMEM((2, *block), jnp.bfloat16),
            pltpu.VMEM((4, *block), jnp.bfloat16),
            pltpu.VMEM((2, *block), jnp.float32),
            pltpu.VMEM(block, jnp.bfloat16),
            pltpu.SemaphoreType.DMA((9,)),
            pltpu.SemaphoreType.DMA((3,)),
            pltpu.SemaphoreType.DMA((18,)),
            pltpu.SemaphoreType.DMA((18,)),
        ],
        compiler_params=pltpu.CompilerParams(
            collective_id=1, has_side_effects=True, vmem_limit_bytes=VMEM
        ),
    )(docs, q, k, v, g, stat, dq_own, dq_other, part)


def publish_kernel(*refs):
    sources, targets, held, get, put = refs[:3], refs[3:6], refs[6:9], refs[9], refs[10]
    pieces = []
    for source, target, mid in zip(sources, targets, held):
        rows = min(source.shape[0], 128 * 1024 // source.shape[1])
        for at in range(0, source.shape[0], rows):
            here = slice(at, at + rows)
            n = len(pieces)
            pieces.append(
                (
                    pltpu.make_async_copy(source.at[here], mid.at[here], get.at[n]),
                    pltpu.make_async_copy(mid.at[here], target.at[here], put.at[n]),
                )
            )
    for into, _ in pieces:
        into.start()
    for into, out in pieces:
        into.wait()
        out.start()
    for _, out in pieces:
        out.wait()


def publish(*results):
    some = pl.BlockSpec(memory_space=pl.ANY)
    return pl.pallas_call(
        publish_kernel,
        out_shape=tuple(jax.ShapeDtypeStruct(x.shape, x.dtype) for x in results),
        in_specs=[some] * 3,
        out_specs=(some,) * 3,
        scratch_shapes=[pltpu.VMEM(x.shape, x.dtype) for x in results]
        + [pltpu.SemaphoreType.DMA((6,))] * 2,
        compiler_params=pltpu.CompilerParams(vmem_limit_bytes=VMEM),
    )(*results)


def solution(mesh):
    columns = mesh.shape["ctx"] // 2

    def on_device(q, k, v, o, g, log_total, doc_lengths):
        docs = doc_lengths[None, :]
        q_other, g_other, stat, window, dq, sums = gather(columns, docs, q, g, o, k, v, log_total)
        dq_own, dq_other, part = attend(docs, q, q_other, g, g_other, stat, window, dq, sums)
        dq, dk, dv = give_back(columns, docs, q, k, v, g, stat, dq_own, dq_other, part)
        return publish(dq, dk, dv)

    rows = P(("ctx", "section"), None)
    return jax.shard_map(
        on_device,
        mesh=mesh,
        in_specs=(rows, rows, rows, rows, rows, P(None, ("ctx", "section")), P()),
        out_specs=(rows, rows, rows),
        check_vma=False,
    )
```

```python
import functools
import math

import jax
import jax.numpy as jnp
from jax import lax
from jax.experimental import pallas as pl
from jax.experimental.pallas import tpu as pltpu
from jax.sharding import PartitionSpec as P

MESH = pl.DeviceIdType.MESH
W = 128
B = 256
VMEM = 58 << 20
LOG2E = math.log2(math.e)
OWN, BEFORE = 1, 0


def nn(a, b):
    return jnp.dot(a, b, preferred_element_type=jnp.float32)


def nt(a, b):
    return lax.dot_general(a, b, (((1,), (1,)), ((), ())), preferred_element_type=jnp.float32)


def place():
    ctx = lax.axis_index("ctx")
    return ctx // 2, lax.axis_index("section"), ctx % 2


def slot(side, z, j):
    return side * 8 + z * 2 + j


def doc_ends(docs_ref):
    lengths = docs_ref[...].astype(jnp.float32)
    docs = lengths.shape[1]
    upto = lax.broadcasted_iota(jnp.int32, (docs, docs), 1) <= lax.broadcasted_iota(
        jnp.int32, (docs, docs), 0
    )
    return jnp.sum(jnp.where(upto, lengths, 0.0), axis=1, keepdims=True)


def positions(first):
    return first.astype(jnp.float32) + lax.broadcasted_iota(jnp.int32, (1, B), 1).astype(
        jnp.float32
    )


def doc_start(ends, pos):
    return jnp.max(jnp.where(ends <= pos, ends, 0.0), axis=0, keepdims=True)


def hidden(key, start, pos):
    kpos = (key + lax.broadcasted_iota(jnp.int32, (B, B), 0)).astype(jnp.float32)
    return jnp.where((kpos >= start) & (kpos <= pos), 0.0, -jnp.inf)


def identity(n):
    at = [lax.broadcasted_iota(jnp.int32, (n, n), d) for d in range(2)]
    return (at[0] == at[1]).astype(jnp.bfloat16)


def gradients(k, v, qs, gs, logs, deltas, bias=None):
    ps, ds = [], []
    for q, g, log, delta in zip(qs, gs, logs, deltas):
        x = nt(k, q) * (LOG2E / math.sqrt(W)) - log
        if bias is not None:
            x = x + bias[...]
        p = jnp.exp2(x)
        d = p * (nt(v, g) - delta)
        ps.append(p.astype(jnp.bfloat16))
        ds.append(d.astype(jnp.bfloat16))
    dh = jnp.concatenate(ds, axis=1)
    dv = nn(jnp.concatenate(ps, axis=1), jnp.concatenate(gs, axis=0))
    dk = nn(dh, jnp.concatenate(qs, axis=0))
    return dk, dv, nn(k.T, dh)


class Links:
    def __init__(self, columns):
        self.column, self.z, self.core = place()
        ctx = lax.axis_index("ctx")
        self.up = lax.rem(self.z + 1, 4)
        self.down = lax.rem(self.z + 3, 4)
        self.across = lax.rem(self.z + 2, 4)
        self.sibling = (ctx + 1 - 2 * self.core, self.z)
        self.above = (ctx, self.up)
        self.below = (ctx, self.down)
        self.has_next = self.column < columns - 1
        self.has_last = self.column > 0
        self.next = (jnp.where(self.has_next, ctx + 2, ctx), self.z)
        self.last = (jnp.where(self.has_last, ctx - 2, ctx), self.z)
        self.next_across = (self.next[0], self.across)
        self.last_across = (self.last[0], self.across)

    def barrier(self, straight=False):
        barrier = pltpu.get_barrier_semaphore()

        def greet(*devices):
            for device in devices:
                pl.semaphore_signal(barrier, inc=1, device_id=device, device_id_type=MESH)

        greet(self.sibling, self.above, self.below)
        later = (self.next, self.next_across) if straight else (self.next,)
        earlier = (self.last, self.last_across) if straight else (self.last,)
        pl.when(self.has_next)(lambda: greet(*later))
        pl.when(self.has_last)(lambda: greet(*earlier))
        columns = self.has_next.astype(jnp.int32) + self.has_last.astype(jnp.int32)
        pl.semaphore_wait(barrier, 3 + len(later) * columns)


def pieces(ref):
    if len(ref.shape) == 3:
        return [part for n in range(ref.shape[0]) for part in pieces(ref.at[n])[:8]]
    count = min(8, max(1, ref.shape[0] // 128)) if ref.shape[1] <= 512 else 8
    rows = ref.shape[0] // count
    return [ref.at[m * rows : (m + 1) * rows] for m in range(count)]


class Route:
    def __init__(self, sems, index, device, source, target, sends=True, gets=True, arrival=None):
        self.sends, self.gets = sends, gets
        send, recv = sems[0].at[index], sems[1].at[index]
        self.make = lambda end, begin=source: pltpu.make_async_remote_copy(
            begin, end, send, recv, device_id=device, device_id_type=MESH
        )
        self.source, self.target = source, target
        self.landed = target if arrival is None else arrival

    @staticmethod
    def only(condition, act):
        if condition is True:
            act()
        else:
            pl.when(condition)(act)

    def start(self):
        def act():
            for begin, end in zip(pieces(self.source), pieces(self.target)):
                self.make(end, begin).start()

        self.only(self.sends, act)

    def arrived(self):
        self.only(self.gets, lambda: self.make(self.landed).wait_recv())

    def sent(self):
        self.only(self.sends, lambda: self.make(self.target).wait_send())


def gather_kernel(
    columns, heads, docs_ref, q_ref, g_ref, o_ref, k_ref, v_ref, log_ref,
    q_other, g_other, stat_both, window_out, dq_out, kv_out,
    q_both, g_both, o_vmem, swap, stat, window, dqt, dkv, bias, local, put, send, recv,
):
    at = Links(columns)
    z, core, up, down, across = at.z, at.core, at.up, at.down, at.across
    sems = (send, recv)
    mine = window.at[slot(OWN, z, core)]
    loads = [
        pltpu.make_async_copy(source, target, local.at[n])
        for n, (source, target) in enumerate(
            (
                (k_ref.at[B:], swap.at[0]), (v_ref.at[B:], swap.at[1]),
                (k_ref.at[:B], mine.at[0]), (v_ref.at[:B], mine.at[1]),
                (q_ref, q_both.at[0]), (g_ref, g_both.at[0]), (o_ref, o_vmem), (log_ref, stat.at[0, 0]),
            )
        )
    ]
    for copy in loads:
        copy.start()
    at.barrier()

    theirs = window.at[slot(OWN, z, 1 - core)]
    halves = Route(sems, 0, at.sibling, swap, mine, arrival=theirs)
    for copy in loads[:4]:
        copy.wait()
    halves.start()
    rows = q_ref.shape[0]
    bulk = []
    for part in range(2):
        some = slice(part * rows // 2, (part + 1) * rows // 2)
        bulk.append(Route(sems, 2 + part, at.sibling, q_both.at[0, some], q_both.at[1, some]))
        bulk.append(Route(sems, 4 + part, at.sibling, g_both.at[0, some], g_both.at[1, some]))

    def passed(index, device, side, sent, j, got, sends=True, gets=True):
        there = window.at[slot(side, sent, j)]
        return Route(sems, index, device, there, there, sends, gets, window.at[slot(side, got, j)])

    up_0 = passed(6, at.above, OWN, z, 0, down)
    up_1 = passed(7, at.above, OWN, z, 1, down)
    down_0 = passed(8, at.below, OWN, z, 0, up)
    down_1 = passed(9, at.below, OWN, z, 1, up, z == 0, z == 3)
    far_0 = passed(10, at.below, OWN, up, 0, across)
    far_1 = passed(11, at.above, OWN, down, 1, across)

    def later(index, zc, j, when=True):
        here = window.at[slot(OWN, zc, j)]
        there = window.at[slot(BEFORE, zc, j)]
        sends = at.has_next if when is True else at.has_next & when
        gets = at.has_last if when is True else at.has_last & when
        return Route(sems, index, at.next, here, there, sends, gets)

    next_0 = later(12, z, 0)
    next_1 = later(13, z, 1)
    next_far_0 = later(14, across, 0, z < 2)
    next_far_1 = later(15, across, 1)
    last = at.has_last
    before_up_0 = passed(16, at.above, BEFORE, z, 0, down, last & (z == 3), last & (z == 0))
    before_up_1 = passed(17, at.above, BEFORE, z, 1, down, last, last)
    before_down_0 = passed(18, at.below, BEFORE, z, 0, up, last & (z != 0), last & (z != 3))
    before_down_1 = passed(19, at.below, BEFORE, z, 1, up, last, last)

    halves.arrived()
    for copy in (up_1, down_0, next_1, up_0, down_1, next_0):
        copy.start()
    loads[4].wait()
    loads[5].wait()
    for copy in bulk:
        copy.start()

    loads[6].wait()
    loads[7].wait()
    ones = jnp.ones((8, W), jnp.bfloat16)
    for h in range(heads):
        cols = slice(h * W, (h + 1) * W)
        product = g_both[0, :, cols].astype(jnp.float32) * o_vmem[:, cols].astype(jnp.float32)
        high = product.astype(jnp.bfloat16)
        low = (product - high.astype(jnp.float32)).astype(jnp.bfloat16)
        total = nt(ones, high) + nt(ones, low)
        stat[0, 1, h : h + 1, :] = total[0:1]
    stat[0, 0] = stat[0, 0] * LOG2E
    stats = Route(sems, 20, at.sibling, stat.at[0], stat.at[1])
    stats.start()

    up_1.arrived()
    far_1.start()
    down_0.arrived()
    far_0.start()

    ends = doc_ends(docs_ref)
    column = at.column * 16 * B
    near_4 = jnp.where(z > 0, slot(OWN, down, 1), slot(OWN, 3, 0))
    near_0 = jnp.where(z > 0, slot(OWN, down, 0), slot(BEFORE, 3, 1))

    def half_of(tile):
        return jnp.where((tile + 8) % 8 >= 4, 1 - core, core)

    def near(side, part, tile, keys, key_tiles, out):
        here = pl.ds(pl.multiple_of(part * B, B), B)
        start = doc_start(ends, positions(column + tile * 2 * B + part * B))
        for n, key_tile in enumerate(key_tiles):
            key = column + key_tile * 2 * B + half_of(key_tile) * B
            kpos = (key + lax.broadcasted_iota(jnp.int32, (B, B), 0)).astype(jnp.float32)
            bias[n * B : (n + 1) * B] = jnp.where(kpos >= start, 0.0, -jnp.inf)
        dk, dv, dq = gradients(
            jnp.concatenate([window[n, 0] for n in keys], axis=0),
            jnp.concatenate([window[n, 1] for n in keys], axis=0),
            [q_both[side, here, h * W : (h + 1) * W] for h in range(heads)],
            [g_both[side, here, h * W : (h + 1) * W] for h in range(heads)],
            [stat[side, 0, h : h + 1, here] for h in range(heads)],
            [stat[side, 1, h : h + 1, here] for h in range(heads)],
            bias.at[: len(keys) * B],
        )
        for n in range(len(keys)):
            dkv[out + n, 0] += dk[n * B : (n + 1) * B]
            dkv[out + n, 1] += dv[n * B : (n + 1) * B]
        dqt[side * 2 + part] = dq

    dkv[...] = jnp.zeros_like(dkv)

    @pl.when(at.column == 0)
    def _():
        window[slot(BEFORE, 3, 1)] = jnp.zeros((2, B, W), window.dtype)

    for copy in bulk:
        copy.arrived()
    stats.arrived()
    up_0.arrived()
    puts = [
        pltpu.make_async_copy(source, target, put.at[n])
        for n, (source, target) in enumerate(
            (
                (q_both.at[1], q_other), (g_both.at[1], g_other), (stat, stat_both),
                (window.at[8:], window_out.at[8:]), (window.at[:8], window_out.at[:8]),
                (dqt, dq_out), (dkv, kv_out),
            )
        )
    ]
    for copy in puts[:3]:
        copy.start()
    near(1 - core, 0, z + 4, [slot(OWN, z, 0), near_4], [z, z + 3], 0)
    next_1.arrived()
    before_down_1.start()
    before_up_1.start()
    far_0.arrived()
    next_far_0.start()
    far_1.arrived()
    next_far_1.start()
    next_0.arrived()
    before_down_0.start()
    before_up_0.start()
    down_1.arrived()
    puts[3].start()
    near(1 - core, 1, z + 4, [slot(OWN, z, 0), near_4], [z, z + 3], 0)
    before_up_1.arrived()
    pl.loop(0, 2)(lambda part: near(core, part, z, [near_0], [z - 1], 2))
    puts[5].start()
    puts[6].start()
    for copy in (before_up_0, before_down_0, before_down_1, next_far_0, next_far_1):
        copy.arrived()
    puts[4].start()
    for copy in (
        [halves, up_0, up_1, down_0, down_1, far_0, far_1, next_0, next_1, next_far_0]
        + [next_far_1, before_up_0, before_up_1, before_down_0, before_down_1, stats]
        + bulk
    ):
        copy.sent()
    for copy in puts:
        copy.wait()


def gather(columns, docs, q, g, o, k, v, log_total):
    rows, features = q.shape
    heads = features // W
    some = pl.BlockSpec(memory_space=pl.ANY)
    window = (16, 2, B, W)
    stat = (2, 2, heads, rows)
    turned = (4, W, heads * B)
    sums = (3, 2, B, W)
    return pl.pallas_call(
        functools.partial(gather_kernel, columns, heads),
        out_shape=(
            jax.ShapeDtypeStruct(q.shape, q.dtype),
            jax.ShapeDtypeStruct(q.shape, q.dtype),
            jax.ShapeDtypeStruct(stat, jnp.float32),
            jax.ShapeDtypeStruct(window, k.dtype),
            jax.ShapeDtypeStruct(turned, jnp.float32),
            jax.ShapeDtypeStruct(sums, jnp.float32),
        ),
        in_specs=[pl.BlockSpec(memory_space=pltpu.VMEM)] + [some] * 6,
        out_specs=(some,) * 6,
        scratch_shapes=[
            pltpu.VMEM((2, rows, features), q.dtype),
            pltpu.VMEM((2, rows, features), q.dtype),
            pltpu.VMEM(q.shape, q.dtype),
            pltpu.VMEM((2, B, W), k.dtype),
            pltpu.VMEM(stat, jnp.float32),
            pltpu.VMEM(window, k.dtype),
            pltpu.VMEM(turned, jnp.float32),
            pltpu.VMEM(sums, jnp.float32),
            pltpu.VMEM((2 * B, B), jnp.float32),
            pltpu.SemaphoreType.DMA((8,)),
            pltpu.SemaphoreType.DMA((7,)),
            pltpu.SemaphoreType.DMA((21,)),
            pltpu.SemaphoreType.DMA((21,)),
        ],
        compiler_params=pltpu.CompilerParams(
            collective_id=0, has_side_effects=True, vmem_limit_bytes=VMEM
        ),
    )(docs, q, g, o, k, v, log_total)


def attend_kernel(
    heads, docs_ref, qa_hbm, qb_hbm, ga_hbm, gb_hbm, stat_hbm, window_hbm, dq_hbm, kv_hbm,
    dq_own, dq_other, part_hbm,
    q_ref, g_ref, stat_ref, window_ref, dqt, dqh, part_ref, dka, dva, dkv, bias, starts, bounds, get, put,
):
    column, z, core = place()
    loads = [
        pltpu.make_async_copy(source, target, get.at[n])
        for n, (source, target) in enumerate(
            (
                (stat_hbm, stat_ref),
                (window_hbm.at[:8], window_ref.at[:8]), (window_hbm.at[8:], window_ref.at[8:]),
                (kv_hbm, dkv), (qa_hbm, q_ref.at[0]), (ga_hbm, g_ref.at[0]),
                (dq_hbm.at[:2], dqt.at[:2]),
                (qb_hbm, q_ref.at[1]), (gb_hbm, g_ref.at[1]), (dq_hbm.at[2:], dqt.at[2:]),
            )
        )
    ]
    for load in loads:
        load.start()
    ends = doc_ends(docs_ref)
    window = (column - 1) * 16 * B

    def half_of(b):
        return jnp.where(b % 8 >= 4, 1 - core, core)

    def tile_of(side):
        return z + 4 * (core if side == 0 else 1 - core)

    for block in range(4):
        side, part = divmod(block, 2)
        first = column * 16 * B + tile_of(side) * 2 * B + part * B
        start = doc_start(ends, positions(first))
        starts[block] = start
        low = jnp.min(start).astype(jnp.int32) - window
        last = jnp.max(start).astype(jnp.int32) - window
        b = low // (2 * B)
        bounds[0, block] = jnp.where(low % (2 * B) >= half_of(b) * B + B, b + 1, b)
        b = last // (2 * B)
        bounds[1, block] = jnp.where(last % (2 * B) > half_of(b) * B, b + 1, b)
    dka[...] = jnp.zeros_like(dka)
    dva[...] = jnp.zeros_like(dva)
    for load in loads[:7]:
        load.wait()
    down = lax.rem(z + 3, 4)
    nears = (
        slot(OWN, z, 0),
        jnp.where(z > 0, slot(OWN, down, 1), slot(OWN, 3, 0)),
        jnp.where(z > 0, slot(OWN, down, 0), slot(BEFORE, 3, 1)),
    )
    for n, at in enumerate(nears):
        dka[at] = dkv[n, 0]
        dva[at] = dkv[n, 1]

    @pl.loop(0, 4)
    def _(block):
        side, part = block // 2, block % 2
        here = pl.ds(pl.multiple_of(part * B, B), B)

        @pl.when(block == 2)
        def _():
            for load in loads[7:]:
                load.wait()

        def work(blocks, mask=None):
            at = [slot(b // 8, b % 4, b % 8 // 4) for b in blocks]
            dk, dv, dq = gradients(
                jnp.concatenate([window_ref[n, 0] for n in at], axis=0),
                jnp.concatenate([window_ref[n, 1] for n in at], axis=0),
                [q_ref[side, here, h * W : (h + 1) * W] for h in range(heads)],
                [g_ref[side, here, h * W : (h + 1) * W] for h in range(heads)],
                [stat_ref[side, 0, h : h + 1, here] for h in range(heads)],
                [stat_ref[side, 1, h : h + 1, here] for h in range(heads)],
                mask,
            )
            for n in range(len(at)):
                dva[at[n]] += dv[n * B : (n + 1) * B]
                dka[at[n]] += dk[n * B : (n + 1) * B]
            dqt[block] += dq

        second = jnp.where(side == 0, core, 1 - core)
        end = 7 + z + 4 * second
        skip = jnp.where(second == 1, 8 + z, 16)

        def counted(b):
            return jnp.where(b > skip, b - 1, b)

        def real(n):
            return jnp.where(n >= skip, n + 1, n)

        end = counted(end)
        low = counted(bounds[0, block])
        cut = jnp.minimum(counted(bounds[1, block]), end)
        cut = cut + (end - cut) % 2

        @pl.loop(low, cut)
        def _(n):
            b = real(n)
            key = window + b * 2 * B + half_of(b) * B
            kpos = (key + lax.broadcasted_iota(jnp.int32, (B, B), 0)).astype(jnp.float32)
            bias[...] = jnp.where(kpos >= starts[block], 0.0, -jnp.inf)
            work([b], bias)

        @pl.loop(0, (end - jnp.maximum(low, cut)) // 2)
        def _(n):
            work([real(cut + 2 * n), real(cut + 2 * n + 1)])

        @pl.when(side == 0)
        def _():
            pltpu.make_async_copy(dqt.at[block], dq_own.at[part], put.at[block]).start()

        @pl.when(side == 1)
        def _():
            dqh[part] = dqt[block].astype(jnp.bfloat16)
            pltpu.make_async_copy(dqh.at[part], dq_other.at[part], put.at[block]).start()

    @pl.loop(0, 16)
    def _(s):
        part_ref[s, 0] = (dka[s] * (1.0 / math.sqrt(W))).astype(jnp.bfloat16)
        part_ref[s, 1] = dva[s].astype(jnp.bfloat16)
        pltpu.make_async_copy(part_ref.at[s], part_hbm.at[s], put.at[4 + s]).start()

    for part in range(2):
        pltpu.make_async_copy(dqt.at[part], dq_own.at[part], put.at[part]).wait()
        pltpu.make_async_copy(dqh.at[part], dq_other.at[part], put.at[2 + part]).wait()
    for s in range(16):
        pltpu.make_async_copy(part_ref.at[s], part_hbm.at[s], put.at[4 + s]).wait()


def attend(docs, q, q_other, g, g_other, stat, window, dq, sums):
    rows, features = q.shape
    heads = features // W
    some = pl.BlockSpec(memory_space=pl.ANY)
    both = (2, rows, features)
    turned = (2, W, heads * B)
    return pl.pallas_call(
        functools.partial(attend_kernel, heads),
        out_shape=(
            jax.ShapeDtypeStruct(turned, jnp.float32),
            jax.ShapeDtypeStruct(turned, jnp.bfloat16),
            jax.ShapeDtypeStruct(window.shape, jnp.bfloat16),
        ),
        in_specs=[pl.BlockSpec(memory_space=pltpu.VMEM)] + [some] * 8,
        out_specs=(some,) * 3,
        scratch_shapes=[
            pltpu.VMEM(both, q.dtype),
            pltpu.VMEM(both, q.dtype),
            pltpu.VMEM(stat.shape, stat.dtype),
            pltpu.VMEM(window.shape, window.dtype),
            pltpu.VMEM((4, W, heads * B), jnp.float32),
            pltpu.VMEM(turned, jnp.bfloat16),
            pltpu.VMEM(window.shape, jnp.bfloat16),
            pltpu.VMEM((16, B, W), jnp.float32),
            pltpu.VMEM((16, B, W), jnp.float32),
            pltpu.VMEM(sums.shape, jnp.float32),
            pltpu.VMEM((B, B), jnp.float32),
            pltpu.VMEM((4, 1, B), jnp.float32),
            pltpu.SMEM((2, 4), jnp.int32),
            pltpu.SemaphoreType.DMA((10,)),
            pltpu.SemaphoreType.DMA((20,)),
        ],
        compiler_params=pltpu.CompilerParams(vmem_limit_bytes=VMEM),
        cost_estimate=pl.CostEstimate(
            flops=20 * 10 * heads * B * B * W, bytes_accessed=16 << 20, transcendentals=0
        ),
    )(docs, q, q_other, g, g_other, stat, window, dq, sums)


def return_kernel(
    columns, heads, docs_ref, q_hbm, k_hbm, v_hbm, g_hbm, stat_hbm, dq_own, dq_other, part_ref,
    dq_hbm, dk_hbm, dv_hbm,
    q_ref, k_ref, v_ref, g_ref, stat, dqt, dq_sent, dq_got, dq_out, dk_ref, dv_ref, dka, dva, bias,
    part, across_got, beside_got, beside_sum, later_got, far_got, near_sum, near_got,
    final, given_half, local, put, send, recv,
):
    at = Links(columns)
    z, core, up, down, across = at.z, at.core, at.up, at.down, at.across
    sems = (send, recv)
    load = pltpu.make_async_copy(part_ref.at[:8], part.at[:8], local.at[0])
    load_own = pltpu.make_async_copy(part_ref.at[8:], part.at[8:], local.at[1])
    load_dq = pltpu.make_async_copy(dq_other, dq_sent, local.at[2])
    load.start()
    load_own.start()
    load_dq.start()
    loads = [
        pltpu.make_async_copy(source, target, local.at[3 + n])
        for n, (source, target) in enumerate(
            (
                (q_hbm, q_ref), (g_hbm, g_ref), (k_hbm, k_ref), (v_hbm, v_ref),
                (stat_hbm.at[0], stat), (dq_own, dqt),
            )
        )
    ]
    for copy in loads:
        copy.start()
    at.barrier(straight=True)
    has_next, has_last = at.has_next, at.has_last

    def given(side, zc, j):
        return part.at[slot(side, zc, j)]

    def held(side, zc, j):
        return part[slot(side, zc, j)].astype(jnp.float32)

    far_back = [
        Route(
            sems, j, at.last_across, given(BEFORE, across, j), across_got.at[j],
            has_last & (z < 2) if j == 0 else has_last,
            has_next & (z >= 2) if j == 0 else has_next,
        )
        for j in range(2)
    ]
    side_up = [
        Route(
            sems, 2 + j, at.above, given(BEFORE, up, j), beside_got.at[0, j],
            has_last & (z != 3) if j == 0 else has_last,
            has_last & (z != 0) if j == 0 else has_last,
        )
        for j in range(2)
    ]
    side_down = [
        Route(
            sems, 4 + j, at.below, given(BEFORE, down, j), beside_got.at[1, j],
            has_last & (z == 0) if j == 0 else has_last,
            has_last & (z == 3) if j == 0 else has_last,
        )
        for j in range(2)
    ]
    bulk = [
        Route(sems, 6 + n, at.sibling, dq_sent.at[n], dq_got.at[n]) for n in range(2)
    ]
    back = [
        Route(sems, 8 + j, at.last, beside_sum.at[j], later_got.at[j], has_last, has_next)
        for j in range(2)
    ]
    far_up = Route(sems, 10, at.above, given(OWN, across, 0), far_got.at[0])
    far_down = Route(
        sems, 11, at.below, given(OWN, across, 1), far_got.at[1], z >= 2, (z == 1) | (z == 2)
    )
    near_up_0 = Route(sems, 12, at.above, near_sum.at[0], near_got.at[0])
    near_up_1 = Route(sems, 13, at.above, given(OWN, up, 1), near_got.at[1], z == 3, z == 0)
    near_down_0 = Route(sems, 14, at.below, given(OWN, down, 0), near_got.at[2])
    near_down_1 = Route(sems, 15, at.below, near_sum.at[1], near_got.at[3], z != 0, z != 3)

    load.wait()
    for copy in (far_back[1], side_up[1], side_down[1], far_back[0], side_up[0], side_down[0]):
        copy.start()
    load_own.wait()
    for copy in (far_up, far_down, near_down_0, near_up_1):
        copy.start()
    load_dq.wait()
    for copy in bulk:
        copy.start()
    for copy in loads:
        copy.wait()
    ends = doc_ends(docs_ref)
    tile = at.column * 16 * B + (z + 4 * core) * 2 * B
    dka[...] = jnp.zeros_like(dka)
    dva[...] = jnp.zeros_like(dva)

    def diagonal(n):
        block, b = (n + 1) // 2, n // 2
        here = pl.ds(pl.multiple_of(block * B, B), B)
        there = pl.ds(pl.multiple_of(b * B, B), B)
        pos = positions(tile + block * B)
        bias[...] = hidden(tile + b * B, doc_start(ends, pos), pos)
        dk, dv, dq = gradients(
            k_ref[there],
            v_ref[there],
            [q_ref[here, h * W : (h + 1) * W] for h in range(heads)],
            [g_ref[here, h * W : (h + 1) * W] for h in range(heads)],
            [stat[0, h : h + 1, here] for h in range(heads)],
            [stat[1, h : h + 1, here] for h in range(heads)],
            bias,
        )
        dka[b] += dk
        dva[b] += dv
        dqt[block] += dq

    pl.loop(0, 3)(diagonal)

    @pl.when(has_last)
    def _():
        for copy in side_up + side_down:
            copy.arrived()
        for j in range(2):
            final[j] = held(BEFORE, z, j)
        final[1] += beside_got[0, 1].astype(jnp.float32) + beside_got[1, 1].astype(jnp.float32)

        @pl.when(z != 0)
        def _():
            final[0] += beside_got[0, 0].astype(jnp.float32)

        @pl.when(z == 3)
        def _():
            final[0] += beside_got[1, 0].astype(jnp.float32)

        beside_sum[...] = final[...].astype(jnp.bfloat16)
        for copy in back:
            copy.start()

    far_up.arrived()
    near_sum[0] = (held(OWN, up, 0) + far_got[0].astype(jnp.float32)).astype(jnp.bfloat16)
    near_up_0.start()

    @pl.when((z == 1) | (z == 2))
    def _():
        far_down.make(far_got.at[1]).wait_recv()
        total = held(OWN, down, 1) + far_got[1].astype(jnp.float32)
        near_sum[1] = total.astype(jnp.bfloat16)

    @pl.when(z == 3)
    def _():
        near_sum[1] = given(OWN, down, 1)[...]

    near_down_1.start()
    for copy in bulk:
        copy.arrived()
    eye = identity(B)
    for block in range(2):
        for h in range(heads):
            rows = slice(h * B, (h + 1) * B)
            total = dqt[block, :, rows] + dq_got[block, :, rows].astype(jnp.float32)
            rounded = (total * (1.0 / math.sqrt(W))).astype(jnp.bfloat16)
            turned = nt(eye, rounded).astype(jnp.bfloat16)
            dq_out[block * B : (block + 1) * B, h * W : (h + 1) * W] = turned
    out_q = pltpu.make_async_copy(dq_out, dq_hbm, put.at[0])
    out_q.start()
    near_down_0.arrived()
    near_up_0.arrived()
    final[0] = (
        held(OWN, z, 0) + near_got[0].astype(jnp.float32) + near_got[2].astype(jnp.float32)
    )
    final[1] = held(OWN, z, 1)

    @pl.when(z == 0)
    def _():
        near_up_1.make(near_got.at[1]).wait_recv()
        final[1] += near_got[1].astype(jnp.float32)

    @pl.when(z != 3)
    def _():
        near_down_1.make(near_got.at[3]).wait_recv()
        final[1] += near_got[3].astype(jnp.float32)

    @pl.when(has_next)
    def _():
        far_back[1].make(across_got.at[1]).wait_recv()
        final[1] += across_got[1].astype(jnp.float32)
        for j in range(2):
            back[j].arrived()
            final[j] += later_got[j].astype(jnp.float32)

    @pl.when(has_next & (z >= 2))
    def _():
        far_back[0].make(across_got.at[0]).wait_recv()
        final[0] += across_got[0].astype(jnp.float32)

    given_half[...] = final[1 - core].astype(jnp.bfloat16)
    give_k = Route(sems, 16, at.sibling, given_half.at[0], dk_ref.at[B:])
    give_v = Route(sems, 17, at.sibling, given_half.at[1], dv_ref.at[B:])
    give_k.start()
    give_v.start()
    scale = 1.0 / math.sqrt(W)
    dk_ref[:B] = (final[core, 0] + dka[0] * scale).astype(jnp.bfloat16)
    dv_ref[:B] = (final[core, 1] + dva[0]).astype(jnp.bfloat16)
    give_k.arrived()
    give_v.arrived()
    dk_ref[B:] = (dk_ref[B:].astype(jnp.float32) + dka[1] * scale).astype(jnp.bfloat16)
    dv_ref[B:] = (dv_ref[B:].astype(jnp.float32) + dva[1]).astype(jnp.bfloat16)
    out_k = pltpu.make_async_copy(dk_ref, dk_hbm, put.at[1])
    out_v = pltpu.make_async_copy(dv_ref, dv_hbm, put.at[2])
    out_k.start()
    out_v.start()
    for copy in (out_q, out_k, out_v):
        copy.wait()
    for copy in (
        far_back + side_up + side_down + bulk + back
        + [far_up, far_down, near_up_0, near_up_1, near_down_0, near_down_1, give_k, give_v]
    ):
        copy.sent()


def give_back(columns, docs, q, k, v, g, stat, dq_own, dq_other, part):
    rows, features = q.shape
    heads = features // W
    some = pl.BlockSpec(memory_space=pl.ANY)
    vmem = pl.BlockSpec(memory_space=pltpu.VMEM)
    block = (2, B, W)
    return pl.pallas_call(
        functools.partial(return_kernel, columns, heads),
        out_shape=(
            jax.ShapeDtypeStruct((rows, features), jnp.bfloat16),
            jax.ShapeDtypeStruct((rows, W), jnp.bfloat16),
            jax.ShapeDtypeStruct((rows, W), jnp.bfloat16),
        ),
        in_specs=[vmem] + [some] * 8,
        out_specs=(some,) * 3,
        scratch_shapes=[
            pltpu.VMEM(q.shape, q.dtype),
            pltpu.VMEM(k.shape, k.dtype),
            pltpu.VMEM(v.shape, v.dtype),
            pltpu.VMEM(g.shape, g.dtype),
            pltpu.VMEM(stat.shape[1:], stat.dtype),
            pltpu.VMEM(dq_own.shape, dq_own.dtype),
            pltpu.VMEM(dq_other.shape, dq_other.dtype),
            pltpu.VMEM(dq_other.shape, dq_other.dtype),
            pltpu.VMEM(q.shape, jnp.bfloat16),
            pltpu.VMEM((rows, W), jnp.bfloat16),
            pltpu.VMEM((rows, W), jnp.bfloat16),
            pltpu.VMEM((2, B, W), jnp.float32),
            pltpu.VMEM((2, B, W), jnp.float32),
            pltpu.VMEM((B, B), jnp.float32),
            pltpu.VMEM((16, *block), jnp.bfloat16),
            pltpu.VMEM((2, *block), jnp.bfloat16),
            pltpu.VMEM((2, 2, *block), jnp.bfloat16),
            pltpu.VMEM((2, *block), jnp.bfloat16),
            pltpu.VMEM((2, *block), jnp.bfloat16),
            pltpu.VMEM((2, *block), jnp.bfloat16),
            pltpu.VMEM((2, *block), jnp.bfloat16),
            pltpu.VMEM((4, *block), jnp.bfloat16),
            pltpu.VMEM((2, *block), jnp.float32),
            pltpu.VMEM(block, jnp.bfloat16),
            pltpu.SemaphoreType.DMA((9,)),
            pltpu.SemaphoreType.DMA((3,)),
            pltpu.SemaphoreType.DMA((18,)),
            pltpu.SemaphoreType.DMA((18,)),
        ],
        compiler_params=pltpu.CompilerParams(
            collective_id=1, has_side_effects=True, vmem_limit_bytes=VMEM
        ),
    )(docs, q, k, v, g, stat, dq_own, dq_other, part)


def publish_kernel(*refs):
    sources, targets, held, get, put = refs[:3], refs[3:6], refs[6:9], refs[9], refs[10]
    pieces = []
    for source, target, mid in zip(sources, targets, held):
        rows = min(source.shape[0], 128 * 1024 // source.shape[1])
        for at in range(0, source.shape[0], rows):
            here = slice(at, at + rows)
            n = len(pieces)
            pieces.append(
                (
                    pltpu.make_async_copy(source.at[here], mid.at[here], get.at[n]),
                    pltpu.make_async_copy(mid.at[here], target.at[here], put.at[n]),
                )
            )
    for into, _ in pieces:
        into.start()
    for into, out in pieces:
        into.wait()
        out.start()
    for _, out in pieces:
        out.wait()


def publish(*results):
    some = pl.BlockSpec(memory_space=pl.ANY)
    return pl.pallas_call(
        publish_kernel,
        out_shape=tuple(jax.ShapeDtypeStruct(x.shape, x.dtype) for x in results),
        in_specs=[some] * 3,
        out_specs=(some,) * 3,
        scratch_shapes=[pltpu.VMEM(x.shape, x.dtype) for x in results]
        + [pltpu.SemaphoreType.DMA((6,))] * 2,
        compiler_params=pltpu.CompilerParams(vmem_limit_bytes=VMEM),
    )(*results)


def solution(mesh):
    columns = mesh.shape["ctx"] // 2

    def on_device(q, k, v, o, g, log_total, doc_lengths):
        docs = doc_lengths[None, :]
        q_other, g_other, stat, window, dq, sums = gather(columns, docs, q, g, o, k, v, log_total)
        dq_own, dq_other, part = attend(docs, q, q_other, g, g_other, stat, window, dq, sums)
        dq, dk, dv = give_back(columns, docs, q, k, v, g, stat, dq_own, dq_other, part)
        return publish(dq, dk, dv)

    rows = P(("ctx", "section"), None)
    return jax.shard_map(
        on_device,
        mesh=mesh,
        in_specs=(rows, rows, rows, rows, rows, P(None, ("ctx", "section")), P()),
        out_specs=(rows, rows, rows),
        check_vma=False,
    )
```

```python
import functools
import math

import jax
import jax.numpy as jnp
from jax import lax
from jax.experimental import pallas as pl
from jax.experimental.pallas import tpu as pltpu
from jax.sharding import PartitionSpec as P

MESH = pl.DeviceIdType.MESH
W = 128
B = 256
VMEM = 58 << 20
LOG2E = math.log2(math.e)
OWN, BEFORE = 1, 0


def nn(a, b):
    return jnp.dot(a, b, preferred_element_type=jnp.float32)


def nt(a, b):
    return lax.dot_general(a, b, (((1,), (1,)), ((), ())), preferred_element_type=jnp.float32)


def place():
    ctx = lax.axis_index("ctx")
    return ctx // 2, lax.axis_index("section"), ctx % 2


def slot(side, z, j):
    return side * 8 + z * 2 + j


def doc_ends(docs_ref):
    lengths = docs_ref[...].astype(jnp.float32)
    docs = lengths.shape[1]
    upto = lax.broadcasted_iota(jnp.int32, (docs, docs), 1) <= lax.broadcasted_iota(
        jnp.int32, (docs, docs), 0
    )
    return jnp.sum(jnp.where(upto, lengths, 0.0), axis=1, keepdims=True)


def positions(first):
    return first.astype(jnp.float32) + lax.broadcasted_iota(jnp.int32, (1, B), 1).astype(
        jnp.float32
    )


def doc_start(ends, pos):
    return jnp.max(jnp.where(ends <= pos, ends, 0.0), axis=0, keepdims=True)


def hidden(key, start, pos):
    kpos = (key + lax.broadcasted_iota(jnp.int32, (B, B), 0)).astype(jnp.float32)
    return jnp.where((kpos >= start) & (kpos <= pos), 0.0, -jnp.inf)


def identity(n):
    at = [lax.broadcasted_iota(jnp.int32, (n, n), d) for d in range(2)]
    return (at[0] == at[1]).astype(jnp.bfloat16)


def gradients(k, v, qs, gs, logs, deltas, bias=None):
    ps, ds = [], []
    for q, g, log, delta in zip(qs, gs, logs, deltas):
        x = nt(k, q) * (LOG2E / math.sqrt(W)) - log
        if bias is not None:
            x = x + bias[...]
        p = jnp.exp2(x)
        d = p * (nt(v, g) - delta)
        ps.append(p.astype(jnp.bfloat16))
        ds.append(d.astype(jnp.bfloat16))
    dh = jnp.concatenate(ds, axis=1)
    dv = nn(jnp.concatenate(ps, axis=1), jnp.concatenate(gs, axis=0))
    dk = nn(dh, jnp.concatenate(qs, axis=0))
    return dk, dv, nn(k.T, dh)


class Links:
    def __init__(self, columns):
        self.column, self.z, self.core = place()
        ctx = lax.axis_index("ctx")
        self.up = lax.rem(self.z + 1, 4)
        self.down = lax.rem(self.z + 3, 4)
        self.across = lax.rem(self.z + 2, 4)
        self.sibling = (ctx + 1 - 2 * self.core, self.z)
        self.above = (ctx, self.up)
        self.below = (ctx, self.down)
        self.has_next = self.column < columns - 1
        self.has_last = self.column > 0
        self.next = (jnp.where(self.has_next, ctx + 2, ctx), self.z)
        self.last = (jnp.where(self.has_last, ctx - 2, ctx), self.z)
        self.next_across = (self.next[0], self.across)
        self.last_across = (self.last[0], self.across)

    def barrier(self, straight=False):
        barrier = pltpu.get_barrier_semaphore()

        def greet(*devices):
            for device in devices:
                pl.semaphore_signal(barrier, inc=1, device_id=device, device_id_type=MESH)

        greet(self.sibling, self.above, self.below)
        later = (self.next, self.next_across) if straight else (self.next,)
        earlier = (self.last, self.last_across) if straight else (self.last,)
        pl.when(self.has_next)(lambda: greet(*later))
        pl.when(self.has_last)(lambda: greet(*earlier))
        columns = self.has_next.astype(jnp.int32) + self.has_last.astype(jnp.int32)
        pl.semaphore_wait(barrier, 3 + len(later) * columns)


class Route:
    def __init__(self, sems, index, device, source, target, sends=True, gets=True, arrival=None):
        self.sends, self.gets = sends, gets
        landed = target if arrival is None else arrival
        send, recv = sems[0].at[index], sems[1].at[index]
        self.make = lambda end: pltpu.make_async_remote_copy(
            source, end, send, recv, device_id=device, device_id_type=MESH
        )
        self.target, self.landed = target, landed

    @staticmethod
    def only(condition, act):
        if condition is True:
            act()
        else:
            pl.when(condition)(act)

    def start(self):
        self.only(self.sends, lambda: self.make(self.target).start())

    def arrived(self):
        self.only(self.gets, lambda: self.make(self.landed).wait_recv())

    def sent(self):
        self.only(self.sends, lambda: self.make(self.target).wait_send())


def gradient_kernel(
    columns, heads, docs_ref, q_hbm, k_hbm, v_hbm, o_hbm, g_hbm, log_hbm,
    dq_hbm, dk_hbm, dv_hbm,
    q_both, g_both, o_ref, k_own, v_own, stat, window, dqt, dka, dva, dk_own, dv_own, bias,
    part, dq_sent, dq_got, dq_out, dk_ref, dv_ref,
    across_got, beside_got, beside_sum, later_got, far_got, near_sum, near_got, final, given_half,
    local, put, send, recv,
):
    at = Links(columns)
    z, core, up, down, across = at.z, at.core, at.up, at.down, at.across
    has_next, has_last = at.has_next, at.has_last
    sems = (send, recv)
    scale = 1.0 / math.sqrt(W)
    mine = window.at[slot(OWN, z, core)]
    loads = [
        pltpu.make_async_copy(source, target, local.at[n])
        for n, (source, target) in enumerate(
            (
                (k_hbm, k_own), (v_hbm, v_own), (g_hbm, g_both.at[0]), (o_hbm, o_ref),
                (log_hbm, stat.at[0, 0]), (q_hbm, q_both.at[0]),
            )
        )
    ]
    for copy in loads:
        copy.start()

    @pl.when(at.column == 0)
    def _():
        window[:8] = jnp.zeros((8, 2, B, W), window.dtype)

    at.barrier(straight=True)

    theirs = window.at[slot(OWN, z, 1 - core)]
    swap_k = Route(sems, 0, at.sibling, k_own.at[B:], mine.at[0], arrival=theirs.at[0])
    swap_v = Route(sems, 1, at.sibling, v_own.at[B:], mine.at[1], arrival=theirs.at[1])
    rows = q_hbm.shape[0]
    bulk = []
    for n in range(2):
        some = slice(n * rows // 2, (n + 1) * rows // 2)
        bulk.append(Route(sems, 2 + n, at.sibling, q_both.at[0, some], q_both.at[1, some]))
        bulk.append(Route(sems, 4 + n, at.sibling, g_both.at[0, some], g_both.at[1, some]))

    def passed(index, device, side, sent, j, got, sends=True, gets=True):
        there = window.at[slot(side, sent, j)]
        return Route(sems, index, device, there, there, sends, gets, window.at[slot(side, got, j)])

    up_0 = passed(6, at.above, OWN, z, 0, down)
    up_1 = passed(7, at.above, OWN, z, 1, down)
    down_0 = passed(8, at.below, OWN, z, 0, up)
    down_1 = passed(9, at.below, OWN, z, 1, up, z == 0, z == 3)
    far_0 = passed(10, at.below, OWN, up, 0, across)
    far_1 = passed(11, at.above, OWN, down, 1, across)

    def later(index, zc, j, when=True):
        here = window.at[slot(OWN, zc, j)]
        there = window.at[slot(BEFORE, zc, j)]
        sends = has_next if when is True else has_next & when
        gets = has_last if when is True else has_last & when
        return Route(sems, index, at.next, here, there, sends, gets)

    next_0 = later(12, z, 0)
    next_1 = later(13, z, 1)
    next_far_0 = later(14, across, 0, z < 2)
    next_far_1 = later(15, across, 1)
    before_up_0 = passed(16, at.above, BEFORE, z, 0, down, has_last & (z == 3), has_last & (z == 0))
    before_up_1 = passed(17, at.above, BEFORE, z, 1, down, has_last, has_last)
    before_down_0 = passed(18, at.below, BEFORE, z, 0, up, has_last & (z != 0), has_last & (z != 3))
    before_down_1 = passed(19, at.below, BEFORE, z, 1, up, has_last, has_last)
    stats = Route(sems, 20, at.sibling, stat.at[0], stat.at[1])

    def given(side, zc, j):
        return part.at[slot(side, zc, j)]

    far_back = [
        Route(
            sems, 21 + j, at.last_across, given(BEFORE, across, j), across_got.at[j],
            has_last & (z < 2) if j == 0 else has_last,
            has_next & (z >= 2) if j == 0 else has_next,
        )
        for j in range(2)
    ]
    side_up = [
        Route(
            sems, 23 + j, at.above, given(BEFORE, up, j), beside_got.at[0, j],
            has_last & (z != 3) if j == 0 else has_last,
            has_last & (z != 0) if j == 0 else has_last,
        )
        for j in range(2)
    ]
    side_down = [
        Route(
            sems, 25 + j, at.below, given(BEFORE, down, j), beside_got.at[1, j],
            has_last & (z == 0) if j == 0 else has_last,
            has_last & (z == 3) if j == 0 else has_last,
        )
        for j in range(2)
    ]
    turned_back = [Route(sems, 27 + n, at.sibling, dq_sent.at[n], dq_got.at[n]) for n in range(2)]
    back = [
        Route(sems, 29 + j, at.last, beside_sum.at[j], later_got.at[j], has_last, has_next)
        for j in range(2)
    ]
    far_up = Route(sems, 31, at.above, given(OWN, across, 0), far_got.at[0])
    far_down = Route(
        sems, 32, at.below, given(OWN, across, 1), far_got.at[1], z >= 2, (z == 1) | (z == 2)
    )
    near_up_0 = Route(sems, 33, at.above, near_sum.at[0], near_got.at[0])
    near_up_1 = Route(sems, 34, at.above, given(OWN, up, 1), near_got.at[1], z == 3, z == 0)
    near_down_0 = Route(sems, 35, at.below, given(OWN, down, 0), near_got.at[2])
    near_down_1 = Route(sems, 36, at.below, near_sum.at[1], near_got.at[3], z != 0, z != 3)
    give_k = Route(sems, 37, at.sibling, given_half.at[0], dk_ref.at[B:])
    give_v = Route(sems, 38, at.sibling, given_half.at[1], dv_ref.at[B:])

    loads[0].wait()
    loads[1].wait()
    swap_k.start()
    swap_v.start()
    mine[0] = k_own[:B]
    mine[1] = v_own[:B]
    dka[...] = jnp.zeros_like(dka)
    dva[...] = jnp.zeros_like(dva)
    dk_own[...] = jnp.zeros_like(dk_own)
    dv_own[...] = jnp.zeros_like(dv_own)
    dqt[...] = jnp.zeros_like(dqt)
    swap_k.arrived()
    swap_v.arrived()
    for copy in (up_1, down_0, next_1, up_0, down_1, next_0):
        copy.start()

    for copy in loads[2:]:
        copy.wait()
    ones = jnp.ones((8, W), jnp.bfloat16)
    for h in range(heads):
        cols = slice(h * W, (h + 1) * W)
        product = g_both[0, :, cols].astype(jnp.float32) * o_ref[:, cols].astype(jnp.float32)
        high = product.astype(jnp.bfloat16)
        low = (product - high.astype(jnp.float32)).astype(jnp.bfloat16)
        total = nt(ones, high) + nt(ones, low)
        stat[0, 1, h : h + 1, :] = total[0:1]
    stat[0, 0] = stat[0, 0] * LOG2E
    stats.start()

    ends = doc_ends(docs_ref)
    column = at.column * 16 * B

    def products(side, block, k, v, mask):
        here = pl.ds(pl.multiple_of(block * B, B), B)
        return gradients(
            k, v,
            [q_both[side, here, h * W : (h + 1) * W] for h in range(heads)],
            [g_both[side, here, h * W : (h + 1) * W] for h in range(heads)],
            [stat[side, 0, h : h + 1, here] for h in range(heads)],
            [stat[side, 1, h : h + 1, here] for h in range(heads)],
            mask,
        )

    def diagonal(n):
        block, b = (n + 1) // 2, n // 2
        there = pl.ds(pl.multiple_of(b * B, B), B)
        tile = column + (z + 4 * core) * 2 * B
        pos = positions(tile + block * B)
        bias[:B] = hidden(tile + b * B, doc_start(ends, pos), pos)
        dk, dv, dq = products(0, block, k_own[there], v_own[there], bias.at[:B])
        dk_own[b] += dk
        dv_own[b] += dv
        dqt[block] += dq

    @pl.loop(0, 3)
    def _(n):
        @pl.when(n == 2)
        def _():
            up_1.arrived()
            far_1.start()
            down_0.arrived()
            far_0.start()

        diagonal(n)

    next_1.arrived()
    before_down_1.start()
    before_up_1.start()
    next_0.arrived()
    before_down_0.start()
    before_up_0.start()
    for copy in bulk:
        copy.start()

    def rounded(zc):
        for side in range(2):
            for j in range(2):
                n = slot(side, zc, j)
                part[n, 0] = (dka[n] * scale).astype(jnp.bfloat16)
                part[n, 1] = dva[n].astype(jnp.bfloat16)

    def before_step(step):
        def when(n):
            return pl.when(step == n)

        @when(1)
        def _():
            far_0.arrived()
            next_far_0.start()
            far_1.arrived()
            next_far_1.start()

        @when(2)
        def _():
            for copy in (down_1, before_down_0, before_down_1):
                copy.arrived()

        @when(4)
        def _():
            for copy in (up_0, before_up_0, before_up_1):
                copy.arrived()

        @when(6)
        def _():
            next_far_0.arrived()
            next_far_1.arrived()

        @when(8)
        def _():
            for copy in bulk:
                copy.arrived()
            stats.arrived()

        @when(12)
        def _():
            dq_sent[0] = dqt[2].astype(jnp.bfloat16)
            turned_back[0].start()

        @when(13)
        def _():
            rounded(down)
            for copy in (side_down[1], side_down[0], near_down_0):
                copy.start()

        @when(14)
        def _():
            rounded(up)
            for copy in (side_up[1], side_up[0], near_up_1):
                copy.start()

        @when(15)
        def _():
            rounded(across)
            for copy in (far_up, far_down, far_back[1], far_back[0]):
                copy.start()

    chips = (0, 0, 1, 1, 3, 3, 2, 2, 2, 1, 3, 0, 3, 1, 2, 0)

    @pl.loop(0, 16)
    def _(step):
        before_step(step)
        chip = 0
        for n, c in enumerate(chips):
            if c:
                chip = chip + jnp.where(step == n, c, 0)
        side = step // 8
        block = jnp.where(side == 0, step % 2, step // 4 - 2)
        tile = z + 4 * jnp.where(side == 0, core, 1 - core)
        start = doc_start(ends, positions(column + tile * 2 * B + block * B))
        found = []
        for n in range(2):
            b = tile + chip + 4 * n
            half = jnp.where(b % 8 >= 4, 1 - core, core)
            key = column + (b - 8) * 2 * B + half * B
            kpos = (key + lax.broadcasted_iota(jnp.int32, (B, B), 0)).astype(jnp.float32)
            bias[n * B : (n + 1) * B] = jnp.where(kpos >= start, 0.0, -jnp.inf)
            found.append(slot(b // 8, b % 4, b % 8 // 4))
        dk, dv, dq = products(
            side, block,
            jnp.concatenate([window[n, 0] for n in found], axis=0),
            jnp.concatenate([window[n, 1] for n in found], axis=0),
            bias,
        )
        for n, where in enumerate(found):
            dka[where] += dk[n * B : (n + 1) * B]
            dva[where] += dv[n * B : (n + 1) * B]
        dqt[side * 2 + block] += dq

    dq_sent[1] = dqt[3].astype(jnp.bfloat16)
    turned_back[1].start()

    def total(side, zc, j):
        n = slot(side, zc, j)
        return jnp.stack([dka[n] * scale, dva[n]])

    @pl.when(has_last)
    def _():
        for copy in side_up + side_down:
            copy.arrived()
        for j in range(2):
            final[j] = total(BEFORE, z, j)
        final[1] += beside_got[0, 1].astype(jnp.float32) + beside_got[1, 1].astype(jnp.float32)

        @pl.when(z != 0)
        def _():
            final[0] += beside_got[0, 0].astype(jnp.float32)

        @pl.when(z == 3)
        def _():
            final[0] += beside_got[1, 0].astype(jnp.float32)

        beside_sum[...] = final[...].astype(jnp.bfloat16)
        for copy in back:
            copy.start()

    far_up.arrived()
    near_sum[0] = (total(OWN, up, 0) + far_got[0].astype(jnp.float32)).astype(jnp.bfloat16)
    near_up_0.start()

    @pl.when((z == 1) | (z == 2))
    def _():
        far_down.make(far_got.at[1]).wait_recv()
        both = total(OWN, down, 1) + far_got[1].astype(jnp.float32)
        near_sum[1] = both.astype(jnp.bfloat16)

    @pl.when(z == 3)
    def _():
        near_sum[1] = given(OWN, down, 1)[...]

    near_down_1.start()
    for copy in turned_back:
        copy.arrived()
    eye = identity(B)
    for block in range(2):
        for h in range(heads):
            there = slice(h * B, (h + 1) * B)
            whole = dqt[block, :, there] + dq_got[block, :, there].astype(jnp.float32)
            turned = nt(eye, (whole * scale).astype(jnp.bfloat16)).astype(jnp.bfloat16)
            dq_out[block * B : (block + 1) * B, h * W : (h + 1) * W] = turned
    out_q = pltpu.make_async_copy(dq_out, dq_hbm, put.at[0])
    out_q.start()
    near_down_0.arrived()
    near_up_0.arrived()
    final[0] = (
        total(OWN, z, 0) + near_got[0].astype(jnp.float32) + near_got[2].astype(jnp.float32)
    )
    final[1] = total(OWN, z, 1)

    @pl.when(z == 0)
    def _():
        near_up_1.make(near_got.at[1]).wait_recv()
        final[1] += near_got[1].astype(jnp.float32)

    @pl.when(z != 3)
    def _():
        near_down_1.make(near_got.at[3]).wait_recv()
        final[1] += near_got[3].astype(jnp.float32)

    @pl.when(has_next)
    def _():
        far_back[1].make(across_got.at[1]).wait_recv()
        final[1] += across_got[1].astype(jnp.float32)
        for j in range(2):
            back[j].make(later_got.at[j]).wait_recv()
            final[j] += later_got[j].astype(jnp.float32)

    @pl.when(has_next & (z >= 2))
    def _():
        far_back[0].make(across_got.at[0]).wait_recv()
        final[0] += across_got[0].astype(jnp.float32)

    given_half[...] = final[1 - core].astype(jnp.bfloat16)
    give_k.start()
    give_v.start()
    dk_ref[:B] = (final[core, 0] + dk_own[0] * scale).astype(jnp.bfloat16)
    dv_ref[:B] = (final[core, 1] + dv_own[0]).astype(jnp.bfloat16)
    give_k.arrived()
    give_v.arrived()
    dk_ref[B:] = (dk_ref[B:].astype(jnp.float32) + dk_own[1] * scale).astype(jnp.bfloat16)
    dv_ref[B:] = (dv_ref[B:].astype(jnp.float32) + dv_own[1]).astype(jnp.bfloat16)
    out_k = pltpu.make_async_copy(dk_ref, dk_hbm, put.at[1])
    out_v = pltpu.make_async_copy(dv_ref, dv_hbm, put.at[2])
    out_k.start()
    out_v.start()
    for copy in (out_q, out_k, out_v):
        copy.wait()
    for copy in (
        [swap_k, swap_v, up_0, up_1, down_0, down_1, far_0, far_1, next_0, next_1, next_far_0]
        + [next_far_1, before_up_0, before_up_1, before_down_0, before_down_1, stats]
        + bulk + far_back + side_up + side_down + turned_back + back
        + [far_up, far_down, near_up_0, near_up_1, near_down_0, near_down_1, give_k, give_v]
    ):
        copy.sent()


def all_gradients(columns, docs, q, k, v, o, g, log_total):
    rows, features = q.shape
    heads = features // W
    some = pl.BlockSpec(memory_space=pl.ANY)
    both = pltpu.VMEM((2, rows, features), q.dtype)
    slots = pltpu.VMEM((16, 2, B, W), k.dtype)
    sums = pltpu.VMEM((16, B, W), jnp.float32)
    halves = pltpu.VMEM((2, B, W), jnp.float32)
    turned = (W, heads * B)
    pair = pltpu.VMEM((2, 2, B, W), jnp.bfloat16)
    quad = pltpu.VMEM((2, 2, 2, B, W), jnp.bfloat16)
    return pl.pallas_call(
        functools.partial(gradient_kernel, columns, heads),
        out_shape=(
            jax.ShapeDtypeStruct((rows, features), jnp.bfloat16),
            jax.ShapeDtypeStruct((rows, W), jnp.bfloat16),
            jax.ShapeDtypeStruct((rows, W), jnp.bfloat16),
        ),
        in_specs=[pl.BlockSpec(memory_space=pltpu.VMEM)] + [some] * 6,
        out_specs=(some,) * 3,
        scratch_shapes=[
            both, both,
            pltpu.VMEM((rows, features), q.dtype),
            pltpu.VMEM((rows, W), k.dtype),
            pltpu.VMEM((rows, W), k.dtype),
            pltpu.VMEM((2, 2, heads, rows), jnp.float32),
            slots,
            pltpu.VMEM((4, *turned), jnp.float32),
            sums, sums, halves, halves,
            pltpu.VMEM((2 * B, B), jnp.float32),
            slots,
            pltpu.VMEM((2, *turned), jnp.bfloat16),
            pltpu.VMEM((2, *turned), jnp.bfloat16),
            pltpu.VMEM((rows, features), jnp.bfloat16),
            pltpu.VMEM((rows, W), jnp.bfloat16),
            pltpu.VMEM((rows, W), jnp.bfloat16),
            pair, quad, pair, pair, pair, pair,
            pltpu.VMEM((4, 2, B, W), jnp.bfloat16),
            pltpu.VMEM((2, 2, B, W), jnp.float32),
            pltpu.VMEM((2, B, W), jnp.bfloat16),
            pltpu.SemaphoreType.DMA((6,)),
            pltpu.SemaphoreType.DMA((3,)),
            pltpu.SemaphoreType.DMA((39,)),
            pltpu.SemaphoreType.DMA((39,)),
        ],
        compiler_params=pltpu.CompilerParams(
            collective_id=0, has_side_effects=True, vmem_limit_bytes=VMEM
        ),
        cost_estimate=pl.CostEstimate(
            flops=35 * 10 * heads * B * B * W, bytes_accessed=16 << 20, transcendentals=0
        ),
    )(docs, q, k, v, o, g, log_total)


def publish_kernel(*refs):
    sources, targets, held, get, put = refs[:3], refs[3:6], refs[6:9], refs[9], refs[10]
    pieces = []
    for source, target, mid in zip(sources, targets, held):
        rows = min(source.shape[0], 128 * 1024 // source.shape[1])
        for at in range(0, source.shape[0], rows):
            here = slice(at, at + rows)
            n = len(pieces)
            pieces.append(
                (
                    pltpu.make_async_copy(source.at[here], mid.at[here], get.at[n]),
                    pltpu.make_async_copy(mid.at[here], target.at[here], put.at[n]),
                )
            )
    for into, _ in pieces:
        into.start()
    for into, out in pieces:
        into.wait()
        out.start()
    for _, out in pieces:
        out.wait()


def publish(*results):
    some = pl.BlockSpec(memory_space=pl.ANY)
    return pl.pallas_call(
        publish_kernel,
        out_shape=tuple(jax.ShapeDtypeStruct(x.shape, x.dtype) for x in results),
        in_specs=[some] * 3,
        out_specs=(some,) * 3,
        scratch_shapes=[pltpu.VMEM(x.shape, x.dtype) for x in results]
        + [pltpu.SemaphoreType.DMA((6,))] * 2,
        compiler_params=pltpu.CompilerParams(vmem_limit_bytes=VMEM),
    )(*results)


def solution(mesh):
    columns = mesh.shape["ctx"] // 2

    def on_device(q, k, v, o, g, log_total, doc_lengths):
        docs = doc_lengths[None, :]
        return publish(*all_gradients(columns, docs, q, k, v, o, g, log_total))

    rows = P(("ctx", "section"), None)
    return jax.shard_map(
        on_device,
        mesh=mesh,
        in_specs=(rows, rows, rows, rows, rows, P(None, ("ctx", "section")), P()),
        out_specs=(rows, rows, rows),
        check_vma=False,
    )
```

```python
import functools
import math

import jax
import jax.numpy as jnp
from jax import lax
from jax.experimental import pallas as pl
from jax.experimental.pallas import tpu as pltpu
from jax.sharding import PartitionSpec as P

MESH = pl.DeviceIdType.MESH
W = 128
STRIP = 32
B = 256
VMEM = 58 << 20
LOG2E = math.log2(math.e)
OWN, BEFORE = 1, 0


def nn(a, b):
    return jnp.dot(a, b, preferred_element_type=jnp.float32)


def nt(a, b):
    return lax.dot_general(a, b, (((1,), (1,)), ((), ())), preferred_element_type=jnp.float32)


def place():
    ctx = lax.axis_index("ctx")
    return ctx // 2, lax.axis_index("section"), ctx % 2


def slot(side, z, j):
    return side * 8 + z * 2 + j


def doc_ends(docs_ref):
    lengths = docs_ref[...].astype(jnp.float32)
    docs = lengths.shape[1]
    upto = lax.broadcasted_iota(jnp.int32, (docs, docs), 1) <= lax.broadcasted_iota(
        jnp.int32, (docs, docs), 0
    )
    return jnp.sum(jnp.where(upto, lengths, 0.0), axis=1, keepdims=True)


def positions(first):
    return first.astype(jnp.float32) + lax.broadcasted_iota(jnp.int32, (1, B), 1).astype(
        jnp.float32
    )


def doc_start(ends, pos):
    return jnp.max(jnp.where(ends <= pos, ends, 0.0), axis=0, keepdims=True)


def hidden(key, start, pos):
    kpos = (key + lax.broadcasted_iota(jnp.int32, (B, B), 0)).astype(jnp.float32)
    return jnp.where((kpos >= start) & (kpos <= pos), 0.0, -jnp.inf)


def identity(n):
    at = [lax.broadcasted_iota(jnp.int32, (n, n), d) for d in range(2)]
    return (at[0] == at[1]).astype(jnp.bfloat16)


def gradients(k, v, qs, gs, logs, deltas, bias=None):
    ps, ds = [], []
    for q, g, log, delta in zip(qs, gs, logs, deltas):
        score, prob_grad = nt(k, q), nt(v, g)
        p_strips, d_strips = [], []
        for at in range(0, k.shape[0], STRIP):
            here = slice(at, at + STRIP)
            x = score[here] * (LOG2E / math.sqrt(W)) - log
            if bias is not None:
                x = x + bias[here]
            p = jnp.exp2(x)
            p_strips.append(p.astype(jnp.bfloat16))
            d_strips.append((p * (prob_grad[here] - delta)).astype(jnp.bfloat16))
        ps.append(jnp.concatenate(p_strips, axis=0))
        ds.append(jnp.concatenate(d_strips, axis=0))
    dh = jnp.concatenate(ds, axis=1)
    dv = nn(jnp.concatenate(ps, axis=1), jnp.concatenate(gs, axis=0))
    dk = nn(dh, jnp.concatenate(qs, axis=0))
    return dk, dv, nn(k.T, dh)


class Links:
    def __init__(self, columns):
        self.column, self.z, self.core = place()
        ctx = lax.axis_index("ctx")
        self.up = lax.rem(self.z + 1, 4)
        self.down = lax.rem(self.z + 3, 4)
        self.across = lax.rem(self.z + 2, 4)
        self.sibling = (ctx + 1 - 2 * self.core, self.z)
        self.above = (ctx, self.up)
        self.below = (ctx, self.down)
        self.has_next = self.column < columns - 1
        self.has_last = self.column > 0
        self.next = (jnp.where(self.has_next, ctx + 2, ctx), self.z)
        self.last = (jnp.where(self.has_last, ctx - 2, ctx), self.z)
        self.next_across = (self.next[0], self.across)
        self.last_across = (self.last[0], self.across)

    def barrier(self, straight=False):
        barrier = pltpu.get_barrier_semaphore()

        def greet(*devices):
            for device in devices:
                pl.semaphore_signal(barrier, inc=1, device_id=device, device_id_type=MESH)

        greet(self.sibling, self.above, self.below)
        later = (self.next, self.next_across) if straight else (self.next,)
        earlier = (self.last, self.last_across) if straight else (self.last,)
        pl.when(self.has_next)(lambda: greet(*later))
        pl.when(self.has_last)(lambda: greet(*earlier))
        columns = self.has_next.astype(jnp.int32) + self.has_last.astype(jnp.int32)
        pl.semaphore_wait(barrier, 3 + len(later) * columns)


class Route:
    def __init__(self, sems, index, device, source, target, sends=True, gets=True, arrival=None):
        self.sends, self.gets = sends, gets
        landed = target if arrival is None else arrival
        send, recv = sems[0].at[index], sems[1].at[index]
        self.make = lambda end: pltpu.make_async_remote_copy(
            source, end, send, recv, device_id=device, device_id_type=MESH
        )
        self.target, self.landed = target, landed

    @staticmethod
    def only(condition, act):
        if condition is True:
            act()
        else:
            pl.when(condition)(act)

    def start(self):
        self.only(self.sends, lambda: self.make(self.target).start())

    def arrived(self):
        self.only(self.gets, lambda: self.make(self.landed).wait_recv())

    def sent(self):
        self.only(self.sends, lambda: self.make(self.target).wait_send())


def gradient_kernel(
    columns, heads, docs_ref, q_hbm, k_hbm, v_hbm, o_hbm, g_hbm, log_hbm,
    dq_hbm, dk_hbm, dv_hbm,
    q_both, g_both, o_ref, k_own, v_own, stat, window, dqt, dka, dva, dk_own, dv_own, bias,
    part, dq_sent, dq_got, dq_out, dk_ref, dv_ref,
    across_got, beside_got, beside_sum, later_got, far_got, near_sum, near_got, final, given_half,
    local, put, send, recv,
):
    at = Links(columns)
    z, core, up, down, across = at.z, at.core, at.up, at.down, at.across
    has_next, has_last = at.has_next, at.has_last
    sems = (send, recv)
    scale = 1.0 / math.sqrt(W)
    mine = window.at[slot(OWN, z, core)]
    loads = [
        pltpu.make_async_copy(source, target, local.at[n])
        for n, (source, target) in enumerate(
            (
                (k_hbm, k_own), (v_hbm, v_own), (g_hbm, g_both.at[0]), (o_hbm, o_ref),
                (log_hbm, stat.at[0, 0]), (q_hbm, q_both.at[0]),
            )
        )
    ]
    for copy in loads:
        copy.start()

    @pl.when(at.column == 0)
    def _():
        window[:8] = jnp.zeros((8, 2, B, W), window.dtype)

    at.barrier(straight=True)

    theirs = window.at[slot(OWN, z, 1 - core)]
    swap_k = Route(sems, 0, at.sibling, k_own.at[B:], mine.at[0], arrival=theirs.at[0])
    swap_v = Route(sems, 1, at.sibling, v_own.at[B:], mine.at[1], arrival=theirs.at[1])
    rows = q_hbm.shape[0]
    bulk = []
    for n in range(2):
        some = slice(n * rows // 2, (n + 1) * rows // 2)
        bulk.append(Route(sems, 2 + n, at.sibling, q_both.at[0, some], q_both.at[1, some]))
        bulk.append(Route(sems, 4 + n, at.sibling, g_both.at[0, some], g_both.at[1, some]))

    def passed(index, device, side, sent, j, got, sends=True, gets=True):
        there = window.at[slot(side, sent, j)]
        return Route(sems, index, device, there, there, sends, gets, window.at[slot(side, got, j)])

    up_0 = passed(6, at.above, OWN, z, 0, down)
    up_1 = passed(7, at.above, OWN, z, 1, down)
    down_0 = passed(8, at.below, OWN, z, 0, up)
    down_1 = passed(9, at.below, OWN, z, 1, up, z == 0, z == 3)
    far_0 = passed(10, at.below, OWN, up, 0, across)
    far_1 = passed(11, at.above, OWN, down, 1, across)

    def later(index, zc, j, when=True):
        here = window.at[slot(OWN, zc, j)]
        there = window.at[slot(BEFORE, zc, j)]
        sends = has_next if when is True else has_next & when
        gets = has_last if when is True else has_last & when
        return Route(sems, index, at.next, here, there, sends, gets)

    next_0 = later(12, z, 0)
    next_1 = later(13, z, 1)
    next_far_0 = later(14, across, 0, z < 2)
    next_far_1 = later(15, across, 1)
    before_up_0 = passed(16, at.above, BEFORE, z, 0, down, has_last & (z == 3), has_last & (z == 0))
    before_up_1 = passed(17, at.above, BEFORE, z, 1, down, has_last, has_last)
    before_down_0 = passed(18, at.below, BEFORE, z, 0, up, has_last & (z != 0), has_last & (z != 3))
    before_down_1 = passed(19, at.below, BEFORE, z, 1, up, has_last, has_last)
    stats = Route(sems, 20, at.sibling, stat.at[0], stat.at[1])

    def given(side, zc, j):
        return part.at[slot(side, zc, j)]

    far_back = [
        Route(
            sems, 21 + j, at.last_across, given(BEFORE, across, j), across_got.at[j],
            has_last & (z < 2) if j == 0 else has_last,
            has_next & (z >= 2) if j == 0 else has_next,
        )
        for j in range(2)
    ]
    side_up = [
        Route(
            sems, 23 + j, at.above, given(BEFORE, up, j), beside_got.at[0, j],
            has_last & (z != 3) if j == 0 else has_last,
            has_last & (z != 0) if j == 0 else has_last,
        )
        for j in range(2)
    ]
    side_down = [
        Route(
            sems, 25 + j, at.below, given(BEFORE, down, j), beside_got.at[1, j],
            has_last & (z == 0) if j == 0 else has_last,
            has_last & (z == 3) if j == 0 else has_last,
        )
        for j in range(2)
    ]
    turned_back = [Route(sems, 27 + n, at.sibling, dq_sent.at[n], dq_got.at[n]) for n in range(2)]
    back = [
        Route(sems, 29 + j, at.last, beside_sum.at[j], later_got.at[j], has_last, has_next)
        for j in range(2)
    ]
    far_up = Route(sems, 31, at.above, given(OWN, across, 0), far_got.at[0])
    far_down = Route(
        sems, 32, at.below, given(OWN, across, 1), far_got.at[1], z >= 2, (z == 1) | (z == 2)
    )
    near_up_0 = Route(sems, 33, at.above, near_sum.at[0], near_got.at[0])
    near_up_1 = Route(sems, 34, at.above, given(OWN, up, 1), near_got.at[1], z == 3, z == 0)
    near_down_0 = Route(sems, 35, at.below, given(OWN, down, 0), near_got.at[2])
    near_down_1 = Route(sems, 36, at.below, near_sum.at[1], near_got.at[3], z != 0, z != 3)
    give_k = Route(sems, 37, at.sibling, given_half.at[0], dk_ref.at[B:])
    give_v = Route(sems, 38, at.sibling, given_half.at[1], dv_ref.at[B:])

    loads[0].wait()
    loads[1].wait()
    swap_k.start()
    swap_v.start()
    mine[0] = k_own[:B]
    mine[1] = v_own[:B]
    dka[...] = jnp.zeros_like(dka)
    dva[...] = jnp.zeros_like(dva)
    dk_own[...] = jnp.zeros_like(dk_own)
    dv_own[...] = jnp.zeros_like(dv_own)
    dqt[...] = jnp.zeros_like(dqt)
    swap_k.arrived()
    swap_v.arrived()
    for copy in (up_1, down_0, next_1, up_0, down_1, next_0):
        copy.start()

    for copy in loads[2:]:
        copy.wait()
    ones = jnp.ones((8, W), jnp.bfloat16)
    for h in range(heads):
        cols = slice(h * W, (h + 1) * W)
        product = g_both[0, :, cols].astype(jnp.float32) * o_ref[:, cols].astype(jnp.float32)
        high = product.astype(jnp.bfloat16)
        low = (product - high.astype(jnp.float32)).astype(jnp.bfloat16)
        total = nt(ones, high) + nt(ones, low)
        stat[0, 1, h : h + 1, :] = total[0:1]
    stat[0, 0] = stat[0, 0] * LOG2E
    stats.start()

    ends = doc_ends(docs_ref)
    column = at.column * 16 * B

    def products(side, block, k, v, mask):
        here = pl.ds(pl.multiple_of(block * B, B), B)
        return gradients(
            k, v,
            [q_both[side, here, h * W : (h + 1) * W] for h in range(heads)],
            [g_both[side, here, h * W : (h + 1) * W] for h in range(heads)],
            [stat[side, 0, h : h + 1, here] for h in range(heads)],
            [stat[side, 1, h : h + 1, here] for h in range(heads)],
            mask,
        )

    def diagonal(n):
        block, b = (n + 1) // 2, n // 2
        there = pl.ds(pl.multiple_of(b * B, B), B)
        tile = column + (z + 4 * core) * 2 * B
        pos = positions(tile + block * B)
        bias[:B] = hidden(tile + b * B, doc_start(ends, pos), pos)
        dk, dv, dq = products(0, block, k_own[there], v_own[there], bias.at[:B])
        dk_own[b] += dk
        dv_own[b] += dv
        dqt[block] += dq

    @pl.loop(0, 3)
    def _(n):
        @pl.when(n == 2)
        def _():
            up_1.arrived()
            far_1.start()
            down_0.arrived()
            far_0.start()

        diagonal(n)

    next_1.arrived()
    before_down_1.start()
    before_up_1.start()
    next_0.arrived()
    before_down_0.start()
    before_up_0.start()
    for copy in bulk:
        copy.start()

    def rounded(zc):
        for side in range(2):
            for j in range(2):
                n = slot(side, zc, j)
                part[n, 0] = (dka[n] * scale).astype(jnp.bfloat16)
                part[n, 1] = dva[n].astype(jnp.bfloat16)

    def before_step(step):
        def when(n):
            return pl.when(step == n)

        @when(1)
        def _():
            far_0.arrived()
            next_far_0.start()
            far_1.arrived()
            next_far_1.start()

        @when(2)
        def _():
            for copy in (down_1, before_down_0, before_down_1):
                copy.arrived()

        @when(4)
        def _():
            for copy in (up_0, before_up_0, before_up_1):
                copy.arrived()

        @when(6)
        def _():
            next_far_0.arrived()
            next_far_1.arrived()

        @when(8)
        def _():
            for copy in bulk:
                copy.arrived()
            stats.arrived()

        @when(12)
        def _():
            dq_sent[0] = dqt[2].astype(jnp.bfloat16)
            turned_back[0].start()

        @when(13)
        def _():
            rounded(down)
            for copy in (side_down[1], side_down[0], near_down_0):
                copy.start()

        @when(14)
        def _():
            rounded(up)
            for copy in (side_up[1], side_up[0], near_up_1):
                copy.start()

        @when(15)
        def _():
            rounded(across)
            for copy in (far_up, far_down, far_back[1], far_back[0]):
                copy.start()

    chips = (0, 0, 1, 1, 3, 3, 2, 2, 2, 1, 3, 0, 3, 1, 2, 0)

    @pl.loop(0, 16)
    def _(step):
        before_step(step)
        chip = 0
        for n, c in enumerate(chips):
            if c:
                chip = chip + jnp.where(step == n, c, 0)
        side = step // 8
        block = jnp.where(side == 0, step % 2, step // 4 - 2)
        tile = z + 4 * jnp.where(side == 0, core, 1 - core)
        start = doc_start(ends, positions(column + tile * 2 * B + block * B))
        found = []
        for n in range(2):
            b = tile + chip + 4 * n
            half = jnp.where(b % 8 >= 4, 1 - core, core)
            key = column + (b - 8) * 2 * B + half * B
            kpos = (key + lax.broadcasted_iota(jnp.int32, (B, B), 0)).astype(jnp.float32)
            bias[n * B : (n + 1) * B] = jnp.where(kpos >= start, 0.0, -jnp.inf)
            found.append(slot(b // 8, b % 4, b % 8 // 4))
        dk, dv, dq = products(
            side, block,
            jnp.concatenate([window[n, 0] for n in found], axis=0),
            jnp.concatenate([window[n, 1] for n in found], axis=0),
            bias,
        )
        for n, where in enumerate(found):
            dka[where] += dk[n * B : (n + 1) * B]
            dva[where] += dv[n * B : (n + 1) * B]
        dqt[side * 2 + block] += dq

    dq_sent[1] = dqt[3].astype(jnp.bfloat16)
    turned_back[1].start()

    def total(side, zc, j):
        n = slot(side, zc, j)
        return jnp.stack([dka[n] * scale, dva[n]])

    @pl.when(has_last)
    def _():
        for copy in side_up + side_down:
            copy.arrived()
        for j in range(2):
            final[j] = total(BEFORE, z, j)
        final[1] += beside_got[0, 1].astype(jnp.float32) + beside_got[1, 1].astype(jnp.float32)

        @pl.when(z != 0)
        def _():
            final[0] += beside_got[0, 0].astype(jnp.float32)

        @pl.when(z == 3)
        def _():
            final[0] += beside_got[1, 0].astype(jnp.float32)

        beside_sum[...] = final[...].astype(jnp.bfloat16)
        for copy in back:
            copy.start()

    far_up.arrived()
    near_sum[0] = (total(OWN, up, 0) + far_got[0].astype(jnp.float32)).astype(jnp.bfloat16)
    near_up_0.start()

    @pl.when((z == 1) | (z == 2))
    def _():
        far_down.make(far_got.at[1]).wait_recv()
        both = total(OWN, down, 1) + far_got[1].astype(jnp.float32)
        near_sum[1] = both.astype(jnp.bfloat16)

    @pl.when(z == 3)
    def _():
        near_sum[1] = given(OWN, down, 1)[...]

    near_down_1.start()
    for copy in turned_back:
        copy.arrived()
    eye = identity(B)
    for block in range(2):
        for h in range(heads):
            there = slice(h * B, (h + 1) * B)
            whole = dqt[block, :, there] + dq_got[block, :, there].astype(jnp.float32)
            turned = nt(eye, (whole * scale).astype(jnp.bfloat16)).astype(jnp.bfloat16)
            dq_out[block * B : (block + 1) * B, h * W : (h + 1) * W] = turned
    out_q = pltpu.make_async_copy(dq_out, dq_hbm, put.at[0])
    out_q.start()
    near_down_0.arrived()
    near_up_0.arrived()
    final[0] = (
        total(OWN, z, 0) + near_got[0].astype(jnp.float32) + near_got[2].astype(jnp.float32)
    )
    final[1] = total(OWN, z, 1)

    @pl.when(z == 0)
    def _():
        near_up_1.make(near_got.at[1]).wait_recv()
        final[1] += near_got[1].astype(jnp.float32)

    @pl.when(z != 3)
    def _():
        near_down_1.make(near_got.at[3]).wait_recv()
        final[1] += near_got[3].astype(jnp.float32)

    @pl.when(has_next)
    def _():
        far_back[1].make(across_got.at[1]).wait_recv()
        final[1] += across_got[1].astype(jnp.float32)
        for j in range(2):
            back[j].make(later_got.at[j]).wait_recv()
            final[j] += later_got[j].astype(jnp.float32)

    @pl.when(has_next & (z >= 2))
    def _():
        far_back[0].make(across_got.at[0]).wait_recv()
        final[0] += across_got[0].astype(jnp.float32)

    given_half[...] = final[1 - core].astype(jnp.bfloat16)
    give_k.start()
    give_v.start()
    dk_ref[:B] = (final[core, 0] + dk_own[0] * scale).astype(jnp.bfloat16)
    dv_ref[:B] = (final[core, 1] + dv_own[0]).astype(jnp.bfloat16)
    give_k.arrived()
    give_v.arrived()
    dk_ref[B:] = (dk_ref[B:].astype(jnp.float32) + dk_own[1] * scale).astype(jnp.bfloat16)
    dv_ref[B:] = (dv_ref[B:].astype(jnp.float32) + dv_own[1]).astype(jnp.bfloat16)
    out_k = pltpu.make_async_copy(dk_ref, dk_hbm, put.at[1])
    out_v = pltpu.make_async_copy(dv_ref, dv_hbm, put.at[2])
    out_k.start()
    out_v.start()
    for copy in (out_q, out_k, out_v):
        copy.wait()
    for copy in (
        [swap_k, swap_v, up_0, up_1, down_0, down_1, far_0, far_1, next_0, next_1, next_far_0]
        + [next_far_1, before_up_0, before_up_1, before_down_0, before_down_1, stats]
        + bulk + far_back + side_up + side_down + turned_back + back
        + [far_up, far_down, near_up_0, near_up_1, near_down_0, near_down_1, give_k, give_v]
    ):
        copy.sent()


def all_gradients(columns, docs, q, k, v, o, g, log_total):
    rows, features = q.shape
    heads = features // W
    some = pl.BlockSpec(memory_space=pl.ANY)
    both = pltpu.VMEM((2, rows, features), q.dtype)
    slots = pltpu.VMEM((16, 2, B, W), k.dtype)
    sums = pltpu.VMEM((16, B, W), jnp.float32)
    halves = pltpu.VMEM((2, B, W), jnp.float32)
    turned = (W, heads * B)
    pair = pltpu.VMEM((2, 2, B, W), jnp.bfloat16)
    quad = pltpu.VMEM((2, 2, 2, B, W), jnp.bfloat16)
    return pl.pallas_call(
        functools.partial(gradient_kernel, columns, heads),
        out_shape=(
            jax.ShapeDtypeStruct((rows, features), jnp.bfloat16),
            jax.ShapeDtypeStruct((rows, W), jnp.bfloat16),
            jax.ShapeDtypeStruct((rows, W), jnp.bfloat16),
        ),
        in_specs=[pl.BlockSpec(memory_space=pltpu.VMEM)] + [some] * 6,
        out_specs=(some,) * 3,
        scratch_shapes=[
            both, both,
            pltpu.VMEM((rows, features), q.dtype),
            pltpu.VMEM((rows, W), k.dtype),
            pltpu.VMEM((rows, W), k.dtype),
            pltpu.VMEM((2, 2, heads, rows), jnp.float32),
            slots,
            pltpu.VMEM((4, *turned), jnp.float32),
            sums, sums, halves, halves,
            pltpu.VMEM((2 * B, B), jnp.float32),
            slots,
            pltpu.VMEM((2, *turned), jnp.bfloat16),
            pltpu.VMEM((2, *turned), jnp.bfloat16),
            pltpu.VMEM((rows, features), jnp.bfloat16),
            pltpu.VMEM((rows, W), jnp.bfloat16),
            pltpu.VMEM((rows, W), jnp.bfloat16),
            pair, quad, pair, pair, pair, pair,
            pltpu.VMEM((4, 2, B, W), jnp.bfloat16),
            pltpu.VMEM((2, 2, B, W), jnp.float32),
            pltpu.VMEM((2, B, W), jnp.bfloat16),
            pltpu.SemaphoreType.DMA((6,)),
            pltpu.SemaphoreType.DMA((3,)),
            pltpu.SemaphoreType.DMA((39,)),
            pltpu.SemaphoreType.DMA((39,)),
        ],
        compiler_params=pltpu.CompilerParams(
            collective_id=0, has_side_effects=True, vmem_limit_bytes=VMEM
        ),
        cost_estimate=pl.CostEstimate(
            flops=35 * 10 * heads * B * B * W, bytes_accessed=16 << 20, transcendentals=0
        ),
    )(docs, q, k, v, o, g, log_total)


def publish_kernel(*refs):
    sources, targets, held, get, put = refs[:3], refs[3:6], refs[6:9], refs[9], refs[10]
    pieces = []
    for source, target, mid in zip(sources, targets, held):
        rows = min(source.shape[0], 128 * 1024 // source.shape[1])
        for at in range(0, source.shape[0], rows):
            here = slice(at, at + rows)
            n = len(pieces)
            pieces.append(
                (
                    pltpu.make_async_copy(source.at[here], mid.at[here], get.at[n]),
                    pltpu.make_async_copy(mid.at[here], target.at[here], put.at[n]),
                )
            )
    for into, _ in pieces:
        into.start()
    for into, out in pieces:
        into.wait()
        out.start()
    for _, out in pieces:
        out.wait()


def publish(*results):
    some = pl.BlockSpec(memory_space=pl.ANY)
    return pl.pallas_call(
        publish_kernel,
        out_shape=tuple(jax.ShapeDtypeStruct(x.shape, x.dtype) for x in results),
        in_specs=[some] * 3,
        out_specs=(some,) * 3,
        scratch_shapes=[pltpu.VMEM(x.shape, x.dtype) for x in results]
        + [pltpu.SemaphoreType.DMA((6,))] * 2,
        compiler_params=pltpu.CompilerParams(vmem_limit_bytes=VMEM),
    )(*results)


def solution(mesh):
    columns = mesh.shape["ctx"] // 2

    def on_device(q, k, v, o, g, log_total, doc_lengths):
        docs = doc_lengths[None, :]
        return publish(*all_gradients(columns, docs, q, k, v, o, g, log_total))

    rows = P(("ctx", "section"), None)
    return jax.shard_map(
        on_device,
        mesh=mesh,
        in_specs=(rows, rows, rows, rows, rows, P(None, ("ctx", "section")), P()),
        out_specs=(rows, rows, rows),
        check_vma=False,
    )
```

```python
import functools
import math

import jax
import jax.numpy as jnp
from jax import lax
from jax.experimental import pallas as pl
from jax.experimental.pallas import tpu as pltpu
from jax.sharding import PartitionSpec as P

MESH = pl.DeviceIdType.MESH
W = 128
B = 256
VMEM = 58 << 20
LOG2E = math.log2(math.e)
OWN, BEFORE = 1, 0


def nn(a, b):
    return jnp.dot(a, b, preferred_element_type=jnp.float32)


def nt(a, b):
    return lax.dot_general(a, b, (((1,), (1,)), ((), ())), preferred_element_type=jnp.float32)


def place():
    ctx = lax.axis_index("ctx")
    return ctx // 2, lax.axis_index("section"), ctx % 2


def slot(side, z, j):
    return side * 8 + z * 2 + j


def doc_ends(docs_ref):
    lengths = docs_ref[...].astype(jnp.float32)
    docs = lengths.shape[1]
    upto = lax.broadcasted_iota(jnp.int32, (docs, docs), 1) <= lax.broadcasted_iota(
        jnp.int32, (docs, docs), 0
    )
    return jnp.sum(jnp.where(upto, lengths, 0.0), axis=1, keepdims=True)


def positions(first):
    return first.astype(jnp.float32) + lax.broadcasted_iota(jnp.int32, (1, B), 1).astype(
        jnp.float32
    )


def doc_start(ends, pos):
    return jnp.max(jnp.where(ends <= pos, ends, 0.0), axis=0, keepdims=True)


def hidden(key, start, pos):
    kpos = (key + lax.broadcasted_iota(jnp.int32, (B, B), 0)).astype(jnp.float32)
    return jnp.where((kpos >= start) & (kpos <= pos), 0.0, -jnp.inf)


def identity(n):
    at = [lax.broadcasted_iota(jnp.int32, (n, n), d) for d in range(2)]
    return (at[0] == at[1]).astype(jnp.bfloat16)


def gradients(k, v, qs, gs, logs, deltas, bias=None):
    ps, ds = [], []
    for q, g, log, delta in zip(qs, gs, logs, deltas):
        x = nt(k, q) * (LOG2E / math.sqrt(W)) - log
        if bias is not None:
            x = x + bias[...]
        p = jnp.exp2(x)
        d = p * (nt(v, g) - delta)
        ps.append(p.astype(jnp.bfloat16))
        ds.append(d.astype(jnp.bfloat16))
    dh = jnp.concatenate(ds, axis=1)
    dv = nn(jnp.concatenate(ps, axis=1), jnp.concatenate(gs, axis=0))
    dk = nn(dh, jnp.concatenate(qs, axis=0))
    return dk, dv, nn(k.T, dh)


class Links:
    def __init__(self, columns):
        self.column, self.z, self.core = place()
        ctx = lax.axis_index("ctx")
        self.up = lax.rem(self.z + 1, 4)
        self.down = lax.rem(self.z + 3, 4)
        self.across = lax.rem(self.z + 2, 4)
        self.sibling = (ctx + 1 - 2 * self.core, self.z)
        self.above = (ctx, self.up)
        self.below = (ctx, self.down)
        self.has_next = self.column < columns - 1
        self.has_last = self.column > 0
        self.next = (jnp.where(self.has_next, ctx + 2, ctx), self.z)
        self.last = (jnp.where(self.has_last, ctx - 2, ctx), self.z)
        self.next_across = (self.next[0], self.across)
        self.last_across = (self.last[0], self.across)

    def barrier(self, straight=False):
        barrier = pltpu.get_barrier_semaphore()

        def greet(*devices):
            for device in devices:
                pl.semaphore_signal(barrier, inc=1, device_id=device, device_id_type=MESH)

        greet(self.sibling, self.above, self.below)
        later = (self.next, self.next_across) if straight else (self.next,)
        earlier = (self.last, self.last_across) if straight else (self.last,)
        pl.when(self.has_next)(lambda: greet(*later))
        pl.when(self.has_last)(lambda: greet(*earlier))
        columns = self.has_next.astype(jnp.int32) + self.has_last.astype(jnp.int32)
        pl.semaphore_wait(barrier, 3 + len(later) * columns)


class Route:
    def __init__(self, sems, index, device, source, target, sends=True, gets=True, arrival=None):
        self.sends, self.gets = sends, gets
        landed = target if arrival is None else arrival
        send, recv = sems[0].at[index], sems[1].at[index]
        self.make = lambda end: pltpu.make_async_remote_copy(
            source, end, send, recv, device_id=device, device_id_type=MESH
        )
        self.target, self.landed = target, landed

    @staticmethod
    def only(condition, act):
        if condition is True:
            act()
        else:
            pl.when(condition)(act)

    def start(self):
        self.only(self.sends, lambda: self.make(self.target).start())

    def arrived(self):
        self.only(self.gets, lambda: self.make(self.landed).wait_recv())

    def sent(self):
        self.only(self.sends, lambda: self.make(self.target).wait_send())


def gather_kernel(
    columns, heads, docs_ref, q_ref, g_ref, o_ref, k_ref, v_ref, log_ref,
    q_other, g_other, stat_both, window_out, dq_out, kv_out,
    q_both, g_both, o_vmem, k_own, v_own, stat, window, dqt, dkv, bias, local, put, send, recv,
):
    at = Links(columns)
    z, core, up, down, across = at.z, at.core, at.up, at.down, at.across
    sems = (send, recv)
    mine = window.at[slot(OWN, z, core)]
    loads = [
        pltpu.make_async_copy(source, target, local.at[n])
        for n, (source, target) in enumerate(
            (
                (k_ref, k_own), (v_ref, v_own), (q_ref, q_both.at[0]), (g_ref, g_both.at[0]),
                (o_ref, o_vmem), (log_ref, stat.at[0, 0]),
            )
        )
    ]
    for copy in loads:
        copy.start()

    @pl.when(at.column == 0)
    def _():
        window[slot(BEFORE, 3, 1)] = jnp.zeros((2, B, W), window.dtype)

    at.barrier()

    theirs = window.at[slot(OWN, z, 1 - core)]
    swap_k = Route(sems, 0, at.sibling, k_own.at[B:], mine.at[0], arrival=theirs.at[0])
    swap_v = Route(sems, 1, at.sibling, v_own.at[B:], mine.at[1], arrival=theirs.at[1])
    loads[0].wait()
    loads[1].wait()
    swap_k.start()
    swap_v.start()
    mine[0] = k_own[:B]
    mine[1] = v_own[:B]
    rows = q_ref.shape[0]
    bulk = []
    for part in range(2):
        some = slice(part * rows // 2, (part + 1) * rows // 2)
        bulk.append(Route(sems, 2 + part, at.sibling, q_both.at[0, some], q_both.at[1, some]))
        bulk.append(Route(sems, 4 + part, at.sibling, g_both.at[0, some], g_both.at[1, some]))

    def passed(index, device, side, sent, j, got, sends=True, gets=True):
        there = window.at[slot(side, sent, j)]
        return Route(sems, index, device, there, there, sends, gets, window.at[slot(side, got, j)])

    up_0 = passed(6, at.above, OWN, z, 0, down)
    up_1 = passed(7, at.above, OWN, z, 1, down)
    down_0 = passed(8, at.below, OWN, z, 0, up)
    down_1 = passed(9, at.below, OWN, z, 1, up, z == 0, z == 3)
    far_0 = passed(10, at.below, OWN, up, 0, across)
    far_1 = passed(11, at.above, OWN, down, 1, across)

    def later(index, zc, j, when=True):
        here = window.at[slot(OWN, zc, j)]
        there = window.at[slot(BEFORE, zc, j)]
        sends = at.has_next if when is True else at.has_next & when
        gets = at.has_last if when is True else at.has_last & when
        return Route(sems, index, at.next, here, there, sends, gets)

    next_0 = later(12, z, 0)
    next_1 = later(13, z, 1)
    next_far_0 = later(14, across, 0, z < 2)
    next_far_1 = later(15, across, 1)
    last = at.has_last
    before_up_0 = passed(16, at.above, BEFORE, z, 0, down, last & (z == 3), last & (z == 0))
    before_up_1 = passed(17, at.above, BEFORE, z, 1, down, last, last)
    before_down_0 = passed(18, at.below, BEFORE, z, 0, up, last & (z != 0), last & (z != 3))
    before_down_1 = passed(19, at.below, BEFORE, z, 1, up, last, last)
    stats = Route(sems, 20, at.sibling, stat.at[0], stat.at[1])

    swap_k.arrived()
    swap_v.arrived()
    for copy in (up_1, down_0, next_1, up_0, down_1, next_0):
        copy.start()
    for copy in loads[2:]:
        copy.wait()
    for copy in bulk:
        copy.start()

    ones = jnp.ones((8, W), jnp.bfloat16)
    for h in range(heads):
        cols = slice(h * W, (h + 1) * W)
        product = g_both[0, :, cols].astype(jnp.float32) * o_vmem[:, cols].astype(jnp.float32)
        high = product.astype(jnp.bfloat16)
        low = (product - high.astype(jnp.float32)).astype(jnp.bfloat16)
        total = nt(ones, high) + nt(ones, low)
        stat[0, 1, h : h + 1, :] = total[0:1]
    stat[0, 0] = stat[0, 0] * LOG2E
    stats.start()

    ends = doc_ends(docs_ref)
    column = at.column * 16 * B
    dkv[...] = jnp.zeros_like(dkv)
    dqt[...] = jnp.zeros_like(dqt)

    def products(side, part, k, v, mask):
        here = pl.ds(pl.multiple_of(part * B, B), B)
        return gradients(
            k, v,
            [q_both[side, here, h * W : (h + 1) * W] for h in range(heads)],
            [g_both[side, here, h * W : (h + 1) * W] for h in range(heads)],
            [stat[side, 0, h : h + 1, here] for h in range(heads)],
            [stat[side, 1, h : h + 1, here] for h in range(heads)],
            mask,
        )

    @pl.loop(0, 3)
    def _(n):
        @pl.when(n == 2)
        def _():
            up_1.arrived()
            far_1.start()
            down_0.arrived()
            far_0.start()

        part, b = (n + 1) // 2, n // 2
        there = pl.ds(pl.multiple_of(b * B, B), B)
        tile = column + (z + 4 * core) * 2 * B
        pos = positions(tile + part * B)
        bias[:B] = hidden(tile + b * B, doc_start(ends, pos), pos)
        dk, dv, dq = products(0, part, k_own[there], v_own[there], bias.at[:B])
        dkv[3 + b, 0] += dk
        dkv[3 + b, 1] += dv
        dqt[part] += dq

    next_1.arrived()
    before_down_1.start()
    before_up_1.start()
    next_0.arrived()
    before_down_0.start()
    before_up_0.start()

    near_4 = jnp.where(z > 0, slot(OWN, down, 1), slot(OWN, 3, 0))
    near_0 = jnp.where(z > 0, slot(OWN, down, 0), slot(BEFORE, 3, 1))

    def half_of(tile):
        return jnp.where((tile + 8) % 8 >= 4, 1 - core, core)

    def near(side, part, tile, keys, key_tiles, out):
        start = doc_start(ends, positions(column + tile * 2 * B + part * B))
        for n, key_tile in enumerate(key_tiles):
            key = column + key_tile * 2 * B + half_of(key_tile) * B
            kpos = (key + lax.broadcasted_iota(jnp.int32, (B, B), 0)).astype(jnp.float32)
            bias[n * B : (n + 1) * B] = jnp.where(kpos >= start, 0.0, -jnp.inf)
        dk, dv, dq = products(
            side, part,
            jnp.concatenate([window[n, 0] for n in keys], axis=0),
            jnp.concatenate([window[n, 1] for n in keys], axis=0),
            bias.at[: len(keys) * B],
        )
        for n in range(len(keys)):
            dkv[out + n, 0] += dk[n * B : (n + 1) * B]
            dkv[out + n, 1] += dv[n * B : (n + 1) * B]
        dqt[side * 2 + part] += dq

    puts = [
        pltpu.make_async_copy(source, target, put.at[n])
        for n, (source, target) in enumerate(
            (
                (q_both.at[1], q_other), (g_both.at[1], g_other), (stat, stat_both),
                (window.at[8:], window_out.at[8:]), (dqt.at[:2], dq_out.at[:2]),
                (window.at[:8], window_out.at[:8]), (dqt.at[2:], dq_out.at[2:]), (dkv, kv_out),
            )
        )
    ]

    @pl.loop(0, 4)
    def _(n):
        @pl.when(n == 0)
        def _():
            up_0.arrived()
            pl.when(core == 0)(before_up_1.arrived)

        @pl.when(n == 1)
        def _():
            far_0.arrived()
            next_far_0.start()
            far_1.arrived()
            next_far_1.start()

        @pl.when(n == 2)
        def _():
            down_1.arrived()
            for copy in bulk:
                copy.arrived()
            stats.arrived()
            pl.when(core == 1)(before_up_1.arrived)
            for copy in puts[:5]:
                copy.start()

        side, part = n // 2, n % 2

        @pl.when(side == core)
        def _():
            near(side, part, z, [near_0], [z - 1], 2)

        @pl.when(side != core)
        def _():
            near(side, part, z + 4, [slot(OWN, z, 0), near_4], [z, z + 3], 0)

    puts[6].start()
    puts[7].start()
    for copy in (before_up_0, before_down_0, before_down_1, next_far_0, next_far_1):
        copy.arrived()
    puts[5].start()
    for copy in (
        [swap_k, swap_v, up_0, up_1, down_0, down_1, far_0, far_1, next_0, next_1, next_far_0]
        + [next_far_1, before_up_0, before_up_1, before_down_0, before_down_1, stats]
        + bulk
    ):
        copy.sent()
    for copy in puts:
        copy.wait()


def gather(columns, docs, q, g, o, k, v, log_total):
    rows, features = q.shape
    heads = features // W
    some = pl.BlockSpec(memory_space=pl.ANY)
    window = (16, 2, B, W)
    stat = (2, 2, heads, rows)
    turned = (4, W, heads * B)
    sums = (5, 2, B, W)
    return pl.pallas_call(
        functools.partial(gather_kernel, columns, heads),
        out_shape=(
            jax.ShapeDtypeStruct(q.shape, q.dtype),
            jax.ShapeDtypeStruct(q.shape, q.dtype),
            jax.ShapeDtypeStruct(stat, jnp.float32),
            jax.ShapeDtypeStruct(window, k.dtype),
            jax.ShapeDtypeStruct(turned, jnp.float32),
            jax.ShapeDtypeStruct(sums, jnp.float32),
        ),
        in_specs=[pl.BlockSpec(memory_space=pltpu.VMEM)] + [some] * 6,
        out_specs=(some,) * 6,
        scratch_shapes=[
            pltpu.VMEM((2, rows, features), q.dtype),
            pltpu.VMEM((2, rows, features), q.dtype),
            pltpu.VMEM(q.shape, q.dtype),
            pltpu.VMEM(k.shape, k.dtype),
            pltpu.VMEM(k.shape, k.dtype),
            pltpu.VMEM(stat, jnp.float32),
            pltpu.VMEM(window, k.dtype),
            pltpu.VMEM(turned, jnp.float32),
            pltpu.VMEM(sums, jnp.float32),
            pltpu.VMEM((2 * B, B), jnp.float32),
            pltpu.SemaphoreType.DMA((6,)),
            pltpu.SemaphoreType.DMA((8,)),
            pltpu.SemaphoreType.DMA((21,)),
            pltpu.SemaphoreType.DMA((21,)),
        ],
        compiler_params=pltpu.CompilerParams(
            collective_id=0, has_side_effects=True, vmem_limit_bytes=VMEM
        ),
    )(docs, q, g, o, k, v, log_total)


def attend_kernel(
    heads, docs_ref, qa_hbm, qb_hbm, ga_hbm, gb_hbm, stat_hbm, window_hbm, dq_hbm, kv_hbm,
    dq_own, dq_other, part_hbm,
    q_ref, g_ref, stat_ref, window_ref, dqt, dqh, part_ref, dka, dva, dkv, bias, starts, bounds, get, put,
):
    column, z, core = place()
    loads = [
        pltpu.make_async_copy(source, target, get.at[n])
        for n, (source, target) in enumerate(
            (
                (stat_hbm, stat_ref),
                (window_hbm.at[:8], window_ref.at[:8]), (window_hbm.at[8:], window_ref.at[8:]),
                (kv_hbm.at[:3], dkv), (qa_hbm, q_ref.at[0]), (ga_hbm, g_ref.at[0]),
                (dq_hbm.at[:2], dqt.at[:2]),
                (qb_hbm, q_ref.at[1]), (gb_hbm, g_ref.at[1]), (dq_hbm.at[2:], dqt.at[2:]),
            )
        )
    ]
    for load in loads:
        load.start()
    ends = doc_ends(docs_ref)
    window = (column - 1) * 16 * B

    def half_of(b):
        return jnp.where(b % 8 >= 4, 1 - core, core)

    def tile_of(side):
        return z + 4 * (core if side == 0 else 1 - core)

    for block in range(4):
        side, part = divmod(block, 2)
        first = column * 16 * B + tile_of(side) * 2 * B + part * B
        start = doc_start(ends, positions(first))
        starts[block] = start
        low = jnp.min(start).astype(jnp.int32) - window
        last = jnp.max(start).astype(jnp.int32) - window
        b = low // (2 * B)
        bounds[0, block] = jnp.where(low % (2 * B) >= half_of(b) * B + B, b + 1, b)
        b = last // (2 * B)
        bounds[1, block] = jnp.where(last % (2 * B) > half_of(b) * B, b + 1, b)
    dka[...] = jnp.zeros_like(dka)
    dva[...] = jnp.zeros_like(dva)
    for load in loads[:7]:
        load.wait()
    down = lax.rem(z + 3, 4)
    nears = (
        slot(OWN, z, 0),
        jnp.where(z > 0, slot(OWN, down, 1), slot(OWN, 3, 0)),
        jnp.where(z > 0, slot(OWN, down, 0), slot(BEFORE, 3, 1)),
    )
    for n, at in enumerate(nears):
        dka[at] = dkv[n, 0]
        dva[at] = dkv[n, 1]

    @pl.loop(0, 4)
    def _(block):
        side, part = block // 2, block % 2
        here = pl.ds(pl.multiple_of(part * B, B), B)

        @pl.when(block == 2)
        def _():
            for load in loads[7:]:
                load.wait()

        def work(blocks, mask=None):
            at = [slot(b // 8, b % 4, b % 8 // 4) for b in blocks]
            dk, dv, dq = gradients(
                jnp.concatenate([window_ref[n, 0] for n in at], axis=0),
                jnp.concatenate([window_ref[n, 1] for n in at], axis=0),
                [q_ref[side, here, h * W : (h + 1) * W] for h in range(heads)],
                [g_ref[side, here, h * W : (h + 1) * W] for h in range(heads)],
                [stat_ref[side, 0, h : h + 1, here] for h in range(heads)],
                [stat_ref[side, 1, h : h + 1, here] for h in range(heads)],
                mask,
            )
            for n in range(len(at)):
                dva[at[n]] += dv[n * B : (n + 1) * B]
                dka[at[n]] += dk[n * B : (n + 1) * B]
            dqt[block] += dq

        second = jnp.where(side == 0, core, 1 - core)
        end = 7 + z + 4 * second
        skip = jnp.where(second == 1, 8 + z, 16)

        def counted(b):
            return jnp.where(b > skip, b - 1, b)

        def real(n):
            return jnp.where(n >= skip, n + 1, n)

        end = counted(end)
        low = counted(bounds[0, block])
        cut = jnp.minimum(counted(bounds[1, block]), end)
        cut = cut + (end - cut) % 2

        @pl.loop(low, cut)
        def _(n):
            b = real(n)
            key = window + b * 2 * B + half_of(b) * B
            kpos = (key + lax.broadcasted_iota(jnp.int32, (B, B), 0)).astype(jnp.float32)
            bias[...] = jnp.where(kpos >= starts[block], 0.0, -jnp.inf)
            work([b], bias)

        @pl.loop(0, (end - jnp.maximum(low, cut)) // 2)
        def _(n):
            work([real(cut + 2 * n), real(cut + 2 * n + 1)])

        @pl.when(side == 0)
        def _():
            pltpu.make_async_copy(dqt.at[block], dq_own.at[part], put.at[block]).start()

        @pl.when(side == 1)
        def _():
            dqh[part] = dqt[block].astype(jnp.bfloat16)
            pltpu.make_async_copy(dqh.at[part], dq_other.at[part], put.at[block]).start()

    @pl.loop(0, 16)
    def _(s):
        part_ref[s, 0] = (dka[s] * (1.0 / math.sqrt(W))).astype(jnp.bfloat16)
        part_ref[s, 1] = dva[s].astype(jnp.bfloat16)
        pltpu.make_async_copy(part_ref.at[s], part_hbm.at[s], put.at[4 + s]).start()

    for part in range(2):
        pltpu.make_async_copy(dqt.at[part], dq_own.at[part], put.at[part]).wait()
        pltpu.make_async_copy(dqh.at[part], dq_other.at[part], put.at[2 + part]).wait()
    for s in range(16):
        pltpu.make_async_copy(part_ref.at[s], part_hbm.at[s], put.at[4 + s]).wait()


def attend(docs, q, q_other, g, g_other, stat, window, dq, sums):
    rows, features = q.shape
    heads = features // W
    some = pl.BlockSpec(memory_space=pl.ANY)
    both = (2, rows, features)
    turned = (2, W, heads * B)
    return pl.pallas_call(
        functools.partial(attend_kernel, heads),
        out_shape=(
            jax.ShapeDtypeStruct(turned, jnp.float32),
            jax.ShapeDtypeStruct(turned, jnp.bfloat16),
            jax.ShapeDtypeStruct(window.shape, jnp.bfloat16),
        ),
        in_specs=[pl.BlockSpec(memory_space=pltpu.VMEM)] + [some] * 8,
        out_specs=(some,) * 3,
        scratch_shapes=[
            pltpu.VMEM(both, q.dtype),
            pltpu.VMEM(both, q.dtype),
            pltpu.VMEM(stat.shape, stat.dtype),
            pltpu.VMEM(window.shape, window.dtype),
            pltpu.VMEM((4, W, heads * B), jnp.float32),
            pltpu.VMEM(turned, jnp.bfloat16),
            pltpu.VMEM(window.shape, jnp.bfloat16),
            pltpu.VMEM((16, B, W), jnp.float32),
            pltpu.VMEM((16, B, W), jnp.float32),
            pltpu.VMEM((3, 2, B, W), jnp.float32),
            pltpu.VMEM((B, B), jnp.float32),
            pltpu.VMEM((4, 1, B), jnp.float32),
            pltpu.SMEM((2, 4), jnp.int32),
            pltpu.SemaphoreType.DMA((10,)),
            pltpu.SemaphoreType.DMA((20,)),
        ],
        compiler_params=pltpu.CompilerParams(vmem_limit_bytes=VMEM),
        cost_estimate=pl.CostEstimate(
            flops=20 * 10 * heads * B * B * W, bytes_accessed=16 << 20, transcendentals=0
        ),
    )(docs, q, q_other, g, g_other, stat, window, dq, sums)


def return_kernel(
    columns, heads, kv_hbm, dq_own, dq_other, part_ref,
    dq_hbm, dk_hbm, dv_hbm,
    dkv, dqt, dq_sent, dq_got, dq_out, dk_ref, dv_ref,
    part, across_got, beside_got, beside_sum, later_got, far_got, near_sum, near_got,
    final, given_half, local, put, send, recv,
):
    at = Links(columns)
    z, core, up, down, across = at.z, at.core, at.up, at.down, at.across
    sems = (send, recv)
    load = pltpu.make_async_copy(part_ref.at[:8], part.at[:8], local.at[0])
    load_own = pltpu.make_async_copy(part_ref.at[8:], part.at[8:], local.at[1])
    load_dq = pltpu.make_async_copy(dq_other, dq_sent, local.at[2])
    load.start()
    load_own.start()
    load_dq.start()
    loads = [
        pltpu.make_async_copy(source, target, local.at[3 + n])
        for n, (source, target) in enumerate(
            (
                (kv_hbm.at[3:], dkv), (dq_own, dqt),
            )
        )
    ]
    for copy in loads:
        copy.start()
    at.barrier(straight=True)
    has_next, has_last = at.has_next, at.has_last

    def given(side, zc, j):
        return part.at[slot(side, zc, j)]

    def held(side, zc, j):
        return part[slot(side, zc, j)].astype(jnp.float32)

    far_back = [
        Route(
            sems, j, at.last_across, given(BEFORE, across, j), across_got.at[j],
            has_last & (z < 2) if j == 0 else has_last,
            has_next & (z >= 2) if j == 0 else has_next,
        )
        for j in range(2)
    ]
    side_up = [
        Route(
            sems, 2 + j, at.above, given(BEFORE, up, j), beside_got.at[0, j],
            has_last & (z != 3) if j == 0 else has_last,
            has_last & (z != 0) if j == 0 else has_last,
        )
        for j in range(2)
    ]
    side_down = [
        Route(
            sems, 4 + j, at.below, given(BEFORE, down, j), beside_got.at[1, j],
            has_last & (z == 0) if j == 0 else has_last,
            has_last & (z == 3) if j == 0 else has_last,
        )
        for j in range(2)
    ]
    bulk = [
        Route(sems, 6 + n, at.sibling, dq_sent.at[n], dq_got.at[n]) for n in range(2)
    ]
    back = [
        Route(sems, 8 + j, at.last, beside_sum.at[j], later_got.at[j], has_last, has_next)
        for j in range(2)
    ]
    far_up = Route(sems, 10, at.above, given(OWN, across, 0), far_got.at[0])
    far_down = Route(
        sems, 11, at.below, given(OWN, across, 1), far_got.at[1], z >= 2, (z == 1) | (z == 2)
    )
    near_up_0 = Route(sems, 12, at.above, near_sum.at[0], near_got.at[0])
    near_up_1 = Route(sems, 13, at.above, given(OWN, up, 1), near_got.at[1], z == 3, z == 0)
    near_down_0 = Route(sems, 14, at.below, given(OWN, down, 0), near_got.at[2])
    near_down_1 = Route(sems, 15, at.below, near_sum.at[1], near_got.at[3], z != 0, z != 3)

    load.wait()
    for copy in (far_back[1], side_up[1], side_down[1], far_back[0], side_up[0], side_down[0]):
        copy.start()
    load_own.wait()
    for copy in (far_up, far_down, near_down_0, near_up_1):
        copy.start()
    load_dq.wait()
    for copy in bulk:
        copy.start()

    @pl.when(has_last)
    def _():
        for copy in side_up + side_down:
            copy.arrived()
        for j in range(2):
            final[j] = held(BEFORE, z, j)
        final[1] += beside_got[0, 1].astype(jnp.float32) + beside_got[1, 1].astype(jnp.float32)

        @pl.when(z != 0)
        def _():
            final[0] += beside_got[0, 0].astype(jnp.float32)

        @pl.when(z == 3)
        def _():
            final[0] += beside_got[1, 0].astype(jnp.float32)

        beside_sum[...] = final[...].astype(jnp.bfloat16)
        for copy in back:
            copy.start()

    far_up.arrived()
    near_sum[0] = (held(OWN, up, 0) + far_got[0].astype(jnp.float32)).astype(jnp.bfloat16)
    near_up_0.start()

    @pl.when((z == 1) | (z == 2))
    def _():
        far_down.make(far_got.at[1]).wait_recv()
        total = held(OWN, down, 1) + far_got[1].astype(jnp.float32)
        near_sum[1] = total.astype(jnp.bfloat16)

    @pl.when(z == 3)
    def _():
        near_sum[1] = given(OWN, down, 1)[...]

    near_down_1.start()
    for copy in loads:
        copy.wait()
    for copy in bulk:
        copy.arrived()
    eye = identity(B)
    for block in range(2):
        for h in range(heads):
            rows = slice(h * B, (h + 1) * B)
            total = dqt[block, :, rows] + dq_got[block, :, rows].astype(jnp.float32)
            rounded = (total * (1.0 / math.sqrt(W))).astype(jnp.bfloat16)
            turned = nt(eye, rounded).astype(jnp.bfloat16)
            dq_out[block * B : (block + 1) * B, h * W : (h + 1) * W] = turned
    out_q = pltpu.make_async_copy(dq_out, dq_hbm, put.at[0])
    out_q.start()
    near_down_0.arrived()
    near_up_0.arrived()
    final[0] = (
        held(OWN, z, 0) + near_got[0].astype(jnp.float32) + near_got[2].astype(jnp.float32)
    )
    final[1] = held(OWN, z, 1)

    @pl.when(z == 0)
    def _():
        near_up_1.make(near_got.at[1]).wait_recv()
        final[1] += near_got[1].astype(jnp.float32)

    @pl.when(z != 3)
    def _():
        near_down_1.make(near_got.at[3]).wait_recv()
        final[1] += near_got[3].astype(jnp.float32)

    @pl.when(has_next)
    def _():
        far_back[1].make(across_got.at[1]).wait_recv()
        final[1] += across_got[1].astype(jnp.float32)
        for j in range(2):
            back[j].arrived()
            final[j] += later_got[j].astype(jnp.float32)

    @pl.when(has_next & (z >= 2))
    def _():
        far_back[0].make(across_got.at[0]).wait_recv()
        final[0] += across_got[0].astype(jnp.float32)

    given_half[...] = final[1 - core].astype(jnp.bfloat16)
    give_k = Route(sems, 16, at.sibling, given_half.at[0], dk_ref.at[B:])
    give_v = Route(sems, 17, at.sibling, given_half.at[1], dv_ref.at[B:])
    give_k.start()
    give_v.start()
    scale = 1.0 / math.sqrt(W)
    dk_ref[:B] = (final[core, 0] + dkv[0, 0] * scale).astype(jnp.bfloat16)
    dv_ref[:B] = (final[core, 1] + dkv[0, 1]).astype(jnp.bfloat16)
    give_k.arrived()
    give_v.arrived()
    dk_ref[B:] = (dk_ref[B:].astype(jnp.float32) + dkv[1, 0] * scale).astype(jnp.bfloat16)
    dv_ref[B:] = (dv_ref[B:].astype(jnp.float32) + dkv[1, 1]).astype(jnp.bfloat16)
    out_k = pltpu.make_async_copy(dk_ref, dk_hbm, put.at[1])
    out_v = pltpu.make_async_copy(dv_ref, dv_hbm, put.at[2])
    out_k.start()
    out_v.start()
    for copy in (out_q, out_k, out_v):
        copy.wait()
    for copy in (
        far_back + side_up + side_down + bulk + back
        + [far_up, far_down, near_up_0, near_up_1, near_down_0, near_down_1, give_k, give_v]
    ):
        copy.sent()


def give_back(columns, sums, dq_own, dq_other, part):
    rows = 2 * B
    heads = dq_own.shape[2] // B
    features = heads * W
    some = pl.BlockSpec(memory_space=pl.ANY)
    block = (2, B, W)
    return pl.pallas_call(
        functools.partial(return_kernel, columns, heads),
        out_shape=(
            jax.ShapeDtypeStruct((rows, features), jnp.bfloat16),
            jax.ShapeDtypeStruct((rows, W), jnp.bfloat16),
            jax.ShapeDtypeStruct((rows, W), jnp.bfloat16),
        ),
        in_specs=[some] * 4,
        out_specs=(some,) * 3,
        scratch_shapes=[
            pltpu.VMEM((2, *block), jnp.float32),
            pltpu.VMEM(dq_own.shape, dq_own.dtype),
            pltpu.VMEM(dq_other.shape, dq_other.dtype),
            pltpu.VMEM(dq_other.shape, dq_other.dtype),
            pltpu.VMEM((rows, features), jnp.bfloat16),
            pltpu.VMEM((rows, W), jnp.bfloat16),
            pltpu.VMEM((rows, W), jnp.bfloat16),
            pltpu.VMEM((16, *block), jnp.bfloat16),
            pltpu.VMEM((2, *block), jnp.bfloat16),
            pltpu.VMEM((2, 2, *block), jnp.bfloat16),
            pltpu.VMEM((2, *block), jnp.bfloat16),
            pltpu.VMEM((2, *block), jnp.bfloat16),
            pltpu.VMEM((2, *block), jnp.bfloat16),
            pltpu.VMEM((2, *block), jnp.bfloat16),
            pltpu.VMEM((4, *block), jnp.bfloat16),
            pltpu.VMEM((2, *block), jnp.float32),
            pltpu.VMEM(block, jnp.bfloat16),
            pltpu.SemaphoreType.DMA((5,)),
            pltpu.SemaphoreType.DMA((3,)),
            pltpu.SemaphoreType.DMA((18,)),
            pltpu.SemaphoreType.DMA((18,)),
        ],
        compiler_params=pltpu.CompilerParams(
            collective_id=1, has_side_effects=True, vmem_limit_bytes=VMEM
        ),
    )(sums, dq_own, dq_other, part)


def publish_kernel(*refs):
    sources, targets, held, get, put = refs[:3], refs[3:6], refs[6:9], refs[9], refs[10]
    pieces = []
    for source, target, mid in zip(sources, targets, held):
        rows = min(source.shape[0], 128 * 1024 // source.shape[1])
        for at in range(0, source.shape[0], rows):
            here = slice(at, at + rows)
            n = len(pieces)
            pieces.append(
                (
                    pltpu.make_async_copy(source.at[here], mid.at[here], get.at[n]),
                    pltpu.make_async_copy(mid.at[here], target.at[here], put.at[n]),
                )
            )
    for into, _ in pieces:
        into.start()
    for into, out in pieces:
        into.wait()
        out.start()
    for _, out in pieces:
        out.wait()


def publish(*results):
    some = pl.BlockSpec(memory_space=pl.ANY)
    return pl.pallas_call(
        publish_kernel,
        out_shape=tuple(jax.ShapeDtypeStruct(x.shape, x.dtype) for x in results),
        in_specs=[some] * 3,
        out_specs=(some,) * 3,
        scratch_shapes=[pltpu.VMEM(x.shape, x.dtype) for x in results]
        + [pltpu.SemaphoreType.DMA((6,))] * 2,
        compiler_params=pltpu.CompilerParams(vmem_limit_bytes=VMEM),
    )(*results)


def solution(mesh):
    columns = mesh.shape["ctx"] // 2

    def on_device(q, k, v, o, g, log_total, doc_lengths):
        docs = doc_lengths[None, :]
        q_other, g_other, stat, window, dq, sums = gather(columns, docs, q, g, o, k, v, log_total)
        dq_own, dq_other, part = attend(docs, q, q_other, g, g_other, stat, window, dq, sums)
        dq, dk, dv = give_back(columns, sums, dq_own, dq_other, part)
        return publish(dq, dk, dv)

    rows = P(("ctx", "section"), None)
    return jax.shard_map(
        on_device,
        mesh=mesh,
        in_specs=(rows, rows, rows, rows, rows, P(None, ("ctx", "section")), P()),
        out_specs=(rows, rows, rows),
        check_vma=False,
    )
```

```python
import functools
import math

import jax
import jax.numpy as jnp
from jax import lax
from jax.experimental import pallas as pl
from jax.experimental.pallas import tpu as pltpu
from jax.sharding import PartitionSpec as P

MESH = pl.DeviceIdType.MESH
W = 128
B = 256
VMEM = 58 << 20
LOG2E = math.log2(math.e)
OWN, BEFORE = 1, 0


def nn(a, b):
    return jnp.dot(a, b, preferred_element_type=jnp.float32)


def nt(a, b):
    return lax.dot_general(a, b, (((1,), (1,)), ((), ())), preferred_element_type=jnp.float32)


def place():
    ctx = lax.axis_index("ctx")
    return ctx // 2, lax.axis_index("section"), ctx % 2


def slot(side, z, j):
    return side * 8 + z * 2 + j


def doc_ends(docs_ref):
    lengths = docs_ref[...].astype(jnp.float32)
    docs = lengths.shape[1]
    upto = lax.broadcasted_iota(jnp.int32, (docs, docs), 1) <= lax.broadcasted_iota(
        jnp.int32, (docs, docs), 0
    )
    return jnp.sum(jnp.where(upto, lengths, 0.0), axis=1, keepdims=True)


def positions(first):
    return first.astype(jnp.float32) + lax.broadcasted_iota(jnp.int32, (1, B), 1).astype(
        jnp.float32
    )


def doc_start(ends, pos):
    return jnp.max(jnp.where(ends <= pos, ends, 0.0), axis=0, keepdims=True)


def hidden(key, start, pos):
    kpos = (key + lax.broadcasted_iota(jnp.int32, (B, B), 0)).astype(jnp.float32)
    return jnp.where((kpos >= start) & (kpos <= pos), 0.0, -jnp.inf)


def identity(n):
    at = [lax.broadcasted_iota(jnp.int32, (n, n), d) for d in range(2)]
    return (at[0] == at[1]).astype(jnp.bfloat16)


def gradients(k, v, qs, gs, logs, deltas, bias=None):
    ps, ds = [], []
    for q, g, log, delta in zip(qs, gs, logs, deltas):
        x = nt(k, q) * (LOG2E / math.sqrt(W)) - log
        if bias is not None:
            x = x + bias[...]
        p = jnp.exp2(x)
        d = p * (nt(v, g) - delta)
        ps.append(p.astype(jnp.bfloat16))
        ds.append(d.astype(jnp.bfloat16))
    dh = jnp.concatenate(ds, axis=1)
    dv = nn(jnp.concatenate(ps, axis=1), jnp.concatenate(gs, axis=0))
    dk = nn(dh, jnp.concatenate(qs, axis=0))
    return dk, dv, nn(k.T, dh)


class Links:
    def __init__(self, columns):
        self.column, self.z, self.core = place()
        ctx = lax.axis_index("ctx")
        self.up = lax.rem(self.z + 1, 4)
        self.down = lax.rem(self.z + 3, 4)
        self.across = lax.rem(self.z + 2, 4)
        self.sibling = (ctx + 1 - 2 * self.core, self.z)
        self.above = (ctx, self.up)
        self.below = (ctx, self.down)
        self.has_next = self.column < columns - 1
        self.has_last = self.column > 0
        self.next = (jnp.where(self.has_next, ctx + 2, ctx), self.z)
        self.last = (jnp.where(self.has_last, ctx - 2, ctx), self.z)
        self.next_across = (self.next[0], self.across)
        self.last_across = (self.last[0], self.across)

    def barrier(self, straight=False):
        barrier = pltpu.get_barrier_semaphore()

        def greet(*devices):
            for device in devices:
                pl.semaphore_signal(barrier, inc=1, device_id=device, device_id_type=MESH)

        greet(self.sibling, self.above, self.below)
        later = (self.next, self.next_across) if straight else (self.next,)
        earlier = (self.last, self.last_across) if straight else (self.last,)
        pl.when(self.has_next)(lambda: greet(*later))
        pl.when(self.has_last)(lambda: greet(*earlier))
        columns = self.has_next.astype(jnp.int32) + self.has_last.astype(jnp.int32)
        pl.semaphore_wait(barrier, 3 + len(later) * columns)


class Route:
    def __init__(self, sems, index, device, source, target, sends=True, gets=True, arrival=None):
        self.sends, self.gets = sends, gets
        landed = target if arrival is None else arrival
        send, recv = sems[0].at[index], sems[1].at[index]
        self.make = lambda end: pltpu.make_async_remote_copy(
            source, end, send, recv, device_id=device, device_id_type=MESH
        )
        self.target, self.landed = target, landed

    @staticmethod
    def only(condition, act):
        if condition is True:
            act()
        else:
            pl.when(condition)(act)

    def start(self):
        self.only(self.sends, lambda: self.make(self.target).start())

    def arrived(self):
        self.only(self.gets, lambda: self.make(self.landed).wait_recv())

    def sent(self):
        self.only(self.sends, lambda: self.make(self.target).wait_send())


def gather_kernel(
    columns, heads, docs_ref, q_ref, g_ref, o_ref, k_ref, v_ref, log_ref,
    q_other, g_other, stat_both, window_out, dq_out, kv_out,
    q_both, g_both, o_vmem, k_own, v_own, stat, window, dqt, dkv, bias, local, put, send, recv,
):
    at = Links(columns)
    z, core, up, down, across = at.z, at.core, at.up, at.down, at.across
    sems = (send, recv)
    mine = window.at[slot(OWN, z, core)]
    loads = [
        pltpu.make_async_copy(source, target, local.at[n])
        for n, (source, target) in enumerate(
            (
                (k_ref, k_own), (v_ref, v_own), (q_ref, q_both.at[0]), (g_ref, g_both.at[0]),
                (o_ref, o_vmem), (log_ref, stat.at[0, 0]),
            )
        )
    ]
    for copy in loads:
        copy.start()

    @pl.when(at.column == 0)
    def _():
        window[slot(BEFORE, 3, 1)] = jnp.zeros((2, B, W), window.dtype)

    at.barrier()

    theirs = window.at[slot(OWN, z, 1 - core)]
    swap_k = Route(sems, 0, at.sibling, k_own.at[B:], mine.at[0], arrival=theirs.at[0])
    swap_v = Route(sems, 1, at.sibling, v_own.at[B:], mine.at[1], arrival=theirs.at[1])
    loads[0].wait()
    loads[1].wait()
    swap_k.start()
    swap_v.start()
    mine[0] = k_own[:B]
    mine[1] = v_own[:B]
    rows = q_ref.shape[0]
    bulk = []
    for part in range(2):
        some = slice(part * rows // 2, (part + 1) * rows // 2)
        bulk.append(Route(sems, 2 + part, at.sibling, q_both.at[0, some], q_both.at[1, some]))
        bulk.append(Route(sems, 4 + part, at.sibling, g_both.at[0, some], g_both.at[1, some]))

    def passed(index, device, side, sent, j, got, sends=True, gets=True):
        there = window.at[slot(side, sent, j)]
        return Route(sems, index, device, there, there, sends, gets, window.at[slot(side, got, j)])

    up_0 = passed(6, at.above, OWN, z, 0, down)
    up_1 = passed(7, at.above, OWN, z, 1, down)
    down_0 = passed(8, at.below, OWN, z, 0, up)
    down_1 = passed(9, at.below, OWN, z, 1, up, z == 0, z == 3)
    far_0 = passed(10, at.below, OWN, up, 0, across)
    far_1 = passed(11, at.above, OWN, down, 1, across)

    def later(index, zc, j, when=True):
        here = window.at[slot(OWN, zc, j)]
        there = window.at[slot(BEFORE, zc, j)]
        sends = at.has_next if when is True else at.has_next & when
        gets = at.has_last if when is True else at.has_last & when
        return Route(sems, index, at.next, here, there, sends, gets)

    next_0 = later(12, z, 0)
    next_1 = later(13, z, 1)
    next_far_0 = later(14, across, 0, z < 2)
    next_far_1 = later(15, across, 1)
    last = at.has_last
    before_up_0 = passed(16, at.above, BEFORE, z, 0, down, last & (z == 3), last & (z == 0))
    before_up_1 = passed(17, at.above, BEFORE, z, 1, down, last, last)
    before_down_0 = passed(18, at.below, BEFORE, z, 0, up, last & (z != 0), last & (z != 3))
    before_down_1 = passed(19, at.below, BEFORE, z, 1, up, last, last)
    stats = Route(sems, 20, at.sibling, stat.at[0], stat.at[1])

    swap_k.arrived()
    swap_v.arrived()
    for copy in (up_1, down_0, next_1):
        copy.start()
    for copy in loads[2:]:
        copy.wait()

    ones = jnp.ones((8, W), jnp.bfloat16)
    for h in range(heads):
        cols = slice(h * W, (h + 1) * W)
        product = g_both[0, :, cols].astype(jnp.float32) * o_vmem[:, cols].astype(jnp.float32)
        high = product.astype(jnp.bfloat16)
        low = (product - high.astype(jnp.float32)).astype(jnp.bfloat16)
        total = nt(ones, high) + nt(ones, low)
        stat[0, 1, h : h + 1, :] = total[0:1]
    stat[0, 0] = stat[0, 0] * LOG2E
    stats.start()
    for copy in (next_0, up_0, down_1):
        copy.start()
    for copy in bulk:
        copy.start()

    ends = doc_ends(docs_ref)
    column = at.column * 16 * B
    dkv[...] = jnp.zeros_like(dkv)
    dqt[...] = jnp.zeros_like(dqt)

    def products(side, part, k, v, mask):
        here = pl.ds(pl.multiple_of(part * B, B), B)
        return gradients(
            k, v,
            [q_both[side, here, h * W : (h + 1) * W] for h in range(heads)],
            [g_both[side, here, h * W : (h + 1) * W] for h in range(heads)],
            [stat[side, 0, h : h + 1, here] for h in range(heads)],
            [stat[side, 1, h : h + 1, here] for h in range(heads)],
            mask,
        )

    up_1.arrived()
    far_1.start()
    down_0.arrived()
    far_0.start()
    next_1.arrived()
    before_down_1.start()
    before_up_1.start()
    next_0.arrived()
    before_down_0.start()
    before_up_0.start()

    near_4 = jnp.where(z > 0, slot(OWN, down, 1), slot(OWN, 3, 0))
    near_0 = jnp.where(z > 0, slot(OWN, down, 0), slot(BEFORE, 3, 1))

    def half_of(tile):
        return jnp.where((tile + 8) % 8 >= 4, 1 - core, core)

    def near(side, part, tile, keys, key_tiles, out):
        start = doc_start(ends, positions(column + tile * 2 * B + part * B))
        for n, key_tile in enumerate(key_tiles):
            key = column + key_tile * 2 * B + half_of(key_tile) * B
            kpos = (key + lax.broadcasted_iota(jnp.int32, (B, B), 0)).astype(jnp.float32)
            bias[n * B : (n + 1) * B] = jnp.where(kpos >= start, 0.0, -jnp.inf)
        dk, dv, dq = products(
            side, part,
            jnp.concatenate([window[n, 0] for n in keys], axis=0),
            jnp.concatenate([window[n, 1] for n in keys], axis=0),
            bias.at[: len(keys) * B],
        )
        for n in range(len(keys)):
            dkv[out + n, 0] += dk[n * B : (n + 1) * B]
            dkv[out + n, 1] += dv[n * B : (n + 1) * B]
        dqt[side * 2 + part] += dq

    puts = [
        pltpu.make_async_copy(source, target, put.at[n])
        for n, (source, target) in enumerate(
            (
                (q_both.at[1], q_other), (g_both.at[1], g_other), (stat, stat_both),
                (window.at[8:], window_out.at[8:]), (dqt.at[:2], dq_out.at[:2]),
                (window.at[:8], window_out.at[:8]), (dqt.at[2:], dq_out.at[2:]), (dkv, kv_out),
            )
        )
    ]

    @pl.loop(0, 4)
    def _(n):
        @pl.when(n == 0)
        def _():
            up_0.arrived()
            pl.when((core == 0) & (z == 0))(before_up_1.arrived)

        @pl.when(n == 1)
        def _():
            far_0.arrived()
            next_far_0.start()
            far_1.arrived()
            next_far_1.start()

        @pl.when(n == 2)
        def _():
            down_1.arrived()
            for copy in bulk:
                copy.arrived()
            stats.arrived()
            pl.when((core == 1) & (z == 0))(before_up_1.arrived)
            for copy in puts[:5]:
                copy.start()

        side, part = n // 2, n % 2

        @pl.when(side == core)
        def _():
            near(side, part, z, [near_0], [z - 1], 2)

        @pl.when(side != core)
        def _():
            near(side, part, z + 4, [slot(OWN, z, 0), near_4], [z, z + 3], 0)

    puts[6].start()
    puts[7].start()
    pl.when(z != 0)(before_up_1.arrived)
    for copy in (before_up_0, before_down_0, before_down_1, next_far_0, next_far_1):
        copy.arrived()
    puts[5].start()
    for copy in (
        [swap_k, swap_v, up_0, up_1, down_0, down_1, far_0, far_1, next_0, next_1, next_far_0]
        + [next_far_1, before_up_0, before_up_1, before_down_0, before_down_1, stats]
        + bulk
    ):
        copy.sent()
    for copy in puts:
        copy.wait()


def gather(columns, docs, q, g, o, k, v, log_total):
    rows, features = q.shape
    heads = features // W
    some = pl.BlockSpec(memory_space=pl.ANY)
    window = (16, 2, B, W)
    stat = (2, 2, heads, rows)
    turned = (4, W, heads * B)
    sums = (3, 2, B, W)
    return pl.pallas_call(
        functools.partial(gather_kernel, columns, heads),
        out_shape=(
            jax.ShapeDtypeStruct(q.shape, q.dtype),
            jax.ShapeDtypeStruct(q.shape, q.dtype),
            jax.ShapeDtypeStruct(stat, jnp.float32),
            jax.ShapeDtypeStruct(window, k.dtype),
            jax.ShapeDtypeStruct(turned, jnp.float32),
            jax.ShapeDtypeStruct(sums, jnp.float32),
        ),
        in_specs=[pl.BlockSpec(memory_space=pltpu.VMEM)] + [some] * 6,
        out_specs=(some,) * 6,
        scratch_shapes=[
            pltpu.VMEM((2, rows, features), q.dtype),
            pltpu.VMEM((2, rows, features), q.dtype),
            pltpu.VMEM(q.shape, q.dtype),
            pltpu.VMEM(k.shape, k.dtype),
            pltpu.VMEM(k.shape, k.dtype),
            pltpu.VMEM(stat, jnp.float32),
            pltpu.VMEM(window, k.dtype),
            pltpu.VMEM(turned, jnp.float32),
            pltpu.VMEM(sums, jnp.float32),
            pltpu.VMEM((2 * B, B), jnp.float32),
            pltpu.SemaphoreType.DMA((6,)),
            pltpu.SemaphoreType.DMA((8,)),
            pltpu.SemaphoreType.DMA((21,)),
            pltpu.SemaphoreType.DMA((21,)),
        ],
        compiler_params=pltpu.CompilerParams(
            collective_id=0, has_side_effects=True, vmem_limit_bytes=VMEM
        ),
    )(docs, q, g, o, k, v, log_total)


def attend_kernel(
    heads, docs_ref, qa_hbm, qb_hbm, ga_hbm, gb_hbm, stat_hbm, window_hbm, dq_hbm, kv_hbm,
    dq_own, dq_other, part_hbm,
    q_ref, g_ref, stat_ref, window_ref, dqt, dqh, part_ref, dka, dva, dkv, bias, starts, bounds, get, put,
):
    column, z, core = place()
    loads = [
        pltpu.make_async_copy(source, target, get.at[n])
        for n, (source, target) in enumerate(
            (
                (stat_hbm, stat_ref),
                (window_hbm.at[:8], window_ref.at[:8]), (window_hbm.at[8:], window_ref.at[8:]),
                (kv_hbm, dkv), (qa_hbm, q_ref.at[0]), (ga_hbm, g_ref.at[0]),
                (dq_hbm.at[:2], dqt.at[:2]),
                (qb_hbm, q_ref.at[1]), (gb_hbm, g_ref.at[1]), (dq_hbm.at[2:], dqt.at[2:]),
            )
        )
    ]
    for load in loads:
        load.start()
    ends = doc_ends(docs_ref)
    window = (column - 1) * 16 * B

    def half_of(b):
        return jnp.where(b % 8 >= 4, 1 - core, core)

    def tile_of(side):
        return z + 4 * (core if side == 0 else 1 - core)

    for block in range(4):
        side, part = divmod(block, 2)
        first = column * 16 * B + tile_of(side) * 2 * B + part * B
        start = doc_start(ends, positions(first))
        starts[block] = start
        low = jnp.min(start).astype(jnp.int32) - window
        last = jnp.max(start).astype(jnp.int32) - window
        b = low // (2 * B)
        bounds[0, block] = jnp.where(low % (2 * B) >= half_of(b) * B + B, b + 1, b)
        b = last // (2 * B)
        bounds[1, block] = jnp.where(last % (2 * B) > half_of(b) * B, b + 1, b)
    dka[...] = jnp.zeros_like(dka)
    dva[...] = jnp.zeros_like(dva)
    for load in loads[:7]:
        load.wait()
    down = lax.rem(z + 3, 4)
    nears = (
        slot(OWN, z, 0),
        jnp.where(z > 0, slot(OWN, down, 1), slot(OWN, 3, 0)),
        jnp.where(z > 0, slot(OWN, down, 0), slot(BEFORE, 3, 1)),
    )
    for n, at in enumerate(nears):
        dka[at] = dkv[n, 0]
        dva[at] = dkv[n, 1]

    @pl.loop(0, 4)
    def _(block):
        side, part = block // 2, block % 2
        here = pl.ds(pl.multiple_of(part * B, B), B)

        @pl.when(block == 2)
        def _():
            for load in loads[7:]:
                load.wait()

        def work(blocks, mask=None):
            at = [slot(b // 8, b % 4, b % 8 // 4) for b in blocks]
            dk, dv, dq = gradients(
                jnp.concatenate([window_ref[n, 0] for n in at], axis=0),
                jnp.concatenate([window_ref[n, 1] for n in at], axis=0),
                [q_ref[side, here, h * W : (h + 1) * W] for h in range(heads)],
                [g_ref[side, here, h * W : (h + 1) * W] for h in range(heads)],
                [stat_ref[side, 0, h : h + 1, here] for h in range(heads)],
                [stat_ref[side, 1, h : h + 1, here] for h in range(heads)],
                mask,
            )
            for n in range(len(at)):
                dva[at[n]] += dv[n * B : (n + 1) * B]
                dka[at[n]] += dk[n * B : (n + 1) * B]
            dqt[block] += dq

        second = jnp.where(side == 0, core, 1 - core)
        end = 7 + z + 4 * second
        skip = jnp.where(second == 1, 8 + z, 16)

        def counted(b):
            return jnp.where(b > skip, b - 1, b)

        def real(n):
            return jnp.where(n >= skip, n + 1, n)

        end = counted(end)
        low = counted(bounds[0, block])
        cut = jnp.minimum(counted(bounds[1, block]), end)
        cut = cut + (end - cut) % 2

        @pl.loop(low, cut)
        def _(n):
            b = real(n)
            key = window + b * 2 * B + half_of(b) * B
            kpos = (key + lax.broadcasted_iota(jnp.int32, (B, B), 0)).astype(jnp.float32)
            bias[...] = jnp.where(kpos >= starts[block], 0.0, -jnp.inf)
            work([b], bias)

        @pl.loop(0, (end - jnp.maximum(low, cut)) // 2)
        def _(n):
            work([real(cut + 2 * n), real(cut + 2 * n + 1)])

        @pl.when(side == 0)
        def _():
            pltpu.make_async_copy(dqt.at[block], dq_own.at[part], put.at[block]).start()

        @pl.when(side == 1)
        def _():
            dqh[part] = dqt[block].astype(jnp.bfloat16)
            pltpu.make_async_copy(dqh.at[part], dq_other.at[part], put.at[block]).start()

    @pl.loop(0, 16)
    def _(s):
        part_ref[s, 0] = (dka[s] * (1.0 / math.sqrt(W))).astype(jnp.bfloat16)
        part_ref[s, 1] = dva[s].astype(jnp.bfloat16)
        pltpu.make_async_copy(part_ref.at[s], part_hbm.at[s], put.at[4 + s]).start()

    for part in range(2):
        pltpu.make_async_copy(dqt.at[part], dq_own.at[part], put.at[part]).wait()
        pltpu.make_async_copy(dqh.at[part], dq_other.at[part], put.at[2 + part]).wait()
    for s in range(16):
        pltpu.make_async_copy(part_ref.at[s], part_hbm.at[s], put.at[4 + s]).wait()


def attend(docs, q, q_other, g, g_other, stat, window, dq, sums):
    rows, features = q.shape
    heads = features // W
    some = pl.BlockSpec(memory_space=pl.ANY)
    both = (2, rows, features)
    turned = (2, W, heads * B)
    return pl.pallas_call(
        functools.partial(attend_kernel, heads),
        out_shape=(
            jax.ShapeDtypeStruct(turned, jnp.float32),
            jax.ShapeDtypeStruct(turned, jnp.bfloat16),
            jax.ShapeDtypeStruct(window.shape, jnp.bfloat16),
        ),
        in_specs=[pl.BlockSpec(memory_space=pltpu.VMEM)] + [some] * 8,
        out_specs=(some,) * 3,
        scratch_shapes=[
            pltpu.VMEM(both, q.dtype),
            pltpu.VMEM(both, q.dtype),
            pltpu.VMEM(stat.shape, stat.dtype),
            pltpu.VMEM(window.shape, window.dtype),
            pltpu.VMEM((4, W, heads * B), jnp.float32),
            pltpu.VMEM(turned, jnp.bfloat16),
            pltpu.VMEM(window.shape, jnp.bfloat16),
            pltpu.VMEM((16, B, W), jnp.float32),
            pltpu.VMEM((16, B, W), jnp.float32),
            pltpu.VMEM(sums.shape, jnp.float32),
            pltpu.VMEM((B, B), jnp.float32),
            pltpu.VMEM((4, 1, B), jnp.float32),
            pltpu.SMEM((2, 4), jnp.int32),
            pltpu.SemaphoreType.DMA((10,)),
            pltpu.SemaphoreType.DMA((20,)),
        ],
        compiler_params=pltpu.CompilerParams(vmem_limit_bytes=VMEM),
        cost_estimate=pl.CostEstimate(
            flops=20 * 10 * heads * B * B * W, bytes_accessed=16 << 20, transcendentals=0
        ),
    )(docs, q, q_other, g, g_other, stat, window, dq, sums)


def return_kernel(
    columns, heads, docs_ref, q_hbm, k_hbm, v_hbm, g_hbm, stat_hbm, dq_own, dq_other, part_ref,
    dq_hbm, dk_hbm, dv_hbm,
    q_ref, k_ref, v_ref, g_ref, stat, dqt, dq_sent, dq_got, dq_out, dk_ref, dv_ref, dka, dva, bias,
    part, across_got, beside_got, beside_sum, later_got, far_got, far_sum, near_sum,
    near_got, final, given_half, local, put, send, recv,
):
    at = Links(columns)
    z, core, up, down, across = at.z, at.core, at.up, at.down, at.across
    sems = (send, recv)
    load = pltpu.make_async_copy(part_ref.at[:8], part.at[:8], local.at[0])
    load_own = pltpu.make_async_copy(part_ref.at[8:], part.at[8:], local.at[1])
    load_dq = pltpu.make_async_copy(dq_other, dq_sent, local.at[2])
    load.start()
    load_own.start()
    load_dq.start()
    loads = [
        pltpu.make_async_copy(source, target, local.at[3 + n])
        for n, (source, target) in enumerate(
            (
                (q_hbm, q_ref), (g_hbm, g_ref), (k_hbm, k_ref), (v_hbm, v_ref),
                (stat_hbm.at[0], stat), (dq_own, dqt),
            )
        )
    ]
    for copy in loads:
        copy.start()
    at.barrier()
    has_next, has_last = at.has_next, at.has_last

    def given(side, zc, j):
        return part.at[slot(side, zc, j)]

    def held(side, zc, j):
        return part[slot(side, zc, j)].astype(jnp.float32)

    far_back = [
        Route(
            sems, j, at.last, given(BEFORE, across, j), across_got.at[j],
            has_last & (z < 2) if j == 0 else has_last,
            has_next & (z < 2) if j == 0 else has_next,
        )
        for j in range(2)
    ]
    side_up = [
        Route(
            sems, 2 + j, at.above, given(BEFORE, up, j), beside_got.at[0, j],
            has_last & (z != 3) if j == 0 else has_last,
            has_last & (z != 0) if j == 0 else has_last,
        )
        for j in range(2)
    ]
    side_down = [
        Route(
            sems, 4 + j, at.below, given(BEFORE, down, j), beside_got.at[1, j],
            has_last & (z == 0) if j == 0 else has_last,
            has_last & (z == 3) if j == 0 else has_last,
        )
        for j in range(2)
    ]
    bulk = [
        Route(sems, 6 + n, at.sibling, dq_sent.at[n], dq_got.at[n]) for n in range(2)
    ]
    back = [
        Route(sems, 8 + j, at.last, beside_sum.at[j], later_got.at[j], has_last, has_next)
        for j in range(2)
    ]
    far_up = Route(sems, 10, at.above, far_sum.at[0], far_got.at[0])
    far_down = Route(sems, 11, at.below, far_sum.at[1], far_got.at[1])
    near_up_0 = Route(sems, 12, at.above, near_sum.at[0], near_got.at[0])
    near_up_1 = Route(sems, 13, at.above, given(OWN, up, 1), near_got.at[1], z == 3, z == 0)
    near_down_0 = Route(sems, 14, at.below, given(OWN, down, 0), near_got.at[2])
    near_down_1 = Route(sems, 15, at.below, near_sum.at[1], near_got.at[3])

    load.wait()
    for copy in (side_down[1], side_up[1], far_back[1], side_up[0], side_down[0], far_back[0]):
        copy.start()
    load_dq.wait()
    for copy in bulk:
        copy.start()
    load_own.wait()
    for copy in loads:
        copy.wait()
    ends = doc_ends(docs_ref)
    tile = at.column * 16 * B + (z + 4 * core) * 2 * B
    dka[...] = jnp.zeros_like(dka)
    dva[...] = jnp.zeros_like(dva)

    def diagonal(n):
        block, b = (n + 1) // 2, n // 2
        here = pl.ds(pl.multiple_of(block * B, B), B)
        there = pl.ds(pl.multiple_of(b * B, B), B)
        pos = positions(tile + block * B)
        bias[...] = hidden(tile + b * B, doc_start(ends, pos), pos)
        dk, dv, dq = gradients(
            k_ref[there],
            v_ref[there],
            [q_ref[here, h * W : (h + 1) * W] for h in range(heads)],
            [g_ref[here, h * W : (h + 1) * W] for h in range(heads)],
            [stat[0, h : h + 1, here] for h in range(heads)],
            [stat[1, h : h + 1, here] for h in range(heads)],
            bias,
        )
        dka[b] += dk
        dva[b] += dv
        dqt[block] += dq

    pl.loop(0, 3)(diagonal)

    @pl.when(has_last)
    def _():
        for copy in side_up + side_down:
            copy.arrived()
        for j in range(2):
            final[j] = held(BEFORE, z, j)
        final[1] += beside_got[0, 1].astype(jnp.float32) + beside_got[1, 1].astype(jnp.float32)

        @pl.when(z != 0)
        def _():
            final[0] += beside_got[0, 0].astype(jnp.float32)

        @pl.when(z == 3)
        def _():
            final[0] += beside_got[1, 0].astype(jnp.float32)

        beside_sum[...] = final[...].astype(jnp.bfloat16)
        for copy in back:
            copy.start()

    def add_across(j):
        far_back[j].make(across_got.at[j]).wait_recv()
        final[j] += across_got[j].astype(jnp.float32)

    for j in range(2):
        final[j] = held(OWN, across, j)
        pl.when(far_back[j].gets)(functools.partial(add_across, j))
        far_sum[j] = final[j].astype(jnp.bfloat16)
    for copy in (far_up, far_down, near_down_0, near_up_1):
        copy.start()
    for copy in bulk:
        copy.arrived()
    eye = identity(B)
    for block in range(2):
        for h in range(heads):
            rows = slice(h * B, (h + 1) * B)
            total = dqt[block, :, rows] + dq_got[block, :, rows].astype(jnp.float32)
            rounded = (total * (1.0 / math.sqrt(W))).astype(jnp.bfloat16)
            turned = nt(eye, rounded).astype(jnp.bfloat16)
            dq_out[block * B : (block + 1) * B, h * W : (h + 1) * W] = turned
    out_q = pltpu.make_async_copy(dq_out, dq_hbm, put.at[0])
    out_q.start()
    far_up.arrived()
    near_sum[0] = (held(OWN, up, 0) + far_got[0].astype(jnp.float32)).astype(jnp.bfloat16)
    near_up_0.start()
    far_down.arrived()
    near_sum[1] = (held(OWN, down, 1) + far_got[1].astype(jnp.float32)).astype(jnp.bfloat16)
    near_down_1.start()
    near_down_0.arrived()
    near_up_0.arrived()
    final[0] = (
        held(OWN, z, 0) + near_got[0].astype(jnp.float32) + near_got[2].astype(jnp.float32)
    )
    near_down_1.arrived()
    final[1] = held(OWN, z, 1) + near_got[3].astype(jnp.float32)

    @pl.when(z == 0)
    def _():
        near_up_1.make(near_got.at[1]).wait_recv()
        final[1] += near_got[1].astype(jnp.float32)

    @pl.when(has_next)
    def _():
        for j in range(2):
            back[j].make(later_got.at[j]).wait_recv()
            final[j] += later_got[j].astype(jnp.float32)

    given_half[...] = final[1 - core].astype(jnp.bfloat16)
    give_k = Route(sems, 16, at.sibling, given_half.at[0], dk_ref.at[B:])
    give_v = Route(sems, 17, at.sibling, given_half.at[1], dv_ref.at[B:])
    give_k.start()
    give_v.start()
    scale = 1.0 / math.sqrt(W)
    dk_ref[:B] = (final[core, 0] + dka[0] * scale).astype(jnp.bfloat16)
    dv_ref[:B] = (final[core, 1] + dva[0]).astype(jnp.bfloat16)
    give_k.arrived()
    give_v.arrived()
    dk_ref[B:] = (dk_ref[B:].astype(jnp.float32) + dka[1] * scale).astype(jnp.bfloat16)
    dv_ref[B:] = (dv_ref[B:].astype(jnp.float32) + dva[1]).astype(jnp.bfloat16)
    out_k = pltpu.make_async_copy(dk_ref, dk_hbm, put.at[1])
    out_v = pltpu.make_async_copy(dv_ref, dv_hbm, put.at[2])
    out_k.start()
    out_v.start()
    for copy in (out_q, out_k, out_v):
        copy.wait()
    for copy in (
        far_back + side_up + side_down + bulk + back
        + [far_up, far_down, near_up_0, near_up_1, near_down_0, near_down_1, give_k, give_v]
    ):
        copy.sent()


def give_back(columns, docs, q, k, v, g, stat, dq_own, dq_other, part):
    rows, features = q.shape
    heads = features // W
    some = pl.BlockSpec(memory_space=pl.ANY)
    vmem = pl.BlockSpec(memory_space=pltpu.VMEM)
    block = (2, B, W)
    return pl.pallas_call(
        functools.partial(return_kernel, columns, heads),
        out_shape=(
            jax.ShapeDtypeStruct((rows, features), jnp.bfloat16),
            jax.ShapeDtypeStruct((rows, W), jnp.bfloat16),
            jax.ShapeDtypeStruct((rows, W), jnp.bfloat16),
        ),
        in_specs=[vmem] + [some] * 8,
        out_specs=(some,) * 3,
        scratch_shapes=[
            pltpu.VMEM(q.shape, q.dtype),
            pltpu.VMEM(k.shape, k.dtype),
            pltpu.VMEM(v.shape, v.dtype),
            pltpu.VMEM(g.shape, g.dtype),
            pltpu.VMEM(stat.shape[1:], stat.dtype),
            pltpu.VMEM(dq_own.shape, dq_own.dtype),
            pltpu.VMEM(dq_other.shape, dq_other.dtype),
            pltpu.VMEM(dq_other.shape, dq_other.dtype),
            pltpu.VMEM(q.shape, jnp.bfloat16),
            pltpu.VMEM((rows, W), jnp.bfloat16),
            pltpu.VMEM((rows, W), jnp.bfloat16),
            pltpu.VMEM((2, B, W), jnp.float32),
            pltpu.VMEM((2, B, W), jnp.float32),
            pltpu.VMEM((B, B), jnp.float32),
            pltpu.VMEM((16, *block), jnp.bfloat16),
            pltpu.VMEM((2, *block), jnp.bfloat16),
            pltpu.VMEM((2, 2, *block), jnp.bfloat16),
            pltpu.VMEM((2, *block), jnp.bfloat16),
            pltpu.VMEM((2, *block), jnp.bfloat16),
            pltpu.VMEM((2, *block), jnp.bfloat16),
            pltpu.VMEM((2, *block), jnp.bfloat16),
            pltpu.VMEM((2, *block), jnp.bfloat16),
            pltpu.VMEM((4, *block), jnp.bfloat16),
            pltpu.VMEM((2, *block), jnp.float32),
            pltpu.VMEM(block, jnp.bfloat16),
            pltpu.SemaphoreType.DMA((9,)),
            pltpu.SemaphoreType.DMA((3,)),
            pltpu.SemaphoreType.DMA((18,)),
            pltpu.SemaphoreType.DMA((18,)),
        ],
        compiler_params=pltpu.CompilerParams(
            collective_id=1, has_side_effects=True, vmem_limit_bytes=VMEM
        ),
    )(docs, q, k, v, g, stat, dq_own, dq_other, part)


def publish_kernel(*refs):
    sources, targets, held, get, put = refs[:3], refs[3:6], refs[6:9], refs[9], refs[10]
    pieces = []
    for source, target, mid in zip(sources, targets, held):
        rows = min(source.shape[0], 128 * 1024 // source.shape[1])
        for at in range(0, source.shape[0], rows):
            here = slice(at, at + rows)
            n = len(pieces)
            pieces.append(
                (
                    pltpu.make_async_copy(source.at[here], mid.at[here], get.at[n]),
                    pltpu.make_async_copy(mid.at[here], target.at[here], put.at[n]),
                )
            )
    for into, _ in pieces:
        into.start()
    for into, out in pieces:
        into.wait()
        out.start()
    for _, out in pieces:
        out.wait()


def publish(*results):
    some = pl.BlockSpec(memory_space=pl.ANY)
    return pl.pallas_call(
        publish_kernel,
        out_shape=tuple(jax.ShapeDtypeStruct(x.shape, x.dtype) for x in results),
        in_specs=[some] * 3,
        out_specs=(some,) * 3,
        scratch_shapes=[pltpu.VMEM(x.shape, x.dtype) for x in results]
        + [pltpu.SemaphoreType.DMA((6,))] * 2,
        compiler_params=pltpu.CompilerParams(vmem_limit_bytes=VMEM),
    )(*results)


def solution(mesh):
    columns = mesh.shape["ctx"] // 2

    def on_device(q, k, v, o, g, log_total, doc_lengths):
        docs = doc_lengths[None, :]
        q_other, g_other, stat, window, dq, sums = gather(columns, docs, q, g, o, k, v, log_total)
        dq_own, dq_other, part = attend(docs, q, q_other, g, g_other, stat, window, dq, sums)
        dq, dk, dv = give_back(columns, docs, q, k, v, g, stat, dq_own, dq_other, part)
        return publish(dq, dk, dv)

    rows = P(("ctx", "section"), None)
    return jax.shard_map(
        on_device,
        mesh=mesh,
        in_specs=(rows, rows, rows, rows, rows, P(None, ("ctx", "section")), P()),
        out_specs=(rows, rows, rows),
        check_vma=False,
    )
```

```python
import functools
import math

import jax
import jax.numpy as jnp
from jax import lax
from jax.experimental import pallas as pl
from jax.experimental.pallas import tpu as pltpu
from jax.sharding import PartitionSpec as P

MESH = pl.DeviceIdType.MESH
W = 128
B = 256
VMEM = 58 << 20
LOG2E = math.log2(math.e)
OWN, BEFORE = 1, 0


def nn(a, b):
    return jnp.dot(a, b, preferred_element_type=jnp.float32)


def nt(a, b):
    return lax.dot_general(a, b, (((1,), (1,)), ((), ())), preferred_element_type=jnp.float32)


def place():
    ctx = lax.axis_index("ctx")
    return ctx // 2, lax.axis_index("section"), ctx % 2


def slot(side, z, j):
    return side * 8 + z * 2 + j


def doc_ends(docs_ref):
    lengths = docs_ref[...].astype(jnp.float32)
    docs = lengths.shape[1]
    upto = lax.broadcasted_iota(jnp.int32, (docs, docs), 1) <= lax.broadcasted_iota(
        jnp.int32, (docs, docs), 0
    )
    return jnp.sum(jnp.where(upto, lengths, 0.0), axis=1, keepdims=True)


def positions(first):
    return first.astype(jnp.float32) + lax.broadcasted_iota(jnp.int32, (1, B), 1).astype(
        jnp.float32
    )


def doc_start(ends, pos):
    return jnp.max(jnp.where(ends <= pos, ends, 0.0), axis=0, keepdims=True)


def hidden(key, start, pos):
    kpos = (key + lax.broadcasted_iota(jnp.int32, (B, B), 0)).astype(jnp.float32)
    return jnp.where((kpos >= start) & (kpos <= pos), 0.0, -jnp.inf)


def identity(n):
    at = [lax.broadcasted_iota(jnp.int32, (n, n), d) for d in range(2)]
    return (at[0] == at[1]).astype(jnp.bfloat16)


def gradients(k, v, qs, gs, logs, deltas, bias=None):
    ps, ds = [], []
    for q, g, log, delta in zip(qs, gs, logs, deltas):
        x = nt(k, q) * (LOG2E / math.sqrt(W)) - log
        if bias is not None:
            x = x + bias[...]
        p = jnp.exp2(x)
        d = p * (nt(v, g) - delta)
        ps.append(p.astype(jnp.bfloat16))
        ds.append(d.astype(jnp.bfloat16))
    dh = jnp.concatenate(ds, axis=1)
    dv = nn(jnp.concatenate(ps, axis=1), jnp.concatenate(gs, axis=0))
    dk = nn(dh, jnp.concatenate(qs, axis=0))
    return dk, dv, nn(k.T, dh)


class Links:
    def __init__(self, columns):
        self.column, self.z, self.core = place()
        ctx = lax.axis_index("ctx")
        self.up = lax.rem(self.z + 1, 4)
        self.down = lax.rem(self.z + 3, 4)
        self.across = lax.rem(self.z + 2, 4)
        self.sibling = (ctx + 1 - 2 * self.core, self.z)
        self.above = (ctx, self.up)
        self.below = (ctx, self.down)
        self.has_next = self.column < columns - 1
        self.has_last = self.column > 0
        self.next = (jnp.where(self.has_next, ctx + 2, ctx), self.z)
        self.last = (jnp.where(self.has_last, ctx - 2, ctx), self.z)
        self.next_across = (self.next[0], self.across)
        self.last_across = (self.last[0], self.across)

    def barrier(self, straight=False):
        barrier = pltpu.get_barrier_semaphore()

        def greet(*devices):
            for device in devices:
                pl.semaphore_signal(barrier, inc=1, device_id=device, device_id_type=MESH)

        greet(self.sibling, self.above, self.below)
        later = (self.next, self.next_across) if straight else (self.next,)
        earlier = (self.last, self.last_across) if straight else (self.last,)
        pl.when(self.has_next)(lambda: greet(*later))
        pl.when(self.has_last)(lambda: greet(*earlier))
        columns = self.has_next.astype(jnp.int32) + self.has_last.astype(jnp.int32)
        pl.semaphore_wait(barrier, 3 + len(later) * columns)


class Route:
    def __init__(self, sems, index, device, source, target, sends=True, gets=True, arrival=None):
        self.sends, self.gets = sends, gets
        landed = target if arrival is None else arrival
        send, recv = sems[0].at[index], sems[1].at[index]
        self.make = lambda end: pltpu.make_async_remote_copy(
            source, end, send, recv, device_id=device, device_id_type=MESH
        )
        self.target, self.landed = target, landed

    @staticmethod
    def only(condition, act):
        if condition is True:
            act()
        else:
            pl.when(condition)(act)

    def start(self):
        self.only(self.sends, lambda: self.make(self.target).start())

    def arrived(self):
        self.only(self.gets, lambda: self.make(self.landed).wait_recv())

    def sent(self):
        self.only(self.sends, lambda: self.make(self.target).wait_send())


def gather_kernel(
    columns, heads, docs_ref, q_ref, g_ref, o_ref, k_ref, v_ref, log_ref,
    q_other, g_other, stat_both, window_out, dq_out, kv_out,
    q_both, g_both, o_vmem, k_own, v_own, stat, window, dqt, dkv, bias, local, put, send, recv,
):
    at = Links(columns)
    z, core, up, down, across = at.z, at.core, at.up, at.down, at.across
    sems = (send, recv)
    mine = window.at[slot(OWN, z, core)]
    loads = [
        pltpu.make_async_copy(source, target, local.at[n])
        for n, (source, target) in enumerate(
            (
                (k_ref, k_own), (v_ref, v_own), (q_ref, q_both.at[0]), (g_ref, g_both.at[0]),
                (o_ref, o_vmem), (log_ref, stat.at[0, 0]),
            )
        )
    ]
    for copy in loads:
        copy.start()

    @pl.when(at.column == 0)
    def _():
        window[slot(BEFORE, 3, 1)] = jnp.zeros((2, B, W), window.dtype)

    at.barrier()

    theirs = window.at[slot(OWN, z, 1 - core)]
    swap_k = Route(sems, 0, at.sibling, k_own.at[B:], mine.at[0], arrival=theirs.at[0])
    swap_v = Route(sems, 1, at.sibling, v_own.at[B:], mine.at[1], arrival=theirs.at[1])
    loads[0].wait()
    loads[1].wait()
    swap_k.start()
    swap_v.start()
    mine[0] = k_own[:B]
    mine[1] = v_own[:B]
    rows = q_ref.shape[0]
    bulk = []
    for part in range(2):
        some = slice(part * rows // 2, (part + 1) * rows // 2)
        bulk.append(Route(sems, 2 + part, at.sibling, q_both.at[0, some], q_both.at[1, some]))
        bulk.append(Route(sems, 4 + part, at.sibling, g_both.at[0, some], g_both.at[1, some]))

    def passed(index, device, side, sent, j, got, sends=True, gets=True):
        there = window.at[slot(side, sent, j)]
        return Route(sems, index, device, there, there, sends, gets, window.at[slot(side, got, j)])

    up_0 = passed(6, at.above, OWN, z, 0, down)
    up_1 = passed(7, at.above, OWN, z, 1, down)
    down_0 = passed(8, at.below, OWN, z, 0, up)
    down_1 = passed(9, at.below, OWN, z, 1, up, z == 0, z == 3)
    far_0 = passed(10, at.below, OWN, up, 0, across)
    far_1 = passed(11, at.above, OWN, down, 1, across)

    def later(index, zc, j, when=True):
        here = window.at[slot(OWN, zc, j)]
        there = window.at[slot(BEFORE, zc, j)]
        sends = at.has_next if when is True else at.has_next & when
        gets = at.has_last if when is True else at.has_last & when
        return Route(sems, index, at.next, here, there, sends, gets)

    next_0 = later(12, z, 0)
    next_1 = later(13, z, 1)
    next_far_0 = later(14, across, 0, z < 2)
    next_far_1 = later(15, across, 1)
    last = at.has_last
    before_up_0 = passed(16, at.above, BEFORE, z, 0, down, last & (z == 3), last & (z == 0))
    before_up_1 = passed(17, at.above, BEFORE, z, 1, down, last, last)
    before_down_0 = passed(18, at.below, BEFORE, z, 0, up, last & (z != 0), last & (z != 3))
    before_down_1 = passed(19, at.below, BEFORE, z, 1, up, last, last)
    stats = Route(sems, 20, at.sibling, stat.at[0], stat.at[1])

    swap_k.arrived()
    swap_v.arrived()
    for copy in (up_1, down_0, next_1):
        copy.start()
    for copy in loads[2:]:
        copy.wait()

    ones = jnp.ones((8, W), jnp.bfloat16)
    for h in range(heads):
        cols = slice(h * W, (h + 1) * W)
        product = g_both[0, :, cols].astype(jnp.float32) * o_vmem[:, cols].astype(jnp.float32)
        high = product.astype(jnp.bfloat16)
        low = (product - high.astype(jnp.float32)).astype(jnp.bfloat16)
        total = nt(ones, high) + nt(ones, low)
        stat[0, 1, h : h + 1, :] = total[0:1]
    stat[0, 0] = stat[0, 0] * LOG2E
    stats.start()
    for copy in (next_0, up_0, down_1):
        copy.start()
    for copy in bulk:
        copy.start()

    ends = doc_ends(docs_ref)
    column = at.column * 16 * B
    dkv[...] = jnp.zeros_like(dkv)
    dqt[...] = jnp.zeros_like(dqt)

    def products(side, part, k, v, mask):
        here = pl.ds(pl.multiple_of(part * B, B), B)
        return gradients(
            k, v,
            [q_both[side, here, h * W : (h + 1) * W] for h in range(heads)],
            [g_both[side, here, h * W : (h + 1) * W] for h in range(heads)],
            [stat[side, 0, h : h + 1, here] for h in range(heads)],
            [stat[side, 1, h : h + 1, here] for h in range(heads)],
            mask,
        )

    up_1.arrived()
    far_1.start()
    down_0.arrived()
    far_0.start()
    next_1.arrived()
    before_down_1.start()
    before_up_1.start()
    next_0.arrived()
    before_down_0.start()
    before_up_0.start()

    near_4 = jnp.where(z > 0, slot(OWN, down, 1), slot(OWN, 3, 0))
    near_0 = jnp.where(z > 0, slot(OWN, down, 0), slot(BEFORE, 3, 1))

    def half_of(tile):
        return jnp.where((tile + 8) % 8 >= 4, 1 - core, core)

    def near(side, part, tile, keys, key_tiles, out):
        start = doc_start(ends, positions(column + tile * 2 * B + part * B))
        for n, key_tile in enumerate(key_tiles):
            key = column + key_tile * 2 * B + half_of(key_tile) * B
            kpos = (key + lax.broadcasted_iota(jnp.int32, (B, B), 0)).astype(jnp.float32)
            bias[n * B : (n + 1) * B] = jnp.where(kpos >= start, 0.0, -jnp.inf)
        dk, dv, dq = products(
            side, part,
            jnp.concatenate([window[n, 0] for n in keys], axis=0),
            jnp.concatenate([window[n, 1] for n in keys], axis=0),
            bias.at[: len(keys) * B],
        )
        for n in range(len(keys)):
            dkv[out + n, 0] += dk[n * B : (n + 1) * B]
            dkv[out + n, 1] += dv[n * B : (n + 1) * B]
        dqt[side * 2 + part] += dq

    puts = [
        pltpu.make_async_copy(source, target, put.at[n])
        for n, (source, target) in enumerate(
            (
                (q_both.at[1], q_other), (g_both.at[1], g_other), (stat, stat_both),
                (window.at[8:], window_out.at[8:]), (dqt.at[:2], dq_out.at[:2]),
                (window.at[:8], window_out.at[:8]), (dqt.at[2:], dq_out.at[2:]), (dkv, kv_out),
            )
        )
    ]

    def sibling_here():
        for copy in bulk:
            copy.arrived()
        stats.arrived()

    flip = (core == 0) & (z == 0)

    @pl.loop(0, 4)
    def _(n):
        @pl.when(n == 0)
        def _():
            up_0.arrived()
            pl.when(flip)(sibling_here)

        @pl.when(n == 1)
        def _():
            far_0.arrived()
            next_far_0.start()
            far_1.arrived()
            next_far_1.start()

        @pl.when(n == 2)
        def _():
            down_1.arrived()
            pl.when(jnp.logical_not(flip))(sibling_here)
            pl.when(z == 0)(before_up_1.arrived)
            for copy in puts[:4]:
                copy.start()

        side, part = jnp.where(flip, 1 - n // 2, n // 2), n % 2

        @pl.when(side == core)
        def _():
            near(side, part, z, [near_0], [z - 1], 2)

        @pl.when(side != core)
        def _():
            near(side, part, z + 4, [slot(OWN, z, 0), near_4], [z, z + 3], 0)

    for copy in (puts[4], puts[6], puts[7]):
        copy.start()
    pl.when(z != 0)(before_up_1.arrived)
    for copy in (before_up_0, before_down_0, before_down_1, next_far_0, next_far_1):
        copy.arrived()
    puts[5].start()
    for copy in (
        [swap_k, swap_v, up_0, up_1, down_0, down_1, far_0, far_1, next_0, next_1, next_far_0]
        + [next_far_1, before_up_0, before_up_1, before_down_0, before_down_1, stats]
        + bulk
    ):
        copy.sent()
    for copy in puts:
        copy.wait()


def gather(columns, docs, q, g, o, k, v, log_total):
    rows, features = q.shape
    heads = features // W
    some = pl.BlockSpec(memory_space=pl.ANY)
    window = (16, 2, B, W)
    stat = (2, 2, heads, rows)
    turned = (4, W, heads * B)
    sums = (3, 2, B, W)
    return pl.pallas_call(
        functools.partial(gather_kernel, columns, heads),
        out_shape=(
            jax.ShapeDtypeStruct(q.shape, q.dtype),
            jax.ShapeDtypeStruct(q.shape, q.dtype),
            jax.ShapeDtypeStruct(stat, jnp.float32),
            jax.ShapeDtypeStruct(window, k.dtype),
            jax.ShapeDtypeStruct(turned, jnp.float32),
            jax.ShapeDtypeStruct(sums, jnp.float32),
        ),
        in_specs=[pl.BlockSpec(memory_space=pltpu.VMEM)] + [some] * 6,
        out_specs=(some,) * 6,
        scratch_shapes=[
            pltpu.VMEM((2, rows, features), q.dtype),
            pltpu.VMEM((2, rows, features), q.dtype),
            pltpu.VMEM(q.shape, q.dtype),
            pltpu.VMEM(k.shape, k.dtype),
            pltpu.VMEM(k.shape, k.dtype),
            pltpu.VMEM(stat, jnp.float32),
            pltpu.VMEM(window, k.dtype),
            pltpu.VMEM(turned, jnp.float32),
            pltpu.VMEM(sums, jnp.float32),
            pltpu.VMEM((2 * B, B), jnp.float32),
            pltpu.SemaphoreType.DMA((6,)),
            pltpu.SemaphoreType.DMA((8,)),
            pltpu.SemaphoreType.DMA((21,)),
            pltpu.SemaphoreType.DMA((21,)),
        ],
        compiler_params=pltpu.CompilerParams(
            collective_id=0, has_side_effects=True, vmem_limit_bytes=VMEM
        ),
    )(docs, q, g, o, k, v, log_total)


def attend_kernel(
    heads, docs_ref, qa_hbm, qb_hbm, ga_hbm, gb_hbm, stat_hbm, window_hbm, dq_hbm, kv_hbm,
    dq_own, dq_other, part_hbm,
    q_ref, g_ref, stat_ref, window_ref, dqt, dqh, part_ref, dka, dva, dkv, bias, starts, bounds, get, put,
):
    column, z, core = place()
    loads = [
        pltpu.make_async_copy(source, target, get.at[n])
        for n, (source, target) in enumerate(
            (
                (stat_hbm, stat_ref),
                (window_hbm.at[:8], window_ref.at[:8]), (window_hbm.at[8:], window_ref.at[8:]),
                (kv_hbm, dkv), (qa_hbm, q_ref.at[0]), (ga_hbm, g_ref.at[0]),
                (qb_hbm, q_ref.at[1]), (gb_hbm, g_ref.at[1]), (dq_hbm.at[2:], dqt.at[2:]),
            )
        )
    ]
    for load in loads:
        load.start()
    ends = doc_ends(docs_ref)
    window = (column - 1) * 16 * B

    def half_of(b):
        return jnp.where(b % 8 >= 4, 1 - core, core)

    def tile_of(side):
        return z + 4 * (core if side == 0 else 1 - core)

    for block in range(4):
        side, part = divmod(block, 2)
        first = column * 16 * B + tile_of(side) * 2 * B + part * B
        start = doc_start(ends, positions(first))
        starts[block] = start
        low = jnp.min(start).astype(jnp.int32) - window
        last = jnp.max(start).astype(jnp.int32) - window
        b = low // (2 * B)
        bounds[0, block] = jnp.where(low % (2 * B) >= half_of(b) * B + B, b + 1, b)
        b = last // (2 * B)
        bounds[1, block] = jnp.where(last % (2 * B) > half_of(b) * B, b + 1, b)
    dka[...] = jnp.zeros_like(dka)
    dva[...] = jnp.zeros_like(dva)
    dqt[:2] = jnp.zeros((2, *dqt.shape[1:]), dqt.dtype)
    for load in loads[:6]:
        load.wait()
    down = lax.rem(z + 3, 4)
    nears = (
        slot(OWN, z, 0),
        jnp.where(z > 0, slot(OWN, down, 1), slot(OWN, 3, 0)),
        jnp.where(z > 0, slot(OWN, down, 0), slot(BEFORE, 3, 1)),
    )
    for n, at in enumerate(nears):
        dka[at] = dkv[n, 0]
        dva[at] = dkv[n, 1]

    @pl.loop(0, 4)
    def _(block):
        side, part = block // 2, block % 2
        here = pl.ds(pl.multiple_of(part * B, B), B)

        @pl.when(block == 2)
        def _():
            for load in loads[6:]:
                load.wait()

        def work(blocks, mask=None):
            at = [slot(b // 8, b % 4, b % 8 // 4) for b in blocks]
            dk, dv, dq = gradients(
                jnp.concatenate([window_ref[n, 0] for n in at], axis=0),
                jnp.concatenate([window_ref[n, 1] for n in at], axis=0),
                [q_ref[side, here, h * W : (h + 1) * W] for h in range(heads)],
                [g_ref[side, here, h * W : (h + 1) * W] for h in range(heads)],
                [stat_ref[side, 0, h : h + 1, here] for h in range(heads)],
                [stat_ref[side, 1, h : h + 1, here] for h in range(heads)],
                mask,
            )
            for n in range(len(at)):
                dva[at[n]] += dv[n * B : (n + 1) * B]
                dka[at[n]] += dk[n * B : (n + 1) * B]
            dqt[block] += dq

        second = jnp.where(side == 0, core, 1 - core)
        end = 7 + z + 4 * second
        skip = jnp.where(second == 1, 8 + z, 16)

        def counted(b):
            return jnp.where(b > skip, b - 1, b)

        def real(n):
            return jnp.where(n >= skip, n + 1, n)

        end = counted(end)
        low = counted(bounds[0, block])
        cut = jnp.minimum(counted(bounds[1, block]), end)
        cut = cut + (end - cut) % 2

        @pl.loop(low, cut)
        def _(n):
            b = real(n)
            key = window + b * 2 * B + half_of(b) * B
            kpos = (key + lax.broadcasted_iota(jnp.int32, (B, B), 0)).astype(jnp.float32)
            bias[...] = jnp.where(kpos >= starts[block], 0.0, -jnp.inf)
            work([b], bias)

        @pl.loop(0, (end - jnp.maximum(low, cut)) // 2)
        def _(n):
            work([real(cut + 2 * n), real(cut + 2 * n + 1)])

        @pl.when(side == 0)
        def _():
            pltpu.make_async_copy(dqt.at[block], dq_own.at[part], put.at[block]).start()

        @pl.when(side == 1)
        def _():
            dqh[part] = dqt[block].astype(jnp.bfloat16)
            pltpu.make_async_copy(dqh.at[part], dq_other.at[part], put.at[block]).start()

    @pl.loop(0, 16)
    def _(s):
        part_ref[s, 0] = (dka[s] * (1.0 / math.sqrt(W))).astype(jnp.bfloat16)
        part_ref[s, 1] = dva[s].astype(jnp.bfloat16)
        pltpu.make_async_copy(part_ref.at[s], part_hbm.at[s], put.at[4 + s]).start()

    for part in range(2):
        pltpu.make_async_copy(dqt.at[part], dq_own.at[part], put.at[part]).wait()
        pltpu.make_async_copy(dqh.at[part], dq_other.at[part], put.at[2 + part]).wait()
    for s in range(16):
        pltpu.make_async_copy(part_ref.at[s], part_hbm.at[s], put.at[4 + s]).wait()


def attend(docs, q, q_other, g, g_other, stat, window, dq, sums):
    rows, features = q.shape
    heads = features // W
    some = pl.BlockSpec(memory_space=pl.ANY)
    both = (2, rows, features)
    turned = (2, W, heads * B)
    return pl.pallas_call(
        functools.partial(attend_kernel, heads),
        out_shape=(
            jax.ShapeDtypeStruct(turned, jnp.float32),
            jax.ShapeDtypeStruct(turned, jnp.bfloat16),
            jax.ShapeDtypeStruct(window.shape, jnp.bfloat16),
        ),
        in_specs=[pl.BlockSpec(memory_space=pltpu.VMEM)] + [some] * 8,
        out_specs=(some,) * 3,
        scratch_shapes=[
            pltpu.VMEM(both, q.dtype),
            pltpu.VMEM(both, q.dtype),
            pltpu.VMEM(stat.shape, stat.dtype),
            pltpu.VMEM(window.shape, window.dtype),
            pltpu.VMEM((4, W, heads * B), jnp.float32),
            pltpu.VMEM(turned, jnp.bfloat16),
            pltpu.VMEM(window.shape, jnp.bfloat16),
            pltpu.VMEM((16, B, W), jnp.float32),
            pltpu.VMEM((16, B, W), jnp.float32),
            pltpu.VMEM(sums.shape, jnp.float32),
            pltpu.VMEM((B, B), jnp.float32),
            pltpu.VMEM((4, 1, B), jnp.float32),
            pltpu.SMEM((2, 4), jnp.int32),
            pltpu.SemaphoreType.DMA((9,)),
            pltpu.SemaphoreType.DMA((20,)),
        ],
        compiler_params=pltpu.CompilerParams(vmem_limit_bytes=VMEM),
        cost_estimate=pl.CostEstimate(
            flops=20 * 10 * heads * B * B * W, bytes_accessed=16 << 20, transcendentals=0
        ),
    )(docs, q, q_other, g, g_other, stat, window, dq, sums)


def return_kernel(
    columns, heads, docs_ref, q_hbm, k_hbm, v_hbm, g_hbm, stat_hbm, dq_near, dq_own, dq_other, part_ref,
    dq_hbm, dk_hbm, dv_hbm,
    q_ref, k_ref, v_ref, g_ref, stat, dqt, dqn, dq_got, dq_out, dk_ref, dv_ref, dka, dva, bias,
    part, across_got, beside_got, beside_sum, later_got, far_got, far_sum, near_sum,
    near_got, final, given_half, local, put, send, recv,
):
    at = Links(columns)
    z, core, up, down, across = at.z, at.core, at.up, at.down, at.across
    sems = (send, recv)
    load = pltpu.make_async_copy(part_ref.at[:8], part.at[:8], local.at[0])
    load_own = pltpu.make_async_copy(part_ref.at[8:], part.at[8:], local.at[1])
    load_dq = pltpu.make_async_copy(dq_near.at[:2], dqn, local.at[2])
    load.start()
    load_own.start()
    load_dq.start()
    loads = [
        pltpu.make_async_copy(source, target, local.at[3 + n])
        for n, (source, target) in enumerate(
            (
                (q_hbm, q_ref), (g_hbm, g_ref), (k_hbm, k_ref), (v_hbm, v_ref),
                (stat_hbm.at[0], stat), (dq_own, dqt),
            )
        )
    ]
    for copy in loads:
        copy.start()
    at.barrier()
    has_next, has_last = at.has_next, at.has_last

    def given(side, zc, j):
        return part_ref.at[slot(side, zc, j)]

    def held(side, zc, j):
        return part[slot(side, zc, j)].astype(jnp.float32)

    far_back = [
        Route(
            sems, j, at.last, given(BEFORE, across, j), across_got.at[j],
            has_last & (z < 2) if j == 0 else has_last,
            has_next & (z < 2) if j == 0 else has_next,
        )
        for j in range(2)
    ]
    side_up = [
        Route(
            sems, 2 + j, at.above, given(BEFORE, up, j), beside_got.at[0, j],
            has_last & (z != 3) if j == 0 else has_last,
            has_last & (z != 0) if j == 0 else has_last,
        )
        for j in range(2)
    ]
    side_down = [
        Route(
            sems, 4 + j, at.below, given(BEFORE, down, j), beside_got.at[1, j],
            has_last & (z == 0) if j == 0 else has_last,
            has_last & (z == 3) if j == 0 else has_last,
        )
        for j in range(2)
    ]
    bulk = [
        Route(sems, 6 + n, at.sibling, dq_other.at[n], dq_got.at[n]) for n in range(2)
    ]
    back = [
        Route(sems, 8 + j, at.last, beside_sum.at[j], later_got.at[j], has_last, has_next)
        for j in range(2)
    ]
    far_up = Route(sems, 10, at.above, far_sum.at[0], far_got.at[0])
    far_down = Route(sems, 11, at.below, far_sum.at[1], far_got.at[1])
    near_up_0 = Route(sems, 12, at.above, near_sum.at[0], near_got.at[0])
    near_up_1 = Route(sems, 13, at.above, given(OWN, up, 1), near_got.at[1], z == 3, z == 0)
    near_down_0 = Route(sems, 14, at.below, given(OWN, down, 0), near_got.at[2])
    near_down_1 = Route(sems, 15, at.below, near_sum.at[1], near_got.at[3])

    for copy in (side_down[1], side_up[1], far_back[1], side_up[0], side_down[0], far_back[0]):
        copy.start()
    for copy in bulk:
        copy.start()
    for copy in (load, load_own, load_dq, *loads):
        copy.wait()
    ends = doc_ends(docs_ref)
    tile = at.column * 16 * B + (z + 4 * core) * 2 * B
    dka[...] = jnp.zeros_like(dka)
    dva[...] = jnp.zeros_like(dva)

    def diagonal(n):
        block, b = (n + 1) // 2, n // 2
        here = pl.ds(pl.multiple_of(block * B, B), B)
        there = pl.ds(pl.multiple_of(b * B, B), B)
        pos = positions(tile + block * B)
        bias[...] = hidden(tile + b * B, doc_start(ends, pos), pos)
        dk, dv, dq = gradients(
            k_ref[there],
            v_ref[there],
            [q_ref[here, h * W : (h + 1) * W] for h in range(heads)],
            [g_ref[here, h * W : (h + 1) * W] for h in range(heads)],
            [stat[0, h : h + 1, here] for h in range(heads)],
            [stat[1, h : h + 1, here] for h in range(heads)],
            bias,
        )
        dka[b] += dk
        dva[b] += dv
        dqt[block] += dq

    pl.loop(0, 3)(diagonal)

    @pl.when(has_last)
    def _():
        for copy in side_up + side_down:
            copy.arrived()
        for j in range(2):
            final[j] = held(BEFORE, z, j)
        final[1] += beside_got[0, 1].astype(jnp.float32) + beside_got[1, 1].astype(jnp.float32)

        @pl.when(z != 0)
        def _():
            final[0] += beside_got[0, 0].astype(jnp.float32)

        @pl.when(z == 3)
        def _():
            final[0] += beside_got[1, 0].astype(jnp.float32)

        beside_sum[...] = final[...].astype(jnp.bfloat16)
        for copy in back:
            copy.start()

    def add_across(j):
        far_back[j].make(across_got.at[j]).wait_recv()
        final[j] += across_got[j].astype(jnp.float32)

    for j in range(2):
        final[j] = held(OWN, across, j)
        pl.when(far_back[j].gets)(functools.partial(add_across, j))
        far_sum[j] = final[j].astype(jnp.bfloat16)
    for copy in (far_up, far_down, near_down_0, near_up_1):
        copy.start()
    for copy in bulk:
        copy.arrived()
    eye = identity(B)
    for block in range(2):
        for h in range(heads):
            rows = slice(h * B, (h + 1) * B)
            total = dqt[block, :, rows] + dqn[block, :, rows]
            total = total + dq_got[block, :, rows].astype(jnp.float32)
            rounded = (total * (1.0 / math.sqrt(W))).astype(jnp.bfloat16)
            turned = nt(eye, rounded).astype(jnp.bfloat16)
            dq_out[block * B : (block + 1) * B, h * W : (h + 1) * W] = turned
    out_q = pltpu.make_async_copy(dq_out, dq_hbm, put.at[0])
    out_q.start()
    far_up.arrived()
    near_sum[0] = (held(OWN, up, 0) + far_got[0].astype(jnp.float32)).astype(jnp.bfloat16)
    near_up_0.start()
    far_down.arrived()
    near_sum[1] = (held(OWN, down, 1) + far_got[1].astype(jnp.float32)).astype(jnp.bfloat16)
    near_down_1.start()
    near_down_0.arrived()
    near_up_0.arrived()
    final[0] = (
        held(OWN, z, 0) + near_got[0].astype(jnp.float32) + near_got[2].astype(jnp.float32)
    )
    near_down_1.arrived()
    final[1] = held(OWN, z, 1) + near_got[3].astype(jnp.float32)

    @pl.when(z == 0)
    def _():
        near_up_1.make(near_got.at[1]).wait_recv()
        final[1] += near_got[1].astype(jnp.float32)

    @pl.when(has_next)
    def _():
        for j in range(2):
            back[j].make(later_got.at[j]).wait_recv()
            final[j] += later_got[j].astype(jnp.float32)

    given_half[...] = final[1 - core].astype(jnp.bfloat16)
    give_k = Route(sems, 16, at.sibling, given_half.at[0], dk_ref.at[B:])
    give_v = Route(sems, 17, at.sibling, given_half.at[1], dv_ref.at[B:])
    give_k.start()
    give_v.start()
    scale = 1.0 / math.sqrt(W)
    dk_ref[:B] = (final[core, 0] + dka[0] * scale).astype(jnp.bfloat16)
    dv_ref[:B] = (final[core, 1] + dva[0]).astype(jnp.bfloat16)
    give_k.arrived()
    give_v.arrived()
    dk_ref[B:] = (dk_ref[B:].astype(jnp.float32) + dka[1] * scale).astype(jnp.bfloat16)
    dv_ref[B:] = (dv_ref[B:].astype(jnp.float32) + dva[1]).astype(jnp.bfloat16)
    out_k = pltpu.make_async_copy(dk_ref, dk_hbm, put.at[1])
    out_v = pltpu.make_async_copy(dv_ref, dv_hbm, put.at[2])
    out_k.start()
    out_v.start()
    for copy in (out_q, out_k, out_v):
        copy.wait()
    for copy in (
        far_back + side_up + side_down + bulk + back
        + [far_up, far_down, near_up_0, near_up_1, near_down_0, near_down_1, give_k, give_v]
    ):
        copy.sent()


def give_back(columns, docs, q, k, v, g, stat, dq_near, dq_own, dq_other, part):
    rows, features = q.shape
    heads = features // W
    some = pl.BlockSpec(memory_space=pl.ANY)
    vmem = pl.BlockSpec(memory_space=pltpu.VMEM)
    block = (2, B, W)
    return pl.pallas_call(
        functools.partial(return_kernel, columns, heads),
        out_shape=(
            jax.ShapeDtypeStruct((rows, features), jnp.bfloat16),
            jax.ShapeDtypeStruct((rows, W), jnp.bfloat16),
            jax.ShapeDtypeStruct((rows, W), jnp.bfloat16),
        ),
        in_specs=[vmem] + [some] * 9,
        out_specs=(some,) * 3,
        scratch_shapes=[
            pltpu.VMEM(q.shape, q.dtype),
            pltpu.VMEM(k.shape, k.dtype),
            pltpu.VMEM(v.shape, v.dtype),
            pltpu.VMEM(g.shape, g.dtype),
            pltpu.VMEM(stat.shape[1:], stat.dtype),
            pltpu.VMEM(dq_own.shape, dq_own.dtype),
            pltpu.VMEM(dq_own.shape, dq_own.dtype),
            pltpu.VMEM(dq_other.shape, dq_other.dtype),
            pltpu.VMEM(q.shape, jnp.bfloat16),
            pltpu.VMEM((rows, W), jnp.bfloat16),
            pltpu.VMEM((rows, W), jnp.bfloat16),
            pltpu.VMEM((2, B, W), jnp.float32),
            pltpu.VMEM((2, B, W), jnp.float32),
            pltpu.VMEM((B, B), jnp.float32),
            pltpu.VMEM((16, *block), jnp.bfloat16),
            pltpu.VMEM((2, *block), jnp.bfloat16),
            pltpu.VMEM((2, 2, *block), jnp.bfloat16),
            pltpu.VMEM((2, *block), jnp.bfloat16),
            pltpu.VMEM((2, *block), jnp.bfloat16),
            pltpu.VMEM((2, *block), jnp.bfloat16),
            pltpu.VMEM((2, *block), jnp.bfloat16),
            pltpu.VMEM((2, *block), jnp.bfloat16),
            pltpu.VMEM((4, *block), jnp.bfloat16),
            pltpu.VMEM((2, *block), jnp.float32),
            pltpu.VMEM(block, jnp.bfloat16),
            pltpu.SemaphoreType.DMA((9,)),
            pltpu.SemaphoreType.DMA((3,)),
            pltpu.SemaphoreType.DMA((18,)),
            pltpu.SemaphoreType.DMA((18,)),
        ],
        compiler_params=pltpu.CompilerParams(
            collective_id=1, has_side_effects=True, vmem_limit_bytes=VMEM
        ),
    )(docs, q, k, v, g, stat, dq_near, dq_own, dq_other, part)


def publish_kernel(*refs):
    sources, targets, held, get, put = refs[:3], refs[3:6], refs[6:9], refs[9], refs[10]
    pieces = []
    for source, target, mid in zip(sources, targets, held):
        rows = min(source.shape[0], 128 * 1024 // source.shape[1])
        for at in range(0, source.shape[0], rows):
            here = slice(at, at + rows)
            n = len(pieces)
            pieces.append(
                (
                    pltpu.make_async_copy(source.at[here], mid.at[here], get.at[n]),
                    pltpu.make_async_copy(mid.at[here], target.at[here], put.at[n]),
                )
            )
    for into, _ in pieces:
        into.start()
    for into, out in pieces:
        into.wait()
        out.start()
    for _, out in pieces:
        out.wait()


def publish(*results):
    some = pl.BlockSpec(memory_space=pl.ANY)
    return pl.pallas_call(
        publish_kernel,
        out_shape=tuple(jax.ShapeDtypeStruct(x.shape, x.dtype) for x in results),
        in_specs=[some] * 3,
        out_specs=(some,) * 3,
        scratch_shapes=[pltpu.VMEM(x.shape, x.dtype) for x in results]
        + [pltpu.SemaphoreType.DMA((6,))] * 2,
        compiler_params=pltpu.CompilerParams(vmem_limit_bytes=VMEM),
    )(*results)


def solution(mesh):
    columns = mesh.shape["ctx"] // 2

    def on_device(q, k, v, o, g, log_total, doc_lengths):
        docs = doc_lengths[None, :]
        q_other, g_other, stat, window, dq, sums = gather(columns, docs, q, g, o, k, v, log_total)
        dq_own, dq_other, part = attend(docs, q, q_other, g, g_other, stat, window, dq, sums)
        dq, dk, dv = give_back(columns, docs, q, k, v, g, stat, dq, dq_own, dq_other, part)
        return publish(dq, dk, dv)

    rows = P(("ctx", "section"), None)
    return jax.shard_map(
        on_device,
        mesh=mesh,
        in_specs=(rows, rows, rows, rows, rows, P(None, ("ctx", "section")), P()),
        out_specs=(rows, rows, rows),
        check_vma=False,
    )
```

```python
import functools
import math

import jax
import jax.numpy as jnp
from jax import lax
from jax.experimental import pallas as pl
from jax.experimental.pallas import tpu as pltpu
from jax.sharding import PartitionSpec as P

MESH = pl.DeviceIdType.MESH
W = 128
B = 256
VMEM = 58 << 20
LOG2E = math.log2(math.e)
OWN, BEFORE = 1, 0


def nn(a, b):
    return jnp.dot(a, b, preferred_element_type=jnp.float32)


def nt(a, b):
    return lax.dot_general(a, b, (((1,), (1,)), ((), ())), preferred_element_type=jnp.float32)


def place():
    ctx = lax.axis_index("ctx")
    return ctx // 2, lax.axis_index("section"), ctx % 2


def slot(side, z, j):
    return side * 8 + z * 2 + j


def doc_ends(docs_ref):
    lengths = docs_ref[...].astype(jnp.float32)
    docs = lengths.shape[1]
    upto = lax.broadcasted_iota(jnp.int32, (docs, docs), 1) <= lax.broadcasted_iota(
        jnp.int32, (docs, docs), 0
    )
    return jnp.sum(jnp.where(upto, lengths, 0.0), axis=1, keepdims=True)


def positions(first):
    return first.astype(jnp.float32) + lax.broadcasted_iota(jnp.int32, (1, B), 1).astype(
        jnp.float32
    )


def doc_start(ends, pos):
    return jnp.max(jnp.where(ends <= pos, ends, 0.0), axis=0, keepdims=True)


def hidden(key, start, pos):
    kpos = (key + lax.broadcasted_iota(jnp.int32, (B, B), 0)).astype(jnp.float32)
    return jnp.where((kpos >= start) & (kpos <= pos), 0.0, -jnp.inf)


def identity(n):
    at = [lax.broadcasted_iota(jnp.int32, (n, n), d) for d in range(2)]
    return (at[0] == at[1]).astype(jnp.bfloat16)


def gradients(k, v, qs, gs, logs, deltas, bias=None):
    ps, ds = [], []
    for q, g, log, delta in zip(qs, gs, logs, deltas):
        x = nt(k, q) * (LOG2E / math.sqrt(W)) - log
        if bias is not None:
            x = x + bias[...]
        p = jnp.exp2(x)
        d = p * (nt(v, g) - delta)
        ps.append(p.astype(jnp.bfloat16))
        ds.append(d.astype(jnp.bfloat16))
    dh = jnp.concatenate(ds, axis=1)
    dv = nn(jnp.concatenate(ps, axis=1), jnp.concatenate(gs, axis=0))
    dk = nn(dh, jnp.concatenate(qs, axis=0))
    return dk, dv, nn(k.T, dh)


class Links:
    def __init__(self, columns):
        self.column, self.z, self.core = place()
        ctx = lax.axis_index("ctx")
        self.up = lax.rem(self.z + 1, 4)
        self.down = lax.rem(self.z + 3, 4)
        self.across = lax.rem(self.z + 2, 4)
        self.sibling = (ctx + 1 - 2 * self.core, self.z)
        self.above = (ctx, self.up)
        self.below = (ctx, self.down)
        self.has_next = self.column < columns - 1
        self.has_last = self.column > 0
        self.next = (jnp.where(self.has_next, ctx + 2, ctx), self.z)
        self.last = (jnp.where(self.has_last, ctx - 2, ctx), self.z)
        self.next_across = (self.next[0], self.across)
        self.last_across = (self.last[0], self.across)

    def barrier(self, to_next=(), to_last=(), expect=0):
        barrier = pltpu.get_barrier_semaphore()

        def greet(*devices):
            for device in devices:
                pl.semaphore_signal(barrier, inc=1, device_id=device, device_id_type=MESH)

        greet(self.sibling, self.above, self.below)
        if to_next:
            pl.when(self.has_next)(lambda: greet(*to_next))
        if to_last:
            pl.when(self.has_last)(lambda: greet(*to_last))
        pl.semaphore_wait(barrier, 3 + expect)


class Route:
    def __init__(self, sems, index, device, source, target, sends=True, gets=True, arrival=None):
        self.sends, self.gets = sends, gets
        landed = target if arrival is None else arrival
        send, recv = sems[0].at[index], sems[1].at[index]
        self.make = lambda end: pltpu.make_async_remote_copy(
            source, end, send, recv, device_id=device, device_id_type=MESH
        )
        self.target, self.landed = target, landed

    @staticmethod
    def only(condition, act):
        if condition is True:
            act()
        else:
            pl.when(condition)(act)

    def start(self):
        self.only(self.sends, lambda: self.make(self.target).start())

    def arrived(self):
        self.only(self.gets, lambda: self.make(self.landed).wait_recv())

    def sent(self):
        self.only(self.sends, lambda: self.make(self.target).wait_send())


def gather_kernel(
    columns, heads, docs_ref, q_ref, g_ref, o_ref, k_ref, v_ref, log_ref,
    q_other, g_other, stat_both, window_out, dq_out, kv_out,
    q_both, g_both, o_vmem, k_own, v_own, stat, window, dqt, dkv, bias, local, put, send, recv,
):
    at = Links(columns)
    z, core, up, down, across = at.z, at.core, at.up, at.down, at.across
    sems = (send, recv)
    mine = window.at[slot(OWN, z, core)]
    loads = [
        pltpu.make_async_copy(source, target, local.at[n])
        for n, (source, target) in enumerate(
            (
                (k_ref, k_own), (v_ref, v_own), (q_ref, q_both.at[0]), (g_ref, g_both.at[0]),
                (o_ref, o_vmem), (log_ref, stat.at[0, 0]),
            )
        )
    ]
    for copy in loads:
        copy.start()

    @pl.when(at.column == 0)
    def _():
        window[slot(BEFORE, 3, 1)] = jnp.zeros((2, B, W), window.dtype)

    at.barrier(to_last=(at.last,), expect=at.has_next.astype(jnp.int32))

    theirs = window.at[slot(OWN, z, 1 - core)]
    swap_k = Route(sems, 0, at.sibling, k_own.at[B:], mine.at[0], arrival=theirs.at[0])
    swap_v = Route(sems, 1, at.sibling, v_own.at[B:], mine.at[1], arrival=theirs.at[1])
    loads[0].wait()
    loads[1].wait()
    swap_k.start()
    swap_v.start()
    mine[0] = k_own[:B]
    mine[1] = v_own[:B]
    rows = q_ref.shape[0]
    bulk = []
    for part in range(2):
        some = slice(part * rows // 2, (part + 1) * rows // 2)
        bulk.append(Route(sems, 2 + part, at.sibling, q_both.at[0, some], q_both.at[1, some]))
        bulk.append(Route(sems, 4 + part, at.sibling, g_both.at[0, some], g_both.at[1, some]))

    def passed(index, device, side, sent, j, got, sends=True, gets=True):
        there = window.at[slot(side, sent, j)]
        return Route(sems, index, device, there, there, sends, gets, window.at[slot(side, got, j)])

    up_0 = passed(6, at.above, OWN, z, 0, down)
    up_1 = passed(7, at.above, OWN, z, 1, down)
    down_0 = passed(8, at.below, OWN, z, 0, up)
    down_1 = passed(9, at.below, OWN, z, 1, up, z == 0, z == 3)
    far_0 = passed(10, at.below, OWN, up, 0, across)
    far_1 = passed(11, at.above, OWN, down, 1, across)

    def later(index, zc, j, when=True):
        here = window.at[slot(OWN, zc, j)]
        there = window.at[slot(BEFORE, zc, j)]
        sends = at.has_next if when is True else at.has_next & when
        gets = at.has_last if when is True else at.has_last & when
        return Route(sems, index, at.next, here, there, sends, gets)

    next_0 = later(12, z, 0)
    next_1 = later(13, z, 1)
    next_far_0 = later(14, across, 0, z < 2)
    next_far_1 = later(15, across, 1)
    last = at.has_last
    before_up_0 = passed(16, at.above, BEFORE, z, 0, down, last & (z == 3), last & (z == 0))
    before_up_1 = passed(17, at.above, BEFORE, z, 1, down, last, last)
    before_down_0 = passed(18, at.below, BEFORE, z, 0, up, last & (z != 0), last & (z != 3))
    before_down_1 = passed(19, at.below, BEFORE, z, 1, up, last, last)
    stats = Route(sems, 20, at.sibling, stat.at[0], stat.at[1])

    swap_k.arrived()
    swap_v.arrived()
    for copy in (up_1, down_0, next_1):
        copy.start()
    for copy in loads[2:]:
        copy.wait()

    ones = jnp.ones((8, W), jnp.bfloat16)
    for h in range(heads):
        cols = slice(h * W, (h + 1) * W)
        product = g_both[0, :, cols].astype(jnp.float32) * o_vmem[:, cols].astype(jnp.float32)
        high = product.astype(jnp.bfloat16)
        low = (product - high.astype(jnp.float32)).astype(jnp.bfloat16)
        total = nt(ones, high) + nt(ones, low)
        stat[0, 1, h : h + 1, :] = total[0:1]
    stat[0, 0] = stat[0, 0] * LOG2E
    stats.start()
    for copy in (next_0, up_0, down_1):
        copy.start()
    for copy in bulk:
        copy.start()

    ends = doc_ends(docs_ref)
    column = at.column * 16 * B
    dkv[...] = jnp.zeros_like(dkv)
    dqt[...] = jnp.zeros_like(dqt)

    def products(side, part, k, v, mask):
        here = pl.ds(pl.multiple_of(part * B, B), B)
        return gradients(
            k, v,
            [q_both[side, here, h * W : (h + 1) * W] for h in range(heads)],
            [g_both[side, here, h * W : (h + 1) * W] for h in range(heads)],
            [stat[side, 0, h : h + 1, here] for h in range(heads)],
            [stat[side, 1, h : h + 1, here] for h in range(heads)],
            mask,
        )

    up_1.arrived()
    far_1.start()
    down_0.arrived()
    far_0.start()
    next_1.arrived()
    before_down_1.start()
    before_up_1.start()
    next_0.arrived()
    before_down_0.start()
    before_up_0.start()

    near_4 = jnp.where(z > 0, slot(OWN, down, 1), slot(OWN, 3, 0))
    near_0 = jnp.where(z > 0, slot(OWN, down, 0), slot(BEFORE, 3, 1))

    def half_of(tile):
        return jnp.where((tile + 8) % 8 >= 4, 1 - core, core)

    def near(side, part, tile, keys, key_tiles, out):
        start = doc_start(ends, positions(column + tile * 2 * B + part * B))
        for n, key_tile in enumerate(key_tiles):
            key = column + key_tile * 2 * B + half_of(key_tile) * B
            kpos = (key + lax.broadcasted_iota(jnp.int32, (B, B), 0)).astype(jnp.float32)
            bias[n * B : (n + 1) * B] = jnp.where(kpos >= start, 0.0, -jnp.inf)
        dk, dv, dq = products(
            side, part,
            jnp.concatenate([window[n, 0] for n in keys], axis=0),
            jnp.concatenate([window[n, 1] for n in keys], axis=0),
            bias.at[: len(keys) * B],
        )
        for n in range(len(keys)):
            dkv[out + n, 0] += dk[n * B : (n + 1) * B]
            dkv[out + n, 1] += dv[n * B : (n + 1) * B]
        dqt[side * 2 + part] += dq

    puts = [
        pltpu.make_async_copy(source, target, put.at[n])
        for n, (source, target) in enumerate(
            (
                (q_both.at[1], q_other), (g_both.at[1], g_other), (stat, stat_both),
                (window.at[8:], window_out.at[8:]), (dqt.at[:2], dq_out.at[:2]),
                (window.at[:8], window_out.at[:8]), (dqt.at[2:], dq_out.at[2:]), (dkv, kv_out),
            )
        )
    ]

    def sibling_here():
        for copy in bulk:
            copy.arrived()
        stats.arrived()

    flip = (core == 0) & (z == 0)

    @pl.loop(0, 4)
    def _(n):
        @pl.when(n == 0)
        def _():
            up_0.arrived()
            pl.when(flip)(sibling_here)

        @pl.when(n == 1)
        def _():
            far_0.arrived()
            next_far_0.start()
            far_1.arrived()
            next_far_1.start()

        @pl.when(n == 2)
        def _():
            down_1.arrived()
            pl.when(jnp.logical_not(flip))(sibling_here)
            pl.when(z == 0)(before_up_1.arrived)
            for copy in puts[:4]:
                copy.start()

        side, part = jnp.where(flip, 1 - n // 2, n // 2), n % 2

        @pl.when(side == core)
        def _():
            near(side, part, z, [near_0], [z - 1], 2)

        @pl.when(side != core)
        def _():
            near(side, part, z + 4, [slot(OWN, z, 0), near_4], [z, z + 3], 0)

    for copy in (puts[4], puts[6], puts[7]):
        copy.start()
    pl.when(z != 0)(before_up_1.arrived)
    for copy in (before_up_0, before_down_0, before_down_1, next_far_0, next_far_1):
        copy.arrived()
    puts[5].start()
    for copy in (
        [swap_k, swap_v, up_0, up_1, down_0, down_1, far_0, far_1, next_0, next_1, next_far_0]
        + [next_far_1, before_up_0, before_up_1, before_down_0, before_down_1, stats]
        + bulk
    ):
        copy.sent()
    for copy in puts:
        copy.wait()


def gather(columns, docs, q, g, o, k, v, log_total):
    rows, features = q.shape
    heads = features // W
    some = pl.BlockSpec(memory_space=pl.ANY)
    window = (16, 2, B, W)
    stat = (2, 2, heads, rows)
    turned = (4, W, heads * B)
    sums = (3, 2, B, W)
    return pl.pallas_call(
        functools.partial(gather_kernel, columns, heads),
        out_shape=(
            jax.ShapeDtypeStruct(q.shape, q.dtype),
            jax.ShapeDtypeStruct(q.shape, q.dtype),
            jax.ShapeDtypeStruct(stat, jnp.float32),
            jax.ShapeDtypeStruct(window, k.dtype),
            jax.ShapeDtypeStruct(turned, jnp.float32),
            jax.ShapeDtypeStruct(sums, jnp.float32),
        ),
        in_specs=[pl.BlockSpec(memory_space=pltpu.VMEM)] + [some] * 6,
        out_specs=(some,) * 6,
        scratch_shapes=[
            pltpu.VMEM((2, rows, features), q.dtype),
            pltpu.VMEM((2, rows, features), q.dtype),
            pltpu.VMEM(q.shape, q.dtype),
            pltpu.VMEM(k.shape, k.dtype),
            pltpu.VMEM(k.shape, k.dtype),
            pltpu.VMEM(stat, jnp.float32),
            pltpu.VMEM(window, k.dtype),
            pltpu.VMEM(turned, jnp.float32),
            pltpu.VMEM(sums, jnp.float32),
            pltpu.VMEM((2 * B, B), jnp.float32),
            pltpu.SemaphoreType.DMA((6,)),
            pltpu.SemaphoreType.DMA((8,)),
            pltpu.SemaphoreType.DMA((21,)),
            pltpu.SemaphoreType.DMA((21,)),
        ],
        compiler_params=pltpu.CompilerParams(
            collective_id=0, has_side_effects=True, vmem_limit_bytes=VMEM
        ),
    )(docs, q, g, o, k, v, log_total)


def attend_kernel(
    heads, docs_ref, qa_hbm, qb_hbm, ga_hbm, gb_hbm, stat_hbm, window_hbm, dq_hbm, kv_hbm,
    dq_own, dq_other, part_hbm,
    q_ref, g_ref, stat_ref, window_ref, dqt, dqh, part_ref, dka, dva, dkv, bias, starts, bounds, get, put,
):
    column, z, core = place()
    loads = [
        pltpu.make_async_copy(source, target, get.at[n])
        for n, (source, target) in enumerate(
            (
                (stat_hbm, stat_ref),
                (window_hbm.at[:8], window_ref.at[:8]), (window_hbm.at[8:], window_ref.at[8:]),
                (kv_hbm, dkv), (qa_hbm, q_ref.at[0]), (ga_hbm, g_ref.at[0]),
                (qb_hbm, q_ref.at[1]), (gb_hbm, g_ref.at[1]), (dq_hbm.at[2:], dqt.at[2:]),
            )
        )
    ]
    for load in loads:
        load.start()
    ends = doc_ends(docs_ref)
    window = (column - 1) * 16 * B

    def half_of(b):
        return jnp.where(b % 8 >= 4, 1 - core, core)

    def tile_of(side):
        return z + 4 * (core if side == 0 else 1 - core)

    for block in range(4):
        side, part = divmod(block, 2)
        first = column * 16 * B + tile_of(side) * 2 * B + part * B
        start = doc_start(ends, positions(first))
        starts[block] = start
        low = jnp.min(start).astype(jnp.int32) - window
        last = jnp.max(start).astype(jnp.int32) - window
        b = low // (2 * B)
        bounds[0, block] = jnp.where(low % (2 * B) >= half_of(b) * B + B, b + 1, b)
        b = last // (2 * B)
        bounds[1, block] = jnp.where(last % (2 * B) > half_of(b) * B, b + 1, b)
    dka[...] = jnp.zeros_like(dka)
    dva[...] = jnp.zeros_like(dva)
    dqt[:2] = jnp.zeros((2, *dqt.shape[1:]), dqt.dtype)
    for load in loads[:6]:
        load.wait()
    down = lax.rem(z + 3, 4)
    nears = (
        slot(OWN, z, 0),
        jnp.where(z > 0, slot(OWN, down, 1), slot(OWN, 3, 0)),
        jnp.where(z > 0, slot(OWN, down, 0), slot(BEFORE, 3, 1)),
    )
    for n, at in enumerate(nears):
        dka[at] = dkv[n, 0]
        dva[at] = dkv[n, 1]

    @pl.loop(0, 4)
    def _(block):
        side, part = block // 2, block % 2
        here = pl.ds(pl.multiple_of(part * B, B), B)

        @pl.when(block == 2)
        def _():
            for load in loads[6:]:
                load.wait()

        def work(blocks, mask=None):
            at = [slot(b // 8, b % 4, b % 8 // 4) for b in blocks]
            dk, dv, dq = gradients(
                jnp.concatenate([window_ref[n, 0] for n in at], axis=0),
                jnp.concatenate([window_ref[n, 1] for n in at], axis=0),
                [q_ref[side, here, h * W : (h + 1) * W] for h in range(heads)],
                [g_ref[side, here, h * W : (h + 1) * W] for h in range(heads)],
                [stat_ref[side, 0, h : h + 1, here] for h in range(heads)],
                [stat_ref[side, 1, h : h + 1, here] for h in range(heads)],
                mask,
            )
            for n in range(len(at)):
                dva[at[n]] += dv[n * B : (n + 1) * B]
                dka[at[n]] += dk[n * B : (n + 1) * B]
            dqt[block] += dq

        second = jnp.where(side == 0, core, 1 - core)
        end = 7 + z + 4 * second
        skip = jnp.where(second == 1, 8 + z, 16)

        def counted(b):
            return jnp.where(b > skip, b - 1, b)

        def real(n):
            return jnp.where(n >= skip, n + 1, n)

        end = counted(end)
        low = counted(bounds[0, block])
        cut = jnp.minimum(counted(bounds[1, block]), end)
        cut = cut + (end - cut) % 2

        @pl.loop(low, cut)
        def _(n):
            b = real(n)
            key = window + b * 2 * B + half_of(b) * B
            kpos = (key + lax.broadcasted_iota(jnp.int32, (B, B), 0)).astype(jnp.float32)
            bias[...] = jnp.where(kpos >= starts[block], 0.0, -jnp.inf)
            work([b], bias)

        @pl.loop(0, (end - jnp.maximum(low, cut)) // 2)
        def _(n):
            work([real(cut + 2 * n), real(cut + 2 * n + 1)])

        @pl.when(side == 0)
        def _():
            pltpu.make_async_copy(dqt.at[block], dq_own.at[part], put.at[block]).start()

        @pl.when(side == 1)
        def _():
            dqh[part] = dqt[block].astype(jnp.bfloat16)
            pltpu.make_async_copy(dqh.at[part], dq_other.at[part], put.at[block]).start()

    @pl.loop(0, 16)
    def _(s):
        part_ref[s, 0] = (dka[s] * (1.0 / math.sqrt(W))).astype(jnp.bfloat16)
        part_ref[s, 1] = dva[s].astype(jnp.bfloat16)
        pltpu.make_async_copy(part_ref.at[s], part_hbm.at[s], put.at[4 + s]).start()

    for part in range(2):
        pltpu.make_async_copy(dqt.at[part], dq_own.at[part], put.at[part]).wait()
        pltpu.make_async_copy(dqh.at[part], dq_other.at[part], put.at[2 + part]).wait()
    for s in range(16):
        pltpu.make_async_copy(part_ref.at[s], part_hbm.at[s], put.at[4 + s]).wait()


def attend(docs, q, q_other, g, g_other, stat, window, dq, sums):
    rows, features = q.shape
    heads = features // W
    some = pl.BlockSpec(memory_space=pl.ANY)
    both = (2, rows, features)
    turned = (2, W, heads * B)
    return pl.pallas_call(
        functools.partial(attend_kernel, heads),
        out_shape=(
            jax.ShapeDtypeStruct(turned, jnp.float32),
            jax.ShapeDtypeStruct(turned, jnp.bfloat16),
            jax.ShapeDtypeStruct(window.shape, jnp.bfloat16),
        ),
        in_specs=[pl.BlockSpec(memory_space=pltpu.VMEM)] + [some] * 8,
        out_specs=(some,) * 3,
        scratch_shapes=[
            pltpu.VMEM(both, q.dtype),
            pltpu.VMEM(both, q.dtype),
            pltpu.VMEM(stat.shape, stat.dtype),
            pltpu.VMEM(window.shape, window.dtype),
            pltpu.VMEM((4, W, heads * B), jnp.float32),
            pltpu.VMEM(turned, jnp.bfloat16),
            pltpu.VMEM(window.shape, jnp.bfloat16),
            pltpu.VMEM((16, B, W), jnp.float32),
            pltpu.VMEM((16, B, W), jnp.float32),
            pltpu.VMEM(sums.shape, jnp.float32),
            pltpu.VMEM((B, B), jnp.float32),
            pltpu.VMEM((4, 1, B), jnp.float32),
            pltpu.SMEM((2, 4), jnp.int32),
            pltpu.SemaphoreType.DMA((9,)),
            pltpu.SemaphoreType.DMA((20,)),
        ],
        compiler_params=pltpu.CompilerParams(vmem_limit_bytes=VMEM),
        cost_estimate=pl.CostEstimate(
            flops=20 * 10 * heads * B * B * W, bytes_accessed=16 << 20, transcendentals=0
        ),
    )(docs, q, q_other, g, g_other, stat, window, dq, sums)


def return_kernel(
    columns, heads, docs_ref, q_hbm, k_hbm, v_hbm, g_hbm, stat_hbm, dq_near, dq_own, dq_other, part_ref,
    dq_hbm, dk_hbm, dv_hbm,
    q_ref, k_ref, v_ref, g_ref, stat, dqt, dqn, dq_got, dq_out, dk_ref, dv_ref, dka, dva, bias,
    part, across_got, beside_got, beside_sum, later_got, far_got, near_sum,
    near_got, final, given_half, local, put, send, recv,
):
    at = Links(columns)
    z, core, up, down, across = at.z, at.core, at.up, at.down, at.across
    sems = (send, recv)
    load = pltpu.make_async_copy(part_ref.at[:8], part.at[:8], local.at[0])
    load_own = pltpu.make_async_copy(part_ref.at[8:], part.at[8:], local.at[1])
    load_dq = pltpu.make_async_copy(dq_near.at[:2], dqn, local.at[2])
    load.start()
    load_own.start()
    load_dq.start()
    loads = [
        pltpu.make_async_copy(source, target, local.at[3 + n])
        for n, (source, target) in enumerate(
            (
                (q_hbm, q_ref), (g_hbm, g_ref), (k_hbm, k_ref), (v_hbm, v_ref),
                (stat_hbm.at[0], stat), (dq_own, dqt),
            )
        )
    ]
    for copy in loads:
        copy.start()
    at.barrier(
        to_next=(at.next, at.next_across), expect=2 * at.has_last.astype(jnp.int32)
    )
    has_next, has_last = at.has_next, at.has_last

    def given(side, zc, j):
        return part_ref.at[slot(side, zc, j)]

    def held(side, zc, j):
        return part[slot(side, zc, j)].astype(jnp.float32)

    far_back = [
        Route(
            sems, j, at.last_across, given(BEFORE, across, j), across_got.at[j],
            has_last & (z < 2) if j == 0 else has_last,
            has_next & (z >= 2) if j == 0 else has_next,
        )
        for j in range(2)
    ]
    side_up = [
        Route(
            sems, 2 + j, at.above, given(BEFORE, up, j), beside_got.at[0, j],
            has_last & (z != 3) if j == 0 else has_last,
            has_last & (z != 0) if j == 0 else has_last,
        )
        for j in range(2)
    ]
    side_down = [
        Route(
            sems, 4 + j, at.below, given(BEFORE, down, j), beside_got.at[1, j],
            has_last & (z == 0) if j == 0 else has_last,
            has_last & (z == 3) if j == 0 else has_last,
        )
        for j in range(2)
    ]
    bulk = [
        Route(sems, 6 + n, at.sibling, dq_other.at[n], dq_got.at[n]) for n in range(2)
    ]
    back = [
        Route(sems, 8 + j, at.last, beside_sum.at[j], later_got.at[j], has_last, has_next)
        for j in range(2)
    ]
    far_up = Route(sems, 10, at.above, given(OWN, across, 0), far_got.at[0])
    far_down = Route(
        sems, 11, at.below, given(OWN, across, 1), far_got.at[1], z >= 2, (z == 1) | (z == 2)
    )
    near_up_0 = Route(sems, 12, at.above, near_sum.at[0], near_got.at[0])
    near_up_1 = Route(sems, 13, at.above, given(OWN, up, 1), near_got.at[1], z == 3, z == 0)
    near_down_0 = Route(sems, 14, at.below, given(OWN, down, 0), near_got.at[2])
    near_down_1 = Route(sems, 15, at.below, near_sum.at[1], near_got.at[3], z != 0, z != 3)

    for copy in (side_down[1], side_up[1], side_up[0], side_down[0], far_back[1], far_back[0]):
        copy.start()
    for copy in (far_up, far_down, *bulk):
        copy.start()
    for copy in (load, load_own, load_dq, *loads):
        copy.wait()

    @pl.when(has_last)
    def _():
        for copy in side_up + side_down:
            copy.arrived()
        for j in range(2):
            final[j] = held(BEFORE, z, j)
        final[1] += beside_got[0, 1].astype(jnp.float32) + beside_got[1, 1].astype(jnp.float32)

        @pl.when(z != 0)
        def _():
            final[0] += beside_got[0, 0].astype(jnp.float32)

        @pl.when(z == 3)
        def _():
            final[0] += beside_got[1, 0].astype(jnp.float32)

        beside_sum[...] = final[...].astype(jnp.bfloat16)
        for copy in back:
            copy.start()

    for copy in (near_down_0, near_up_1):
        copy.start()
    far_up.arrived()
    near_sum[0] = (held(OWN, up, 0) + far_got[0].astype(jnp.float32)).astype(jnp.bfloat16)
    near_up_0.start()

    @pl.when((z == 1) | (z == 2))
    def _():
        far_down.make(far_got.at[1]).wait_recv()
        total = held(OWN, down, 1) + far_got[1].astype(jnp.float32)
        near_sum[1] = total.astype(jnp.bfloat16)

    @pl.when(z == 3)
    def _():
        near_sum[1] = part[slot(OWN, down, 1)]

    near_down_1.start()
    ends = doc_ends(docs_ref)
    tile = at.column * 16 * B + (z + 4 * core) * 2 * B
    dka[...] = jnp.zeros_like(dka)
    dva[...] = jnp.zeros_like(dva)

    def diagonal(n):
        block, b = (n + 1) // 2, n // 2
        here = pl.ds(pl.multiple_of(block * B, B), B)
        there = pl.ds(pl.multiple_of(b * B, B), B)
        pos = positions(tile + block * B)
        bias[...] = hidden(tile + b * B, doc_start(ends, pos), pos)
        dk, dv, dq = gradients(
            k_ref[there],
            v_ref[there],
            [q_ref[here, h * W : (h + 1) * W] for h in range(heads)],
            [g_ref[here, h * W : (h + 1) * W] for h in range(heads)],
            [stat[0, h : h + 1, here] for h in range(heads)],
            [stat[1, h : h + 1, here] for h in range(heads)],
            bias,
        )
        dka[b] += dk
        dva[b] += dv
        dqt[block] += dq

    pl.loop(0, 3)(diagonal)
    for copy in bulk:
        copy.arrived()
    eye = identity(B)
    for block in range(2):
        for h in range(heads):
            rows = slice(h * B, (h + 1) * B)
            total = dqt[block, :, rows] + dqn[block, :, rows]
            total = total + dq_got[block, :, rows].astype(jnp.float32)
            rounded = (total * (1.0 / math.sqrt(W))).astype(jnp.bfloat16)
            turned = nt(eye, rounded).astype(jnp.bfloat16)
            dq_out[block * B : (block + 1) * B, h * W : (h + 1) * W] = turned
    out_q = pltpu.make_async_copy(dq_out, dq_hbm, put.at[0])
    out_q.start()
    near_down_0.arrived()
    near_up_0.arrived()
    final[0] = (
        held(OWN, z, 0) + near_got[0].astype(jnp.float32) + near_got[2].astype(jnp.float32)
    )
    final[1] = held(OWN, z, 1)

    @pl.when(z == 0)
    def _():
        near_up_1.make(near_got.at[1]).wait_recv()
        final[1] += near_got[1].astype(jnp.float32)

    @pl.when(z != 3)
    def _():
        near_down_1.make(near_got.at[3]).wait_recv()
        final[1] += near_got[3].astype(jnp.float32)

    @pl.when(has_next)
    def _():
        far_back[1].make(across_got.at[1]).wait_recv()
        final[1] += across_got[1].astype(jnp.float32)

    @pl.when(has_next & (z >= 2))
    def _():
        far_back[0].make(across_got.at[0]).wait_recv()
        final[0] += across_got[0].astype(jnp.float32)

    @pl.when(has_next)
    def _():
        for j in range(2):
            back[j].make(later_got.at[j]).wait_recv()
            final[j] += later_got[j].astype(jnp.float32)

    given_half[...] = final[1 - core].astype(jnp.bfloat16)
    give_k = Route(sems, 16, at.sibling, given_half.at[0], dk_ref.at[B:])
    give_v = Route(sems, 17, at.sibling, given_half.at[1], dv_ref.at[B:])
    give_k.start()
    give_v.start()
    scale = 1.0 / math.sqrt(W)
    dk_ref[:B] = (final[core, 0] + dka[0] * scale).astype(jnp.bfloat16)
    dv_ref[:B] = (final[core, 1] + dva[0]).astype(jnp.bfloat16)
    give_k.arrived()
    give_v.arrived()
    dk_ref[B:] = (dk_ref[B:].astype(jnp.float32) + dka[1] * scale).astype(jnp.bfloat16)
    dv_ref[B:] = (dv_ref[B:].astype(jnp.float32) + dva[1]).astype(jnp.bfloat16)
    out_k = pltpu.make_async_copy(dk_ref, dk_hbm, put.at[1])
    out_v = pltpu.make_async_copy(dv_ref, dv_hbm, put.at[2])
    out_k.start()
    out_v.start()
    for copy in (out_q, out_k, out_v):
        copy.wait()
    for copy in (
        far_back + side_up + side_down + bulk + back
        + [far_up, far_down, near_up_0, near_up_1, near_down_0, near_down_1, give_k, give_v]
    ):
        copy.sent()


def give_back(columns, docs, q, k, v, g, stat, dq_near, dq_own, dq_other, part):
    rows, features = q.shape
    heads = features // W
    some = pl.BlockSpec(memory_space=pl.ANY)
    vmem = pl.BlockSpec(memory_space=pltpu.VMEM)
    block = (2, B, W)
    return pl.pallas_call(
        functools.partial(return_kernel, columns, heads),
        out_shape=(
            jax.ShapeDtypeStruct((rows, features), jnp.bfloat16),
            jax.ShapeDtypeStruct((rows, W), jnp.bfloat16),
            jax.ShapeDtypeStruct((rows, W), jnp.bfloat16),
        ),
        in_specs=[vmem] + [some] * 9,
        out_specs=(some,) * 3,
        scratch_shapes=[
            pltpu.VMEM(q.shape, q.dtype),
            pltpu.VMEM(k.shape, k.dtype),
            pltpu.VMEM(v.shape, v.dtype),
            pltpu.VMEM(g.shape, g.dtype),
            pltpu.VMEM(stat.shape[1:], stat.dtype),
            pltpu.VMEM(dq_own.shape, dq_own.dtype),
            pltpu.VMEM(dq_own.shape, dq_own.dtype),
            pltpu.VMEM(dq_other.shape, dq_other.dtype),
            pltpu.VMEM(q.shape, jnp.bfloat16),
            pltpu.VMEM((rows, W), jnp.bfloat16),
            pltpu.VMEM((rows, W), jnp.bfloat16),
            pltpu.VMEM((2, B, W), jnp.float32),
            pltpu.VMEM((2, B, W), jnp.float32),
            pltpu.VMEM((B, B), jnp.float32),
            pltpu.VMEM((16, *block), jnp.bfloat16),
            pltpu.VMEM((2, *block), jnp.bfloat16),
            pltpu.VMEM((2, 2, *block), jnp.bfloat16),
            pltpu.VMEM((2, *block), jnp.bfloat16),
            pltpu.VMEM((2, *block), jnp.bfloat16),
            pltpu.VMEM((2, *block), jnp.bfloat16),
            pltpu.VMEM((2, *block), jnp.bfloat16),
            pltpu.VMEM((4, *block), jnp.bfloat16),
            pltpu.VMEM((2, *block), jnp.float32),
            pltpu.VMEM(block, jnp.bfloat16),
            pltpu.SemaphoreType.DMA((9,)),
            pltpu.SemaphoreType.DMA((3,)),
            pltpu.SemaphoreType.DMA((18,)),
            pltpu.SemaphoreType.DMA((18,)),
        ],
        compiler_params=pltpu.CompilerParams(
            collective_id=1, has_side_effects=True, vmem_limit_bytes=VMEM
        ),
    )(docs, q, k, v, g, stat, dq_near, dq_own, dq_other, part)


def publish_kernel(*refs):
    sources, targets, held, get, put = refs[:3], refs[3:6], refs[6:9], refs[9], refs[10]
    pieces = []
    for source, target, mid in zip(sources, targets, held):
        rows = min(source.shape[0], 128 * 1024 // source.shape[1])
        for at in range(0, source.shape[0], rows):
            here = slice(at, at + rows)
            n = len(pieces)
            pieces.append(
                (
                    pltpu.make_async_copy(source.at[here], mid.at[here], get.at[n]),
                    pltpu.make_async_copy(mid.at[here], target.at[here], put.at[n]),
                )
            )
    for into, _ in pieces:
        into.start()
    for into, out in pieces:
        into.wait()
        out.start()
    for _, out in pieces:
        out.wait()


def publish(*results):
    some = pl.BlockSpec(memory_space=pl.ANY)
    return pl.pallas_call(
        publish_kernel,
        out_shape=tuple(jax.ShapeDtypeStruct(x.shape, x.dtype) for x in results),
        in_specs=[some] * 3,
        out_specs=(some,) * 3,
        scratch_shapes=[pltpu.VMEM(x.shape, x.dtype) for x in results]
        + [pltpu.SemaphoreType.DMA((6,))] * 2,
        compiler_params=pltpu.CompilerParams(vmem_limit_bytes=VMEM),
    )(*results)


def solution(mesh):
    columns = mesh.shape["ctx"] // 2

    def on_device(q, k, v, o, g, log_total, doc_lengths):
        docs = doc_lengths[None, :]
        q_other, g_other, stat, window, dq, sums = gather(columns, docs, q, g, o, k, v, log_total)
        dq_own, dq_other, part = attend(docs, q, q_other, g, g_other, stat, window, dq, sums)
        dq, dk, dv = give_back(columns, docs, q, k, v, g, stat, dq, dq_own, dq_other, part)
        return publish(dq, dk, dv)

    rows = P(("ctx", "section"), None)
    return jax.shard_map(
        on_device,
        mesh=mesh,
        in_specs=(rows, rows, rows, rows, rows, P(None, ("ctx", "section")), P()),
        out_specs=(rows, rows, rows),
        check_vma=False,
    )
```

```python
import functools
import math

import jax
import jax.numpy as jnp
from jax import lax
from jax.experimental import pallas as pl
from jax.experimental.pallas import tpu as pltpu
from jax.sharding import PartitionSpec as P

MESH = pl.DeviceIdType.MESH
W = 128
B = 256
VMEM = 58 << 20
LOG2E = math.log2(math.e)
OWN, BEFORE = 1, 0


def nn(a, b):
    return jnp.dot(a, b, preferred_element_type=jnp.float32)


def nt(a, b):
    return lax.dot_general(a, b, (((1,), (1,)), ((), ())), preferred_element_type=jnp.float32)


def place():
    ctx = lax.axis_index("ctx")
    return ctx // 2, lax.axis_index("section"), ctx % 2


def slot(side, z, j):
    return side * 8 + z * 2 + j


def doc_ends(docs_ref):
    lengths = docs_ref[...].astype(jnp.float32)
    docs = lengths.shape[1]
    upto = lax.broadcasted_iota(jnp.int32, (docs, docs), 1) <= lax.broadcasted_iota(
        jnp.int32, (docs, docs), 0
    )
    return jnp.sum(jnp.where(upto, lengths, 0.0), axis=1, keepdims=True)


def positions(first):
    return first.astype(jnp.float32) + lax.broadcasted_iota(jnp.int32, (1, B), 1).astype(
        jnp.float32
    )


def doc_start(ends, pos):
    return jnp.max(jnp.where(ends <= pos, ends, 0.0), axis=0, keepdims=True)


def hidden(key, start, pos):
    kpos = (key + lax.broadcasted_iota(jnp.int32, (B, B), 0)).astype(jnp.float32)
    return jnp.where((kpos >= start) & (kpos <= pos), 0.0, -jnp.inf)


def identity(n):
    at = [lax.broadcasted_iota(jnp.int32, (n, n), d) for d in range(2)]
    return (at[0] == at[1]).astype(jnp.bfloat16)


def gradients(k, v, qs, gs, logs, deltas, bias=None):
    ps, ds = [], []
    for q, g, log, delta in zip(qs, gs, logs, deltas):
        x = nt(k, q) * (LOG2E / math.sqrt(W)) - log
        if bias is not None:
            x = x + bias[...]
        p = jnp.exp2(x)
        d = p * (nt(v, g) - delta)
        ps.append(p.astype(jnp.bfloat16))
        ds.append(d.astype(jnp.bfloat16))
    dh = jnp.concatenate(ds, axis=1)
    dv = nn(jnp.concatenate(ps, axis=1), jnp.concatenate(gs, axis=0))
    dk = nn(dh, jnp.concatenate(qs, axis=0))
    return dk, dv, nn(k.T, dh)


class Links:
    def __init__(self, columns):
        self.column, self.z, self.core = place()
        ctx = lax.axis_index("ctx")
        self.up = lax.rem(self.z + 1, 4)
        self.down = lax.rem(self.z + 3, 4)
        self.across = lax.rem(self.z + 2, 4)
        self.sibling = (ctx + 1 - 2 * self.core, self.z)
        self.above = (ctx, self.up)
        self.below = (ctx, self.down)
        self.has_next = self.column < columns - 1
        self.has_last = self.column > 0
        self.next = (jnp.where(self.has_next, ctx + 2, ctx), self.z)
        self.last = (jnp.where(self.has_last, ctx - 2, ctx), self.z)

    def barrier(self, to_next=(), to_last=(), expect=0):
        barrier = pltpu.get_barrier_semaphore()

        def greet(*devices):
            for device in devices:
                pl.semaphore_signal(barrier, inc=1, device_id=device, device_id_type=MESH)

        greet(self.sibling, self.above, self.below)
        if to_next:
            pl.when(self.has_next)(lambda: greet(*to_next))
        if to_last:
            pl.when(self.has_last)(lambda: greet(*to_last))
        pl.semaphore_wait(barrier, 3 + expect)


class Route:
    def __init__(self, sems, index, device, source, target, sends=True, gets=True, arrival=None):
        self.sends, self.gets = sends, gets
        landed = target if arrival is None else arrival
        send, recv = sems[0].at[index], sems[1].at[index]
        self.make = lambda end: pltpu.make_async_remote_copy(
            source, end, send, recv, device_id=device, device_id_type=MESH
        )
        self.target, self.landed = target, landed

    @staticmethod
    def only(condition, act):
        if condition is True:
            act()
        else:
            pl.when(condition)(act)

    def start(self):
        self.only(self.sends, lambda: self.make(self.target).start())

    def arrived(self):
        self.only(self.gets, lambda: self.make(self.landed).wait_recv())

    def sent(self):
        self.only(self.sends, lambda: self.make(self.target).wait_send())


def gather_kernel(
    columns, heads, docs_ref, q_ref, g_ref, o_ref, k_ref, v_ref, log_ref,
    q_other, g_other, stat_both, window_out, dq_out, kv_out,
    q_both, g_both, o_vmem, k_own, v_own, stat, window, dqt, dkv, bias, local, put, send, recv,
):
    at = Links(columns)
    z, core, up, down, across = at.z, at.core, at.up, at.down, at.across
    sems = (send, recv)
    mine = window.at[slot(OWN, z, core)]
    loads = [
        pltpu.make_async_copy(source, target, local.at[n])
        for n, (source, target) in enumerate(
            (
                (k_ref, k_own), (v_ref, v_own), (q_ref, q_both.at[0]), (g_ref, g_both.at[0]),
                (o_ref, o_vmem), (log_ref, stat.at[0, 0]),
            )
        )
    ]
    for copy in loads:
        copy.start()

    @pl.when(at.column == 0)
    def _():
        window[slot(BEFORE, 3, 1)] = jnp.zeros((2, B, W), window.dtype)

    at.barrier(to_last=(at.last,), expect=at.has_next.astype(jnp.int32))

    theirs = window.at[slot(OWN, z, 1 - core)]
    swap_k = Route(sems, 0, at.sibling, k_own.at[B:], mine.at[0], arrival=theirs.at[0])
    swap_v = Route(sems, 1, at.sibling, v_own.at[B:], mine.at[1], arrival=theirs.at[1])
    loads[0].wait()
    loads[1].wait()
    swap_k.start()
    swap_v.start()
    mine[0] = k_own[:B]
    mine[1] = v_own[:B]
    rows = q_ref.shape[0]
    bulk = []
    for part in range(2):
        some = slice(part * rows // 2, (part + 1) * rows // 2)
        bulk.append(Route(sems, 2 + part, at.sibling, q_both.at[0, some], q_both.at[1, some]))
        bulk.append(Route(sems, 4 + part, at.sibling, g_both.at[0, some], g_both.at[1, some]))

    def passed(index, device, side, sent, j, got, sends=True, gets=True):
        there = window.at[slot(side, sent, j)]
        return Route(sems, index, device, there, there, sends, gets, window.at[slot(side, got, j)])

    up_0 = passed(6, at.above, OWN, z, 0, down)
    up_1 = passed(7, at.above, OWN, z, 1, down)
    down_0 = passed(8, at.below, OWN, z, 0, up)
    down_1 = passed(9, at.below, OWN, z, 1, up, z == 0, z == 3)
    far_0 = passed(10, at.below, OWN, up, 0, across)
    far_1 = passed(11, at.above, OWN, down, 1, across)

    def later(index, zc, j, when=True):
        here = window.at[slot(OWN, zc, j)]
        there = window.at[slot(BEFORE, zc, j)]
        sends = at.has_next if when is True else at.has_next & when
        gets = at.has_last if when is True else at.has_last & when
        return Route(sems, index, at.next, here, there, sends, gets)

    next_0 = later(12, z, 0)
    next_1 = later(13, z, 1)
    next_far_0 = later(14, across, 0, z < 2)
    next_far_1 = later(15, across, 1)
    last = at.has_last
    before_up_0 = passed(16, at.above, BEFORE, z, 0, down, last & (z == 3), last & (z == 0))
    before_up_1 = passed(17, at.above, BEFORE, z, 1, down, last, last)
    before_down_0 = passed(18, at.below, BEFORE, z, 0, up, last & (z != 0), last & (z != 3))
    before_down_1 = passed(19, at.below, BEFORE, z, 1, up, last, last)
    stats = Route(sems, 20, at.sibling, stat.at[0], stat.at[1])

    swap_k.arrived()
    swap_v.arrived()
    for copy in (up_1, down_0, next_1):
        copy.start()
    for copy in loads[2:]:
        copy.wait()

    ones = jnp.ones((8, W), jnp.bfloat16)
    for h in range(heads):
        cols = slice(h * W, (h + 1) * W)
        product = g_both[0, :, cols].astype(jnp.float32) * o_vmem[:, cols].astype(jnp.float32)
        high = product.astype(jnp.bfloat16)
        low = (product - high.astype(jnp.float32)).astype(jnp.bfloat16)
        total = nt(ones, high) + nt(ones, low)
        stat[0, 1, h : h + 1, :] = total[0:1]
    stat[0, 0] = stat[0, 0] * LOG2E
    stats.start()
    for copy in (next_0, up_0, down_1):
        copy.start()
    for copy in bulk:
        copy.start()

    ends = doc_ends(docs_ref)
    column = at.column * 16 * B
    dkv[...] = jnp.zeros_like(dkv)
    dqt[...] = jnp.zeros_like(dqt)

    def products(side, part, k, v, mask):
        here = pl.ds(pl.multiple_of(part * B, B), B)
        return gradients(
            k, v,
            [q_both[side, here, h * W : (h + 1) * W] for h in range(heads)],
            [g_both[side, here, h * W : (h + 1) * W] for h in range(heads)],
            [stat[side, 0, h : h + 1, here] for h in range(heads)],
            [stat[side, 1, h : h + 1, here] for h in range(heads)],
            mask,
        )

    up_1.arrived()
    far_1.start()
    down_0.arrived()
    far_0.start()
    next_1.arrived()
    before_down_1.start()
    before_up_1.start()
    next_0.arrived()
    before_down_0.start()
    before_up_0.start()

    near_4 = jnp.where(z > 0, slot(OWN, down, 1), slot(OWN, 3, 0))
    near_0 = jnp.where(z > 0, slot(OWN, down, 0), slot(BEFORE, 3, 1))

    def half_of(tile):
        return jnp.where((tile + 8) % 8 >= 4, 1 - core, core)

    def near(side, part, tile, keys, key_tiles, out):
        start = doc_start(ends, positions(column + tile * 2 * B + part * B))
        for n, key_tile in enumerate(key_tiles):
            key = column + key_tile * 2 * B + half_of(key_tile) * B
            kpos = (key + lax.broadcasted_iota(jnp.int32, (B, B), 0)).astype(jnp.float32)
            bias[n * B : (n + 1) * B] = jnp.where(kpos >= start, 0.0, -jnp.inf)
        dk, dv, dq = products(
            side, part,
            jnp.concatenate([window[n, 0] for n in keys], axis=0),
            jnp.concatenate([window[n, 1] for n in keys], axis=0),
            bias.at[: len(keys) * B],
        )
        for n in range(len(keys)):
            dkv[out + n, 0] += dk[n * B : (n + 1) * B]
            dkv[out + n, 1] += dv[n * B : (n + 1) * B]
        dqt[side * 2 + part] += dq

    puts = [
        pltpu.make_async_copy(source, target, put.at[n])
        for n, (source, target) in enumerate(
            (
                (q_both.at[1], q_other), (g_both.at[1], g_other), (stat, stat_both),
                (window.at[8:], window_out.at[8:]), (dqt.at[:2], dq_out.at[:2]),
                (window.at[:8], window_out.at[:8]), (dqt.at[2:], dq_out.at[2:]), (dkv, kv_out),
            )
        )
    ]

    def sibling_here():
        for copy in bulk:
            copy.arrived()
        stats.arrived()

    flip = (core == 0) & (z == 0)

    @pl.loop(0, 4)
    def _(n):
        @pl.when(n == 0)
        def _():
            up_0.arrived()
            pl.when(flip)(sibling_here)

        @pl.when(n == 1)
        def _():
            far_0.arrived()
            next_far_0.start()
            far_1.arrived()
            next_far_1.start()

        @pl.when(n == 2)
        def _():
            down_1.arrived()
            pl.when(jnp.logical_not(flip))(sibling_here)
            pl.when(z == 0)(before_up_1.arrived)
            for copy in puts[:4]:
                copy.start()

        side, part = jnp.where(flip, 1 - n // 2, n // 2), n % 2

        @pl.when(side == core)
        def _():
            near(side, part, z, [near_0], [z - 1], 2)

        @pl.when(side != core)
        def _():
            near(side, part, z + 4, [slot(OWN, z, 0), near_4], [z, z + 3], 0)

    for copy in (puts[4], puts[6], puts[7]):
        copy.start()
    pl.when(z != 0)(before_up_1.arrived)
    for copy in (before_up_0, before_down_0, before_down_1, next_far_0, next_far_1):
        copy.arrived()
    puts[5].start()
    for copy in (
        [swap_k, swap_v, up_0, up_1, down_0, down_1, far_0, far_1, next_0, next_1, next_far_0]
        + [next_far_1, before_up_0, before_up_1, before_down_0, before_down_1, stats]
        + bulk
    ):
        copy.sent()
    for copy in puts:
        copy.wait()


def gather(columns, docs, q, g, o, k, v, log_total):
    rows, features = q.shape
    heads = features // W
    some = pl.BlockSpec(memory_space=pl.ANY)
    window = (16, 2, B, W)
    stat = (2, 2, heads, rows)
    turned = (4, W, heads * B)
    sums = (3, 2, B, W)
    return pl.pallas_call(
        functools.partial(gather_kernel, columns, heads),
        out_shape=(
            jax.ShapeDtypeStruct(q.shape, q.dtype),
            jax.ShapeDtypeStruct(q.shape, q.dtype),
            jax.ShapeDtypeStruct(stat, jnp.float32),
            jax.ShapeDtypeStruct(window, k.dtype),
            jax.ShapeDtypeStruct(turned, jnp.float32),
            jax.ShapeDtypeStruct(sums, jnp.float32),
        ),
        in_specs=[pl.BlockSpec(memory_space=pltpu.VMEM)] + [some] * 6,
        out_specs=(some,) * 6,
        scratch_shapes=[
            pltpu.VMEM((2, rows, features), q.dtype),
            pltpu.VMEM((2, rows, features), q.dtype),
            pltpu.VMEM(q.shape, q.dtype),
            pltpu.VMEM(k.shape, k.dtype),
            pltpu.VMEM(k.shape, k.dtype),
            pltpu.VMEM(stat, jnp.float32),
            pltpu.VMEM(window, k.dtype),
            pltpu.VMEM(turned, jnp.float32),
            pltpu.VMEM(sums, jnp.float32),
            pltpu.VMEM((2 * B, B), jnp.float32),
            pltpu.SemaphoreType.DMA((6,)),
            pltpu.SemaphoreType.DMA((8,)),
            pltpu.SemaphoreType.DMA((21,)),
            pltpu.SemaphoreType.DMA((21,)),
        ],
        compiler_params=pltpu.CompilerParams(
            collective_id=0, has_side_effects=True, vmem_limit_bytes=VMEM
        ),
    )(docs, q, g, o, k, v, log_total)


def attend_kernel(
    heads, docs_ref, qa_hbm, qb_hbm, ga_hbm, gb_hbm, stat_hbm, window_hbm, dq_hbm, kv_hbm,
    dq_own, dq_other, part_hbm,
    q_ref, g_ref, stat_ref, window_ref, dqt, dqh, part_ref, dka, dva, dkv, bias, starts, bounds, get, put,
):
    column, z, core = place()
    loads = [
        pltpu.make_async_copy(source, target, get.at[n])
        for n, (source, target) in enumerate(
            (
                (stat_hbm, stat_ref),
                (window_hbm.at[:8], window_ref.at[:8]), (window_hbm.at[8:], window_ref.at[8:]),
                (kv_hbm, dkv), (qa_hbm, q_ref.at[0]), (ga_hbm, g_ref.at[0]),
                (qb_hbm, q_ref.at[1]), (gb_hbm, g_ref.at[1]), (dq_hbm.at[2:], dqt.at[2:]),
            )
        )
    ]
    for load in loads:
        load.start()
    ends = doc_ends(docs_ref)
    window = (column - 1) * 16 * B

    def half_of(b):
        return jnp.where(b % 8 >= 4, 1 - core, core)

    def tile_of(side):
        return z + 4 * (core if side == 0 else 1 - core)

    for block in range(4):
        side, part = divmod(block, 2)
        first = column * 16 * B + tile_of(side) * 2 * B + part * B
        start = doc_start(ends, positions(first))
        starts[block] = start
        low = jnp.min(start).astype(jnp.int32) - window
        last = jnp.max(start).astype(jnp.int32) - window
        b = low // (2 * B)
        bounds[0, block] = jnp.where(low % (2 * B) >= half_of(b) * B + B, b + 1, b)
        b = last // (2 * B)
        bounds[1, block] = jnp.where(last % (2 * B) > half_of(b) * B, b + 1, b)
    dka[...] = jnp.zeros_like(dka)
    dva[...] = jnp.zeros_like(dva)
    dqt[:2] = jnp.zeros((2, *dqt.shape[1:]), dqt.dtype)
    for load in loads[:6]:
        load.wait()
    down = lax.rem(z + 3, 4)
    nears = (
        slot(OWN, z, 0),
        jnp.where(z > 0, slot(OWN, down, 1), slot(OWN, 3, 0)),
        jnp.where(z > 0, slot(OWN, down, 0), slot(BEFORE, 3, 1)),
    )
    for n, at in enumerate(nears):
        dka[at] = dkv[n, 0]
        dva[at] = dkv[n, 1]

    @pl.loop(0, 4)
    def _(block):
        side, part = block // 2, block % 2
        here = pl.ds(pl.multiple_of(part * B, B), B)

        @pl.when(block == 2)
        def _():
            for load in loads[6:]:
                load.wait()

        def work(blocks, mask=None):
            at = [slot(b // 8, b % 4, b % 8 // 4) for b in blocks]
            dk, dv, dq = gradients(
                jnp.concatenate([window_ref[n, 0] for n in at], axis=0),
                jnp.concatenate([window_ref[n, 1] for n in at], axis=0),
                [q_ref[side, here, h * W : (h + 1) * W] for h in range(heads)],
                [g_ref[side, here, h * W : (h + 1) * W] for h in range(heads)],
                [stat_ref[side, 0, h : h + 1, here] for h in range(heads)],
                [stat_ref[side, 1, h : h + 1, here] for h in range(heads)],
                mask,
            )
            for n in range(len(at)):
                dva[at[n]] += dv[n * B : (n + 1) * B]
                dka[at[n]] += dk[n * B : (n + 1) * B]
            dqt[block] += dq

        second = jnp.where(side == 0, core, 1 - core)
        end = 7 + z + 4 * second
        skip = jnp.where(second == 1, 8 + z, 16)

        def counted(b):
            return jnp.where(b > skip, b - 1, b)

        def real(n):
            return jnp.where(n >= skip, n + 1, n)

        end = counted(end)
        low = counted(bounds[0, block])
        cut = jnp.minimum(counted(bounds[1, block]), end)
        cut = cut + (end - cut) % 2

        @pl.loop(low, cut)
        def _(n):
            b = real(n)
            key = window + b * 2 * B + half_of(b) * B
            kpos = (key + lax.broadcasted_iota(jnp.int32, (B, B), 0)).astype(jnp.float32)
            bias[...] = jnp.where(kpos >= starts[block], 0.0, -jnp.inf)
            work([b], bias)

        pairs = jnp.maximum(end - jnp.maximum(low, cut), 0) // 2
        odd = pairs % 2

        @pl.loop(0, odd)
        def _(n):
            work([real(cut), real(cut + 1)])

        @pl.loop(0, pairs // 2)
        def _(n):
            first = cut + 2 * odd + 4 * n
            work([real(first + m) for m in range(4)])

        @pl.when(side == 0)
        def _():
            pltpu.make_async_copy(dqt.at[block], dq_own.at[part], put.at[block]).start()

        @pl.when(side == 1)
        def _():
            dqh[part] = dqt[block].astype(jnp.bfloat16)
            pltpu.make_async_copy(dqh.at[part], dq_other.at[part], put.at[block]).start()

    @pl.loop(0, 16)
    def _(s):
        part_ref[s, 0] = (dka[s] * (1.0 / math.sqrt(W))).astype(jnp.bfloat16)
        part_ref[s, 1] = dva[s].astype(jnp.bfloat16)
        pltpu.make_async_copy(part_ref.at[s], part_hbm.at[s], put.at[4 + s]).start()

    for part in range(2):
        pltpu.make_async_copy(dqt.at[part], dq_own.at[part], put.at[part]).wait()
        pltpu.make_async_copy(dqh.at[part], dq_other.at[part], put.at[2 + part]).wait()
    for s in range(16):
        pltpu.make_async_copy(part_ref.at[s], part_hbm.at[s], put.at[4 + s]).wait()


def attend(docs, q, q_other, g, g_other, stat, window, dq, sums):
    rows, features = q.shape
    heads = features // W
    some = pl.BlockSpec(memory_space=pl.ANY)
    both = (2, rows, features)
    turned = (2, W, heads * B)
    return pl.pallas_call(
        functools.partial(attend_kernel, heads),
        out_shape=(
            jax.ShapeDtypeStruct(turned, jnp.float32),
            jax.ShapeDtypeStruct(turned, jnp.bfloat16),
            jax.ShapeDtypeStruct(window.shape, jnp.bfloat16),
        ),
        in_specs=[pl.BlockSpec(memory_space=pltpu.VMEM)] + [some] * 8,
        out_specs=(some,) * 3,
        scratch_shapes=[
            pltpu.VMEM(both, q.dtype),
            pltpu.VMEM(both, q.dtype),
            pltpu.VMEM(stat.shape, stat.dtype),
            pltpu.VMEM(window.shape, window.dtype),
            pltpu.VMEM((4, W, heads * B), jnp.float32),
            pltpu.VMEM(turned, jnp.bfloat16),
            pltpu.VMEM(window.shape, jnp.bfloat16),
            pltpu.VMEM((16, B, W), jnp.float32),
            pltpu.VMEM((16, B, W), jnp.float32),
            pltpu.VMEM(sums.shape, jnp.float32),
            pltpu.VMEM((B, B), jnp.float32),
            pltpu.VMEM((4, 1, B), jnp.float32),
            pltpu.SMEM((2, 4), jnp.int32),
            pltpu.SemaphoreType.DMA((9,)),
            pltpu.SemaphoreType.DMA((20,)),
        ],
        compiler_params=pltpu.CompilerParams(vmem_limit_bytes=VMEM),
        cost_estimate=pl.CostEstimate(
            flops=20 * 10 * heads * B * B * W, bytes_accessed=16 << 20, transcendentals=0
        ),
    )(docs, q, q_other, g, g_other, stat, window, dq, sums)


def return_kernel(
    columns, heads, docs_ref, q_hbm, k_hbm, v_hbm, g_hbm, stat_hbm, dq_near, dq_own, dq_other, part_ref,
    dq_hbm, dk_hbm, dv_hbm,
    q_ref, k_ref, v_ref, g_ref, stat, dqt, dqn, dq_got, dq_out, dk_ref, dv_ref, dka, dva, bias,
    part, across_got, beside_got, beside_sum, later_got, far_got, far_sum, near_sum,
    near_got, final, given_half, local, put, send, recv,
):
    at = Links(columns)
    z, core, up, down, across = at.z, at.core, at.up, at.down, at.across
    sems = (send, recv)
    load = pltpu.make_async_copy(part_ref.at[:8], part.at[:8], local.at[0])
    load_own = pltpu.make_async_copy(part_ref.at[8:], part.at[8:], local.at[1])
    load_dq = pltpu.make_async_copy(dq_near.at[:2], dqn, local.at[2])
    load.start()
    load_own.start()
    load_dq.start()
    loads = [
        pltpu.make_async_copy(source, target, local.at[3 + n])
        for n, (source, target) in enumerate(
            (
                (q_hbm, q_ref), (g_hbm, g_ref), (k_hbm, k_ref), (v_hbm, v_ref),
                (stat_hbm.at[0], stat), (dq_own, dqt),
            )
        )
    ]
    for copy in loads:
        copy.start()
    at.barrier(to_next=(at.next,), expect=at.has_last.astype(jnp.int32))
    has_next, has_last = at.has_next, at.has_last

    def given(side, zc, j):
        return part_ref.at[slot(side, zc, j)]

    def held(side, zc, j):
        return part[slot(side, zc, j)].astype(jnp.float32)

    far_back = [
        Route(
            sems, j, at.last, given(BEFORE, across, j), across_got.at[j],
            has_last & (z < 2) if j == 0 else has_last,
            has_next & (z < 2) if j == 0 else has_next,
        )
        for j in range(2)
    ]
    side_up = [
        Route(
            sems, 2 + j, at.above, given(BEFORE, up, j), beside_got.at[0, j],
            has_last & (z != 3) if j == 0 else has_last,
            has_last & (z != 0) if j == 0 else has_last,
        )
        for j in range(2)
    ]
    side_down = [
        Route(
            sems, 4 + j, at.below, given(BEFORE, down, j), beside_got.at[1, j],
            has_last & (z == 0) if j == 0 else has_last,
            has_last & (z == 3) if j == 0 else has_last,
        )
        for j in range(2)
    ]
    bulk = [
        Route(sems, 6 + n, at.sibling, dq_other.at[n], dq_got.at[n]) for n in range(2)
    ]
    back = [
        Route(sems, 8 + j, at.last, beside_sum.at[j], later_got.at[j], has_last, has_next)
        for j in range(2)
    ]
    far_up = Route(sems, 10, at.above, far_sum.at[0], far_got.at[0])
    far_down = Route(sems, 11, at.below, far_sum.at[1], far_got.at[1])
    near_up_0 = Route(sems, 12, at.above, near_sum.at[0], near_got.at[0])
    near_up_1 = Route(sems, 13, at.above, given(OWN, up, 1), near_got.at[1], z == 3, z == 0)
    near_down_0 = Route(sems, 14, at.below, given(OWN, down, 0), near_got.at[2])
    near_down_1 = Route(sems, 15, at.below, near_sum.at[1], near_got.at[3])

    for copy in (side_down[1], side_up[1], far_back[1], side_up[0], side_down[0], far_back[0]):
        copy.start()
    for copy in bulk:
        copy.start()
    for copy in (load, load_own, load_dq, *loads):
        copy.wait()
    ends = doc_ends(docs_ref)
    tile = at.column * 16 * B + (z + 4 * core) * 2 * B
    dka[...] = jnp.zeros_like(dka)
    dva[...] = jnp.zeros_like(dva)

    def diagonal(n):
        block, b = (n + 1) // 2, n // 2
        here = pl.ds(pl.multiple_of(block * B, B), B)
        there = pl.ds(pl.multiple_of(b * B, B), B)
        pos = positions(tile + block * B)
        bias[...] = hidden(tile + b * B, doc_start(ends, pos), pos)
        dk, dv, dq = gradients(
            k_ref[there],
            v_ref[there],
            [q_ref[here, h * W : (h + 1) * W] for h in range(heads)],
            [g_ref[here, h * W : (h + 1) * W] for h in range(heads)],
            [stat[0, h : h + 1, here] for h in range(heads)],
            [stat[1, h : h + 1, here] for h in range(heads)],
            bias,
        )
        dka[b] += dk
        dva[b] += dv
        dqt[block] += dq

    pl.loop(0, 3)(diagonal)

    @pl.when(has_last)
    def _():
        for copy in side_up + side_down:
            copy.arrived()
        for j in range(2):
            final[j] = held(BEFORE, z, j)
        final[1] += beside_got[0, 1].astype(jnp.float32) + beside_got[1, 1].astype(jnp.float32)

        @pl.when(z != 0)
        def _():
            final[0] += beside_got[0, 0].astype(jnp.float32)

        @pl.when(z == 3)
        def _():
            final[0] += beside_got[1, 0].astype(jnp.float32)

        beside_sum[...] = final[...].astype(jnp.bfloat16)
        for copy in back:
            copy.start()

    def add_across(j):
        far_back[j].make(across_got.at[j]).wait_recv()
        final[j] += across_got[j].astype(jnp.float32)

    for j in range(2):
        final[j] = held(OWN, across, j)
        pl.when(far_back[j].gets)(functools.partial(add_across, j))
        far_sum[j] = final[j].astype(jnp.bfloat16)
    for copy in (far_up, far_down, near_down_0, near_up_1):
        copy.start()
    for copy in bulk:
        copy.arrived()
    eye = identity(B)
    for block in range(2):
        for h in range(heads):
            rows = slice(h * B, (h + 1) * B)
            total = dqt[block, :, rows] + dqn[block, :, rows]
            total = total + dq_got[block, :, rows].astype(jnp.float32)
            rounded = (total * (1.0 / math.sqrt(W))).astype(jnp.bfloat16)
            turned = nt(eye, rounded).astype(jnp.bfloat16)
            dq_out[block * B : (block + 1) * B, h * W : (h + 1) * W] = turned
    out_q = pltpu.make_async_copy(dq_out, dq_hbm, put.at[0])
    out_q.start()
    far_up.arrived()
    near_sum[0] = (held(OWN, up, 0) + far_got[0].astype(jnp.float32)).astype(jnp.bfloat16)
    near_up_0.start()
    far_down.arrived()
    near_sum[1] = (held(OWN, down, 1) + far_got[1].astype(jnp.float32)).astype(jnp.bfloat16)
    near_down_1.start()
    near_down_0.arrived()
    near_up_0.arrived()
    final[0] = (
        held(OWN, z, 0) + near_got[0].astype(jnp.float32) + near_got[2].astype(jnp.float32)
    )
    near_down_1.arrived()
    final[1] = held(OWN, z, 1) + near_got[3].astype(jnp.float32)

    @pl.when(z == 0)
    def _():
        near_up_1.make(near_got.at[1]).wait_recv()
        final[1] += near_got[1].astype(jnp.float32)

    @pl.when(has_next)
    def _():
        for j in range(2):
            back[j].make(later_got.at[j]).wait_recv()
            final[j] += later_got[j].astype(jnp.float32)

    given_half[...] = final[1 - core].astype(jnp.bfloat16)
    give_k = Route(sems, 16, at.sibling, given_half.at[0], dk_ref.at[B:])
    give_v = Route(sems, 17, at.sibling, given_half.at[1], dv_ref.at[B:])
    give_k.start()
    give_v.start()
    scale = 1.0 / math.sqrt(W)
    dk_ref[:B] = (final[core, 0] + dka[0] * scale).astype(jnp.bfloat16)
    dv_ref[:B] = (final[core, 1] + dva[0]).astype(jnp.bfloat16)
    give_k.arrived()
    give_v.arrived()
    dk_ref[B:] = (dk_ref[B:].astype(jnp.float32) + dka[1] * scale).astype(jnp.bfloat16)
    dv_ref[B:] = (dv_ref[B:].astype(jnp.float32) + dva[1]).astype(jnp.bfloat16)
    out_k = pltpu.make_async_copy(dk_ref, dk_hbm, put.at[1])
    out_v = pltpu.make_async_copy(dv_ref, dv_hbm, put.at[2])
    out_k.start()
    out_v.start()
    for copy in (out_q, out_k, out_v):
        copy.wait()
    for copy in (
        far_back + side_up + side_down + bulk + back
        + [far_up, far_down, near_up_0, near_up_1, near_down_0, near_down_1, give_k, give_v]
    ):
        copy.sent()


def give_back(columns, docs, q, k, v, g, stat, dq_near, dq_own, dq_other, part):
    rows, features = q.shape
    heads = features // W
    some = pl.BlockSpec(memory_space=pl.ANY)
    vmem = pl.BlockSpec(memory_space=pltpu.VMEM)
    block = (2, B, W)
    return pl.pallas_call(
        functools.partial(return_kernel, columns, heads),
        out_shape=(
            jax.ShapeDtypeStruct((rows, features), jnp.bfloat16),
            jax.ShapeDtypeStruct((rows, W), jnp.bfloat16),
            jax.ShapeDtypeStruct((rows, W), jnp.bfloat16),
        ),
        in_specs=[vmem] + [some] * 9,
        out_specs=(some,) * 3,
        scratch_shapes=[
            pltpu.VMEM(q.shape, q.dtype),
            pltpu.VMEM(k.shape, k.dtype),
            pltpu.VMEM(v.shape, v.dtype),
            pltpu.VMEM(g.shape, g.dtype),
            pltpu.VMEM(stat.shape[1:], stat.dtype),
            pltpu.VMEM(dq_own.shape, dq_own.dtype),
            pltpu.VMEM(dq_own.shape, dq_own.dtype),
            pltpu.VMEM(dq_other.shape, dq_other.dtype),
            pltpu.VMEM(q.shape, jnp.bfloat16),
            pltpu.VMEM((rows, W), jnp.bfloat16),
            pltpu.VMEM((rows, W), jnp.bfloat16),
            pltpu.VMEM((2, B, W), jnp.float32),
            pltpu.VMEM((2, B, W), jnp.float32),
            pltpu.VMEM((B, B), jnp.float32),
            pltpu.VMEM((16, *block), jnp.bfloat16),
            pltpu.VMEM((2, *block), jnp.bfloat16),
            pltpu.VMEM((2, 2, *block), jnp.bfloat16),
            pltpu.VMEM((2, *block), jnp.bfloat16),
            pltpu.VMEM((2, *block), jnp.bfloat16),
            pltpu.VMEM((2, *block), jnp.bfloat16),
            pltpu.VMEM((2, *block), jnp.bfloat16),
            pltpu.VMEM((2, *block), jnp.bfloat16),
            pltpu.VMEM((4, *block), jnp.bfloat16),
            pltpu.VMEM((2, *block), jnp.float32),
            pltpu.VMEM(block, jnp.bfloat16),
            pltpu.SemaphoreType.DMA((9,)),
            pltpu.SemaphoreType.DMA((3,)),
            pltpu.SemaphoreType.DMA((18,)),
            pltpu.SemaphoreType.DMA((18,)),
        ],
        compiler_params=pltpu.CompilerParams(
            collective_id=1, has_side_effects=True, vmem_limit_bytes=VMEM
        ),
    )(docs, q, k, v, g, stat, dq_near, dq_own, dq_other, part)


def publish_kernel(*refs):
    sources, targets, held, get, put = refs[:3], refs[3:6], refs[6:9], refs[9], refs[10]
    pieces = []
    for source, target, mid in zip(sources, targets, held):
        rows = min(source.shape[0], 128 * 1024 // source.shape[1])
        for at in range(0, source.shape[0], rows):
            here = slice(at, at + rows)
            n = len(pieces)
            pieces.append(
                (
                    pltpu.make_async_copy(source.at[here], mid.at[here], get.at[n]),
                    pltpu.make_async_copy(mid.at[here], target.at[here], put.at[n]),
                )
            )
    for into, _ in pieces:
        into.start()
    for into, out in pieces:
        into.wait()
        out.start()
    for _, out in pieces:
        out.wait()


def publish(*results):
    some = pl.BlockSpec(memory_space=pl.ANY)
    return pl.pallas_call(
        publish_kernel,
        out_shape=tuple(jax.ShapeDtypeStruct(x.shape, x.dtype) for x in results),
        in_specs=[some] * 3,
        out_specs=(some,) * 3,
        scratch_shapes=[pltpu.VMEM(x.shape, x.dtype) for x in results]
        + [pltpu.SemaphoreType.DMA((6,))] * 2,
        compiler_params=pltpu.CompilerParams(vmem_limit_bytes=VMEM),
    )(*results)


def solution(mesh):
    columns = mesh.shape["ctx"] // 2

    def on_device(q, k, v, o, g, log_total, doc_lengths):
        docs = doc_lengths[None, :]
        q_other, g_other, stat, window, dq, sums = gather(columns, docs, q, g, o, k, v, log_total)
        dq_own, dq_other, part = attend(docs, q, q_other, g, g_other, stat, window, dq, sums)
        dq, dk, dv = give_back(columns, docs, q, k, v, g, stat, dq, dq_own, dq_other, part)
        return publish(dq, dk, dv)

    rows = P(("ctx", "section"), None)
    return jax.shard_map(
        on_device,
        mesh=mesh,
        in_specs=(rows, rows, rows, rows, rows, P(None, ("ctx", "section")), P()),
        out_specs=(rows, rows, rows),
        check_vma=False,
    )
```

```python
import functools
import math

import jax
import jax.numpy as jnp
from jax import lax
from jax.experimental import pallas as pl
from jax.experimental.pallas import tpu as pltpu
from jax.sharding import PartitionSpec as P

MESH = pl.DeviceIdType.MESH
W = 128
B = 256
VMEM = 58 << 20
LOG2E = math.log2(math.e)
OWN, BEFORE = 1, 0


def nn(a, b):
    return jnp.dot(a, b, preferred_element_type=jnp.float32)


def nt(a, b):
    return lax.dot_general(a, b, (((1,), (1,)), ((), ())), preferred_element_type=jnp.float32)


def place():
    ctx = lax.axis_index("ctx")
    return ctx // 2, lax.axis_index("section"), ctx % 2


def slot(side, z, j):
    return side * 8 + z * 2 + j


def doc_ends(docs_ref):
    lengths = docs_ref[...].astype(jnp.float32)
    docs = lengths.shape[1]
    upto = lax.broadcasted_iota(jnp.int32, (docs, docs), 1) <= lax.broadcasted_iota(
        jnp.int32, (docs, docs), 0
    )
    return jnp.sum(jnp.where(upto, lengths, 0.0), axis=1, keepdims=True)


def positions(first):
    return first.astype(jnp.float32) + lax.broadcasted_iota(jnp.int32, (1, B), 1).astype(
        jnp.float32
    )


def doc_start(ends, pos):
    return jnp.max(jnp.where(ends <= pos, ends, 0.0), axis=0, keepdims=True)


def hidden(key, start, pos):
    kpos = (key + lax.broadcasted_iota(jnp.int32, (B, B), 0)).astype(jnp.float32)
    return jnp.where((kpos >= start) & (kpos <= pos), 0.0, -jnp.inf)


def identity(n):
    at = [lax.broadcasted_iota(jnp.int32, (n, n), d) for d in range(2)]
    return (at[0] == at[1]).astype(jnp.bfloat16)


def gradients(k, v, qs, gs, logs, deltas, bias=None):
    ps, ds = [], []
    for q, g, log, delta in zip(qs, gs, logs, deltas):
        x = nt(k, q) * (LOG2E / math.sqrt(W)) - log
        if bias is not None:
            x = x + bias[...]
        p = jnp.exp2(x)
        d = p * (nt(v, g) - delta)
        ps.append(p.astype(jnp.bfloat16))
        ds.append(d.astype(jnp.bfloat16))
    dh = jnp.concatenate(ds, axis=1)
    dv = nn(jnp.concatenate(ps, axis=1), jnp.concatenate(gs, axis=0))
    dk = nn(dh, jnp.concatenate(qs, axis=0))
    return dk, dv, nn(k.T, dh)


class Links:
    def __init__(self, columns):
        self.column, self.z, self.core = place()
        ctx = lax.axis_index("ctx")
        self.up = lax.rem(self.z + 1, 4)
        self.down = lax.rem(self.z + 3, 4)
        self.across = lax.rem(self.z + 2, 4)
        self.sibling = (ctx + 1 - 2 * self.core, self.z)
        self.above = (ctx, self.up)
        self.below = (ctx, self.down)
        self.has_next = self.column < columns - 1
        self.has_last = self.column > 0
        self.next = (jnp.where(self.has_next, ctx + 2, ctx), self.z)
        self.last = (jnp.where(self.has_last, ctx - 2, ctx), self.z)

    def barrier(self, to_next=(), to_last=(), expect=0):
        barrier = pltpu.get_barrier_semaphore()

        def greet(*devices):
            for device in devices:
                pl.semaphore_signal(barrier, inc=1, device_id=device, device_id_type=MESH)

        greet(self.sibling, self.above, self.below)
        if to_next:
            pl.when(self.has_next)(lambda: greet(*to_next))
        if to_last:
            pl.when(self.has_last)(lambda: greet(*to_last))
        pl.semaphore_wait(barrier, 3 + expect)


class Route:
    def __init__(self, sems, index, device, source, target, sends=True, gets=True, arrival=None):
        self.sends, self.gets = sends, gets
        landed = target if arrival is None else arrival
        send, recv = sems[0].at[index], sems[1].at[index]
        self.make = lambda end: pltpu.make_async_remote_copy(
            source, end, send, recv, device_id=device, device_id_type=MESH
        )
        self.target, self.landed = target, landed

    @staticmethod
    def only(condition, act):
        if condition is True:
            act()
        else:
            pl.when(condition)(act)

    def start(self):
        self.only(self.sends, lambda: self.make(self.target).start())

    def arrived(self):
        self.only(self.gets, lambda: self.make(self.landed).wait_recv())

    def sent(self):
        self.only(self.sends, lambda: self.make(self.target).wait_send())


def gather_kernel(
    columns, heads, docs_ref, q_ref, g_ref, o_ref, k_ref, v_ref, log_ref,
    q_other, g_other, stat_both, window_out, dq_out, kv_out,
    q_both, g_both, o_vmem, k_own, v_own, stat, window, dqt, dkv, bias, local, put, send, recv,
):
    at = Links(columns)
    z, core, up, down, across = at.z, at.core, at.up, at.down, at.across
    sems = (send, recv)
    mine = window.at[slot(OWN, z, core)]
    loads = [
        pltpu.make_async_copy(source, target, local.at[n])
        for n, (source, target) in enumerate(
            (
                (k_ref, k_own), (v_ref, v_own), (q_ref, q_both.at[0]), (g_ref, g_both.at[0]),
                (o_ref, o_vmem), (log_ref, stat.at[0, 0]),
            )
        )
    ]
    for copy in loads:
        copy.start()

    @pl.when(at.column == 0)
    def _():
        window[slot(BEFORE, 3, 1)] = jnp.zeros((2, B, W), window.dtype)

    at.barrier(to_last=(at.last,), expect=at.has_next.astype(jnp.int32))

    theirs = window.at[slot(OWN, z, 1 - core)]
    swap_k = Route(sems, 0, at.sibling, k_own.at[B:], mine.at[0], arrival=theirs.at[0])
    swap_v = Route(sems, 1, at.sibling, v_own.at[B:], mine.at[1], arrival=theirs.at[1])
    loads[0].wait()
    loads[1].wait()
    swap_k.start()
    swap_v.start()
    mine[0] = k_own[:B]
    mine[1] = v_own[:B]
    rows = q_ref.shape[0]
    bulk = []
    for part in range(2):
        some = slice(part * rows // 2, (part + 1) * rows // 2)
        bulk.append(Route(sems, 2 + part, at.sibling, q_both.at[0, some], q_both.at[1, some]))
        bulk.append(Route(sems, 4 + part, at.sibling, g_both.at[0, some], g_both.at[1, some]))

    def passed(index, device, side, sent, j, got, sends=True, gets=True):
        there = window.at[slot(side, sent, j)]
        return Route(sems, index, device, there, there, sends, gets, window.at[slot(side, got, j)])

    up_0 = passed(6, at.above, OWN, z, 0, down)
    up_1 = passed(7, at.above, OWN, z, 1, down)
    down_0 = passed(8, at.below, OWN, z, 0, up)
    down_1 = passed(9, at.below, OWN, z, 1, up, z == 0, z == 3)
    far_0 = passed(10, at.below, OWN, up, 0, across)
    far_1 = passed(11, at.above, OWN, down, 1, across)

    def later(index, zc, j, when=True):
        here = window.at[slot(OWN, zc, j)]
        there = window.at[slot(BEFORE, zc, j)]
        sends = at.has_next if when is True else at.has_next & when
        gets = at.has_last if when is True else at.has_last & when
        return Route(sems, index, at.next, here, there, sends, gets)

    next_0 = later(12, z, 0)
    next_1 = later(13, z, 1)
    next_far_0 = later(14, across, 0, z < 2)
    next_far_1 = later(15, across, 1)
    last = at.has_last
    before_up_0 = passed(16, at.above, BEFORE, z, 0, down, last & (z == 3), last & (z == 0))
    before_up_1 = passed(17, at.above, BEFORE, z, 1, down, last, last)
    before_down_0 = passed(18, at.below, BEFORE, z, 0, up, last & (z != 0), last & (z != 3))
    before_down_1 = passed(19, at.below, BEFORE, z, 1, up, last, last)
    stats = Route(sems, 20, at.sibling, stat.at[0], stat.at[1])

    swap_k.arrived()
    swap_v.arrived()
    for copy in (up_1, down_0, next_1):
        copy.start()
    for copy in loads[2:]:
        copy.wait()

    ones = jnp.ones((8, W), jnp.bfloat16)
    for h in range(heads):
        cols = slice(h * W, (h + 1) * W)
        product = g_both[0, :, cols].astype(jnp.float32) * o_vmem[:, cols].astype(jnp.float32)
        high = product.astype(jnp.bfloat16)
        low = (product - high.astype(jnp.float32)).astype(jnp.bfloat16)
        total = nt(ones, high) + nt(ones, low)
        stat[0, 1, h : h + 1, :] = total[0:1]
    stat[0, 0] = stat[0, 0] * LOG2E
    stats.start()
    for copy in (next_0, up_0, down_1):
        copy.start()
    for copy in bulk:
        copy.start()

    ends = doc_ends(docs_ref)
    column = at.column * 16 * B
    dkv[...] = jnp.zeros_like(dkv)
    dqt[...] = jnp.zeros_like(dqt)

    def products(side, part, k, v, mask):
        here = pl.ds(pl.multiple_of(part * B, B), B)
        return gradients(
            k, v,
            [q_both[side, here, h * W : (h + 1) * W] for h in range(heads)],
            [g_both[side, here, h * W : (h + 1) * W] for h in range(heads)],
            [stat[side, 0, h : h + 1, here] for h in range(heads)],
            [stat[side, 1, h : h + 1, here] for h in range(heads)],
            mask,
        )

    up_1.arrived()
    far_1.start()
    down_0.arrived()
    far_0.start()
    next_1.arrived()
    before_down_1.start()
    before_up_1.start()
    next_0.arrived()
    before_down_0.start()
    before_up_0.start()

    near_4 = jnp.where(z > 0, slot(OWN, down, 1), slot(OWN, 3, 0))
    near_0 = jnp.where(z > 0, slot(OWN, down, 0), slot(BEFORE, 3, 1))

    def half_of(tile):
        return jnp.where((tile + 8) % 8 >= 4, 1 - core, core)

    def near(side, part, tile, keys, key_tiles, out):
        start = doc_start(ends, positions(column + tile * 2 * B + part * B))
        for n, key_tile in enumerate(key_tiles):
            key = column + key_tile * 2 * B + half_of(key_tile) * B
            kpos = (key + lax.broadcasted_iota(jnp.int32, (B, B), 0)).astype(jnp.float32)
            bias[n * B : (n + 1) * B] = jnp.where(kpos >= start, 0.0, -jnp.inf)
        dk, dv, dq = products(
            side, part,
            jnp.concatenate([window[n, 0] for n in keys], axis=0),
            jnp.concatenate([window[n, 1] for n in keys], axis=0),
            bias.at[: len(keys) * B],
        )
        for n in range(len(keys)):
            dkv[out + n, 0] += dk[n * B : (n + 1) * B]
            dkv[out + n, 1] += dv[n * B : (n + 1) * B]
        dqt[side * 2 + part] += dq

    puts = [
        pltpu.make_async_copy(source, target, put.at[n])
        for n, (source, target) in enumerate(
            (
                (q_both.at[1], q_other), (g_both.at[1], g_other), (stat, stat_both),
                (window.at[8:], window_out.at[8:]), (dqt.at[:2], dq_out.at[:2]),
                (window.at[:8], window_out.at[:8]), (dqt.at[2:], dq_out.at[2:]), (dkv, kv_out),
            )
        )
    ]

    def sibling_here():
        for copy in bulk:
            copy.arrived()
        stats.arrived()

    flip = (core == 0) & (z == 0)

    @pl.loop(0, 4)
    def _(n):
        @pl.when(n == 0)
        def _():
            up_0.arrived()
            pl.when(flip)(sibling_here)

        @pl.when(n == 1)
        def _():
            far_0.arrived()
            next_far_0.start()
            far_1.arrived()
            next_far_1.start()

        @pl.when(n == 2)
        def _():
            down_1.arrived()
            pl.when(jnp.logical_not(flip))(sibling_here)
            pl.when(z == 0)(before_up_1.arrived)
            for copy in puts[:4]:
                copy.start()

        side, part = jnp.where(flip, 1 - n // 2, n // 2), n % 2

        @pl.when(side == core)
        def _():
            near(side, part, z, [near_0], [z - 1], 2)

        @pl.when(side != core)
        def _():
            near(side, part, z + 4, [slot(OWN, z, 0), near_4], [z, z + 3], 0)

    for copy in (puts[4], puts[6], puts[7]):
        copy.start()
    pl.when(z != 0)(before_up_1.arrived)
    for copy in (before_up_0, before_down_0, before_down_1, next_far_0, next_far_1):
        copy.arrived()
    puts[5].start()
    for copy in (
        [swap_k, swap_v, up_0, up_1, down_0, down_1, far_0, far_1, next_0, next_1, next_far_0]
        + [next_far_1, before_up_0, before_up_1, before_down_0, before_down_1, stats]
        + bulk
    ):
        copy.sent()
    for copy in puts:
        copy.wait()


def gather(columns, docs, q, g, o, k, v, log_total):
    rows, features = q.shape
    heads = features // W
    some = pl.BlockSpec(memory_space=pl.ANY)
    window = (16, 2, B, W)
    stat = (2, 2, heads, rows)
    turned = (4, W, heads * B)
    sums = (3, 2, B, W)
    return pl.pallas_call(
        functools.partial(gather_kernel, columns, heads),
        out_shape=(
            jax.ShapeDtypeStruct(q.shape, q.dtype),
            jax.ShapeDtypeStruct(q.shape, q.dtype),
            jax.ShapeDtypeStruct(stat, jnp.float32),
            jax.ShapeDtypeStruct(window, k.dtype),
            jax.ShapeDtypeStruct(turned, jnp.float32),
            jax.ShapeDtypeStruct(sums, jnp.float32),
        ),
        in_specs=[pl.BlockSpec(memory_space=pltpu.VMEM)] + [some] * 6,
        out_specs=(some,) * 6,
        scratch_shapes=[
            pltpu.VMEM((2, rows, features), q.dtype),
            pltpu.VMEM((2, rows, features), q.dtype),
            pltpu.VMEM(q.shape, q.dtype),
            pltpu.VMEM(k.shape, k.dtype),
            pltpu.VMEM(k.shape, k.dtype),
            pltpu.VMEM(stat, jnp.float32),
            pltpu.VMEM(window, k.dtype),
            pltpu.VMEM(turned, jnp.float32),
            pltpu.VMEM(sums, jnp.float32),
            pltpu.VMEM((2 * B, B), jnp.float32),
            pltpu.SemaphoreType.DMA((6,)),
            pltpu.SemaphoreType.DMA((8,)),
            pltpu.SemaphoreType.DMA((21,)),
            pltpu.SemaphoreType.DMA((21,)),
        ],
        compiler_params=pltpu.CompilerParams(
            collective_id=0, has_side_effects=True, vmem_limit_bytes=VMEM
        ),
    )(docs, q, g, o, k, v, log_total)


def attend_kernel(
    heads, docs_ref, qa_hbm, qb_hbm, ga_hbm, gb_hbm, stat_hbm, window_hbm, dq_hbm, kv_hbm,
    dq_own, dq_other, part_hbm,
    q_ref, g_ref, stat_ref, window_ref, dqt, dqh, part_ref, dka, dva, dkv, bias, starts, bounds, get, put,
):
    column, z, core = place()
    loads = [
        pltpu.make_async_copy(source, target, get.at[n])
        for n, (source, target) in enumerate(
            (
                (stat_hbm, stat_ref),
                (window_hbm.at[:8], window_ref.at[:8]), (window_hbm.at[8:], window_ref.at[8:]),
                (kv_hbm, dkv), (qa_hbm, q_ref.at[0]), (ga_hbm, g_ref.at[0]),
                (qb_hbm, q_ref.at[1]), (gb_hbm, g_ref.at[1]), (dq_hbm.at[2:], dqt.at[2:]),
            )
        )
    ]
    for load in loads:
        load.start()
    ends = doc_ends(docs_ref)
    window = (column - 1) * 16 * B

    def half_of(b):
        return jnp.where(b % 8 >= 4, 1 - core, core)

    def tile_of(side):
        return z + 4 * (core if side == 0 else 1 - core)

    for block in range(4):
        side, part = divmod(block, 2)
        first = column * 16 * B + tile_of(side) * 2 * B + part * B
        start = doc_start(ends, positions(first))
        starts[block] = start
        low = jnp.min(start).astype(jnp.int32) - window
        last = jnp.max(start).astype(jnp.int32) - window
        b = low // (2 * B)
        bounds[0, block] = jnp.where(low % (2 * B) >= half_of(b) * B + B, b + 1, b)
        b = last // (2 * B)
        bounds[1, block] = jnp.where(last % (2 * B) > half_of(b) * B, b + 1, b)
    dka[...] = jnp.zeros_like(dka)
    dva[...] = jnp.zeros_like(dva)
    dqt[:2] = jnp.zeros((2, *dqt.shape[1:]), dqt.dtype)
    for load in loads[:6]:
        load.wait()
    down = lax.rem(z + 3, 4)
    nears = (
        slot(OWN, z, 0),
        jnp.where(z > 0, slot(OWN, down, 1), slot(OWN, 3, 0)),
        jnp.where(z > 0, slot(OWN, down, 0), slot(BEFORE, 3, 1)),
    )
    for n, at in enumerate(nears):
        dka[at] = dkv[n, 0]
        dva[at] = dkv[n, 1]

    @pl.loop(0, 4)
    def _(block):
        side, part = block // 2, block % 2
        here = pl.ds(pl.multiple_of(part * B, B), B)

        @pl.when(block == 2)
        def _():
            for load in loads[6:]:
                load.wait()

        def work(blocks, mask=None):
            at = [slot(b // 8, b % 4, b % 8 // 4) for b in blocks]
            dk, dv, dq = gradients(
                jnp.concatenate([window_ref[n, 0] for n in at], axis=0),
                jnp.concatenate([window_ref[n, 1] for n in at], axis=0),
                [q_ref[side, here, h * W : (h + 1) * W] for h in range(heads)],
                [g_ref[side, here, h * W : (h + 1) * W] for h in range(heads)],
                [stat_ref[side, 0, h : h + 1, here] for h in range(heads)],
                [stat_ref[side, 1, h : h + 1, here] for h in range(heads)],
                mask,
            )
            for n in range(len(at)):
                dva[at[n]] += dv[n * B : (n + 1) * B]
                dka[at[n]] += dk[n * B : (n + 1) * B]
            dqt[block] += dq

        second = jnp.where(side == 0, core, 1 - core)
        end = 7 + z + 4 * second
        skip = jnp.where(second == 1, 8 + z, 16)

        def counted(b):
            return jnp.where(b > skip, b - 1, b)

        def real(n):
            return jnp.where(n >= skip, n + 1, n)

        end = counted(end)
        low = counted(bounds[0, block])
        cut = jnp.minimum(counted(bounds[1, block]), end)
        cut = cut + (end - cut) % 2

        @pl.loop(low, cut)
        def _(n):
            b = real(n)
            key = window + b * 2 * B + half_of(b) * B
            kpos = (key + lax.broadcasted_iota(jnp.int32, (B, B), 0)).astype(jnp.float32)
            bias[...] = jnp.where(kpos >= starts[block], 0.0, -jnp.inf)
            work([b], bias)

        pairs = jnp.maximum(end - jnp.maximum(low, cut), 0) // 2
        odd = pairs % 2

        @pl.loop(0, odd)
        def _(n):
            work([real(cut), real(cut + 1)])

        @pl.loop(0, pairs // 2)
        def _(n):
            first = cut + 2 * odd + 4 * n
            work([real(first + m) for m in range(4)])

        @pl.when(side == 0)
        def _():
            pltpu.make_async_copy(dqt.at[block], dq_own.at[part], put.at[block]).start()

        @pl.when(side == 1)
        def _():
            dqh[part] = dqt[block].astype(jnp.bfloat16)
            pltpu.make_async_copy(dqh.at[part], dq_other.at[part], put.at[block]).start()

    @pl.loop(0, 16)
    def _(s):
        part_ref[s, 0] = (dka[s] * (1.0 / math.sqrt(W))).astype(jnp.bfloat16)
        part_ref[s, 1] = dva[s].astype(jnp.bfloat16)
        pltpu.make_async_copy(part_ref.at[s], part_hbm.at[s], put.at[4 + s]).start()

    for part in range(2):
        pltpu.make_async_copy(dqt.at[part], dq_own.at[part], put.at[part]).wait()
        pltpu.make_async_copy(dqh.at[part], dq_other.at[part], put.at[2 + part]).wait()
    for s in range(16):
        pltpu.make_async_copy(part_ref.at[s], part_hbm.at[s], put.at[4 + s]).wait()


def attend(docs, q, q_other, g, g_other, stat, window, dq, sums):
    rows, features = q.shape
    heads = features // W
    some = pl.BlockSpec(memory_space=pl.ANY)
    both = (2, rows, features)
    turned = (2, W, heads * B)
    return pl.pallas_call(
        functools.partial(attend_kernel, heads),
        out_shape=(
            jax.ShapeDtypeStruct(turned, jnp.float32),
            jax.ShapeDtypeStruct(turned, jnp.bfloat16),
            jax.ShapeDtypeStruct(window.shape, jnp.bfloat16),
        ),
        in_specs=[pl.BlockSpec(memory_space=pltpu.VMEM)] + [some] * 8,
        out_specs=(some,) * 3,
        scratch_shapes=[
            pltpu.VMEM(both, q.dtype),
            pltpu.VMEM(both, q.dtype),
            pltpu.VMEM(stat.shape, stat.dtype),
            pltpu.VMEM(window.shape, window.dtype),
            pltpu.VMEM((4, W, heads * B), jnp.float32),
            pltpu.VMEM(turned, jnp.bfloat16),
            pltpu.VMEM(window.shape, jnp.bfloat16),
            pltpu.VMEM((16, B, W), jnp.float32),
            pltpu.VMEM((16, B, W), jnp.float32),
            pltpu.VMEM(sums.shape, jnp.float32),
            pltpu.VMEM((B, B), jnp.float32),
            pltpu.VMEM((4, 1, B), jnp.float32),
            pltpu.SMEM((2, 4), jnp.int32),
            pltpu.SemaphoreType.DMA((9,)),
            pltpu.SemaphoreType.DMA((20,)),
        ],
        compiler_params=pltpu.CompilerParams(vmem_limit_bytes=VMEM),
        cost_estimate=pl.CostEstimate(
            flops=20 * 10 * heads * B * B * W, bytes_accessed=16 << 20, transcendentals=0
        ),
    )(docs, q, q_other, g, g_other, stat, window, dq, sums)


def return_kernel(
    columns, heads, docs_ref, q_hbm, k_hbm, v_hbm, g_hbm, stat_hbm, dq_near, dq_own, dq_other, part_ref,
    dq_hbm, own_hbm, got_hbm, rest_hbm,
    q_ref, k_ref, v_ref, g_ref, stat, dqt, dqn, dq_got, dq_out, own_half, rest, dka, dva, bias,
    part, across_got, beside_got, beside_sum, later_got, far_got, far_sum, near_sum,
    near_got, final, given_half, local, put, send, recv,
):
    at = Links(columns)
    z, core, up, down, across = at.z, at.core, at.up, at.down, at.across
    sems = (send, recv)
    load = pltpu.make_async_copy(part_ref.at[:8], part.at[:8], local.at[0])
    load_own = pltpu.make_async_copy(part_ref.at[8:], part.at[8:], local.at[1])
    load_dq = pltpu.make_async_copy(dq_near.at[:2], dqn, local.at[2])
    load.start()
    load_own.start()
    load_dq.start()
    loads = [
        pltpu.make_async_copy(source, target, local.at[3 + n])
        for n, (source, target) in enumerate(
            (
                (q_hbm, q_ref), (g_hbm, g_ref), (k_hbm, k_ref), (v_hbm, v_ref),
                (stat_hbm.at[0], stat), (dq_own, dqt),
            )
        )
    ]
    for copy in loads:
        copy.start()
    at.barrier(to_next=(at.next,), expect=at.has_last.astype(jnp.int32))
    has_next, has_last = at.has_next, at.has_last

    def given(side, zc, j):
        return part_ref.at[slot(side, zc, j)]

    def held(side, zc, j):
        return part[slot(side, zc, j)].astype(jnp.float32)

    far_back = [
        Route(
            sems, j, at.last, given(BEFORE, across, j), across_got.at[j],
            has_last & (z < 2) if j == 0 else has_last,
            has_next & (z < 2) if j == 0 else has_next,
        )
        for j in range(2)
    ]
    side_up = [
        Route(
            sems, 2 + j, at.above, given(BEFORE, up, j), beside_got.at[0, j],
            has_last & (z != 3) if j == 0 else has_last,
            has_last & (z != 0) if j == 0 else has_last,
        )
        for j in range(2)
    ]
    side_down = [
        Route(
            sems, 4 + j, at.below, given(BEFORE, down, j), beside_got.at[1, j],
            has_last & (z == 0) if j == 0 else has_last,
            has_last & (z == 3) if j == 0 else has_last,
        )
        for j in range(2)
    ]
    bulk = [
        Route(sems, 6 + n, at.sibling, dq_other.at[n], dq_got.at[n]) for n in range(2)
    ]
    back = [
        Route(sems, 8 + j, at.last, beside_sum.at[j], later_got.at[j], has_last, has_next)
        for j in range(2)
    ]
    far_up = Route(sems, 10, at.above, far_sum.at[0], far_got.at[0])
    far_down = Route(sems, 11, at.below, far_sum.at[1], far_got.at[1])
    near_up_0 = Route(sems, 12, at.above, near_sum.at[0], near_got.at[0])
    near_up_1 = Route(sems, 13, at.above, given(OWN, up, 1), near_got.at[1], z == 3, z == 0)
    near_down_0 = Route(sems, 14, at.below, given(OWN, down, 0), near_got.at[2])
    near_down_1 = Route(sems, 15, at.below, near_sum.at[1], near_got.at[3])

    for copy in (side_down[1], side_up[1], far_back[1], side_up[0], side_down[0], far_back[0]):
        copy.start()
    for copy in bulk:
        copy.start()
    for copy in (load, load_own, load_dq, *loads):
        copy.wait()
    ends = doc_ends(docs_ref)
    tile = at.column * 16 * B + (z + 4 * core) * 2 * B
    dka[...] = jnp.zeros_like(dka)
    dva[...] = jnp.zeros_like(dva)

    def diagonal(n):
        block, b = (n + 1) // 2, n // 2
        here = pl.ds(pl.multiple_of(block * B, B), B)
        there = pl.ds(pl.multiple_of(b * B, B), B)
        pos = positions(tile + block * B)
        bias[...] = hidden(tile + b * B, doc_start(ends, pos), pos)
        dk, dv, dq = gradients(
            k_ref[there],
            v_ref[there],
            [q_ref[here, h * W : (h + 1) * W] for h in range(heads)],
            [g_ref[here, h * W : (h + 1) * W] for h in range(heads)],
            [stat[0, h : h + 1, here] for h in range(heads)],
            [stat[1, h : h + 1, here] for h in range(heads)],
            bias,
        )
        dka[b] += dk
        dva[b] += dv
        dqt[block] += dq

    pl.loop(0, 3)(diagonal)
    scale = 1.0 / math.sqrt(W)
    rest[0] = dka[1] * scale
    rest[1] = dva[1]
    out_rest = pltpu.make_async_copy(rest, rest_hbm, put.at[2])
    out_rest.start()

    @pl.when(has_last)
    def _():
        for copy in side_up + side_down:
            copy.arrived()
        for j in range(2):
            final[j] = held(BEFORE, z, j)
        final[1] += beside_got[0, 1].astype(jnp.float32) + beside_got[1, 1].astype(jnp.float32)

        @pl.when(z != 0)
        def _():
            final[0] += beside_got[0, 0].astype(jnp.float32)

        @pl.when(z == 3)
        def _():
            final[0] += beside_got[1, 0].astype(jnp.float32)

        beside_sum[...] = final[...].astype(jnp.bfloat16)
        for copy in back:
            copy.start()

    def add_across(j):
        far_back[j].make(across_got.at[j]).wait_recv()
        final[j] += across_got[j].astype(jnp.float32)

    for j in range(2):
        final[j] = held(OWN, across, j)
        pl.when(far_back[j].gets)(functools.partial(add_across, j))
        far_sum[j] = final[j].astype(jnp.bfloat16)
    for copy in (far_up, far_down, near_down_0, near_up_1):
        copy.start()
    for copy in bulk:
        copy.arrived()
    eye = identity(B)
    for block in range(2):
        for h in range(heads):
            rows = slice(h * B, (h + 1) * B)
            total = dqt[block, :, rows] + dqn[block, :, rows]
            total = total + dq_got[block, :, rows].astype(jnp.float32)
            rounded = (total * (1.0 / math.sqrt(W))).astype(jnp.bfloat16)
            turned = nt(eye, rounded).astype(jnp.bfloat16)
            dq_out[block * B : (block + 1) * B, h * W : (h + 1) * W] = turned
    out_q = pltpu.make_async_copy(dq_out, dq_hbm, put.at[0])
    out_q.start()
    far_up.arrived()
    near_sum[0] = (held(OWN, up, 0) + far_got[0].astype(jnp.float32)).astype(jnp.bfloat16)
    near_up_0.start()
    far_down.arrived()
    near_sum[1] = (held(OWN, down, 1) + far_got[1].astype(jnp.float32)).astype(jnp.bfloat16)
    near_down_1.start()
    near_down_0.arrived()
    near_up_0.arrived()
    final[0] = (
        held(OWN, z, 0) + near_got[0].astype(jnp.float32) + near_got[2].astype(jnp.float32)
    )
    near_down_1.arrived()
    final[1] = held(OWN, z, 1) + near_got[3].astype(jnp.float32)

    @pl.when(z == 0)
    def _():
        near_up_1.make(near_got.at[1]).wait_recv()
        final[1] += near_got[1].astype(jnp.float32)

    @pl.when(has_next)
    def _():
        for j in range(2):
            back[j].make(later_got.at[j]).wait_recv()
            final[j] += later_got[j].astype(jnp.float32)

    given_half[...] = final[1 - core].astype(jnp.bfloat16)
    give = Route(sems, 16, at.sibling, given_half, got_hbm)
    give.start()
    own_half[0] = (final[core, 0] + dka[0] * scale).astype(jnp.bfloat16)
    own_half[1] = (final[core, 1] + dva[0]).astype(jnp.bfloat16)
    out_own = pltpu.make_async_copy(own_half, own_hbm, put.at[1])
    out_own.start()
    give.arrived()
    for copy in (out_q, out_own, out_rest):
        copy.wait()
    for copy in (
        far_back + side_up + side_down + bulk + back
        + [far_up, far_down, near_up_0, near_up_1, near_down_0, near_down_1, give]
    ):
        copy.sent()


def give_back(columns, docs, q, k, v, g, stat, dq_near, dq_own, dq_other, part):
    rows, features = q.shape
    heads = features // W
    some = pl.BlockSpec(memory_space=pl.ANY)
    vmem = pl.BlockSpec(memory_space=pltpu.VMEM)
    block = (2, B, W)
    return pl.pallas_call(
        functools.partial(return_kernel, columns, heads),
        out_shape=(
            jax.ShapeDtypeStruct((rows, features), jnp.bfloat16),
            jax.ShapeDtypeStruct(block, jnp.bfloat16),
            jax.ShapeDtypeStruct(block, jnp.bfloat16),
            jax.ShapeDtypeStruct(block, jnp.float32),
        ),
        in_specs=[vmem] + [some] * 9,
        out_specs=(some,) * 4,
        scratch_shapes=[
            pltpu.VMEM(q.shape, q.dtype),
            pltpu.VMEM(k.shape, k.dtype),
            pltpu.VMEM(v.shape, v.dtype),
            pltpu.VMEM(g.shape, g.dtype),
            pltpu.VMEM(stat.shape[1:], stat.dtype),
            pltpu.VMEM(dq_own.shape, dq_own.dtype),
            pltpu.VMEM(dq_own.shape, dq_own.dtype),
            pltpu.VMEM(dq_other.shape, dq_other.dtype),
            pltpu.VMEM(q.shape, jnp.bfloat16),
            pltpu.VMEM(block, jnp.bfloat16),
            pltpu.VMEM(block, jnp.float32),
            pltpu.VMEM((2, B, W), jnp.float32),
            pltpu.VMEM((2, B, W), jnp.float32),
            pltpu.VMEM((B, B), jnp.float32),
            pltpu.VMEM((16, *block), jnp.bfloat16),
            pltpu.VMEM((2, *block), jnp.bfloat16),
            pltpu.VMEM((2, 2, *block), jnp.bfloat16),
            pltpu.VMEM((2, *block), jnp.bfloat16),
            pltpu.VMEM((2, *block), jnp.bfloat16),
            pltpu.VMEM((2, *block), jnp.bfloat16),
            pltpu.VMEM((2, *block), jnp.bfloat16),
            pltpu.VMEM((2, *block), jnp.bfloat16),
            pltpu.VMEM((4, *block), jnp.bfloat16),
            pltpu.VMEM((2, *block), jnp.float32),
            pltpu.VMEM(block, jnp.bfloat16),
            pltpu.SemaphoreType.DMA((9,)),
            pltpu.SemaphoreType.DMA((3,)),
            pltpu.SemaphoreType.DMA((18,)),
            pltpu.SemaphoreType.DMA((18,)),
        ],
        compiler_params=pltpu.CompilerParams(
            collective_id=1, has_side_effects=True, vmem_limit_bytes=VMEM
        ),
    )(docs, q, k, v, g, stat, dq_near, dq_own, dq_other, part)


def publish_kernel(
    dq_ref, own_ref, got_ref, rest_ref, dq_out, dk_out, dv_out,
    dq, own, got, rest, dk, dv, get, put,
):
    loads, outs = [], []
    for n in range(4):
        here = slice(n * B // 2, (n + 1) * B // 2)
        loads.append(pltpu.make_async_copy(dq_ref.at[here], dq.at[here], get.at[n]))
        outs.append(pltpu.make_async_copy(dq.at[here], dq_out.at[here], put.at[n]))
    for n, (source, target) in enumerate(((own_ref, own), (got_ref, got), (rest_ref, rest))):
        loads.append(pltpu.make_async_copy(source, target, get.at[4 + n]))
    outs.append(pltpu.make_async_copy(dk, dk_out, put.at[4]))
    outs.append(pltpu.make_async_copy(dv, dv_out, put.at[5]))
    for copy in loads:
        copy.start()
    for load, out in zip(loads[:4], outs[:4]):
        load.wait()
        out.start()
    for copy in loads[4:]:
        copy.wait()
    for n, target in enumerate((dk, dv)):
        target[:B] = own[n]
        target[B:] = (got[n].astype(jnp.float32) + rest[n]).astype(jnp.bfloat16)
    for copy in outs[4:]:
        copy.start()
    for copy in outs:
        copy.wait()


def publish(dq, own, got, rest):
    some = pl.BlockSpec(memory_space=pl.ANY)
    keys = (2 * B, W)
    return pl.pallas_call(
        publish_kernel,
        out_shape=(
            jax.ShapeDtypeStruct(dq.shape, dq.dtype),
            jax.ShapeDtypeStruct(keys, jnp.bfloat16),
            jax.ShapeDtypeStruct(keys, jnp.bfloat16),
        ),
        in_specs=[some] * 4,
        out_specs=(some,) * 3,
        scratch_shapes=[pltpu.VMEM(x.shape, x.dtype) for x in (dq, own, got, rest)]
        + [pltpu.VMEM(keys, jnp.bfloat16)] * 2
        + [pltpu.SemaphoreType.DMA((7,)), pltpu.SemaphoreType.DMA((6,))],
        compiler_params=pltpu.CompilerParams(vmem_limit_bytes=VMEM),
    )(dq, own, got, rest)


def solution(mesh):
    columns = mesh.shape["ctx"] // 2

    def on_device(q, k, v, o, g, log_total, doc_lengths):
        docs = doc_lengths[None, :]
        q_other, g_other, stat, window, dq, sums = gather(columns, docs, q, g, o, k, v, log_total)
        dq_own, dq_other, part = attend(docs, q, q_other, g, g_other, stat, window, dq, sums)
        return publish(*give_back(columns, docs, q, k, v, g, stat, dq, dq_own, dq_other, part))

    rows = P(("ctx", "section"), None)
    return jax.shard_map(
        on_device,
        mesh=mesh,
        in_specs=(rows, rows, rows, rows, rows, P(None, ("ctx", "section")), P()),
        out_specs=(rows, rows, rows),
        check_vma=False,
    )
```

```python
import functools
import math

import jax
import jax.numpy as jnp
from jax import lax
from jax.experimental import pallas as pl
from jax.experimental.pallas import tpu as pltpu
from jax.sharding import PartitionSpec as P

MESH = pl.DeviceIdType.MESH
W = 128
B = 256
VMEM = 58 << 20
LOG2E = math.log2(math.e)
OWN, BEFORE = 1, 0


def nn(a, b):
    return jnp.dot(a, b, preferred_element_type=jnp.float32)


def nt(a, b):
    return lax.dot_general(a, b, (((1,), (1,)), ((), ())), preferred_element_type=jnp.float32)


def place():
    ctx = lax.axis_index("ctx")
    return ctx // 2, lax.axis_index("section"), ctx % 2


def slot(side, z, j):
    return side * 8 + z * 2 + j


def doc_ends(docs_ref):
    lengths = docs_ref[...].astype(jnp.float32)
    docs = lengths.shape[1]
    upto = lax.broadcasted_iota(jnp.int32, (docs, docs), 1) <= lax.broadcasted_iota(
        jnp.int32, (docs, docs), 0
    )
    return jnp.sum(jnp.where(upto, lengths, 0.0), axis=1, keepdims=True)


def positions(first):
    return first.astype(jnp.float32) + lax.broadcasted_iota(jnp.int32, (1, B), 1).astype(
        jnp.float32
    )


def doc_start(ends, pos):
    return jnp.max(jnp.where(ends <= pos, ends, 0.0), axis=0, keepdims=True)


def hidden(key, start, pos):
    kpos = (key + lax.broadcasted_iota(jnp.int32, (B, B), 0)).astype(jnp.float32)
    return jnp.where((kpos >= start) & (kpos <= pos), 0.0, -jnp.inf)


def identity(n):
    at = [lax.broadcasted_iota(jnp.int32, (n, n), d) for d in range(2)]
    return (at[0] == at[1]).astype(jnp.bfloat16)


def gradients(k, v, qs, gs, logs, deltas, bias=None):
    ps, ds = [], []
    for q, g, log, delta in zip(qs, gs, logs, deltas):
        x = nt(k, q) * (LOG2E / math.sqrt(W)) - log
        if bias is not None:
            x = x + bias[...]
        p = jnp.exp2(x)
        d = p * (nt(v, g) - delta)
        ps.append(p.astype(jnp.bfloat16))
        ds.append(d.astype(jnp.bfloat16))
    dh = jnp.concatenate(ds, axis=1)
    dv = nn(jnp.concatenate(ps, axis=1), jnp.concatenate(gs, axis=0))
    dk = nn(dh, jnp.concatenate(qs, axis=0))
    return dk, dv, nn(k.T, dh)


class Links:
    def __init__(self, columns):
        self.column, self.z, self.core = place()
        ctx = lax.axis_index("ctx")
        self.up = lax.rem(self.z + 1, 4)
        self.down = lax.rem(self.z + 3, 4)
        self.across = lax.rem(self.z + 2, 4)
        self.sibling = (ctx + 1 - 2 * self.core, self.z)
        self.above = (ctx, self.up)
        self.below = (ctx, self.down)
        self.has_next = self.column < columns - 1
        self.has_last = self.column > 0
        self.next = (jnp.where(self.has_next, ctx + 2, ctx), self.z)
        self.last = (jnp.where(self.has_last, ctx - 2, ctx), self.z)

    def barrier(self, to_next=(), to_last=(), expect=0):
        barrier = pltpu.get_barrier_semaphore()

        def greet(*devices):
            for device in devices:
                pl.semaphore_signal(barrier, inc=1, device_id=device, device_id_type=MESH)

        greet(self.sibling, self.above, self.below)
        if to_next:
            pl.when(self.has_next)(lambda: greet(*to_next))
        if to_last:
            pl.when(self.has_last)(lambda: greet(*to_last))
        pl.semaphore_wait(barrier, 3 + expect)


class Route:
    def __init__(self, sems, index, device, source, target, sends=True, gets=True, arrival=None):
        self.sends, self.gets = sends, gets
        landed = target if arrival is None else arrival
        send, recv = sems[0].at[index], sems[1].at[index]
        self.make = lambda end: pltpu.make_async_remote_copy(
            source, end, send, recv, device_id=device, device_id_type=MESH
        )
        self.target, self.landed = target, landed

    @staticmethod
    def only(condition, act):
        if condition is True:
            act()
        else:
            pl.when(condition)(act)

    def start(self):
        self.only(self.sends, lambda: self.make(self.target).start())

    def arrived(self):
        self.only(self.gets, lambda: self.make(self.landed).wait_recv())

    def sent(self):
        self.only(self.sends, lambda: self.make(self.target).wait_send())


def gather_kernel(
    columns, heads, docs_ref, q_ref, g_ref, o_ref, k_ref, v_ref, log_ref,
    q_other, g_other, stat_both, window_out, dq_out, kv_out,
    q_both, g_both, o_vmem, k_own, v_own, stat, window, dqt, dkv, bias, local, put, send, recv,
):
    at = Links(columns)
    z, core, up, down, across = at.z, at.core, at.up, at.down, at.across
    sems = (send, recv)
    mine = window.at[slot(OWN, z, core)]
    loads = [
        pltpu.make_async_copy(source, target, local.at[n])
        for n, (source, target) in enumerate(
            (
                (k_ref, k_own), (v_ref, v_own), (q_ref, q_both.at[0]), (g_ref, g_both.at[0]),
                (o_ref, o_vmem), (log_ref, stat.at[0, 0]),
            )
        )
    ]
    for copy in loads:
        copy.start()

    @pl.when(at.column == 0)
    def _():
        window[slot(BEFORE, 3, 1)] = jnp.zeros((2, B, W), window.dtype)

    at.barrier(to_last=(at.last,), expect=at.has_next.astype(jnp.int32))

    theirs = window.at[slot(OWN, z, 1 - core)]
    swap_k = Route(sems, 0, at.sibling, k_own.at[B:], mine.at[0], arrival=theirs.at[0])
    swap_v = Route(sems, 1, at.sibling, v_own.at[B:], mine.at[1], arrival=theirs.at[1])
    loads[0].wait()
    loads[1].wait()
    swap_k.start()
    swap_v.start()
    mine[0] = k_own[:B]
    mine[1] = v_own[:B]
    rows = q_ref.shape[0]
    bulk = []
    for part in range(2):
        some = slice(part * rows // 2, (part + 1) * rows // 2)
        bulk.append(Route(sems, 2 + part, at.sibling, q_both.at[0, some], q_both.at[1, some]))
        bulk.append(Route(sems, 4 + part, at.sibling, g_both.at[0, some], g_both.at[1, some]))

    def passed(index, device, side, sent, j, got, sends=True, gets=True):
        there = window.at[slot(side, sent, j)]
        return Route(sems, index, device, there, there, sends, gets, window.at[slot(side, got, j)])

    up_0 = passed(6, at.above, OWN, z, 0, down)
    up_1 = passed(7, at.above, OWN, z, 1, down)
    down_0 = passed(8, at.below, OWN, z, 0, up)
    down_1 = passed(9, at.below, OWN, z, 1, up, z == 0, z == 3)
    far_0 = passed(10, at.below, OWN, up, 0, across)
    far_1 = passed(11, at.above, OWN, down, 1, across)

    def later(index, zc, j, when=True):
        here = window.at[slot(OWN, zc, j)]
        there = window.at[slot(BEFORE, zc, j)]
        sends = at.has_next if when is True else at.has_next & when
        gets = at.has_last if when is True else at.has_last & when
        return Route(sems, index, at.next, here, there, sends, gets)

    next_0 = later(12, z, 0)
    next_1 = later(13, z, 1)
    next_far_0 = later(14, across, 0, z < 2)
    next_far_1 = later(15, across, 1)
    last = at.has_last
    before_up_0 = passed(16, at.above, BEFORE, z, 0, down, last & (z == 3), last & (z == 0))
    before_up_1 = passed(17, at.above, BEFORE, z, 1, down, last, last)
    before_down_0 = passed(18, at.below, BEFORE, z, 0, up, last & (z != 0), last & (z != 3))
    before_down_1 = passed(19, at.below, BEFORE, z, 1, up, last, last)
    stats = Route(sems, 20, at.sibling, stat.at[0], stat.at[1])

    swap_k.arrived()
    swap_v.arrived()
    for copy in (up_1, down_0, next_1):
        copy.start()
    for copy in loads[2:]:
        copy.wait()

    ones = jnp.ones((8, W), jnp.bfloat16)
    for h in range(heads):
        cols = slice(h * W, (h + 1) * W)
        product = g_both[0, :, cols].astype(jnp.float32) * o_vmem[:, cols].astype(jnp.float32)
        high = product.astype(jnp.bfloat16)
        low = (product - high.astype(jnp.float32)).astype(jnp.bfloat16)
        total = nt(ones, high) + nt(ones, low)
        stat[0, 1, h : h + 1, :] = total[0:1]
    stat[0, 0] = stat[0, 0] * LOG2E
    stats.start()
    for copy in (next_0, up_0, down_1):
        copy.start()
    for copy in bulk:
        copy.start()

    ends = doc_ends(docs_ref)
    column = at.column * 16 * B
    dkv[...] = jnp.zeros_like(dkv)
    dqt[...] = jnp.zeros_like(dqt)

    def products(side, part, k, v, mask):
        here = pl.ds(pl.multiple_of(part * B, B), B)
        return gradients(
            k, v,
            [q_both[side, here, h * W : (h + 1) * W] for h in range(heads)],
            [g_both[side, here, h * W : (h + 1) * W] for h in range(heads)],
            [stat[side, 0, h : h + 1, here] for h in range(heads)],
            [stat[side, 1, h : h + 1, here] for h in range(heads)],
            mask,
        )

    up_1.arrived()
    far_1.start()
    down_0.arrived()
    far_0.start()
    next_1.arrived()
    before_down_1.start()
    before_up_1.start()
    next_0.arrived()
    before_down_0.start()
    before_up_0.start()

    near_4 = jnp.where(z > 0, slot(OWN, down, 1), slot(OWN, 3, 0))
    near_0 = jnp.where(z > 0, slot(OWN, down, 0), slot(BEFORE, 3, 1))

    def half_of(tile):
        return jnp.where((tile + 8) % 8 >= 4, 1 - core, core)

    def near(side, part, tile, keys, key_tiles, out):
        start = doc_start(ends, positions(column + tile * 2 * B + part * B))
        for n, key_tile in enumerate(key_tiles):
            key = column + key_tile * 2 * B + half_of(key_tile) * B
            kpos = (key + lax.broadcasted_iota(jnp.int32, (B, B), 0)).astype(jnp.float32)
            bias[n * B : (n + 1) * B] = jnp.where(kpos >= start, 0.0, -jnp.inf)
        dk, dv, dq = products(
            side, part,
            jnp.concatenate([window[n, 0] for n in keys], axis=0),
            jnp.concatenate([window[n, 1] for n in keys], axis=0),
            bias.at[: len(keys) * B],
        )
        for n in range(len(keys)):
            dkv[out + n, 0] += dk[n * B : (n + 1) * B]
            dkv[out + n, 1] += dv[n * B : (n + 1) * B]
        dqt[side * 2 + part] += dq

    puts = [
        pltpu.make_async_copy(source, target, put.at[n])
        for n, (source, target) in enumerate(
            (
                (q_both.at[1], q_other), (g_both.at[1], g_other), (stat, stat_both),
                (window.at[8:], window_out.at[8:]), (dqt.at[:2], dq_out.at[:2]),
                (window.at[:8], window_out.at[:8]), (dqt.at[2:], dq_out.at[2:]), (dkv, kv_out),
            )
        )
    ]

    def sibling_here():
        for copy in bulk:
            copy.arrived()
        stats.arrived()

    flip = (core == 0) & (z == 0)

    @pl.loop(0, 4)
    def _(n):
        @pl.when(n == 0)
        def _():
            up_0.arrived()
            pl.when(flip)(sibling_here)

        @pl.when(n == 1)
        def _():
            far_0.arrived()
            next_far_0.start()
            far_1.arrived()
            next_far_1.start()

        @pl.when(n == 2)
        def _():
            down_1.arrived()
            pl.when(jnp.logical_not(flip))(sibling_here)
            pl.when(z == 0)(before_up_1.arrived)
            for copy in puts[:4]:
                copy.start()

        side, part = jnp.where(flip, 1 - n // 2, n // 2), n % 2

        @pl.when(side == core)
        def _():
            near(side, part, z, [near_0], [z - 1], 2)

        @pl.when(side != core)
        def _():
            near(side, part, z + 4, [slot(OWN, z, 0), near_4], [z, z + 3], 0)

    for copy in (puts[4], puts[6], puts[7]):
        copy.start()
    pl.when(z != 0)(before_up_1.arrived)
    for copy in (before_up_0, before_down_0, before_down_1, next_far_0, next_far_1):
        copy.arrived()
    puts[5].start()
    for copy in (
        [swap_k, swap_v, up_0, up_1, down_0, down_1, far_0, far_1, next_0, next_1, next_far_0]
        + [next_far_1, before_up_0, before_up_1, before_down_0, before_down_1, stats]
        + bulk
    ):
        copy.sent()
    for copy in puts:
        copy.wait()


def gather(columns, docs, q, g, o, k, v, log_total):
    rows, features = q.shape
    heads = features // W
    some = pl.BlockSpec(memory_space=pl.ANY)
    window = (16, 2, B, W)
    stat = (2, 2, heads, rows)
    turned = (4, W, heads * B)
    sums = (3, 2, B, W)
    return pl.pallas_call(
        functools.partial(gather_kernel, columns, heads),
        out_shape=(
            jax.ShapeDtypeStruct(q.shape, q.dtype),
            jax.ShapeDtypeStruct(q.shape, q.dtype),
            jax.ShapeDtypeStruct(stat, jnp.float32),
            jax.ShapeDtypeStruct(window, k.dtype),
            jax.ShapeDtypeStruct(turned, jnp.float32),
            jax.ShapeDtypeStruct(sums, jnp.float32),
        ),
        in_specs=[pl.BlockSpec(memory_space=pltpu.VMEM)] + [some] * 6,
        out_specs=(some,) * 6,
        scratch_shapes=[
            pltpu.VMEM((2, rows, features), q.dtype),
            pltpu.VMEM((2, rows, features), q.dtype),
            pltpu.VMEM(q.shape, q.dtype),
            pltpu.VMEM(k.shape, k.dtype),
            pltpu.VMEM(k.shape, k.dtype),
            pltpu.VMEM(stat, jnp.float32),
            pltpu.VMEM(window, k.dtype),
            pltpu.VMEM(turned, jnp.float32),
            pltpu.VMEM(sums, jnp.float32),
            pltpu.VMEM((2 * B, B), jnp.float32),
            pltpu.SemaphoreType.DMA((6,)),
            pltpu.SemaphoreType.DMA((8,)),
            pltpu.SemaphoreType.DMA((21,)),
            pltpu.SemaphoreType.DMA((21,)),
        ],
        compiler_params=pltpu.CompilerParams(
            collective_id=0, has_side_effects=True, vmem_limit_bytes=VMEM
        ),
    )(docs, q, g, o, k, v, log_total)


def attend_kernel(
    heads, docs_ref, qa_hbm, qb_hbm, ga_hbm, gb_hbm, stat_hbm, window_hbm, dq_hbm, kv_hbm,
    dq_own, dq_other, part_hbm,
    q_ref, g_ref, stat_ref, window_ref, dqt, dqh, part_ref, dka, dva, dkv, bias, starts, bounds, get, put,
):
    column, z, core = place()
    loads = [
        pltpu.make_async_copy(source, target, get.at[n])
        for n, (source, target) in enumerate(
            (
                (stat_hbm, stat_ref),
                (window_hbm.at[:8], window_ref.at[:8]), (window_hbm.at[8:], window_ref.at[8:]),
                (kv_hbm, dkv), (qa_hbm, q_ref.at[0]), (ga_hbm, g_ref.at[0]),
                (qb_hbm, q_ref.at[1]), (gb_hbm, g_ref.at[1]), (dq_hbm.at[2:], dqt.at[2:]),
            )
        )
    ]
    for load in loads:
        load.start()
    ends = doc_ends(docs_ref)
    window = (column - 1) * 16 * B

    def half_of(b):
        return jnp.where(b % 8 >= 4, 1 - core, core)

    def tile_of(side):
        return z + 4 * (core if side == 0 else 1 - core)

    for block in range(4):
        side, part = divmod(block, 2)
        first = column * 16 * B + tile_of(side) * 2 * B + part * B
        start = doc_start(ends, positions(first))
        starts[block] = start
        low = jnp.min(start).astype(jnp.int32) - window
        last = jnp.max(start).astype(jnp.int32) - window
        b = low // (2 * B)
        bounds[0, block] = jnp.where(low % (2 * B) >= half_of(b) * B + B, b + 1, b)
        b = last // (2 * B)
        bounds[1, block] = jnp.where(last % (2 * B) > half_of(b) * B, b + 1, b)
    dka[...] = jnp.zeros_like(dka)
    dva[...] = jnp.zeros_like(dva)
    dqt[:2] = jnp.zeros((2, *dqt.shape[1:]), dqt.dtype)
    for load in loads[:6]:
        load.wait()
    down = lax.rem(z + 3, 4)
    nears = (
        slot(OWN, z, 0),
        jnp.where(z > 0, slot(OWN, down, 1), slot(OWN, 3, 0)),
        jnp.where(z > 0, slot(OWN, down, 0), slot(BEFORE, 3, 1)),
    )
    for n, at in enumerate(nears):
        dka[at] = dkv[n, 0]
        dva[at] = dkv[n, 1]

    @pl.loop(0, 4)
    def _(block):
        side, part = block // 2, block % 2
        here = pl.ds(pl.multiple_of(part * B, B), B)

        @pl.when(block == 2)
        def _():
            for load in loads[6:]:
                load.wait()

        def work(blocks, mask=None):
            at = [slot(b // 8, b % 4, b % 8 // 4) for b in blocks]
            dk, dv, dq = gradients(
                jnp.concatenate([window_ref[n, 0] for n in at], axis=0),
                jnp.concatenate([window_ref[n, 1] for n in at], axis=0),
                [q_ref[side, here, h * W : (h + 1) * W] for h in range(heads)],
                [g_ref[side, here, h * W : (h + 1) * W] for h in range(heads)],
                [stat_ref[side, 0, h : h + 1, here] for h in range(heads)],
                [stat_ref[side, 1, h : h + 1, here] for h in range(heads)],
                mask,
            )
            for n in range(len(at)):
                dva[at[n]] += dv[n * B : (n + 1) * B]
                dka[at[n]] += dk[n * B : (n + 1) * B]
            dqt[block] += dq

        second = jnp.where(side == 0, core, 1 - core)
        end = 7 + z + 4 * second
        skip = jnp.where(second == 1, 8 + z, 16)

        def counted(b):
            return jnp.where(b > skip, b - 1, b)

        def real(n):
            return jnp.where(n >= skip, n + 1, n)

        end = counted(end)
        low = counted(bounds[0, block])
        cut = jnp.minimum(counted(bounds[1, block]), end)
        cut = cut + (end - cut) % 2

        @pl.loop(low, cut)
        def _(n):
            b = real(n)
            key = window + b * 2 * B + half_of(b) * B
            kpos = (key + lax.broadcasted_iota(jnp.int32, (B, B), 0)).astype(jnp.float32)
            bias[...] = jnp.where(kpos >= starts[block], 0.0, -jnp.inf)
            work([b], bias)

        pairs = jnp.maximum(end - jnp.maximum(low, cut), 0) // 2
        odd = pairs % 2

        @pl.loop(0, odd)
        def _(n):
            work([real(cut), real(cut + 1)])

        @pl.loop(0, pairs // 2)
        def _(n):
            first = cut + 2 * odd + 4 * n
            work([real(first + m) for m in range(4)])

        @pl.when(side == 0)
        def _():
            pltpu.make_async_copy(dqt.at[block], dq_own.at[part], put.at[block]).start()

        @pl.when(side == 1)
        def _():
            dqh[part] = dqt[block].astype(jnp.bfloat16)
            pltpu.make_async_copy(dqh.at[part], dq_other.at[part], put.at[block]).start()

    @pl.loop(0, 16)
    def _(s):
        part_ref[s, 0] = (dka[s] * (1.0 / math.sqrt(W))).astype(jnp.bfloat16)
        part_ref[s, 1] = dva[s].astype(jnp.bfloat16)
        pltpu.make_async_copy(part_ref.at[s], part_hbm.at[s], put.at[4 + s]).start()

    for part in range(2):
        pltpu.make_async_copy(dqt.at[part], dq_own.at[part], put.at[part]).wait()
        pltpu.make_async_copy(dqh.at[part], dq_other.at[part], put.at[2 + part]).wait()
    for s in range(16):
        pltpu.make_async_copy(part_ref.at[s], part_hbm.at[s], put.at[4 + s]).wait()


def attend(docs, q, q_other, g, g_other, stat, window, dq, sums):
    rows, features = q.shape
    heads = features // W
    some = pl.BlockSpec(memory_space=pl.ANY)
    both = (2, rows, features)
    turned = (2, W, heads * B)
    return pl.pallas_call(
        functools.partial(attend_kernel, heads),
        out_shape=(
            jax.ShapeDtypeStruct(turned, jnp.float32),
            jax.ShapeDtypeStruct(turned, jnp.bfloat16),
            jax.ShapeDtypeStruct(window.shape, jnp.bfloat16),
        ),
        in_specs=[pl.BlockSpec(memory_space=pltpu.VMEM)] + [some] * 8,
        out_specs=(some,) * 3,
        scratch_shapes=[
            pltpu.VMEM(both, q.dtype),
            pltpu.VMEM(both, q.dtype),
            pltpu.VMEM(stat.shape, stat.dtype),
            pltpu.VMEM(window.shape, window.dtype),
            pltpu.VMEM((4, W, heads * B), jnp.float32),
            pltpu.VMEM(turned, jnp.bfloat16),
            pltpu.VMEM(window.shape, jnp.bfloat16),
            pltpu.VMEM((16, B, W), jnp.float32),
            pltpu.VMEM((16, B, W), jnp.float32),
            pltpu.VMEM(sums.shape, jnp.float32),
            pltpu.VMEM((B, B), jnp.float32),
            pltpu.VMEM((4, 1, B), jnp.float32),
            pltpu.SMEM((2, 4), jnp.int32),
            pltpu.SemaphoreType.DMA((9,)),
            pltpu.SemaphoreType.DMA((20,)),
        ],
        compiler_params=pltpu.CompilerParams(vmem_limit_bytes=VMEM),
        cost_estimate=pl.CostEstimate(
            flops=20 * 10 * heads * B * B * W, bytes_accessed=16 << 20, transcendentals=0
        ),
    )(docs, q, q_other, g, g_other, stat, window, dq, sums)


def return_kernel(
    columns, heads, docs_ref, q_hbm, k_hbm, v_hbm, g_hbm, stat_hbm, dq_near, dq_own, dq_other, part_ref,
    dq_hbm, own_hbm, got_hbm, rest_hbm,
    q_ref, k_ref, v_ref, g_ref, stat, dqt, dqn, dq_got, dq_out, own_half, rest, dka, dva, bias,
    part, across_got, beside_got, beside_sum, later_got, far_got, far_sum, near_sum,
    near_got, final, given_half, local, put, send, recv,
):
    at = Links(columns)
    z, core, up, down, across = at.z, at.core, at.up, at.down, at.across
    sems = (send, recv)
    load = pltpu.make_async_copy(part_ref.at[:8], part.at[:8], local.at[0])
    load_own = pltpu.make_async_copy(part_ref.at[8:], part.at[8:], local.at[1])
    load_dq = pltpu.make_async_copy(dq_near.at[:2], dqn, local.at[2])
    loads = [
        pltpu.make_async_copy(source, target, local.at[3 + n])
        for n, (source, target) in enumerate(
            (
                (q_hbm, q_ref), (g_hbm, g_ref), (k_hbm, k_ref), (v_hbm, v_ref),
                (stat_hbm.at[0], stat), (dq_own, dqt),
            )
        )
    ]
    for copy in (*loads, load, load_own, load_dq):
        copy.start()
    at.barrier(to_next=(at.next,), expect=at.has_last.astype(jnp.int32))
    has_next, has_last = at.has_next, at.has_last

    def given(side, zc, j):
        return part_ref.at[slot(side, zc, j)]

    def held(side, zc, j):
        return part[slot(side, zc, j)].astype(jnp.float32)

    far_back = [
        Route(
            sems, j, at.last, given(BEFORE, across, j), across_got.at[j],
            has_last & (z < 2) if j == 0 else has_last,
            has_next & (z < 2) if j == 0 else has_next,
        )
        for j in range(2)
    ]
    side_up = [
        Route(
            sems, 2 + j, at.above, given(BEFORE, up, j), beside_got.at[0, j],
            has_last & (z != 3) if j == 0 else has_last,
            has_last & (z != 0) if j == 0 else has_last,
        )
        for j in range(2)
    ]
    side_down = [
        Route(
            sems, 4 + j, at.below, given(BEFORE, down, j), beside_got.at[1, j],
            has_last & (z == 0) if j == 0 else has_last,
            has_last & (z == 3) if j == 0 else has_last,
        )
        for j in range(2)
    ]
    bulk = [
        Route(sems, 6 + n, at.sibling, dq_other.at[n], dq_got.at[n]) for n in range(2)
    ]
    back = [
        Route(sems, 8 + j, at.last, beside_sum.at[j], later_got.at[j], has_last, has_next)
        for j in range(2)
    ]
    far_up = Route(sems, 10, at.above, far_sum.at[0], far_got.at[0])
    far_down = Route(sems, 11, at.below, far_sum.at[1], far_got.at[1])
    near_up_0 = Route(sems, 12, at.above, near_sum.at[0], near_got.at[0])
    near_up_1 = Route(sems, 13, at.above, given(OWN, up, 1), near_got.at[1], z == 3, z == 0)
    near_down_0 = Route(sems, 14, at.below, given(OWN, down, 0), near_got.at[2])
    near_down_1 = Route(sems, 15, at.below, near_sum.at[1], near_got.at[3])

    for copy in (side_down[1], side_up[1], far_back[1], side_up[0], side_down[0], far_back[0]):
        copy.start()
    for copy in bulk:
        copy.start()
    for copy in loads:
        copy.wait()
    ends = doc_ends(docs_ref)
    tile = at.column * 16 * B + (z + 4 * core) * 2 * B
    dka[...] = jnp.zeros_like(dka)
    dva[...] = jnp.zeros_like(dva)

    def diagonal(n):
        block, b = (n + 1) // 2, n // 2
        here = pl.ds(pl.multiple_of(block * B, B), B)
        there = pl.ds(pl.multiple_of(b * B, B), B)
        pos = positions(tile + block * B)
        bias[...] = hidden(tile + b * B, doc_start(ends, pos), pos)
        dk, dv, dq = gradients(
            k_ref[there],
            v_ref[there],
            [q_ref[here, h * W : (h + 1) * W] for h in range(heads)],
            [g_ref[here, h * W : (h + 1) * W] for h in range(heads)],
            [stat[0, h : h + 1, here] for h in range(heads)],
            [stat[1, h : h + 1, here] for h in range(heads)],
            bias,
        )
        dka[b] += dk
        dva[b] += dv
        dqt[block] += dq

    pl.loop(0, 3)(diagonal)
    scale = 1.0 / math.sqrt(W)
    rest[0] = dka[1] * scale
    rest[1] = dva[1]
    out_rest = pltpu.make_async_copy(rest, rest_hbm, put.at[2])
    out_rest.start()
    for copy in (load, load_own, load_dq):
        copy.wait()

    @pl.when(has_last)
    def _():
        for copy in side_up + side_down:
            copy.arrived()
        for j in range(2):
            final[j] = held(BEFORE, z, j)
        final[1] += beside_got[0, 1].astype(jnp.float32) + beside_got[1, 1].astype(jnp.float32)

        @pl.when(z != 0)
        def _():
            final[0] += beside_got[0, 0].astype(jnp.float32)

        @pl.when(z == 3)
        def _():
            final[0] += beside_got[1, 0].astype(jnp.float32)

        beside_sum[...] = final[...].astype(jnp.bfloat16)
        for copy in back:
            copy.start()

    def add_across(j):
        far_back[j].make(across_got.at[j]).wait_recv()
        final[j] += across_got[j].astype(jnp.float32)

    for j in range(2):
        final[j] = held(OWN, across, j)
        pl.when(far_back[j].gets)(functools.partial(add_across, j))
        far_sum[j] = final[j].astype(jnp.bfloat16)
    for copy in (far_up, far_down, near_down_0, near_up_1):
        copy.start()
    for copy in bulk:
        copy.arrived()
    eye = identity(B)
    for block in range(2):
        for h in range(heads):
            rows = slice(h * B, (h + 1) * B)
            total = dqt[block, :, rows] + dqn[block, :, rows]
            total = total + dq_got[block, :, rows].astype(jnp.float32)
            rounded = (total * (1.0 / math.sqrt(W))).astype(jnp.bfloat16)
            turned = nt(eye, rounded).astype(jnp.bfloat16)
            dq_out[block * B : (block + 1) * B, h * W : (h + 1) * W] = turned
    out_q = pltpu.make_async_copy(dq_out, dq_hbm, put.at[0])
    out_q.start()
    far_up.arrived()
    near_sum[0] = (held(OWN, up, 0) + far_got[0].astype(jnp.float32)).astype(jnp.bfloat16)
    near_up_0.start()
    far_down.arrived()
    near_sum[1] = (held(OWN, down, 1) + far_got[1].astype(jnp.float32)).astype(jnp.bfloat16)
    near_down_1.start()
    near_down_0.arrived()
    near_up_0.arrived()
    final[0] = (
        held(OWN, z, 0) + near_got[0].astype(jnp.float32) + near_got[2].astype(jnp.float32)
    )
    near_down_1.arrived()
    final[1] = held(OWN, z, 1) + near_got[3].astype(jnp.float32)

    @pl.when(z == 0)
    def _():
        near_up_1.make(near_got.at[1]).wait_recv()
        final[1] += near_got[1].astype(jnp.float32)

    @pl.when(has_next)
    def _():
        for j in range(2):
            back[j].make(later_got.at[j]).wait_recv()
            final[j] += later_got[j].astype(jnp.float32)

    given_half[...] = final[1 - core].astype(jnp.bfloat16)
    give = Route(sems, 16, at.sibling, given_half, got_hbm)
    give.start()
    own_half[0] = (final[core, 0] + dka[0] * scale).astype(jnp.bfloat16)
    own_half[1] = (final[core, 1] + dva[0]).astype(jnp.bfloat16)
    out_own = pltpu.make_async_copy(own_half, own_hbm, put.at[1])
    out_own.start()
    give.arrived()
    for copy in (out_q, out_own, out_rest):
        copy.wait()
    for copy in (
        far_back + side_up + side_down + bulk + back
        + [far_up, far_down, near_up_0, near_up_1, near_down_0, near_down_1, give]
    ):
        copy.sent()


def give_back(columns, docs, q, k, v, g, stat, dq_near, dq_own, dq_other, part):
    rows, features = q.shape
    heads = features // W
    some = pl.BlockSpec(memory_space=pl.ANY)
    vmem = pl.BlockSpec(memory_space=pltpu.VMEM)
    block = (2, B, W)
    return pl.pallas_call(
        functools.partial(return_kernel, columns, heads),
        out_shape=(
            jax.ShapeDtypeStruct((rows, features), jnp.bfloat16),
            jax.ShapeDtypeStruct(block, jnp.bfloat16),
            jax.ShapeDtypeStruct(block, jnp.bfloat16),
            jax.ShapeDtypeStruct(block, jnp.float32),
        ),
        in_specs=[vmem] + [some] * 9,
        out_specs=(some,) * 4,
        scratch_shapes=[
            pltpu.VMEM(q.shape, q.dtype),
            pltpu.VMEM(k.shape, k.dtype),
            pltpu.VMEM(v.shape, v.dtype),
            pltpu.VMEM(g.shape, g.dtype),
            pltpu.VMEM(stat.shape[1:], stat.dtype),
            pltpu.VMEM(dq_own.shape, dq_own.dtype),
            pltpu.VMEM(dq_own.shape, dq_own.dtype),
            pltpu.VMEM(dq_other.shape, dq_other.dtype),
            pltpu.VMEM(q.shape, jnp.bfloat16),
            pltpu.VMEM(block, jnp.bfloat16),
            pltpu.VMEM(block, jnp.float32),
            pltpu.VMEM((2, B, W), jnp.float32),
            pltpu.VMEM((2, B, W), jnp.float32),
            pltpu.VMEM((B, B), jnp.float32),
            pltpu.VMEM((16, *block), jnp.bfloat16),
            pltpu.VMEM((2, *block), jnp.bfloat16),
            pltpu.VMEM((2, 2, *block), jnp.bfloat16),
            pltpu.VMEM((2, *block), jnp.bfloat16),
            pltpu.VMEM((2, *block), jnp.bfloat16),
            pltpu.VMEM((2, *block), jnp.bfloat16),
            pltpu.VMEM((2, *block), jnp.bfloat16),
            pltpu.VMEM((2, *block), jnp.bfloat16),
            pltpu.VMEM((4, *block), jnp.bfloat16),
            pltpu.VMEM((2, *block), jnp.float32),
            pltpu.VMEM(block, jnp.bfloat16),
            pltpu.SemaphoreType.DMA((9,)),
            pltpu.SemaphoreType.DMA((3,)),
            pltpu.SemaphoreType.DMA((18,)),
            pltpu.SemaphoreType.DMA((18,)),
        ],
        compiler_params=pltpu.CompilerParams(
            collective_id=1, has_side_effects=True, vmem_limit_bytes=VMEM
        ),
    )(docs, q, k, v, g, stat, dq_near, dq_own, dq_other, part)


def publish_kernel(
    dq_ref, own_ref, got_ref, rest_ref, dq_out, dk_out, dv_out,
    dq, own, got, rest, dk, dv, get, put,
):
    loads, outs = [], []
    for n in range(4):
        here = slice(n * B // 2, (n + 1) * B // 2)
        loads.append(pltpu.make_async_copy(dq_ref.at[here], dq.at[here], get.at[n]))
        outs.append(pltpu.make_async_copy(dq.at[here], dq_out.at[here], put.at[n]))
    for n, (source, target) in enumerate(((own_ref, own), (got_ref, got), (rest_ref, rest))):
        loads.append(pltpu.make_async_copy(source, target, get.at[4 + n]))
    outs.append(pltpu.make_async_copy(dk, dk_out, put.at[4]))
    outs.append(pltpu.make_async_copy(dv, dv_out, put.at[5]))
    for copy in loads:
        copy.start()
    for load, out in zip(loads[:4], outs[:4]):
        load.wait()
        out.start()
    for copy in loads[4:]:
        copy.wait()
    for n, target in enumerate((dk, dv)):
        target[:B] = own[n]
        target[B:] = (got[n].astype(jnp.float32) + rest[n]).astype(jnp.bfloat16)
    for copy in outs[4:]:
        copy.start()
    for copy in outs:
        copy.wait()


def publish(dq, own, got, rest):
    some = pl.BlockSpec(memory_space=pl.ANY)
    keys = (2 * B, W)
    return pl.pallas_call(
        publish_kernel,
        out_shape=(
            jax.ShapeDtypeStruct(dq.shape, dq.dtype),
            jax.ShapeDtypeStruct(keys, jnp.bfloat16),
            jax.ShapeDtypeStruct(keys, jnp.bfloat16),
        ),
        in_specs=[some] * 4,
        out_specs=(some,) * 3,
        scratch_shapes=[pltpu.VMEM(x.shape, x.dtype) for x in (dq, own, got, rest)]
        + [pltpu.VMEM(keys, jnp.bfloat16)] * 2
        + [pltpu.SemaphoreType.DMA((7,)), pltpu.SemaphoreType.DMA((6,))],
        compiler_params=pltpu.CompilerParams(vmem_limit_bytes=VMEM),
    )(dq, own, got, rest)


def solution(mesh):
    columns = mesh.shape["ctx"] // 2

    def on_device(q, k, v, o, g, log_total, doc_lengths):
        docs = doc_lengths[None, :]
        q_other, g_other, stat, window, dq, sums = gather(columns, docs, q, g, o, k, v, log_total)
        dq_own, dq_other, part = attend(docs, q, q_other, g, g_other, stat, window, dq, sums)
        return publish(*give_back(columns, docs, q, k, v, g, stat, dq, dq_own, dq_other, part))

    rows = P(("ctx", "section"), None)
    return jax.shard_map(
        on_device,
        mesh=mesh,
        in_specs=(rows, rows, rows, rows, rows, P(None, ("ctx", "section")), P()),
        out_specs=(rows, rows, rows),
        check_vma=False,
    )
```
